32 devices in a mesh: seq: 4 (over y, x), fsdp: 8 (over z, core).
Axes of the slice: x: 2, y: 2, z: 4, core: 2. Of those that a mesh axis runs over, the one named last changes fastest.
Arguments:
- tokens: bfloat16 [16, 1024, 2048], P('fsdp', 'seq'), may hold values from -6 to 6
- cotangent: bfloat16 [16, 1024, 2048], P('fsdp', 'seq'), may hold values from -6 to 6
- lengths: int32 [16], P('fsdp'), may hold values from 256 to 1024, as said below
- attn_gain: float32 [2048], replicated, may hold values from 0.25 to 1.75
- query_weight: bfloat16 [2048, 2048], P('fsdp'), may hold values from -0.125 to 0.125
- key_weight: bfloat16 [2048, 512], P('fsdp'), may hold values from -0.125 to 0.125
- value_weight: bfloat16 [2048, 512], P('fsdp'), may hold values from -0.125 to 0.125
- query_gain: float32 [64], replicated, may hold values from 0.25 to 1.75
- key_gain: float32 [64], replicated, may hold values from 0.25 to 1.75
- out_weight: bfloat16 [2048, 2048], P('fsdp'), may hold values from -0.375 to 0.375
- ffn_gain: float32 [2048], replicated, may hold values from 0.25 to 1.75
- gate_weight: bfloat16 [8192, 2048], P('fsdp'), may hold values from -0.125 to 0.125
- up_weight: bfloat16 [8192, 2048], P('fsdp'), may hold values from -0.125 to 0.125
- down_weight: bfloat16 [8192, 2048], P('fsdp'), may hold values from -0.0625 to 0.0625
Outputs:
- output: bfloat16 [16, 1024, 2048], P('fsdp', 'seq')
- grad_tokens: bfloat16 [16, 1024, 2048], P('fsdp', 'seq')
- grad_attn_gain: float32 [2048], P('fsdp')
- grad_query_weight: float32 [2048, 2048], P('fsdp')
- grad_key_weight: float32 [2048, 512], P('fsdp')
- grad_value_weight: float32 [2048, 512], P('fsdp')
- grad_query_gain: float32 [64], P('fsdp')
- grad_key_gain: float32 [64], P('fsdp')
- grad_out_weight: float32 [2048, 2048], P('fsdp')
- grad_ffn_gain: float32 [2048], P('fsdp')
- grad_gate_weight: float32 [8192, 2048], P('fsdp')
- grad_up_weight: float32 [8192, 2048], P('fsdp')
- grad_down_weight: float32 [8192, 2048], P('fsdp')
The draws below stay inside these ranges and needn't reach their ends.
Inputs may be any that keep to these rules, and one draw needn't show every extreme that they name: `lengths`: of the 2 slots of each index of fsdp, one, which one drawn from the seed, holds 1024 valid tokens.
All inputs are finite; a program needn't handle non-finite values.
Results may differ from the reference program's by a relative error of at most 0.02.
Values may be sent and summed in bfloat16 or wider, within the bound.
A program may use at most 768 MiB of HBM per device.

```python
import jax
import jax.numpy as jnp
from jax import lax

D = 2048
HEADS = 32
KV = 8
HEAD = 64
FF = 8192
SLOT = 1024
SLOTS = 2
BATCH = 16
N_FSDP = 8


def draw_lengths(key, part):
    key = jax.random.fold_in(key, 7)
    pick_key, size_key = jax.random.split(key)
    pair_count = BATCH // SLOTS
    full_slot = jax.random.randint(pick_key, (pair_count, 1), 0, SLOTS)
    other_len = jax.random.randint(size_key, (pair_count, SLOTS), SLOT // 4, SLOT + 1)
    slot_ids = jnp.arange(SLOTS, dtype=jnp.int32)[None, :]
    return jnp.where(slot_ids == full_slot, SLOT, other_len).reshape(BATCH).astype(jnp.int32)


def levels(stream_key, extent, cuts, smallest, high):
    loudness = 1.0
    for position, shards_of in cuts:
        steps = jax.random.uniform(jax.random.fold_in(jax.random.fold_in(stream_key, 6), position), (shards_of,), jnp.float32, smallest / len(cuts), high / len(cuts))
        loudness = loudness * jnp.repeat(jnp.exp(steps), extent[position] // shards_of).reshape((-1,) + (1,) * (len(extent) - 1 - position))
    return loudness


def scatter_about(own_key, dims, spread, limit, cuts=(), kind=jnp.bfloat16):
    gain = levels(own_key, dims, cuts, -0.22, 0.18) if cuts else 1.0
    drawn = jax.random.normal(own_key, dims, jnp.float32) * spread * gain
    return jnp.minimum(jnp.maximum(drawn, -limit), limit).astype(kind)


def setup_inputs(seed: int = 0) -> dict:
    key_list = jax.random.split(jax.random.key(seed), 15)
    return {
        "tokens": scatter_about(key_list[0], (BATCH, SLOT, D), 1.0, 6.0, ((0, 8), (1, 4))),
        "cotangent": scatter_about(key_list[1], (BATCH, SLOT, D), 1.0, 6.0, ((0, 8), (1, 4))),
        "lengths": draw_lengths(jax.random.fold_in(key_list[14], 71), 0),
        "attn_gain": jnp.clip(1.0 + 0.15 * jax.random.normal(key_list[3], (D,), jnp.float32), 0.25, 1.75),
        "query_weight": scatter_about(key_list[4], (D, HEADS * HEAD), D ** -0.5, 0.125, ((0, 8),)),
        "key_weight": scatter_about(key_list[5], (D, KV * HEAD), D ** -0.5, 0.125, ((0, 8),)),
        "value_weight": scatter_about(key_list[6], (D, KV * HEAD), D ** -0.5, 0.125, ((0, 8),)),
        "query_gain": jnp.clip(1.0 + 0.15 * jax.random.normal(key_list[7], (HEAD,), jnp.float32), 0.25, 1.75),
        "key_gain": jnp.clip(1.0 + 0.15 * jax.random.normal(key_list[8], (HEAD,), jnp.float32), 0.25, 1.75),
        "out_weight": scatter_about(key_list[9], (HEADS * HEAD, D), (HEAD * 4) ** -0.5, 0.375, ((0, 8),)),
        "ffn_gain": jnp.clip(1.0 + 0.15 * jax.random.normal(key_list[10], (D,), jnp.float32), 0.25, 1.75),
        "gate_weight": scatter_about(key_list[11], (FF, D), D ** -0.5, 0.125, ((0, 8),)),
        "up_weight": scatter_about(key_list[12], (FF, D), D ** -0.5, 0.125, ((0, 8),)),
        "down_weight": scatter_about(key_list[13], (FF, D), FF ** -0.5, 0.0625, ((0, 8),)),
    }


@jax.custom_vjp
def low(v):
    return lax.optimization_barrier(v.astype(jnp.bfloat16)).astype(jnp.float32)

@jax.custom_vjp
def low_back(v):
    return v

def low_keep(v):
    return (low(v), None)

def low_pass(kept, grad):
    return (grad,)

def back_keep(v):
    return (v, None)

def back_low(kept, grad):
    return (low(grad),)
low.defvjp(low_keep, low_pass)
low_back.defvjp(back_keep, back_low)
EPSILON = 1e-05
ROPE_BASE = 1000000.0
NEGATIVE = -1e+30
HIGHEST = lax.Precision.HIGHEST

def normed(values, gain_vec):
    return values * lax.rsqrt(lax.optimization_barrier(jnp.mean(values * values, axis=-1, keepdims=True)) + EPSILON) * gain_vec

def rotate(values):
    length = values.shape[1]
    head_width = values.shape[-1]
    half_width = head_width // 2
    places = jnp.arange(length, dtype=jnp.float32)
    freqs = ROPE_BASE ** (-(jnp.arange(half_width, dtype=jnp.float32) * 2.0) / head_width)
    angles = places[:, None] * freqs[None, :]
    shaped = (1, length) + (1,) * (values.ndim - 3) + (half_width,)
    cosine = jnp.cos(angles).reshape(shaped)
    sine = jnp.sin(angles).reshape(shaped)
    front = values[..., :half_width]
    behind = values[..., half_width:]
    return jnp.concatenate([front * cosine - behind * sine, behind * cosine + front * sine], axis=-1)

def prepare(raw_heads, gain_vec):
    return rotate(normed(raw_heads, gain_vec))

def block_forward(inputs, live_mask, allowed, weights):
    attn_gain, query_weight, key_weight, value_weight, query_gain, key_gain, out_weight, ffn_gain, gate_weight, up_weight, down_weight = weights
    slot_count = inputs.shape[0]
    length = inputs.shape[1]
    normal_in = low(normed(inputs, attn_gain))
    q_raw = low(low_back(jnp.einsum('bsd,de->bse', normal_in, query_weight, precision=HIGHEST)))
    k_raw = low(low_back(jnp.einsum('bsd,de->bse', normal_in, key_weight, precision=HIGHEST)))
    v_raw = low(low_back(jnp.einsum('bsd,de->bse', normal_in, value_weight, precision=HIGHEST)))
    queries = low(prepare(q_raw.reshape(slot_count, length, HEADS, HEAD), query_gain))
    queries = queries.reshape(slot_count, length, KV, HEADS // KV, HEAD)
    keys = low(prepare(k_raw.reshape(slot_count, length, KV, HEAD), key_gain))
    values = v_raw.reshape(slot_count, length, KV, HEAD)
    scores = low_back(jnp.einsum('bqhgd,bkhd->bhgqk', queries, keys, precision=HIGHEST))
    logits = jnp.where(allowed[:, None, None], scores * HEAD ** (-0.5), NEGATIVE)
    probs = low(jax.nn.softmax(logits, axis=-1))
    attended = low(low_back(jnp.einsum('bhgqk,bkhd->bqhgd', probs, values, precision=HIGHEST)))
    attended = attended.reshape(slot_count, length, HEADS * HEAD)
    hidden_res = inputs + low_back(jnp.einsum('bse,ed->bsd', attended, out_weight, precision=HIGHEST))
    normal_mid = low(normed(hidden_res, ffn_gain))
    gate_vals = low_back(jnp.einsum('bsd,fd->bsf', normal_mid, gate_weight, precision=HIGHEST))
    up_vals = low_back(jnp.einsum('bsd,fd->bsf', normal_mid, up_weight, precision=HIGHEST))
    mids = low(jax.nn.silu(gate_vals) * up_vals)
    ffn_out = low_back(jnp.einsum('bsf,fd->bsd', mids, down_weight, precision=HIGHEST))
    return live_mask[..., None] * (hidden_res + ffn_out)

def reference(tokens, cotangent, lengths, attn_gain, query_weight, key_weight, value_weight, query_gain, key_gain, out_weight, ffn_gain, gate_weight, up_weight, down_weight):
    weights = tuple((array_in.astype(jnp.float32) for array_in in (attn_gain, query_weight, key_weight, value_weight, query_gain, key_gain, out_weight, ffn_gain, gate_weight, up_weight, down_weight)))
    places = jnp.arange(SLOT, dtype=jnp.int32)
    inputs = tokens.astype(jnp.float32).reshape(N_FSDP, SLOTS, SLOT, D)
    grads_in = cotangent.astype(jnp.float32).reshape(N_FSDP, SLOTS, SLOT, D)
    slot_lengths = lengths.astype(jnp.int32).reshape(N_FSDP, SLOTS)

    def group_step(running, group_data):
        group_in, group_grad, group_len = group_data
        live_mask = (places[None, :] < group_len[:, None]).astype(jnp.float32)
        allowed = (places[None, :] <= places[:, None])[None] & (places[None, None, :] < group_len[:, None, None])
        result, pull_back = jax.vjp(lambda inner_in, inner_wts: block_forward(inner_in, live_mask, allowed, inner_wts), group_in, weights)
        grad_in, grad_weights = pull_back(group_grad)
        running = tuple((first_term + second_term for first_term, second_term in zip(running, grad_weights)))
        return (running, (result.astype(jnp.bfloat16), grad_in.astype(jnp.bfloat16)))
    initial = tuple((jnp.zeros_like(array_in) for array_in in weights))
    totals, (outputs, grad_rows) = lax.scan(group_step, initial, (inputs, grads_in, slot_lengths))
    return (outputs.reshape(BATCH, SLOT, D), grad_rows.reshape(BATCH, SLOT, D), totals[0], totals[1], totals[2], totals[3], totals[4], totals[5], totals[6], totals[7], totals[8], totals[9], totals[10])
```

```python
import functools

import jax
import jax.numpy as jnp
import numpy as np
from jax import lax
from jax.experimental import pallas as pl
from jax.experimental.pallas import tpu as pltpu
from jax.sharding import PartitionSpec as P

EPSILON = 1e-05
ROPE_BASE = 1000000.0
NEGATIVE = -1e30
F32 = jnp.float32
BF16 = jnp.bfloat16
NN = (((1,), (0,)), ((), ()))
NT = (((1,), (1,)), ((), ()))
TN = (((0,), (0,)), ((), ()))
SMEM = pl.BlockSpec(memory_space=pltpu.SMEM)
VMEM = pl.BlockSpec(memory_space=pltpu.VMEM)
VMEM_LIMIT = 58 << 20
HEAD = 64
BLOCK = 256
CHUNKS = 2


def dot(a, b, dims=NN):
    return lax.dot_general(a, b, dims, preferred_element_type=F32)


def partner(v):
    lane = lax.broadcasted_iota(jnp.int32, v.shape, 1)
    return jnp.where(lane % HEAD < HEAD // 2, pltpu.roll(v, 96, 1), pltpu.roll(v, 32, 1))


def head_mean(v, ones):
    high = v.astype(BF16)
    rest = (v - high.astype(F32)).astype(BF16)
    return dot(high, ones) + dot(rest, ones)


def prepare_heads(sizes, place, qkv_ref, qg_ref, kg_ref, cos_ref, sin_ref, ones, q_s, k_s, v_s):
    hq, hkv, _ = sizes
    seqs, rows_in, _ = qkv_ref.shape
    for c in range(seqs):
        j = jnp.bitwise_xor(place, c)
        rows = slice(c * rows_in, (c + 1) * rows_in)
        cos = cos_ref[rows, :]
        sin = sin_ref[rows, :]
        for p in range((hq + hkv) // 2):
            is_query = p < hq // 2
            x = qkv_ref[j, :, p * 128 : (p + 1) * 128].astype(F32)
            gain = qg_ref[...] * HEAD**-0.5 if is_query else kg_ref[...]
            y = x * lax.rsqrt(head_mean(x * x, ones) + EPSILON) * gain
            y = (y * cos + partner(y) * sin).astype(BF16)
            for t in range(2):
                part = y[:, t * HEAD : (t + 1) * HEAD]
                if is_query:
                    q_s[2 * p + t, rows, :] = part
                else:
                    k_s[2 * p - hq + t, rows, :] = part
        for t in range(hkv):
            start = (hq + hkv + t) * HEAD
            v_s[t, rows, :] = qkv_ref[j, :, start : start + HEAD]


def allowed_keys(block, first, keys, length):
    bound = jnp.minimum(first + lax.broadcasted_iota(jnp.int32, (block, 1), 0), length - 1)
    return lax.broadcasted_iota(jnp.int32, (block, keys), 1) <= bound


def attend_kernel(
    sizes, place_ref, len_ref, qkv_ref, qg_ref, kg_ref, cos_ref, sin_ref, ones_ref,
    out_ref, lse_ref, q_s, k_s, v_s, o_s,
):
    hq, hkv, group = sizes
    seqs, rows_in, _ = qkv_ref.shape
    place = place_ref[0]
    prepare_heads(
        sizes, place, qkv_ref, qg_ref, kg_ref, cos_ref, sin_ref, ones_ref[...], q_s, k_s, v_s
    )
    for i in range(seqs * rows_in // BLOCK):
        keys = (i + 1) * BLOCK
        rows = slice(i * BLOCK, (i + 1) * BLOCK)
        keep = allowed_keys(BLOCK, i * BLOCK, keys, len_ref[0])

        def one_head(h, _):
            kv = h // group
            scores = dot(q_s[h, rows, :], k_s[kv, :keys, :], NT)
            scores = jnp.where(keep, scores, NEGATIVE)
            highest = jnp.max(scores, axis=1, keepdims=True)
            shifted = jnp.exp(scores - highest)
            total = jnp.sum(shifted, axis=1, keepdims=True)
            mixed = dot(shifted.astype(BF16), v_s[kv, :keys, :]) / total
            o_s[h, rows, :] = mixed.astype(BF16)
            lse_ref[h, rows, :] = highest + jnp.log(total)
            return 0

        lax.fori_loop(0, hq, one_head, 0)
    for c in range(seqs):
        j = jnp.bitwise_xor(place, c)
        rows = slice(c * rows_in, (c + 1) * rows_in)
        for p in range(hq // 2):
            out_ref[j, :, p * 128 : (p + 1) * 128] = jnp.concatenate(
                [o_s[2 * p, rows, :], o_s[2 * p + 1, rows, :]], axis=1
            )


def attend_back_kernel(
    sizes, place_ref, len_ref, qkv_ref, cot_ref, lse_ref, qg_ref, kg_ref, cos_ref, sin_ref,
    ones_ref, dqkv_ref, dgain_ref, q_s, k_s, v_s, cot_s, dq_s, dk_s, dv_s,
):
    hq, hkv, group = sizes
    seqs, rows_in, _ = qkv_ref.shape
    place = place_ref[0]
    ones = ones_ref[...]
    prepare_heads(sizes, place, qkv_ref, qg_ref, kg_ref, cos_ref, sin_ref, ones, q_s, k_s, v_s)
    for c in range(seqs):
        j = jnp.bitwise_xor(place, c)
        for h in range(hq):
            cot_s[h, c * rows_in : (c + 1) * rows_in, :] = cot_ref[
                j, :, h * HEAD : (h + 1) * HEAD
            ]
    dk_s[...] = jnp.zeros_like(dk_s)
    dv_s[...] = jnp.zeros_like(dv_s)
    for i in range(seqs * rows_in // BLOCK):
        keys = (i + 1) * BLOCK
        rows = slice(i * BLOCK, (i + 1) * BLOCK)
        keep = allowed_keys(BLOCK, i * BLOCK, keys, len_ref[0])

        def one_head(h, _):
            kv = h // group
            q = q_s[h, rows, :]
            cot = cot_s[h, rows, :]
            k = k_s[kv, :keys, :]
            scores = jnp.where(keep, dot(q, k, NT), NEGATIVE)
            probs = jnp.exp(scores - lse_ref[h, rows, :])
            prob_cot = dot(cot, v_s[kv, :keys, :], NT)
            inner = jnp.sum(probs * prob_cot, axis=1, keepdims=True)
            score_cot = (probs * (prob_cot - inner)).astype(BF16)
            dq_s[h, rows, :] = dot(score_cot, k) * HEAD**-0.5
            dk_s[kv, :keys, :] += dot(score_cot, q, TN)
            dv_s[kv, :keys, :] += dot(probs.astype(BF16), cot, TN)
            return 0

        lax.fori_loop(0, hq, one_head, 0)
    gain_sums = [jnp.zeros((1, 128), F32), jnp.zeros((1, 128), F32)]
    for c in range(seqs):
        j = jnp.bitwise_xor(place, c)
        rows = slice(c * rows_in, (c + 1) * rows_in)
        cos = cos_ref[rows, :]
        sin = sin_ref[rows, :]
        for p in range((hq + hkv) // 2):
            is_query = p < hq // 2
            x = qkv_ref[j, :, p * 128 : (p + 1) * 128].astype(F32)
            gain = qg_ref[...] if is_query else kg_ref[...]
            source, first = (dq_s, 2 * p) if is_query else (dk_s, 2 * p - hq)
            turned = jnp.concatenate([source[first, rows, :], source[first + 1, rows, :]], axis=1)
            scale = lax.rsqrt(head_mean(x * x, ones) + EPSILON)
            straight = turned * cos + partner(turned * sin)
            unit = x * scale
            which = 0 if is_query else 1
            gain_sums[which] += jnp.sum(straight * unit, axis=0, keepdims=True)
            pulled = gain * straight
            dx = scale * (pulled - unit * head_mean(unit * pulled, ones))
            dqkv_ref[j, :, p * 128 : (p + 1) * 128] = dx.astype(BF16)
        for p in range(hkv // 2):
            start = (hq + hkv) * HEAD + p * 128
            dqkv_ref[j, :, start : start + 128] = jnp.concatenate(
                [dv_s[2 * p, rows, :], dv_s[2 * p + 1, rows, :]], axis=1
            ).astype(BF16)
    dgain_ref[0:1, :] = gain_sums[0]
    dgain_ref[1:2, :] = gain_sums[1]


def position_tables(length):
    places = np.arange(length, dtype=np.float32)
    half = HEAD // 2
    freqs = np.float32(ROPE_BASE) ** (-(np.arange(half, dtype=np.float32) * 2.0) / HEAD)
    angles = places[:, None] * freqs.astype(np.float32)[None, :]
    cos = np.cos(angles).astype(np.float32)
    sin = np.sin(angles).astype(np.float32)
    ones = np.kron(np.eye(2), np.ones((HEAD, HEAD)) / HEAD)
    return (
        jnp.asarray(np.concatenate([cos] * 4, axis=1)),
        jnp.asarray(np.concatenate([-sin, sin, -sin, sin], axis=1)),
        jnp.asarray(ones, dtype=BF16),
    )


def attend(sizes, place, length, qkv, gains, tables):
    seqs, rows_in, _ = qkv.shape
    hq, hkv, _ = sizes
    slot = seqs * rows_in
    return pl.pallas_call(
        functools.partial(attend_kernel, sizes),
        out_shape=(
            jax.ShapeDtypeStruct((seqs, rows_in, hq * HEAD), BF16),
            jax.ShapeDtypeStruct((hq, slot, 1), F32),
        ),
        in_specs=[SMEM, SMEM] + [VMEM] * 6,
        out_specs=(VMEM, VMEM),
        scratch_shapes=[
            pltpu.VMEM((hq, slot, HEAD), BF16),
            pltpu.VMEM((hkv, slot, HEAD), BF16),
            pltpu.VMEM((hkv, slot, HEAD), BF16),
            pltpu.VMEM((hq, slot, HEAD), BF16),
        ],
        compiler_params=pltpu.CompilerParams(vmem_limit_bytes=VMEM_LIMIT),
        cost_estimate=pl.CostEstimate(
            flops=20 * hq * slot * slot * HEAD, bytes_accessed=1 << 23, transcendentals=0
        ),
        name="attend",
    )(place, length, qkv, *gains, *tables)


def attend_back(sizes, place, length, qkv, cot, lse, gains, tables):
    seqs, rows_in, width = qkv.shape
    hq, hkv, _ = sizes
    slot = seqs * rows_in
    return pl.pallas_call(
        functools.partial(attend_back_kernel, sizes),
        out_shape=(
            jax.ShapeDtypeStruct((seqs, rows_in, width), BF16),
            jax.ShapeDtypeStruct((2, 128), F32),
        ),
        in_specs=[SMEM, SMEM] + [VMEM] * 8,
        out_specs=(VMEM, VMEM),
        scratch_shapes=[
            pltpu.VMEM((hq, slot, HEAD), BF16),
            pltpu.VMEM((hkv, slot, HEAD), BF16),
            pltpu.VMEM((hkv, slot, HEAD), BF16),
            pltpu.VMEM((hq, slot, HEAD), BF16),
            pltpu.VMEM((hq, slot, HEAD), F32),
            pltpu.VMEM((hkv, slot, HEAD), F32),
            pltpu.VMEM((hkv, slot, HEAD), F32),
        ],
        compiler_params=pltpu.CompilerParams(vmem_limit_bytes=VMEM_LIMIT),
        cost_estimate=pl.CostEstimate(
            flops=36 * hq * slot * slot * HEAD, bytes_accessed=1 << 23, transcendentals=0
        ),
        name="attend_back",
    )(place, length, qkv, cot, lse, *gains, *tables)


def ffn_kernel(has_sum, mid_ref, cot_ref, gate_ref, up_ref, down_ref, *refs):
    if has_sum:
        sum_ref, acts_ref, pull_ref = refs
    else:
        acts_ref, pull_ref = refs
    model = mid_ref.shape[-1]
    hidden = acts_ref.shape[-1]
    gate_w = gate_ref[...].reshape(hidden, model)
    up_w = up_ref[...].reshape(hidden, model)
    down_w = down_ref[...].reshape(hidden, model)
    mid = mid_ref[...]
    gate = dot(mid, gate_w, NT)
    up = dot(mid, up_w, NT)
    mids_cot = dot(cot_ref[...], down_w, NT)
    sigmoid = jax.nn.sigmoid(gate)
    active = gate * sigmoid
    gate_cot = (mids_cot * up * sigmoid * (1.0 + gate * (1.0 - sigmoid))).astype(BF16)
    up_cot = (mids_cot * active).astype(BF16)
    acts_ref[0] = gate_cot
    acts_ref[1] = up_cot
    acts_ref[2] = (active * up).astype(BF16)
    pulled = dot(gate_cot, gate_w) + dot(up_cot, up_w)
    if has_sum:
        pulled = pulled + sum_ref[...]
    pull_ref[...] = pulled.astype(pull_ref.dtype)


def ffn_both(mid, cot, weights, summed, last):
    tokens, model = mid.shape
    shards, _, part, _ = weights.shape
    hidden = shards * part
    tile = min(256, tokens)

    def weight_spec(kind):
        return pl.BlockSpec(
            (shards, 1, part, model),
            lambda i: (0, kind, 0, 0),
            pipeline_mode=pl.Buffered(buffer_count=1),
        )

    row_spec = pl.BlockSpec((tile, model), lambda i: (i, 0))
    extra = () if summed is None else (summed,)
    return pl.pallas_call(
        functools.partial(ffn_kernel, summed is not None),
        grid=(tokens // tile,),
        out_shape=(
            jax.ShapeDtypeStruct((3, tokens, hidden), BF16),
            jax.ShapeDtypeStruct((tokens, model), BF16 if last else F32),
        ),
        in_specs=[row_spec, row_spec, weight_spec(0), weight_spec(1), weight_spec(2)]
        + [row_spec] * len(extra),
        out_specs=(pl.BlockSpec((3, tile, hidden), lambda i: (0, i, 0)), row_spec),
        compiler_params=pltpu.CompilerParams(vmem_limit_bytes=VMEM_LIMIT),
        cost_estimate=pl.CostEstimate(
            flops=10 * tokens * model * hidden,
            bytes_accessed=4 * tokens * model + 6 * hidden * model,
            transcendentals=0,
        ),
        name="ffn_both",
    )(mid, cot, weights, weights, weights, *extra)


def ffn_grad_kernel(slots, *refs):
    acts = refs[:slots]
    mids = refs[slots : 2 * slots]
    cots = refs[2 * slots : 3 * slots]
    out_ref = refs[3 * slots]
    kind = pl.program_id(0)

    def store(others):
        total = dot(acts[0][0], others[0][...], TN)
        for act, other in zip(acts[1:], others[1:]):
            total = total + dot(act[0], other[...], TN)
        out_ref[...] = total.astype(BF16).reshape(out_ref.shape)

    @pl.when(kind < 2)
    def _():
        store(mids)

    @pl.when(kind == 2)
    def _():
        store(cots)


def ffn_grads(acts, mids, cots, shards):
    slots = len(acts)
    _, tokens, hidden = acts[0].shape
    model = mids[0].shape[-1]
    part = hidden // shards
    tile = 256
    per = tile // part
    whole = pl.BlockSpec(
        (tokens, model), lambda k, i: (0, 0), pipeline_mode=pl.Buffered(buffer_count=1)
    )
    return pl.pallas_call(
        functools.partial(ffn_grad_kernel, slots),
        grid=(3, hidden // tile),
        out_shape=jax.ShapeDtypeStruct((shards, 3, part, model), BF16),
        in_specs=[pl.BlockSpec((1, tokens, tile), lambda k, i: (k, 0, i))] * slots
        + [whole] * (2 * slots),
        out_specs=pl.BlockSpec((per, 1, part, model), lambda k, i: (i, k, 0, 0)),
        compiler_params=pltpu.CompilerParams(vmem_limit_bytes=VMEM_LIMIT),
        cost_estimate=pl.CostEstimate(
            flops=6 * slots * tokens * model * hidden,
            bytes_accessed=4 * slots * tokens * model,
            transcendentals=0,
        ),
        name="ffn_grads",
    )(*acts, *mids, *cots)


def ffn_down_kernel(chunks, *refs):
    acts = refs[:chunks]
    downs = refs[chunks : 2 * chunks]
    out_ref = refs[2 * chunks]
    total = None
    for act, down in zip(acts, downs):
        hidden = act.shape[-1]
        term = dot(act[0], down[...].reshape(hidden, down.shape[-1]))
        total = term if total is None else total + term
    out_ref[...] = total.astype(BF16)


def ffn_down(acts, weights):
    chunks = len(acts)
    _, tokens, hidden = acts[0].shape
    shards, _, part, model = weights[0].shape
    tile = min(256, tokens)
    act_spec = pl.BlockSpec((1, tile, hidden), lambda i: (2, i, 0))
    down_spec = pl.BlockSpec(
        (shards, 1, part, model),
        lambda i: (0, 2, 0, 0),
        pipeline_mode=pl.Buffered(buffer_count=1),
    )
    return pl.pallas_call(
        functools.partial(ffn_down_kernel, chunks),
        grid=(tokens // tile,),
        out_shape=jax.ShapeDtypeStruct((tokens, model), BF16),
        in_specs=[act_spec] * chunks + [down_spec] * chunks,
        out_specs=pl.BlockSpec((tile, model), lambda i: (i, 0)),
        compiler_params=pltpu.CompilerParams(vmem_limit_bytes=VMEM_LIMIT),
        cost_estimate=pl.CostEstimate(
            flops=2 * chunks * tokens * model * hidden,
            bytes_accessed=chunks * hidden * (tokens + model) * 2,
            transcendentals=0,
        ),
        name="ffn_down",
    )(*acts, *weights)


def ring_places(count):
    return (
        [(i, i ^ 1) for i in range(count)],
        [(i, i ^ 2) for i in range(count)],
    )


def seq_gather(rows):
    count = lax.axis_size("seq")
    if count != 4:
        return lax.all_gather(rows, "seq", axis=0)
    over_one, over_two = ring_places(count)
    half = rows.shape[0] // 2
    one = lax.ppermute(rows, "seq", over_one)
    two = lax.ppermute(rows, "seq", over_two)
    top = lax.ppermute(two[:half], "seq", over_one)
    low = lax.ppermute(one[half:], "seq", over_two)
    return jnp.concatenate([rows, one, two, top, low], axis=0).reshape(
        (count,) + rows.shape
    )


def seq_scatter(parts):
    count = lax.axis_size("seq")
    if count != 4:
        return lax.psum_scatter(parts, "seq", scatter_dimension=0).astype(F32)
    over_one, over_two = ring_places(count)
    half = parts.shape[1] // 2
    top = lax.ppermute(
        jnp.concatenate([parts[3, :half], parts[1, :half]], axis=0), "seq", over_one
    )
    low = lax.ppermute(
        jnp.concatenate([parts[3, half:], parts[2, half:]], axis=0), "seq", over_two
    )
    top_on = (parts[2, :half].astype(F32) + top[:half].astype(F32)).astype(BF16)
    low_on = (parts[1, half:].astype(F32) + low[:half].astype(F32)).astype(BF16)
    top_last = lax.ppermute(top_on, "seq", over_two)
    low_last = lax.ppermute(low_on, "seq", over_one)
    first = jnp.concatenate([top[half:], low[half:]], axis=0).astype(F32)
    last = jnp.concatenate([top_last, low_last], axis=0).astype(F32)
    return parts[0].astype(F32) + first + last


def seq_spread(rows):
    count = lax.axis_size("seq")
    parts = seq_gather(rows)
    if count != 4:
        return parts
    place = lax.axis_index("seq")
    return jnp.stack(
        [lax.dynamic_index_in_dim(parts, place ^ j, 0, keepdims=False) for j in range(count)]
    )


def scale_of(values):
    return lax.rsqrt(jnp.mean(values * values, axis=-1, keepdims=True) + EPSILON)


def normed(values, gain):
    return values * scale_of(values) * gain


def normed_back(values, gain, cot):
    scale = scale_of(values)
    pulled = cot * gain
    mean = jnp.mean(values * pulled, axis=-1, keepdims=True)
    return (
        scale * pulled - values * (scale * scale * scale) * mean,
        jnp.sum(cot * values * scale, axis=0),
    )


def own_columns(weight, heads, place):
    width = heads * HEAD
    part = lax.dynamic_slice_in_dim(weight, place * width, width, 1)
    if heads % 2:
        part = jnp.pad(part, ((0, 0), (0, HEAD)))
    return part


def on_device(
    tokens,
    cotangent,
    lengths,
    attn_gain,
    query_weight,
    key_weight,
    value_weight,
    query_gain,
    key_gain,
    out_weight,
    ffn_gain,
    gate_weight,
    up_weight,
    down_weight,
):
    slots, rows, model = tokens.shape
    seqs = lax.axis_size("seq")
    shards = lax.axis_size("fsdp")
    place = lax.axis_index("seq")
    shard = lax.axis_index("fsdp")
    slot_len = rows * seqs
    query_width = query_weight.shape[1]
    kv_width = key_weight.shape[1]
    hq = query_width // seqs // HEAD
    hkv = kv_width // seqs // HEAD
    hkv_held = hkv + hkv % 2
    sizes = (hq, hkv_held, hq // hkv)
    order = (place if seqs == 4 else place * 0).reshape(1)
    tables = position_tables(slot_len)
    gains = (
        jnp.concatenate([query_gain, query_gain]).reshape(1, 2 * HEAD),
        jnp.concatenate([key_gain, key_gain]).reshape(1, 2 * HEAD),
    )

    qkv_own = jnp.concatenate(
        [
            own_columns(query_weight, hq, place),
            own_columns(key_weight, hkv, place),
            own_columns(value_weight, hkv, place),
        ],
        axis=1,
    )
    qkv_weight = lax.all_gather(qkv_own, "fsdp", axis=0, tiled=True)
    per = shards // seqs
    piece = out_weight.shape[0] // seqs
    out_own = None
    for j in range(seqs):
        moves = [
            (s * shards + s * per + h, s * shards + h * seqs + j)
            for s in range(seqs)
            for h in range(per)
        ]
        got = lax.ppermute(out_weight[j * piece : (j + 1) * piece], ("seq", "fsdp"), moves)
        out_own = got if out_own is None else out_own + got
    out_rows = lax.all_gather(out_own, "fsdp", axis=0, tiled=True)
    hidden_own = gate_weight.shape[0] // seqs
    part = hidden_own // CHUNKS
    ffn_weights = []
    for c in range(CHUNKS):
        start = place * hidden_own + c * part
        mine = jnp.stack(
            [
                lax.dynamic_slice_in_dim(w, start, part, 0)
                for w in (gate_weight, up_weight, down_weight)
            ]
        )
        ffn_weights.append(lax.all_gather(mine, "fsdp", axis=0))

    places = place * rows + jnp.arange(rows, dtype=jnp.int32)
    live = (places[None, :] < lengths[:, None]).astype(F32)[..., None]
    inputs = tokens.astype(F32)
    out_cot = cotangent.astype(F32) * live
    normal_in = [normed(inputs[b], attn_gain).astype(BF16) for b in range(slots)]
    normal_full = [seq_gather(v).reshape(slot_len, model) for v in normal_in]

    qkv = []
    attended = []
    log_sums = []
    hidden_res = []
    mid_full = []
    for b in range(slots):
        raw = dot(normal_full[b], qkv_weight).astype(BF16).reshape(seqs, rows, -1)
        mixed, lse = attend(sizes, order, lengths[b : b + 1], raw, gains, tables)
        mixed = mixed.reshape(slot_len, hq * HEAD)
        qkv.append(raw)
        attended.append(mixed)
        log_sums.append(lse)
        proj = dot(mixed, out_rows).astype(BF16).reshape(seqs, rows, model)
        res = inputs[b] + seq_scatter(proj)
        hidden_res.append(res)
        mid = normed(res, ffn_gain).astype(BF16)
        mid_full.append(seq_gather(mid).reshape(slot_len, model))
    cot_full = [seq_gather(out_cot[b].astype(BF16)).reshape(slot_len, model) for b in range(slots)]

    acts = [[None] * slots for _ in range(CHUNKS)]
    pulled = [None] * slots
    for c in range(CHUNKS):
        for b in range(slots):
            acts[c][b], pulled[b] = ffn_both(
                mid_full[b], cot_full[b], ffn_weights[c], pulled[b], c == CHUNKS - 1
            )
    ffn_sums = []
    for c in range(CHUNKS):
        grads = ffn_grads(acts[c], mid_full, cot_full, shards).reshape(shards, 3 * part, model)
        ffn_sums.append(lax.psum_scatter(grads, "fsdp", scatter_dimension=0))

    output = []
    res_cot = []
    res_full = []
    dqkv = []
    grad_ffn_gain = 0.0
    head_gain = 0.0
    for b in range(slots):
        pull, gain_part = normed_back(
            hidden_res[b], ffn_gain, seq_scatter(pulled[b].reshape(seqs, rows, model))
        )
        grad_ffn_gain = grad_ffn_gain + gain_part
        cot = out_cot[b] + pull
        res_cot.append(cot)
        full = seq_gather(cot.astype(BF16)).reshape(slot_len, model)
        res_full.append(full)
        attended_cot = dot(full, out_rows, NT).astype(BF16).reshape(seqs, rows, hq * HEAD)
        back, gain_part = attend_back(
            sizes, order, lengths[b : b + 1], qkv[b], attended_cot, log_sums[b], gains, tables
        )
        head_gain = head_gain + gain_part
        dqkv.append(back.reshape(slot_len, -1))
    for b in range(slots):
        ffn_out = ffn_down([acts[c][b] for c in range(CHUNKS)], ffn_weights)
        total = hidden_res[b] + seq_scatter(ffn_out.reshape(seqs, rows, model))
        output.append((live[b] * total).astype(BF16))

    grad_tokens = []
    grad_attn_gain = 0.0
    for b in range(slots):
        in_cot = seq_scatter(
            dot(dqkv[b], qkv_weight, NT).astype(BF16).reshape(seqs, rows, model)
        )
        pull, gain_part = normed_back(inputs[b], attn_gain, in_cot)
        grad_attn_gain = grad_attn_gain + gain_part
        grad_tokens.append((res_cot[b] + pull).astype(BF16))

    out_grads = sum(dot(attended[b], res_full[b], TN) for b in range(slots)).astype(BF16)
    out_sums = lax.psum_scatter(out_grads, "fsdp", scatter_dimension=0, tiled=True)
    out_parts = []
    for j in range(seqs):
        moves = [
            (s * shards + h * seqs + j, s * shards + s * per + h)
            for s in range(seqs)
            for h in range(per)
        ]
        out_parts.append(lax.ppermute(out_sums, ("seq", "fsdp"), moves))
    grad_out = lax.psum(jnp.concatenate(out_parts, axis=0), "seq").astype(F32)

    qkv_grads = sum(dot(normal_full[b], dqkv[b], TN) for b in range(slots)).astype(BF16)
    qkv_sums = lax.psum_scatter(qkv_grads, "fsdp", scatter_dimension=0, tiled=True)
    qkv_all = jnp.moveaxis(seq_spread(qkv_sums), 0, 1).astype(F32)
    held = qkv_all.shape[0]
    edge = hq * HEAD
    kv_edge = edge + hkv_held * HEAD
    grad_query = qkv_all[..., :edge].reshape(held, query_width)
    grad_key = qkv_all[..., edge : edge + hkv * HEAD].reshape(held, kv_width)
    grad_value = qkv_all[..., kv_edge : kv_edge + hkv * HEAD].reshape(held, kv_width)

    spread = [seq_spread(v).reshape(seqs, 3, part, model) for v in ffn_sums]
    ffn_grad = [
        jnp.stack([v[:, kind] for v in spread], axis=1).reshape(seqs * hidden_own, model).astype(F32)
        for kind in range(3)
    ]

    gain_sums = lax.psum(
        jnp.concatenate(
            [
                grad_attn_gain,
                grad_ffn_gain,
                (head_gain[0, :HEAD] + head_gain[0, HEAD:]),
                (head_gain[1, :HEAD] + head_gain[1, HEAD:]),
            ]
        ),
        ("seq", "fsdp"),
    )

    def own_gain(start, length):
        width = length // shards
        return lax.dynamic_slice_in_dim(gain_sums, start + shard * width, width, 0)

    return (
        jnp.stack(output),
        jnp.stack(grad_tokens),
        own_gain(0, model),
        grad_query,
        grad_key,
        grad_value,
        own_gain(2 * model, HEAD),
        own_gain(2 * model + HEAD, HEAD),
        grad_out,
        own_gain(model, model),
        ffn_grad[0],
        ffn_grad[1],
        ffn_grad[2],
    )


def solution(mesh):
    return jax.shard_map(
        on_device,
        mesh=mesh,
        in_specs=(
            P("fsdp", "seq", None),
            P("fsdp", "seq", None),
            P("fsdp"),
            P(),
            P("fsdp", None),
            P("fsdp", None),
            P("fsdp", None),
            P(),
            P(),
            P("fsdp", None),
            P(),
            P("fsdp", None),
            P("fsdp", None),
            P("fsdp", None),
        ),
        out_specs=(
            P("fsdp", "seq", None),
            P("fsdp", "seq", None),
            P("fsdp"),
            P("fsdp", None),
            P("fsdp", None),
            P("fsdp", None),
            P("fsdp"),
            P("fsdp"),
            P("fsdp", None),
            P("fsdp"),
            P("fsdp", None),
            P("fsdp", None),
            P("fsdp", None),
        ),
        check_vma=False,
    )
```

```python
import functools

import jax
import jax.numpy as jnp
import numpy as np
from jax import lax
from jax.experimental import pallas as pl
from jax.experimental.pallas import tpu as pltpu
from jax.sharding import PartitionSpec as P

EPSILON = 1e-05
ROPE_BASE = 1000000.0
NEGATIVE = -1e30
F32 = jnp.float32
BF16 = jnp.bfloat16
NN = (((1,), (0,)), ((), ()))
NT = (((1,), (1,)), ((), ()))
TN = (((0,), (0,)), ((), ()))
SMEM = pl.BlockSpec(memory_space=pltpu.SMEM)
VMEM = pl.BlockSpec(memory_space=pltpu.VMEM)
VMEM_LIMIT = 58 << 20
HEAD = 64
BLOCK = 256
CHUNKS = 4
ANY = pl.BlockSpec(memory_space=pl.ANY)


def dot(a, b, dims=NN):
    return lax.dot_general(a, b, dims, preferred_element_type=F32)


def partner(v):
    lane = lax.broadcasted_iota(jnp.int32, v.shape, 1)
    return jnp.where(lane % HEAD < HEAD // 2, pltpu.roll(v, 96, 1), pltpu.roll(v, 32, 1))


def head_mean(v, ones):
    high = v.astype(BF16)
    rest = (v - high.astype(F32)).astype(BF16)
    return dot(high, ones) + dot(rest, ones)


def prepare_heads(sizes, place, qkv_ref, qg_ref, kg_ref, cos_ref, sin_ref, ones, q_s, k_s, v_s):
    hq, hkv, _ = sizes
    seqs, rows_in, _ = qkv_ref.shape
    for c in range(seqs):
        j = jnp.bitwise_xor(place, c)
        rows = slice(c * rows_in, (c + 1) * rows_in)
        cos = cos_ref[rows, :]
        sin = sin_ref[rows, :]
        for p in range((hq + hkv) // 2):
            is_query = p < hq // 2
            x = qkv_ref[j, :, p * 128 : (p + 1) * 128].astype(F32)
            gain = qg_ref[...] * HEAD**-0.5 if is_query else kg_ref[...]
            y = x * lax.rsqrt(head_mean(x * x, ones) + EPSILON) * gain
            y = (y * cos + partner(y) * sin).astype(BF16)
            for t in range(2):
                part = y[:, t * HEAD : (t + 1) * HEAD]
                if is_query:
                    q_s[2 * p + t, rows, :] = part
                else:
                    k_s[2 * p - hq + t, rows, :] = part
        for t in range(hkv):
            start = (hq + hkv + t) * HEAD
            v_s[t, rows, :] = qkv_ref[j, :, start : start + HEAD]


def allowed_keys(block, first, keys, length):
    bound = jnp.minimum(first + lax.broadcasted_iota(jnp.int32, (block, 1), 0), length - 1)
    return lax.broadcasted_iota(jnp.int32, (block, keys), 1) <= bound


def attend_kernel(
    sizes, place_ref, len_ref, qkv_ref, qg_ref, kg_ref, cos_ref, sin_ref, ones_ref, after_ref,
    out_ref, lse_ref, q_s, k_s, v_s, o_s,
):
    hq, hkv, group = sizes
    seqs, rows_in, _ = qkv_ref.shape
    place = place_ref[0]
    prepare_heads(
        sizes, place, qkv_ref, qg_ref, kg_ref, cos_ref, sin_ref, ones_ref[...], q_s, k_s, v_s
    )
    for i in range(seqs * rows_in // BLOCK):
        keys = (i + 1) * BLOCK
        rows = slice(i * BLOCK, (i + 1) * BLOCK)
        keep = allowed_keys(BLOCK, i * BLOCK, keys, len_ref[0])

        def one_head(h, _):
            kv = h // group
            scores = dot(q_s[h, rows, :], k_s[kv, :keys, :], NT)
            scores = jnp.where(keep, scores, NEGATIVE)
            highest = jnp.max(scores, axis=1, keepdims=True)
            shifted = jnp.exp(scores - highest)
            total = jnp.sum(shifted, axis=1, keepdims=True)
            mixed = dot(shifted.astype(BF16), v_s[kv, :keys, :]) / total
            o_s[h, rows, :] = mixed.astype(BF16)
            lse_ref[h, rows, :] = highest + jnp.log(total)
            return 0

        lax.fori_loop(0, hq, one_head, 0)
    for c in range(seqs):
        j = jnp.bitwise_xor(place, c)
        rows = slice(c * rows_in, (c + 1) * rows_in)
        for p in range(hq // 2):
            out_ref[j, :, p * 128 : (p + 1) * 128] = jnp.concatenate(
                [o_s[2 * p, rows, :], o_s[2 * p + 1, rows, :]], axis=1
            )


def attend_back_kernel(
    sizes, place_ref, len_ref, qkv_ref, cot_ref, lse_ref, qg_ref, kg_ref, cos_ref, sin_ref,
    ones_ref, after_ref, dqkv_ref, dgain_ref, q_s, k_s, v_s, cot_s, dq_s, dk_s, dv_s,
):
    hq, hkv, group = sizes
    seqs, rows_in, _ = qkv_ref.shape
    place = place_ref[0]
    ones = ones_ref[...]
    prepare_heads(sizes, place, qkv_ref, qg_ref, kg_ref, cos_ref, sin_ref, ones, q_s, k_s, v_s)
    for c in range(seqs):
        j = jnp.bitwise_xor(place, c)
        for h in range(hq):
            cot_s[h, c * rows_in : (c + 1) * rows_in, :] = cot_ref[
                j, :, h * HEAD : (h + 1) * HEAD
            ]
    dk_s[...] = jnp.zeros_like(dk_s)
    dv_s[...] = jnp.zeros_like(dv_s)
    for i in range(seqs * rows_in // BLOCK):
        keys = (i + 1) * BLOCK
        rows = slice(i * BLOCK, (i + 1) * BLOCK)
        keep = allowed_keys(BLOCK, i * BLOCK, keys, len_ref[0])

        def one_head(h, _):
            kv = h // group
            q = q_s[h, rows, :]
            cot = cot_s[h, rows, :]
            k = k_s[kv, :keys, :]
            scores = jnp.where(keep, dot(q, k, NT), NEGATIVE)
            probs = jnp.exp(scores - lse_ref[h, rows, :])
            prob_cot = dot(cot, v_s[kv, :keys, :], NT)
            inner = jnp.sum(probs * prob_cot, axis=1, keepdims=True)
            score_cot = (probs * (prob_cot - inner)).astype(BF16)
            dq_s[h, rows, :] = dot(score_cot, k) * HEAD**-0.5
            dk_s[kv, :keys, :] += dot(score_cot, q, TN)
            dv_s[kv, :keys, :] += dot(probs.astype(BF16), cot, TN)
            return 0

        lax.fori_loop(0, hq, one_head, 0)
    gain_sums = [jnp.zeros((1, 128), F32), jnp.zeros((1, 128), F32)]
    for c in range(seqs):
        j = jnp.bitwise_xor(place, c)
        rows = slice(c * rows_in, (c + 1) * rows_in)
        cos = cos_ref[rows, :]
        sin = sin_ref[rows, :]
        for p in range((hq + hkv) // 2):
            is_query = p < hq // 2
            x = qkv_ref[j, :, p * 128 : (p + 1) * 128].astype(F32)
            gain = qg_ref[...] if is_query else kg_ref[...]
            source, first = (dq_s, 2 * p) if is_query else (dk_s, 2 * p - hq)
            turned = jnp.concatenate([source[first, rows, :], source[first + 1, rows, :]], axis=1)
            scale = lax.rsqrt(head_mean(x * x, ones) + EPSILON)
            straight = turned * cos + partner(turned * sin)
            unit = x * scale
            which = 0 if is_query else 1
            gain_sums[which] += jnp.sum(straight * unit, axis=0, keepdims=True)
            pulled = gain * straight
            dx = scale * (pulled - unit * head_mean(unit * pulled, ones))
            dqkv_ref[j, :, p * 128 : (p + 1) * 128] = dx.astype(BF16)
        for p in range(hkv // 2):
            start = (hq + hkv) * HEAD + p * 128
            dqkv_ref[j, :, start : start + 128] = jnp.concatenate(
                [dv_s[2 * p, rows, :], dv_s[2 * p + 1, rows, :]], axis=1
            ).astype(BF16)
    dgain_ref[0:1, :] = gain_sums[0]
    dgain_ref[1:2, :] = gain_sums[1]


def position_tables(length):
    places = np.arange(length, dtype=np.float32)
    half = HEAD // 2
    freqs = np.float32(ROPE_BASE) ** (-(np.arange(half, dtype=np.float32) * 2.0) / HEAD)
    angles = places[:, None] * freqs.astype(np.float32)[None, :]
    cos = np.cos(angles).astype(np.float32)
    sin = np.sin(angles).astype(np.float32)
    ones = np.kron(np.eye(2), np.ones((HEAD, HEAD)) / HEAD)
    return (
        jnp.asarray(np.concatenate([cos] * 4, axis=1)),
        jnp.asarray(np.concatenate([-sin, sin, -sin, sin], axis=1)),
        jnp.asarray(ones, dtype=BF16),
    )


def attend(sizes, place, length, qkv, gains, tables, after):
    seqs, rows_in, _ = qkv.shape
    hq, hkv, _ = sizes
    slot = seqs * rows_in
    return pl.pallas_call(
        functools.partial(attend_kernel, sizes),
        out_shape=(
            jax.ShapeDtypeStruct((seqs, rows_in, hq * HEAD), BF16),
            jax.ShapeDtypeStruct((hq, slot, 1), F32),
        ),
        in_specs=[SMEM, SMEM] + [VMEM] * 6 + [ANY],
        out_specs=(VMEM, VMEM),
        scratch_shapes=[
            pltpu.VMEM((hq, slot, HEAD), BF16),
            pltpu.VMEM((hkv, slot, HEAD), BF16),
            pltpu.VMEM((hkv, slot, HEAD), BF16),
            pltpu.VMEM((hq, slot, HEAD), BF16),
        ],
        compiler_params=pltpu.CompilerParams(vmem_limit_bytes=VMEM_LIMIT),
        cost_estimate=pl.CostEstimate(
            flops=56 * hq * slot * slot * HEAD, bytes_accessed=1 << 23, transcendentals=0
        ),
        name="attend",
    )(place, length, qkv, *gains, *tables, after)


def attend_back(sizes, place, length, qkv, cot, lse, gains, tables, after):
    seqs, rows_in, width = qkv.shape
    hq, hkv, _ = sizes
    slot = seqs * rows_in
    return pl.pallas_call(
        functools.partial(attend_back_kernel, sizes),
        out_shape=(
            jax.ShapeDtypeStruct((seqs, rows_in, width), BF16),
            jax.ShapeDtypeStruct((2, 128), F32),
        ),
        in_specs=[SMEM, SMEM] + [VMEM] * 8 + [ANY],
        out_specs=(VMEM, VMEM),
        scratch_shapes=[
            pltpu.VMEM((hq, slot, HEAD), BF16),
            pltpu.VMEM((hkv, slot, HEAD), BF16),
            pltpu.VMEM((hkv, slot, HEAD), BF16),
            pltpu.VMEM((hq, slot, HEAD), BF16),
            pltpu.VMEM((hq, slot, HEAD), F32),
            pltpu.VMEM((hkv, slot, HEAD), F32),
            pltpu.VMEM((hkv, slot, HEAD), F32),
        ],
        compiler_params=pltpu.CompilerParams(vmem_limit_bytes=VMEM_LIMIT),
        cost_estimate=pl.CostEstimate(
            flops=88 * hq * slot * slot * HEAD, bytes_accessed=1 << 23, transcendentals=0
        ),
        name="attend_back",
    )(place, length, qkv, cot, lse, *gains, *tables, after)


def ffn_kernel(has_sum, mid_ref, cot_ref, gate_ref, up_ref, down_ref, *refs):
    if has_sum:
        sum_ref, after_ref, acts_ref, pull_ref = refs
    else:
        after_ref, acts_ref, pull_ref = refs
    model = mid_ref.shape[-1]
    hidden = acts_ref.shape[-1]
    gate_w = gate_ref[...].reshape(hidden, model)
    up_w = up_ref[...].reshape(hidden, model)
    down_w = down_ref[...].reshape(hidden, model)
    mid = mid_ref[...]
    gate = dot(mid, gate_w, NT)
    up = dot(mid, up_w, NT)
    mids_cot = dot(cot_ref[...], down_w, NT)
    sigmoid = jax.nn.sigmoid(gate)
    active = gate * sigmoid
    gate_cot = (mids_cot * up * sigmoid * (1.0 + gate * (1.0 - sigmoid))).astype(BF16)
    up_cot = (mids_cot * active).astype(BF16)
    acts_ref[0] = gate_cot
    acts_ref[1] = up_cot
    acts_ref[2] = (active * up).astype(BF16)
    pulled = dot(gate_cot, gate_w) + dot(up_cot, up_w)
    if has_sum:
        pulled = pulled + sum_ref[...]
    pull_ref[...] = pulled.astype(pull_ref.dtype)


def ffn_both(mid, cot, weights, summed, last, after):
    tokens, model = mid.shape
    shards, _, part, _ = weights.shape
    hidden = shards * part
    tile = min(256, tokens)

    def weight_spec(kind):
        return pl.BlockSpec(
            (shards, 1, part, model),
            lambda i: (0, kind, 0, 0),
            pipeline_mode=pl.Buffered(buffer_count=1),
        )

    row_spec = pl.BlockSpec((tile, model), lambda i: (i, 0))
    extra = () if summed is None else (summed,)
    return pl.pallas_call(
        functools.partial(ffn_kernel, summed is not None),
        grid=(tokens // tile,),
        out_shape=(
            jax.ShapeDtypeStruct((3, tokens, hidden), BF16),
            jax.ShapeDtypeStruct((tokens, model), BF16 if last else F32),
        ),
        in_specs=[row_spec, row_spec, weight_spec(0), weight_spec(1), weight_spec(2)]
        + [row_spec] * len(extra)
        + [ANY],
        out_specs=(pl.BlockSpec((3, tile, hidden), lambda i: (0, i, 0)), row_spec),
        compiler_params=pltpu.CompilerParams(vmem_limit_bytes=VMEM_LIMIT),
        cost_estimate=pl.CostEstimate(
            flops=16 * tokens * model * hidden,
            bytes_accessed=4 * tokens * model + 6 * hidden * model,
            transcendentals=0,
        ),
        name="ffn_both",
    )(mid, cot, weights, weights, weights, *extra, after)


def ffn_grad_kernel(slots, *refs):
    acts = refs[:slots]
    mids = refs[slots : 2 * slots]
    cots = refs[2 * slots : 3 * slots]
    out_ref = refs[3 * slots + 1]
    kind = pl.program_id(0)

    def store(others):
        total = dot(acts[0][0], others[0][...], TN)
        for act, other in zip(acts[1:], others[1:]):
            total = total + dot(act[0], other[...], TN)
        out_ref[...] = total.astype(BF16).reshape(out_ref.shape)

    @pl.when(kind < 2)
    def _():
        store(mids)

    @pl.when(kind == 2)
    def _():
        store(cots)


def ffn_grads(acts, mids, cots, shards, after):
    slots = len(acts)
    _, tokens, hidden = acts[0].shape
    model = mids[0].shape[-1]
    part = hidden // shards
    tile = 256
    per = tile // part
    whole = pl.BlockSpec(
        (tokens, model), lambda k, i: (0, 0), pipeline_mode=pl.Buffered(buffer_count=1)
    )
    return pl.pallas_call(
        functools.partial(ffn_grad_kernel, slots),
        grid=(3, hidden // tile),
        out_shape=jax.ShapeDtypeStruct((shards, 3, part, model), BF16),
        in_specs=[pl.BlockSpec((1, tokens, tile), lambda k, i: (k, 0, i))] * slots
        + [whole] * (2 * slots)
        + [ANY],
        out_specs=pl.BlockSpec((per, 1, part, model), lambda k, i: (i, k, 0, 0)),
        compiler_params=pltpu.CompilerParams(vmem_limit_bytes=VMEM_LIMIT),
        cost_estimate=pl.CostEstimate(
            flops=9 * slots * tokens * model * hidden,
            bytes_accessed=4 * slots * tokens * model,
            transcendentals=0,
        ),
        name="ffn_grads",
    )(*acts, *mids, *cots, after)


def ffn_down_kernel(chunks, *refs):
    acts = refs[:chunks]
    downs = refs[chunks : 2 * chunks]
    out_ref = refs[2 * chunks + 1]
    total = None
    for act, down in zip(acts, downs):
        hidden = act.shape[-1]
        term = dot(act[0], down[...].reshape(hidden, down.shape[-1]))
        total = term if total is None else total + term
    out_ref[...] = total.astype(BF16)


def ffn_down(acts, weights, after):
    chunks = len(acts)
    _, tokens, hidden = acts[0].shape
    shards, _, part, model = weights[0].shape
    tile = min(256, tokens)
    act_spec = pl.BlockSpec((1, tile, hidden), lambda i: (2, i, 0))
    down_spec = pl.BlockSpec(
        (shards, 1, part, model),
        lambda i: (0, 2, 0, 0),
        pipeline_mode=pl.Buffered(buffer_count=1),
    )
    return pl.pallas_call(
        functools.partial(ffn_down_kernel, chunks),
        grid=(tokens // tile,),
        out_shape=jax.ShapeDtypeStruct((tokens, model), BF16),
        in_specs=[act_spec] * chunks + [down_spec] * chunks + [ANY],
        out_specs=pl.BlockSpec((tile, model), lambda i: (i, 0)),
        compiler_params=pltpu.CompilerParams(vmem_limit_bytes=VMEM_LIMIT),
        cost_estimate=pl.CostEstimate(
            flops=4 * chunks * tokens * model * hidden,
            bytes_accessed=chunks * hidden * (tokens + model) * 2,
            transcendentals=0,
        ),
        name="ffn_down",
    )(*acts, *weights, after)


def place_kernel(place_ref, parts_ref, *refs):
    for kind, out_ref in enumerate(refs[-3:]):
        out_ref[0, 0] = parts_ref[0, kind].astype(F32)


def place_parts(place, parts, chunk, held):
    seqs, _, part, model = parts.shape
    out = jax.ShapeDtypeStruct((seqs, CHUNKS, part, model), F32)
    out_spec = pl.BlockSpec(
        (1, 1, part, model), lambda j, at: (jnp.bitwise_xor(at[0], j), chunk, 0, 0)
    )
    return pl.pallas_call(
        place_kernel,
        out_shape=(out,) * 3,
        grid_spec=pltpu.PrefetchScalarGridSpec(
            num_scalar_prefetch=1,
            grid=(seqs,),
            in_specs=[pl.BlockSpec((1, 3, part, model), lambda j, at: (j, 0, 0, 0))]
            + [ANY] * len(held),
            out_specs=(out_spec,) * 3,
        ),
        input_output_aliases={2 + k: k for k in range(len(held))},
        compiler_params=pltpu.CompilerParams(vmem_limit_bytes=VMEM_LIMIT),
        cost_estimate=pl.CostEstimate(
            flops=0, bytes_accessed=18 * seqs * part * model, transcendentals=0
        ),
        name="place_parts",
    )(place, parts, *held)


def ring_places(count):
    return (
        [(i, i ^ 1) for i in range(count)],
        [(i, i ^ 2) for i in range(count)],
    )


def seq_gather(rows):
    count = lax.axis_size("seq")
    if count != 4:
        return lax.all_gather(rows, "seq", axis=0)
    over_one, over_two = ring_places(count)
    half = rows.shape[0] // 2
    one = lax.ppermute(rows, "seq", over_one)
    two = lax.ppermute(rows, "seq", over_two)
    top = lax.ppermute(two[:half], "seq", over_one)
    low = lax.ppermute(one[half:], "seq", over_two)
    return jnp.concatenate([rows, one, two, top, low], axis=0).reshape(
        (count,) + rows.shape
    )


def seq_scatter(parts):
    count = lax.axis_size("seq")
    if count != 4:
        return lax.psum_scatter(parts, "seq", scatter_dimension=0).astype(F32)
    over_one, over_two = ring_places(count)
    half = parts.shape[1] // 2
    top = lax.ppermute(
        jnp.concatenate([parts[3, :half], parts[1, :half]], axis=0), "seq", over_one
    )
    low = lax.ppermute(
        jnp.concatenate([parts[3, half:], parts[2, half:]], axis=0), "seq", over_two
    )
    top_on = (parts[2, :half].astype(F32) + top[:half].astype(F32)).astype(BF16)
    low_on = (parts[1, half:].astype(F32) + low[:half].astype(F32)).astype(BF16)
    top_last = lax.ppermute(top_on, "seq", over_two)
    low_last = lax.ppermute(low_on, "seq", over_one)
    first = jnp.concatenate([top[half:], low[half:]], axis=0).astype(F32)
    last = jnp.concatenate([top_last, low_last], axis=0).astype(F32)
    return parts[0].astype(F32) + first + last


def seq_spread(rows):
    count = lax.axis_size("seq")
    parts = seq_gather(rows)
    if count != 4:
        return parts
    place = lax.axis_index("seq")
    return jnp.stack(
        [lax.dynamic_index_in_dim(parts, place ^ j, 0, keepdims=False) for j in range(count)]
    )


def out_home(sums):
    seqs = lax.axis_size("seq")
    shards = lax.axis_size("fsdp")
    per = shards // seqs
    held = []
    for j in range(seqs):
        moves = [
            (s * shards + h * seqs + j, s * shards + s * per + h)
            for s in range(seqs)
            for h in range(per)
        ]
        held.append(lax.ppermute(sums, ("seq", "fsdp"), moves))
    held = jnp.concatenate(held, axis=0)
    if seqs != 4:
        return lax.psum(held, "seq")

    def hop(values, start, end):
        moves = [
            ((s ^ start) * shards + s * per + h, (s ^ end) * shards + s * per + h)
            for s in range(seqs)
            for h in range(per)
        ]
        return lax.ppermute(values, ("seq", "fsdp"), moves)

    half = held.shape[0] // 2
    one = hop(held, 0, 1)
    two = hop(held, 0, 2)
    top = hop(two[:half], 2, 3)
    low = hop(one[half:], 1, 3)
    return held + one + two + jnp.concatenate([top, low], axis=0)


def scale_of(values):
    return lax.rsqrt(jnp.mean(values * values, axis=-1, keepdims=True) + EPSILON)


def normed(values, gain):
    return values * scale_of(values) * gain


def normed_back(values, gain, cot):
    scale = scale_of(values)
    pulled = cot * gain
    mean = jnp.mean(values * pulled, axis=-1, keepdims=True)
    return (
        scale * pulled - values * (scale * scale * scale) * mean,
        jnp.sum(cot * values * scale, axis=0),
    )


def follow(values, earlier):
    return lax.optimization_barrier((values, *earlier))[0]


def own_columns(weight, heads, place):
    width = heads * HEAD
    part = lax.dynamic_slice_in_dim(weight, place * width, width, 1)
    if heads % 2:
        part = jnp.pad(part, ((0, 0), (0, HEAD)))
    return part


def on_device(
    tokens,
    cotangent,
    lengths,
    attn_gain,
    query_weight,
    key_weight,
    value_weight,
    query_gain,
    key_gain,
    out_weight,
    ffn_gain,
    gate_weight,
    up_weight,
    down_weight,
):
    slots, rows, model = tokens.shape
    seqs = lax.axis_size("seq")
    shards = lax.axis_size("fsdp")
    place = lax.axis_index("seq")
    shard = lax.axis_index("fsdp")
    slot_len = rows * seqs
    query_width = query_weight.shape[1]
    kv_width = key_weight.shape[1]
    hq = query_width // seqs // HEAD
    hkv = kv_width // seqs // HEAD
    hkv_held = hkv + hkv % 2
    sizes = (hq, hkv_held, hq // hkv)
    order = (place if seqs == 4 else place * 0).reshape(1)
    tables = position_tables(slot_len)
    gains = (
        jnp.concatenate([query_gain, query_gain]).reshape(1, 2 * HEAD),
        jnp.concatenate([key_gain, key_gain]).reshape(1, 2 * HEAD),
    )

    places = place * rows + jnp.arange(rows, dtype=jnp.int32)
    live = (places[None, :] < lengths[:, None]).astype(F32)[..., None]
    inputs = tokens.astype(F32)
    out_cot = cotangent.astype(F32) * live
    normal_in = [normed(inputs[b], attn_gain).astype(BF16) for b in range(slots)]

    qkv_own = jnp.concatenate(
        [
            own_columns(query_weight, hq, place),
            own_columns(key_weight, hkv, place),
            own_columns(value_weight, hkv, place),
        ],
        axis=1,
    )
    qkv_weight = lax.all_gather(qkv_own, "fsdp", axis=0, tiled=True)
    normal_full = [seq_gather(v).reshape(slot_len, model) for v in normal_in]
    out_weight = follow(out_weight, normal_full[:1])
    per = shards // seqs
    piece = out_weight.shape[0] // seqs
    out_own = None
    for j in range(seqs):
        moves = [
            (s * shards + s * per + h, s * shards + h * seqs + j)
            for s in range(seqs)
            for h in range(per)
        ]
        got = lax.ppermute(out_weight[j * piece : (j + 1) * piece], ("seq", "fsdp"), moves)
        out_own = got if out_own is None else out_own + got
    out_rows = lax.all_gather(out_own, "fsdp", axis=0, tiled=True)
    hidden_own = gate_weight.shape[0] // seqs
    part = hidden_own // CHUNKS
    ffn_weights = []
    for c in range(CHUNKS):
        start = place * hidden_own + c * part
        mine = jnp.stack(
            [
                lax.dynamic_slice_in_dim(w, start, part, 0)
                for w in (gate_weight, up_weight, down_weight)
            ]
        )
        ffn_weights.append(lax.all_gather(mine, "fsdp", axis=0))

    after = order
    qkv = []
    attended = []
    log_sums = []
    hidden_res = []
    mid_full = []
    for b in range(slots):
        raw = dot(normal_full[b], qkv_weight).astype(BF16).reshape(seqs, rows, -1)
        mixed, lse = attend(sizes, order, lengths[b : b + 1], raw, gains, tables, after)
        after = mixed
        mixed = mixed.reshape(slot_len, hq * HEAD)
        qkv.append(raw)
        attended.append(mixed)
        log_sums.append(lse)
    for b in range(slots):
        proj = dot(attended[b], out_rows).astype(BF16).reshape(seqs, rows, model)
        res = inputs[b] + seq_scatter(proj)
        hidden_res.append(res)
        mid = normed(res, ffn_gain).astype(BF16)
        mid_full.append(seq_gather(mid).reshape(slot_len, model))
    cot_full = [seq_gather(out_cot[b].astype(BF16)).reshape(slot_len, model) for b in range(slots)]

    acts = [[None] * slots for _ in range(CHUNKS)]
    pulled = [None] * slots
    ffn_parts = []
    ffn_sums = []

    def ffn_step(b, c, after):
        acts[c][b], pulled[b] = ffn_both(
            mid_full[b], cot_full[b], ffn_weights[c], pulled[b], c == CHUNKS - 1, after
        )
        return acts[c][b]

    def grad_step(c, after):
        ffn_parts.append(ffn_grads(acts[c], mid_full, cot_full, shards, after))
        return ffn_parts[-1]

    def sum_next(*earlier):
        sent = ffn_parts[len(ffn_sums)].reshape(shards, 3 * part, model)
        sent = follow(sent, [*ffn_sums[-1:], *earlier])
        ffn_sums.append(lax.psum_scatter(sent, "fsdp", scatter_dimension=0))

    early = CHUNKS // 2
    for b in range(slots):
        for c in range(early):
            after = ffn_step(b, c, after)
    after = grad_step(0, after)
    sum_next()
    for c in range(early, CHUNKS):
        for b in range(slots):
            after = ffn_step(b, c, after)
    for c in range(1, CHUNKS):
        after = grad_step(c, after)
    for _ in range(early - 1):
        sum_next()

    output = []
    res_cot = []
    res_full = []
    dqkv = []
    grad_ffn_gain = 0.0
    head_gain = 0.0
    for b in range(slots):
        pull, gain_part = normed_back(
            hidden_res[b], ffn_gain, seq_scatter(pulled[b].reshape(seqs, rows, model))
        )
        grad_ffn_gain = grad_ffn_gain + gain_part
        cot = out_cot[b] + pull
        res_cot.append(cot)
        full = seq_gather(cot.astype(BF16)).reshape(slot_len, model)
        res_full.append(full)
        attended_cot = dot(full, out_rows, NT).astype(BF16).reshape(seqs, rows, hq * HEAD)
        back, gain_part = attend_back(
            sizes, order, lengths[b : b + 1], qkv[b], attended_cot, log_sums[b], gains, tables,
            after,
        )
        after = back
        sum_next(back)
        head_gain = head_gain + gain_part
        dqkv.append(back.reshape(slot_len, -1))
    for b in range(slots):
        ffn_out = ffn_down([acts[c][b] for c in range(CHUNKS)], ffn_weights, after)
        after = ffn_out
        total = hidden_res[b] + seq_scatter(ffn_out.reshape(seqs, rows, model))
        output.append((live[b] * total).astype(BF16))

    while len(ffn_sums) < CHUNKS:
        sum_next()

    grad_tokens = []
    grad_attn_gain = 0.0
    for b in range(slots):
        in_cot = seq_scatter(
            dot(dqkv[b], qkv_weight, NT).astype(BF16).reshape(seqs, rows, model)
        )
        pull, gain_part = normed_back(inputs[b], attn_gain, in_cot)
        grad_attn_gain = grad_attn_gain + gain_part
        grad_tokens.append((res_cot[b] + pull).astype(BF16))

    out_grads = sum(dot(attended[b], res_full[b], TN) for b in range(slots)).astype(BF16)
    out_grads = follow(out_grads, ffn_sums[-1:])
    out_sums = lax.psum_scatter(out_grads, "fsdp", scatter_dimension=0, tiled=True)
    grad_out = out_home(out_sums).astype(F32)

    head_sums = jnp.pad(
        (head_gain[:, :HEAD] + head_gain[:, HEAD:]).reshape(2, shards, 1, HEAD // shards),
        ((0, 0), (0, 0), (0, 0), (0, model // shards - HEAD // shards)),
    ).reshape(2, model)
    gain_columns = jnp.stack(
        [grad_attn_gain, grad_ffn_gain, head_sums[0], head_sums[1]], axis=1
    ).astype(BF16)
    qkv_grads = jnp.concatenate(
        [
            sum(dot(normal_full[b], dqkv[b], TN) for b in range(slots)).astype(BF16),
            jnp.pad(gain_columns, ((0, 0), (0, 124))),
        ],
        axis=1,
    )
    qkv_grads = follow(qkv_grads, [out_sums])
    qkv_sums = lax.psum_scatter(qkv_grads, "fsdp", scatter_dimension=0, tiled=True)
    qkv_all = jnp.moveaxis(seq_spread(qkv_sums), 0, 1).astype(F32)
    held = qkv_all.shape[0]
    edge = hq * HEAD
    kv_edge = edge + hkv_held * HEAD
    last_edge = kv_edge + hkv_held * HEAD
    grad_query = qkv_all[..., :edge].reshape(held, query_width)
    grad_key = qkv_all[..., edge : edge + hkv * HEAD].reshape(held, kv_width)
    grad_value = qkv_all[..., kv_edge : kv_edge + hkv * HEAD].reshape(held, kv_width)
    gain_sums = jnp.sum(qkv_all[..., last_edge : last_edge + 4], axis=1)

    ffn_grad = ()
    for c in range(CHUNKS):
        parts = seq_gather(ffn_sums[c]).reshape(seqs, 3, part, model)
        ffn_grad = place_parts(order, parts, c, ffn_grad)
    ffn_grad = [v.reshape(seqs * hidden_own, model) for v in ffn_grad]

    return (
        jnp.stack(output),
        jnp.stack(grad_tokens),
        gain_sums[:, 0],
        grad_query,
        grad_key,
        grad_value,
        gain_sums[: HEAD // shards, 2],
        gain_sums[: HEAD // shards, 3],
        grad_out,
        gain_sums[:, 1],
        ffn_grad[0],
        ffn_grad[1],
        ffn_grad[2],
    )


def solution(mesh):
    return jax.shard_map(
        on_device,
        mesh=mesh,
        in_specs=(
            P("fsdp", "seq", None),
            P("fsdp", "seq", None),
            P("fsdp"),
            P(),
            P("fsdp", None),
            P("fsdp", None),
            P("fsdp", None),
            P(),
            P(),
            P("fsdp", None),
            P(),
            P("fsdp", None),
            P("fsdp", None),
            P("fsdp", None),
        ),
        out_specs=(
            P("fsdp", "seq", None),
            P("fsdp", "seq", None),
            P("fsdp"),
            P("fsdp", None),
            P("fsdp", None),
            P("fsdp", None),
            P("fsdp"),
            P("fsdp"),
            P("fsdp", None),
            P("fsdp"),
            P("fsdp", None),
            P("fsdp", None),
            P("fsdp", None),
        ),
        check_vma=False,
    )
```

```python
import functools

import jax
import jax.numpy as jnp
import numpy as np
from jax import lax
from jax.experimental import pallas as pl
from jax.experimental.pallas import tpu as pltpu
from jax.sharding import PartitionSpec as P

EPSILON = 1e-05
ROPE_BASE = 1000000.0
NEGATIVE = -1e30
F32 = jnp.float32
BF16 = jnp.bfloat16
NN = (((1,), (0,)), ((), ()))
NT = (((1,), (1,)), ((), ()))
TN = (((0,), (0,)), ((), ()))
SMEM = pl.BlockSpec(memory_space=pltpu.SMEM)
VMEM = pl.BlockSpec(memory_space=pltpu.VMEM)
VMEM_LIMIT = 58 << 20
HEAD = 64
BLOCK = 256
CHUNKS = 2
ANY = pl.BlockSpec(memory_space=pl.ANY)


def dot(a, b, dims=NN):
    return lax.dot_general(a, b, dims, preferred_element_type=F32)


def over_one(place):
    return place + 1 - 2 * (place % 2)


def over_two(place):
    return (place + 2) % 4


def send(source, target, device, out_sem, in_sem):
    return pltpu.make_async_remote_copy(
        src_ref=source,
        dst_ref=target,
        send_sem=out_sem,
        recv_sem=in_sem,
        device_id={"seq": device},
        device_id_type=pl.DeviceIdType.MESH,
    )


def gather_job(source, target, scratch):
    outs, ins, here = scratch
    place = lax.axis_index("seq")
    one, two = over_one(place), over_two(place)
    half = source.shape[0] // 2
    own = pltpu.make_async_copy(source, target.at[0], here.at[0])
    first = send(source, target.at[1], one, outs.at[0], ins.at[0])
    second = send(source, target.at[2], two, outs.at[1], ins.at[1])
    top = pl.ds(0, half)
    low = pl.ds(half, half)
    third = send(target.at[2, top], target.at[3, top], one, outs.at[2], ins.at[2])
    fourth = send(target.at[1, low], target.at[3, low], two, outs.at[3], ins.at[3])

    def begin():
        own.start()
        first.start()
        second.start()

    def middle():
        second.wait_recv()
        third.start()
        first.wait_recv()
        fourth.start()

    def finish():
        third.wait_recv()
        fourth.wait_recv()
        for copy in (first, second, third, fourth):
            copy.wait_send()
        own.wait()

    return begin, middle, finish


def scatter_job(parts, total, scratch):
    outs, ins, here, got_one, got_two, kept, own, last, summed = scratch
    place = lax.axis_index("seq")
    one, two = over_one(place), over_two(place)
    half = parts.shape[1] // 2
    top = pl.ds(0, half)
    low = pl.ds(half, half)
    sends = [
        send(parts.at[3, top], got_one.at[0], one, outs.at[0], ins.at[0]),
        send(parts.at[3, low], got_two.at[0], two, outs.at[1], ins.at[1]),
        send(parts.at[1, top], got_one.at[1], one, outs.at[2], ins.at[2]),
        send(parts.at[2, low], got_two.at[1], two, outs.at[3], ins.at[3]),
        send(kept.at[0], last.at[0], two, outs.at[4], ins.at[4]),
        send(kept.at[1], last.at[1], one, outs.at[5], ins.at[5]),
    ]
    loads = [
        pltpu.make_async_copy(parts.at[2, top], kept.at[0], here.at[0]),
        pltpu.make_async_copy(parts.at[1, low], kept.at[1], here.at[1]),
        pltpu.make_async_copy(parts.at[0], own, here.at[2]),
    ]
    store = pltpu.make_async_copy(summed, total, here.at[3])

    def begin():
        for copy in sends[:4]:
            copy.start()
        for copy in loads:
            copy.start()

    def middle():
        for k, got in enumerate((got_one, got_two)):
            loads[k].wait()
            sends[k].wait_recv()
            kept[k] = (kept[k].astype(F32) + got[0].astype(F32)).astype(BF16)
            sends[4 + k].start()

    def finish():
        loads[2].wait()
        for k, got in enumerate((got_one, got_two)):
            sends[2 + k].wait_recv()
            sends[4 + k].wait_recv()
            rows = slice(k * half, (k + 1) * half)
            summed[rows, :] = (
                own[rows, :].astype(F32) + got[1].astype(F32) + last[k].astype(F32)
            )
        store.start()
        for copy in sends:
            copy.wait_send()
        store.wait()

    return begin, middle, finish


def job_scratch(job):
    kind, array = job
    if kind == "gather":
        return [
            pltpu.SemaphoreType.DMA((4,)),
            pltpu.SemaphoreType.DMA((4,)),
            pltpu.SemaphoreType.DMA((1,)),
        ]
    _, rows, width = array.shape
    halves = pltpu.VMEM((2, rows // 2, width), BF16)
    return [
        pltpu.SemaphoreType.DMA((6,)),
        pltpu.SemaphoreType.DMA((6,)),
        pltpu.SemaphoreType.DMA((4,)),
        halves,
        halves,
        halves,
        pltpu.VMEM((rows, width), BF16),
        halves,
        pltpu.VMEM((rows, width), F32),
    ]


def job_result(job):
    kind, array = job
    if kind == "gather":
        return jax.ShapeDtypeStruct((4,) + array.shape, BF16)
    return jax.ShapeDtypeStruct(array.shape[1:], F32)


def plain_job(job):
    kind, array = job
    if kind == "gather":
        return lax.all_gather(array, "seq", axis=0)
    return lax.psum_scatter(array, "seq", scatter_dimension=0).astype(F32)


def meet():
    place = lax.axis_index("seq")
    barrier = pltpu.get_barrier_semaphore()
    for device in (over_one(place), over_two(place)):
        pl.semaphore_signal(
            barrier, inc=1, device_id={"seq": device}, device_id_type=pl.DeviceIdType.MESH
        )
    pl.semaphore_wait(barrier, 2)


def call(
    body, operands, in_specs, out_shape, out_specs, jobs, number, after=None,
    grid=(), scratch=(), cost=None, name=None,
):
    plain = lax.axis_size("seq") != 4
    results = [plain_job(job) for job in jobs] if plain else []
    inside = [] if plain else jobs
    extra = [] if after is None else [after]
    job_shapes = [job_scratch(job) for job in inside]
    n_in = len(operands)
    n_out = len(out_shape)

    def kernel(*refs):
        ins = refs[:n_in]
        rest = refs[n_in + len(extra) :]
        sources, rest = rest[: len(inside)], rest[len(inside) :]
        outs, rest = rest[:n_out], rest[n_out:]
        targets, rest = rest[: len(inside)], rest[len(inside) :]
        held, rest = rest[: len(scratch)], rest[len(scratch) :]
        phases = []
        for job, source, target, shapes in zip(inside, sources, targets, job_shapes):
            mine, rest = rest[: len(shapes)], rest[len(shapes) :]
            make = gather_job if job[0] == "gather" else scatter_job
            phases.append(make(source, target, mine))

        def hook(k):
            if k == 0 and phases:
                meet()
            for phase in phases:
                phase[k]()

        body(hook, ins, outs, held)

    given = {}
    if inside:
        given = {"collective_id": number, "has_side_effects": True}
    made = pl.pallas_call(
        kernel,
        grid=grid,
        out_shape=tuple(out_shape) + tuple(job_result(job) for job in inside),
        in_specs=list(in_specs) + [ANY] * (len(extra) + len(inside)),
        out_specs=tuple(out_specs) + (ANY,) * len(inside),
        scratch_shapes=list(scratch) + [shape for shapes in job_shapes for shape in shapes],
        compiler_params=pltpu.CompilerParams(vmem_limit_bytes=VMEM_LIMIT, **given),
        cost_estimate=cost,
        name=name,
    )(*operands, *extra, *[job[1] for job in inside])
    return made[:n_out], list(made[n_out:]) + results


def transfer(jobs, number, after=None):
    if lax.axis_size("seq") != 4:
        return [plain_job(job) for job in jobs]

    def body(hook, ins, outs, held):
        for k in range(3):
            hook(k)

    return call(body, [], [], [], [], jobs, number, after, name="transfer")[1]


def partner(v):
    lane = lax.broadcasted_iota(jnp.int32, v.shape, 1)
    return jnp.where(lane % HEAD < HEAD // 2, pltpu.roll(v, 96, 1), pltpu.roll(v, 32, 1))


def head_mean(v, ones):
    high = v.astype(BF16)
    rest = (v - high.astype(F32)).astype(BF16)
    return dot(high, ones) + dot(rest, ones)


def true_chunk(place, c, count):
    if count != 4:
        return c
    low = 1 - place % 2 if c % 2 else place % 2
    high = 1 - place // 2 if c // 2 else place // 2
    return low + 2 * high


def prepare_heads(sizes, place, qkv_ref, qg_ref, kg_ref, cos_ref, sin_ref, ones, q_s, k_s, v_s):
    hq, hkv, _ = sizes
    seqs, rows_in, _ = qkv_ref.shape
    for c in range(seqs):
        j = true_chunk(place, c, seqs)
        rows = slice(c * rows_in, (c + 1) * rows_in)
        cos = cos_ref[rows, :]
        sin = sin_ref[rows, :]
        for p in range((hq + hkv) // 2):
            is_query = p < hq // 2
            x = qkv_ref[j, :, p * 128 : (p + 1) * 128].astype(F32)
            gain = qg_ref[...] * HEAD**-0.5 if is_query else kg_ref[...]
            y = x * lax.rsqrt(head_mean(x * x, ones) + EPSILON) * gain
            y = (y * cos + partner(y) * sin).astype(BF16)
            for t in range(2):
                part = y[:, t * HEAD : (t + 1) * HEAD]
                if is_query:
                    q_s[2 * p + t, rows, :] = part
                else:
                    k_s[2 * p - hq + t, rows, :] = part
        for t in range(hkv):
            start = (hq + hkv + t) * HEAD
            v_s[t, rows, :] = qkv_ref[j, :, start : start + HEAD]


def allowed_keys(block, first, keys, length):
    bound = jnp.minimum(first + lax.broadcasted_iota(jnp.int32, (block, 1), 0), length - 1)
    return lax.broadcasted_iota(jnp.int32, (block, keys), 1) <= bound


def attend_kernel(sizes, hook, ins, outs, held):
    len_ref, qkv_ref, qg_ref, kg_ref, cos_ref, sin_ref, ones_ref = ins
    out_ref, lse_ref = outs
    q_s, k_s, v_s, o_s = held
    hook(0)
    hq, hkv, group = sizes
    seqs, rows_in, _ = qkv_ref.shape
    place = lax.axis_index("seq")
    prepare_heads(
        sizes, place, qkv_ref, qg_ref, kg_ref, cos_ref, sin_ref, ones_ref[...], q_s, k_s, v_s
    )
    for i in range(seqs * rows_in // BLOCK):
        keys = (i + 1) * BLOCK
        rows = slice(i * BLOCK, (i + 1) * BLOCK)
        keep = allowed_keys(BLOCK, i * BLOCK, keys, len_ref[0])

        def one_head(h, _):
            kv = h // group
            scores = dot(q_s[h, rows, :], k_s[kv, :keys, :], NT)
            scores = jnp.where(keep, scores, NEGATIVE)
            highest = jnp.max(scores, axis=1, keepdims=True)
            shifted = jnp.exp(scores - highest)
            total = jnp.sum(shifted, axis=1, keepdims=True)
            mixed = dot(shifted.astype(BF16), v_s[kv, :keys, :]) / total
            o_s[h, rows, :] = mixed.astype(BF16)
            lse_ref[h, rows, :] = highest + jnp.log(total)
            return 0

        lax.fori_loop(0, hq, one_head, 0)
        if i == seqs * rows_in // BLOCK - 2:
            hook(1)
    for c in range(seqs):
        j = true_chunk(place, c, seqs)
        rows = slice(c * rows_in, (c + 1) * rows_in)
        for p in range(hq // 2):
            out_ref[j, :, p * 128 : (p + 1) * 128] = jnp.concatenate(
                [o_s[2 * p, rows, :], o_s[2 * p + 1, rows, :]], axis=1
            )
    hook(2)


def attend_back_kernel(sizes, hook, ins, outs, held):
    len_ref, qkv_ref, cot_ref, lse_ref, qg_ref, kg_ref, cos_ref, sin_ref, ones_ref = ins
    dqkv_ref, dgain_ref = outs
    q_s, k_s, v_s, cot_s, dq_s, dk_s, dv_s = held
    hook(0)
    hq, hkv, group = sizes
    seqs, rows_in, _ = qkv_ref.shape
    place = lax.axis_index("seq")
    ones = ones_ref[...]
    prepare_heads(sizes, place, qkv_ref, qg_ref, kg_ref, cos_ref, sin_ref, ones, q_s, k_s, v_s)
    for c in range(seqs):
        j = true_chunk(place, c, seqs)
        for h in range(hq):
            cot_s[h, c * rows_in : (c + 1) * rows_in, :] = cot_ref[
                j, :, h * HEAD : (h + 1) * HEAD
            ]
    dk_s[...] = jnp.zeros_like(dk_s)
    dv_s[...] = jnp.zeros_like(dv_s)
    for i in range(seqs * rows_in // BLOCK):
        keys = (i + 1) * BLOCK
        rows = slice(i * BLOCK, (i + 1) * BLOCK)
        keep = allowed_keys(BLOCK, i * BLOCK, keys, len_ref[0])

        def one_head(h, _):
            kv = h // group
            q = q_s[h, rows, :]
            cot = cot_s[h, rows, :]
            k = k_s[kv, :keys, :]
            scores = jnp.where(keep, dot(q, k, NT), NEGATIVE)
            probs = jnp.exp(scores - lse_ref[h, rows, :])
            prob_cot = dot(cot, v_s[kv, :keys, :], NT)
            inner = jnp.sum(probs * prob_cot, axis=1, keepdims=True)
            score_cot = (probs * (prob_cot - inner)).astype(BF16)
            dq_s[h, rows, :] = dot(score_cot, k) * HEAD**-0.5
            dk_s[kv, :keys, :] += dot(score_cot, q, TN)
            dv_s[kv, :keys, :] += dot(probs.astype(BF16), cot, TN)
            return 0

        lax.fori_loop(0, hq, one_head, 0)
        if i == seqs * rows_in // BLOCK - 2:
            hook(1)
    gain_sums = [jnp.zeros((1, 128), F32), jnp.zeros((1, 128), F32)]
    for c in range(seqs):
        j = true_chunk(place, c, seqs)
        rows = slice(c * rows_in, (c + 1) * rows_in)
        cos = cos_ref[rows, :]
        sin = sin_ref[rows, :]
        for p in range((hq + hkv) // 2):
            is_query = p < hq // 2
            x = qkv_ref[j, :, p * 128 : (p + 1) * 128].astype(F32)
            gain = qg_ref[...] if is_query else kg_ref[...]
            source, first = (dq_s, 2 * p) if is_query else (dk_s, 2 * p - hq)
            turned = jnp.concatenate([source[first, rows, :], source[first + 1, rows, :]], axis=1)
            scale = lax.rsqrt(head_mean(x * x, ones) + EPSILON)
            straight = turned * cos + partner(turned * sin)
            unit = x * scale
            which = 0 if is_query else 1
            gain_sums[which] += jnp.sum(straight * unit, axis=0, keepdims=True)
            pulled = gain * straight
            dx = scale * (pulled - unit * head_mean(unit * pulled, ones))
            dqkv_ref[j, :, p * 128 : (p + 1) * 128] = dx.astype(BF16)
        for p in range(hkv // 2):
            start = (hq + hkv) * HEAD + p * 128
            dqkv_ref[j, :, start : start + 128] = jnp.concatenate(
                [dv_s[2 * p, rows, :], dv_s[2 * p + 1, rows, :]], axis=1
            ).astype(BF16)
    dgain_ref[0:1, :] = gain_sums[0]
    dgain_ref[1:2, :] = gain_sums[1]
    hook(2)


def position_tables(length):
    places = np.arange(length, dtype=np.float32)
    half = HEAD // 2
    freqs = np.float32(ROPE_BASE) ** (-(np.arange(half, dtype=np.float32) * 2.0) / HEAD)
    angles = places[:, None] * freqs.astype(np.float32)[None, :]
    cos = np.cos(angles).astype(np.float32)
    sin = np.sin(angles).astype(np.float32)
    ones = np.kron(np.eye(2), np.ones((HEAD, HEAD)) / HEAD)
    return (
        jnp.asarray(np.concatenate([cos] * 4, axis=1)),
        jnp.asarray(np.concatenate([-sin, sin, -sin, sin], axis=1)),
        jnp.asarray(ones, dtype=BF16),
    )


def attend(sizes, length, qkv, gains, tables, jobs, number, after):
    seqs, rows_in, _ = qkv.shape
    hq, hkv, _ = sizes
    slot = seqs * rows_in
    return call(
        functools.partial(attend_kernel, sizes),
        [length, qkv, *gains, *tables],
        [SMEM] + [VMEM] * 6,
        [
            jax.ShapeDtypeStruct((seqs, rows_in, hq * HEAD), BF16),
            jax.ShapeDtypeStruct((hq, slot, 1), F32),
        ],
        [VMEM, VMEM],
        jobs,
        number,
        after,
        scratch=[
            pltpu.VMEM((hq, slot, HEAD), BF16),
            pltpu.VMEM((hkv, slot, HEAD), BF16),
            pltpu.VMEM((hkv, slot, HEAD), BF16),
            pltpu.VMEM((hq, slot, HEAD), BF16),
        ],
        cost=pl.CostEstimate(
            flops=56 * hq * slot * slot * HEAD, bytes_accessed=1 << 23, transcendentals=0
        ),
        name="attend",
    )


def attend_back(sizes, length, qkv, cot, lse, gains, tables, jobs, number, after):
    seqs, rows_in, width = qkv.shape
    hq, hkv, _ = sizes
    slot = seqs * rows_in
    return call(
        functools.partial(attend_back_kernel, sizes),
        [length, qkv, cot, lse, *gains, *tables],
        [SMEM] + [VMEM] * 8,
        [
            jax.ShapeDtypeStruct((seqs, rows_in, width), BF16),
            jax.ShapeDtypeStruct((2, 128), F32),
        ],
        [VMEM, VMEM],
        jobs,
        number,
        after,
        scratch=[
            pltpu.VMEM((hq, slot, HEAD), BF16),
            pltpu.VMEM((hkv, slot, HEAD), BF16),
            pltpu.VMEM((hkv, slot, HEAD), BF16),
            pltpu.VMEM((hq, slot, HEAD), BF16),
            pltpu.VMEM((hq, slot, HEAD), F32),
            pltpu.VMEM((hkv, slot, HEAD), F32),
            pltpu.VMEM((hkv, slot, HEAD), F32),
        ],
        cost=pl.CostEstimate(
            flops=88 * hq * slot * slot * HEAD, bytes_accessed=1 << 23, transcendentals=0
        ),
        name="attend_back",
    )


def hooked(hook, step, steps, work):
    pl.when(step == 0)(lambda: hook(0))
    pl.when(step == (2 * steps) // 3)(lambda: hook(1))
    work()
    pl.when(step == steps - 1)(lambda: hook(2))


def ffn_kernel(steps, hook, ins, outs, held):
    hooked(hook, pl.program_id(0), steps, lambda: ffn_tile(*ins[:5], ins[5:], *outs))


def ffn_tile(mid_ref, cot_ref, gate_ref, up_ref, down_ref, sums, acts_ref, pull_ref):
    model = mid_ref.shape[-1]
    hidden = acts_ref.shape[-1]
    gate_w = gate_ref[...].reshape(hidden, model)
    up_w = up_ref[...].reshape(hidden, model)
    down_w = down_ref[...].reshape(hidden, model)
    mid = mid_ref[...]
    gate = dot(mid, gate_w, NT)
    up = dot(mid, up_w, NT)
    mids_cot = dot(cot_ref[...], down_w, NT)
    sigmoid = jax.nn.sigmoid(gate)
    active = gate * sigmoid
    gate_cot = (mids_cot * up * sigmoid * (1.0 + gate * (1.0 - sigmoid))).astype(BF16)
    up_cot = (mids_cot * active).astype(BF16)
    acts_ref[0] = gate_cot
    acts_ref[1] = up_cot
    acts_ref[2] = (active * up).astype(BF16)
    pulled = dot(gate_cot, gate_w) + dot(up_cot, up_w)
    for sum_ref in sums:
        pulled = pulled + sum_ref[...]
    pull_ref[...] = pulled.astype(pull_ref.dtype)


def ffn_both(mid, cot, weights, summed, last, jobs, number, after):
    tokens, model = mid.shape
    shards, _, part, _ = weights.shape
    hidden = shards * part
    tile = min(256, tokens)

    def weight_spec(kind):
        return pl.BlockSpec(
            (shards, 1, part, model),
            lambda i: (0, kind, 0, 0),
            pipeline_mode=pl.Buffered(buffer_count=1),
        )

    row_spec = pl.BlockSpec((tile, model), lambda i: (i, 0))
    extra = () if summed is None else (summed,)
    return call(
        functools.partial(ffn_kernel, tokens // tile),
        [mid, cot, weights, weights, weights, *extra],
        [row_spec, row_spec, weight_spec(0), weight_spec(1), weight_spec(2)]
        + [row_spec] * len(extra),
        [
            jax.ShapeDtypeStruct((3, tokens, hidden), BF16),
            jax.ShapeDtypeStruct((tokens, model), BF16 if last else F32),
        ],
        [pl.BlockSpec((3, tile, hidden), lambda i: (0, i, 0)), row_spec],
        jobs,
        number,
        after,
        grid=(tokens // tile,),
        cost=pl.CostEstimate(
            flops=16 * tokens * model * hidden,
            bytes_accessed=4 * tokens * model + 6 * hidden * model,
            transcendentals=0,
        ),
        name="ffn_both",
    )


def ffn_grad_kernel(slots, tiles, hook, ins, outs, held):
    acts = ins[:slots]
    mids = ins[slots : 2 * slots]
    cots = ins[2 * slots :]
    (out_ref,) = outs
    kind = pl.program_id(0)

    def store(others):
        total = dot(acts[0][0], others[0][...], TN)
        for act, other in zip(acts[1:], others[1:]):
            total = total + dot(act[0], other[...], TN)
        out_ref[...] = total.astype(BF16).reshape(out_ref.shape)

    def work():
        pl.when(kind < 2)(lambda: store(mids))
        pl.when(kind == 2)(lambda: store(cots))

    hooked(hook, kind * tiles + pl.program_id(1), 3 * tiles, work)


def ffn_grads(acts, mids, cots, shards, jobs, number, after):
    slots = len(acts)
    _, tokens, hidden = acts[0].shape
    model = mids[0].shape[-1]
    part = hidden // shards
    tile = 256
    per = tile // part
    whole = pl.BlockSpec(
        (tokens, model), lambda k, i: (0, 0), pipeline_mode=pl.Buffered(buffer_count=1)
    )
    return call(
        functools.partial(ffn_grad_kernel, slots, hidden // tile),
        [*acts, *mids, *cots],
        [pl.BlockSpec((1, tokens, tile), lambda k, i: (k, 0, i))] * slots
        + [whole] * (2 * slots),
        [jax.ShapeDtypeStruct((shards, 3, part, model), BF16)],
        [pl.BlockSpec((per, 1, part, model), lambda k, i: (i, k, 0, 0))],
        jobs,
        number,
        after,
        grid=(3, hidden // tile),
        cost=pl.CostEstimate(
            flops=9 * slots * tokens * model * hidden,
            bytes_accessed=4 * slots * tokens * model,
            transcendentals=0,
        ),
        name="ffn_grads",
    )


def ffn_down_kernel(chunks, steps, hook, ins, outs, held):
    acts = ins[:chunks]
    downs = ins[chunks:]
    (out_ref,) = outs

    def work():
        total = None
        for act, down in zip(acts, downs):
            hidden = act.shape[-1]
            term = dot(act[0], down[...].reshape(hidden, down.shape[-1]))
            total = term if total is None else total + term
        out_ref[...] = total.astype(BF16)

    hooked(hook, pl.program_id(0), steps, work)


def ffn_down(acts, weights, jobs, number, after):
    chunks = len(acts)
    _, tokens, hidden = acts[0].shape
    shards, _, part, model = weights[0].shape
    tile = min(256, tokens)
    act_spec = pl.BlockSpec((1, tile, hidden), lambda i: (2, i, 0))
    down_spec = pl.BlockSpec(
        (shards, 1, part, model),
        lambda i: (0, 2, 0, 0),
        pipeline_mode=pl.Buffered(buffer_count=1),
    )
    return call(
        functools.partial(ffn_down_kernel, chunks, tokens // tile),
        [*acts, *weights],
        [act_spec] * chunks + [down_spec] * chunks,
        [jax.ShapeDtypeStruct((tokens, model), BF16)],
        [pl.BlockSpec((tile, model), lambda i: (i, 0))],
        jobs,
        number,
        after,
        grid=(tokens // tile,),
        cost=pl.CostEstimate(
            flops=4 * chunks * tokens * model * hidden,
            bytes_accessed=chunks * hidden * (tokens + model) * 2,
            transcendentals=0,
        ),
        name="ffn_down",
    )


def place_kernel(place_ref, parts_ref, *refs):
    for kind, out_ref in enumerate(refs[-3:]):
        out_ref[0, 0] = parts_ref[0, kind].astype(F32)


def place_parts(place, parts, chunk, held):
    seqs, _, part, model = parts.shape
    out = jax.ShapeDtypeStruct((seqs, CHUNKS, part, model), F32)
    out_spec = pl.BlockSpec(
        (1, 1, part, model), lambda j, at: (jnp.bitwise_xor(at[0], j), chunk, 0, 0)
    )
    return pl.pallas_call(
        place_kernel,
        out_shape=(out,) * 3,
        grid_spec=pltpu.PrefetchScalarGridSpec(
            num_scalar_prefetch=1,
            grid=(seqs,),
            in_specs=[pl.BlockSpec((1, 3, part, model), lambda j, at: (j, 0, 0, 0))]
            + [ANY] * len(held),
            out_specs=(out_spec,) * 3,
        ),
        input_output_aliases={2 + k: k for k in range(len(held))},
        compiler_params=pltpu.CompilerParams(vmem_limit_bytes=VMEM_LIMIT),
        cost_estimate=pl.CostEstimate(
            flops=0, bytes_accessed=18 * seqs * part * model, transcendentals=0
        ),
        name="place_parts",
    )(place, parts, *held)


def ring_places(count):
    return (
        [(i, i ^ 1) for i in range(count)],
        [(i, i ^ 2) for i in range(count)],
    )


def seq_gather(rows):
    count = lax.axis_size("seq")
    if count != 4:
        return lax.all_gather(rows, "seq", axis=0)
    over_one, over_two = ring_places(count)
    half = rows.shape[0] // 2
    one = lax.ppermute(rows, "seq", over_one)
    two = lax.ppermute(rows, "seq", over_two)
    top = lax.ppermute(two[:half], "seq", over_one)
    low = lax.ppermute(one[half:], "seq", over_two)
    return jnp.concatenate([rows, one, two, top, low], axis=0).reshape(
        (count,) + rows.shape
    )


def seq_spread(rows):
    count = lax.axis_size("seq")
    parts = seq_gather(rows)
    if count != 4:
        return parts
    place = lax.axis_index("seq")
    return jnp.stack(
        [lax.dynamic_index_in_dim(parts, place ^ j, 0, keepdims=False) for j in range(count)]
    )


def out_home(sums):
    seqs = lax.axis_size("seq")
    shards = lax.axis_size("fsdp")
    per = shards // seqs
    held = []
    for j in range(seqs):
        moves = [
            (s * shards + h * seqs + j, s * shards + s * per + h)
            for s in range(seqs)
            for h in range(per)
        ]
        held.append(lax.ppermute(sums, ("seq", "fsdp"), moves))
    held = jnp.concatenate(held, axis=0)
    if seqs != 4:
        return lax.psum(held, "seq")

    def hop(values, start, end):
        moves = [
            ((s ^ start) * shards + s * per + h, (s ^ end) * shards + s * per + h)
            for s in range(seqs)
            for h in range(per)
        ]
        return lax.ppermute(values, ("seq", "fsdp"), moves)

    half = held.shape[0] // 2
    one = hop(held, 0, 1)
    two = hop(held, 0, 2)
    top = hop(two[:half], 2, 3)
    low = hop(one[half:], 1, 3)
    return held + one + two + jnp.concatenate([top, low], axis=0)


def scale_of(values):
    return lax.rsqrt(jnp.mean(values * values, axis=-1, keepdims=True) + EPSILON)


def normed(values, gain):
    return values * scale_of(values) * gain


def normed_back(values, gain, cot):
    scale = scale_of(values)
    pulled = cot * gain
    mean = jnp.mean(values * pulled, axis=-1, keepdims=True)
    return (
        scale * pulled - values * (scale * scale * scale) * mean,
        jnp.sum(cot * values * scale, axis=0),
    )


def follow(values, earlier):
    return lax.optimization_barrier((values, *earlier))[0]


def own_columns(weight, heads, place):
    width = heads * HEAD
    part = lax.dynamic_slice_in_dim(weight, place * width, width, 1)
    if heads % 2:
        part = jnp.pad(part, ((0, 0), (0, HEAD)))
    return part


def on_device(
    tokens,
    cotangent,
    lengths,
    attn_gain,
    query_weight,
    key_weight,
    value_weight,
    query_gain,
    key_gain,
    out_weight,
    ffn_gain,
    gate_weight,
    up_weight,
    down_weight,
):
    slots, rows, model = tokens.shape
    seqs = lax.axis_size("seq")
    shards = lax.axis_size("fsdp")
    place = lax.axis_index("seq")
    shard = lax.axis_index("fsdp")
    slot_len = rows * seqs
    query_width = query_weight.shape[1]
    kv_width = key_weight.shape[1]
    hq = query_width // seqs // HEAD
    hkv = kv_width // seqs // HEAD
    hkv_held = hkv + hkv % 2
    sizes = (hq, hkv_held, hq // hkv)
    order = (place if seqs == 4 else place * 0).reshape(1)
    tables = position_tables(slot_len)
    gains = (
        jnp.concatenate([query_gain, query_gain]).reshape(1, 2 * HEAD),
        jnp.concatenate([key_gain, key_gain]).reshape(1, 2 * HEAD),
    )

    flat = (slot_len, model)
    chunked = (seqs, rows, model)
    places = place * rows + jnp.arange(rows, dtype=jnp.int32)
    live = (places[None, :] < lengths[:, None]).astype(F32)[..., None]
    inputs = tokens.astype(F32)
    out_cot = cotangent.astype(F32) * live
    out_low = [out_cot[b].astype(BF16) for b in range(slots)]
    normal_in = [normed(inputs[b], attn_gain).astype(BF16) for b in range(slots)]

    qkv_own = jnp.concatenate(
        [
            own_columns(query_weight, hq, place),
            own_columns(key_weight, hkv, place),
            own_columns(value_weight, hkv, place),
        ],
        axis=1,
    )
    qkv_weight = lax.all_gather(qkv_own, "fsdp", axis=0, tiled=True)
    per = shards // seqs
    piece = out_weight.shape[0] // seqs
    out_own = None
    for j in range(seqs):
        moves = [
            (s * shards + s * per + h, s * shards + h * seqs + j)
            for s in range(seqs)
            for h in range(per)
        ]
        got = lax.ppermute(out_weight[j * piece : (j + 1) * piece], ("seq", "fsdp"), moves)
        out_own = got if out_own is None else out_own + got
    out_rows = lax.all_gather(out_own, "fsdp", axis=0, tiled=True)
    hidden_own = gate_weight.shape[0] // seqs
    part = hidden_own // CHUNKS
    ffn_weights = []
    for c in range(CHUNKS):
        start = place * hidden_own + c * part
        mine = jnp.stack(
            [
                lax.dynamic_slice_in_dim(w, start, part, 0)
                for w in (gate_weight, up_weight, down_weight)
            ]
        )
        ffn_weights.append(lax.all_gather(mine, "fsdp", axis=0))

    def project(full):
        return dot(full.reshape(flat), qkv_weight).astype(BF16).reshape(seqs, rows, -1)

    def leave(mixed):
        return dot(mixed.reshape(slot_len, -1), out_rows).astype(BF16).reshape(chunked)

    def enter_ffn(b, total):
        res = inputs[b] + total
        return res, normed(res, ffn_gain).astype(BF16)

    def heads(b, raw, jobs, number, after):
        return attend(sizes, lengths[b : b + 1], raw, gains, tables, jobs, number, after)

    normal_full = [None] * slots
    cot_full = [None] * slots
    mid_full = [None] * slots
    (normal_full[0],) = transfer([("gather", normal_in[0])], 1)
    qkv_0 = project(normal_full[0])
    (mixed_0, lse_0), (normal_full[1],) = heads(
        0, qkv_0, [("gather", normal_in[1])], 2, normal_full[0]
    )
    qkv_1 = project(normal_full[1])
    (mixed_1, lse_1), (total_0,) = heads(1, qkv_1, [("scatter", leave(mixed_0))], 3, mixed_0)
    qkv = [qkv_0, qkv_1]
    log_sums = [lse_0, lse_1]
    attended = [v.reshape(slot_len, hq * HEAD) for v in (mixed_0, mixed_1)]
    res_0, mid_0 = enter_ffn(0, total_0)
    mid_full[0], cot_full[0] = [
        v.reshape(flat)
        for v in transfer([("gather", mid_0), ("gather", out_low[0])], 4, mixed_1)
    ]

    acts = [[None] * slots for _ in range(CHUNKS)]
    pulled = [None] * slots

    def ffn_step(b, c, jobs, number, after):
        (acts[c][b], pulled[b]), results = ffn_both(
            mid_full[b], cot_full[b], ffn_weights[c], pulled[b], c == CHUNKS - 1,
            jobs, number, after,
        )
        return results

    def grad_step(c, jobs, number, after):
        (grads,), results = ffn_grads(
            acts[c], mid_full, cot_full, shards, jobs, number, after
        )
        return grads.reshape(shards, 3 * part, model), results

    def leave_ffn(b, jobs, number, after):
        (out,), results = ffn_down(
            [acts[c][b] for c in range(CHUNKS)], ffn_weights, jobs, number, after
        )
        return out.reshape(chunked), results

    total_1, full = ffn_step(
        0, 0, [("scatter", leave(mixed_1)), ("gather", out_low[1])], 5, mid_full[0]
    )
    cot_full[1] = full.reshape(flat)
    res_1, mid_1 = enter_ffn(1, total_1)
    hidden_res = [res_0, res_1]
    (full,) = ffn_step(0, 1, [("gather", mid_1)], 6, acts[0][0])
    mid_full[1] = full.reshape(flat)
    (mid_total_0,) = ffn_step(1, 0, [("scatter", pulled[0].reshape(chunked))], 7, acts[1][0])

    def pull_mid(b, total):
        pull, gain_part = normed_back(hidden_res[b], ffn_gain, total)
        cot = out_cot[b] + pull
        return cot, cot.astype(BF16), gain_part

    res_cot_0, low_0, ffn_gain_0 = pull_mid(0, mid_total_0)
    grads_0, (res_full_0,) = grad_step(0, [("gather", low_0)], 8, acts[0][1])
    ffn_sums = [lax.psum_scatter(grads_0, "fsdp", scatter_dimension=0)]
    out_0, _ = leave_ffn(0, [], 0, grads_0)
    (out_total_0,) = ffn_step(1, 1, [("scatter", out_0)], 9, out_0)
    grads_1, (mid_total_1,) = grad_step(
        1, [("scatter", pulled[1].reshape(chunked))], 10, acts[1][1]
    )
    ffn_sums.append(
        lax.psum_scatter(follow(grads_1, ffn_sums), "fsdp", scatter_dimension=0)
    )
    res_cot_1, low_1, ffn_gain_1 = pull_mid(1, mid_total_1)
    grad_ffn_gain = ffn_gain_0 + ffn_gain_1

    def back(b, full, jobs, number, after):
        attended_cot = dot(full, out_rows, NT).astype(BF16).reshape(seqs, rows, hq * HEAD)
        (cots, gain_part), results = attend_back(
            sizes, lengths[b : b + 1], qkv[b], attended_cot, log_sums[b], gains, tables,
            jobs, number, after,
        )
        return cots.reshape(slot_len, -1), gain_part, results

    def pull_heads(cots):
        return dot(cots, qkv_weight, NT).astype(BF16).reshape(chunked)

    dqkv_0, heads_gain_0, (res_full_1,) = back(
        0, res_full_0.reshape(flat), [("gather", low_1)], 11, grads_1
    )
    dqkv_1, heads_gain_1, (in_total_0,) = back(
        1, res_full_1.reshape(flat), [("scatter", pull_heads(dqkv_0))], 12, dqkv_0
    )
    head_gain = heads_gain_0 + heads_gain_1
    dqkv = [dqkv_0, dqkv_1]
    res_full = [v.reshape(flat) for v in (res_full_0, res_full_1)]
    out_1, (in_total_1,) = leave_ffn(1, [("scatter", pull_heads(dqkv_1))], 13, dqkv_1)
    (out_total_1,) = transfer([("scatter", out_1)], 14, out_1)

    output = [
        (live[b] * (hidden_res[b] + total)).astype(BF16)
        for b, total in enumerate((out_total_0, out_total_1))
    ]
    grad_tokens = []
    grad_attn_gain = 0.0
    for b, (in_cot, cot) in enumerate(((in_total_0, res_cot_0), (in_total_1, res_cot_1))):
        pull, gain_part = normed_back(inputs[b], attn_gain, in_cot)
        grad_attn_gain = grad_attn_gain + gain_part
        grad_tokens.append((cot + pull).astype(BF16))

    out_grads = sum(dot(attended[b], res_full[b], TN) for b in range(slots)).astype(BF16)
    out_grads = follow(out_grads, ffn_sums[-1:])
    out_sums = lax.psum_scatter(out_grads, "fsdp", scatter_dimension=0, tiled=True)
    grad_out = out_home(out_sums).astype(F32)

    head_sums = jnp.pad(
        (head_gain[:, :HEAD] + head_gain[:, HEAD:]).reshape(2, shards, 1, HEAD // shards),
        ((0, 0), (0, 0), (0, 0), (0, model // shards - HEAD // shards)),
    ).reshape(2, model)
    gain_columns = jnp.stack(
        [grad_attn_gain, grad_ffn_gain, head_sums[0], head_sums[1]], axis=1
    ).astype(BF16)
    qkv_grads = jnp.concatenate(
        [
            sum(dot(normal_full[b].reshape(flat), dqkv[b], TN) for b in range(slots)).astype(BF16),
            jnp.pad(gain_columns, ((0, 0), (0, 124))),
        ],
        axis=1,
    )
    qkv_grads = follow(qkv_grads, [out_sums])
    qkv_sums = lax.psum_scatter(qkv_grads, "fsdp", scatter_dimension=0, tiled=True)
    qkv_all = jnp.moveaxis(seq_spread(qkv_sums), 0, 1).astype(F32)
    held = qkv_all.shape[0]
    edge = hq * HEAD
    kv_edge = edge + hkv_held * HEAD
    last_edge = kv_edge + hkv_held * HEAD
    grad_query = qkv_all[..., :edge].reshape(held, query_width)
    grad_key = qkv_all[..., edge : edge + hkv * HEAD].reshape(held, kv_width)
    grad_value = qkv_all[..., kv_edge : kv_edge + hkv * HEAD].reshape(held, kv_width)
    gain_sums = jnp.sum(qkv_all[..., last_edge : last_edge + 4], axis=1)

    ffn_grad = ()
    for c in range(CHUNKS):
        parts = seq_gather(ffn_sums[c]).reshape(seqs, 3, part, model)
        ffn_grad = place_parts(order, parts, c, ffn_grad)
    ffn_grad = [v.reshape(seqs * hidden_own, model) for v in ffn_grad]

    return (
        jnp.stack(output),
        jnp.stack(grad_tokens),
        gain_sums[:, 0],
        grad_query,
        grad_key,
        grad_value,
        gain_sums[: HEAD // shards, 2],
        gain_sums[: HEAD // shards, 3],
        grad_out,
        gain_sums[:, 1],
        ffn_grad[0],
        ffn_grad[1],
        ffn_grad[2],
    )


def solution(mesh):
    return jax.shard_map(
        on_device,
        mesh=mesh,
        in_specs=(
            P("fsdp", "seq", None),
            P("fsdp", "seq", None),
            P("fsdp"),
            P(),
            P("fsdp", None),
            P("fsdp", None),
            P("fsdp", None),
            P(),
            P(),
            P("fsdp", None),
            P(),
            P("fsdp", None),
            P("fsdp", None),
            P("fsdp", None),
        ),
        out_specs=(
            P("fsdp", "seq", None),
            P("fsdp", "seq", None),
            P("fsdp"),
            P("fsdp", None),
            P("fsdp", None),
            P("fsdp", None),
            P("fsdp"),
            P("fsdp"),
            P("fsdp", None),
            P("fsdp"),
            P("fsdp", None),
            P("fsdp", None),
            P("fsdp", None),
        ),
        check_vma=False,
    )
```

```python
import functools

import jax
import jax.numpy as jnp
import numpy as np
from jax import lax
from jax.experimental import pallas as pl
from jax.experimental.pallas import tpu as pltpu
from jax.sharding import PartitionSpec as P

EPSILON = 1e-05
ROPE_BASE = 1000000.0
NEGATIVE = -1e30
F32 = jnp.float32
BF16 = jnp.bfloat16
NN = (((1,), (0,)), ((), ()))
NT = (((1,), (1,)), ((), ()))
TN = (((0,), (0,)), ((), ()))
SMEM = pl.BlockSpec(memory_space=pltpu.SMEM)
VMEM = pl.BlockSpec(memory_space=pltpu.VMEM)
VMEM_LIMIT = 58 << 20
HEAD = 64
BLOCK = 256
CHUNKS = 2
ANY = pl.BlockSpec(memory_space=pl.ANY)


def dot(a, b, dims=NN):
    return lax.dot_general(a, b, dims, preferred_element_type=F32)


def over_one(place):
    return place + 1 - 2 * (place % 2)


def over_two(place):
    return (place + 2) % 4


def send(source, target, device, out_sem, in_sem):
    return pltpu.make_async_remote_copy(
        src_ref=source,
        dst_ref=target,
        send_sem=out_sem,
        recv_sem=in_sem,
        device_id={"seq": device},
        device_id_type=pl.DeviceIdType.MESH,
    )


def gather_job(sources, targets, scratch):
    (source,) = sources
    (target,) = targets
    outs, ins, here = scratch
    place = lax.axis_index("seq")
    one, two = over_one(place), over_two(place)
    half = source.shape[0] // 2
    own = pltpu.make_async_copy(source, target.at[0], here.at[0])
    first = send(source, target.at[1], one, outs.at[0], ins.at[0])
    second = send(source, target.at[2], two, outs.at[1], ins.at[1])
    top = pl.ds(0, half)
    low = pl.ds(half, half)
    third = send(target.at[2, top], target.at[3, top], one, outs.at[2], ins.at[2])
    fourth = send(target.at[1, low], target.at[3, low], two, outs.at[3], ins.at[3])

    def begin():
        own.start()
        first.start()
        second.start()

    def middle():
        second.wait_recv()
        third.start()
        first.wait_recv()
        fourth.start()

    def finish():
        third.wait_recv()
        fourth.wait_recv()
        for copy in (first, second, third, fourth):
            copy.wait_send()
        own.wait()

    return no_greeting, begin, middle, finish


def scatter_job(sources, targets, scratch):
    (parts,) = sources
    (total,) = targets
    outs, ins, here, got_one, got_two, kept, own, last, summed = scratch
    place = lax.axis_index("seq")
    one, two = over_one(place), over_two(place)
    half = parts.shape[1] // 2
    top = pl.ds(0, half)
    low = pl.ds(half, half)
    sends = [
        send(parts.at[3, top], got_one.at[0], one, outs.at[0], ins.at[0]),
        send(parts.at[3, low], got_two.at[0], two, outs.at[1], ins.at[1]),
        send(parts.at[1, top], got_one.at[1], one, outs.at[2], ins.at[2]),
        send(parts.at[2, low], got_two.at[1], two, outs.at[3], ins.at[3]),
        send(kept.at[0], last.at[0], two, outs.at[4], ins.at[4]),
        send(kept.at[1], last.at[1], one, outs.at[5], ins.at[5]),
    ]
    loads = [
        pltpu.make_async_copy(parts.at[2, top], kept.at[0], here.at[0]),
        pltpu.make_async_copy(parts.at[1, low], kept.at[1], here.at[1]),
        pltpu.make_async_copy(parts.at[0], own, here.at[2]),
    ]
    store = pltpu.make_async_copy(summed, total, here.at[3])

    def begin():
        for copy in sends[:4]:
            copy.start()
        for copy in loads:
            copy.start()

    def middle():
        for k, got in enumerate((got_one, got_two)):
            loads[k].wait()
            sends[k].wait_recv()
            kept[k] = (kept[k].astype(F32) + got[0].astype(F32)).astype(BF16)
            sends[4 + k].start()

    def finish():
        loads[2].wait()
        for k, got in enumerate((got_one, got_two)):
            sends[2 + k].wait_recv()
            sends[4 + k].wait_recv()
            rows = slice(k * half, (k + 1) * half)
            summed[rows, :] = (
                own[rows, :].astype(F32) + got[1].astype(F32) + last[k].astype(F32)
            )
        store.start()
        for copy in sends:
            copy.wait_send()
        store.wait()

    return no_greeting, begin, middle, finish


def no_greeting(barrier):
    return 0


def nothing():
    pass


def greet(barrier, device):
    pl.semaphore_signal(
        barrier, inc=1, device_id=device, device_id_type=pl.DeviceIdType.MESH
    )


def deal_job(sources, targets, scratch):
    (source,) = sources
    (target,) = targets
    outs, ins, here = scratch
    rows = target.shape[0]
    count = source.shape[0] // rows
    place = lax.axis_index("seq")
    shard = lax.axis_index("fsdp")
    per = lax.axis_size("fsdp") // count
    part = shard % per
    is_source = shard // per == place
    to_self = jnp.logical_and(is_source, shard // count == part)
    origin = place * per + shard // count

    def copy(j):
        return pltpu.make_async_remote_copy(
            src_ref=source.at[pl.ds(j * rows, rows)],
            dst_ref=target,
            send_sem=outs.at[j],
            recv_sem=ins.at[0],
            device_id={"fsdp": part * count + j},
            device_id_type=pl.DeviceIdType.MESH,
        )

    def local(j):
        return pltpu.make_async_copy(source.at[pl.ds(j * rows, rows)], target, here.at[0])

    def greeting(barrier):
        pl.when(origin != shard)(lambda: greet(barrier, {"fsdp": origin}))
        return jnp.where(is_source, count, 0) - jnp.where(to_self, 1, 0)

    def each(act_remote, act_local):
        for j in range(count):
            mine = part * count + j == shard
            pl.when(jnp.logical_and(is_source, mine))(lambda j=j: act_local(local(j)))
            pl.when(jnp.logical_and(is_source, jnp.logical_not(mine)))(
                lambda j=j: act_remote(copy(j))
            )

    def begin():
        each(lambda c: c.start(), lambda c: c.start())

    def finish():
        each(lambda c: c.wait_send(), lambda c: c.wait())
        pl.when(origin != shard)(lambda: copy(0).wait_recv())

    return greeting, begin, nothing, finish


def home_job(sources, targets, scratch):
    (source,) = sources
    (target,) = targets
    outs, ins, here = scratch
    rows = source.shape[0]
    count = target.shape[0] // rows
    place = lax.axis_index("seq")
    shard = lax.axis_index("fsdp")
    per = lax.axis_size("fsdp") // count
    piece = shard % count
    owner = place * per + shard // count
    spot = pl.ds(pl.multiple_of(piece * rows, rows), rows)

    def copy(s):
        return pltpu.make_async_remote_copy(
            src_ref=source,
            dst_ref=target.at[spot],
            send_sem=outs.at[s],
            recv_sem=ins.at[piece],
            device_id={"seq": s, "fsdp": owner},
            device_id_type=pl.DeviceIdType.MESH,
        )

    def arrival(j):
        return pltpu.make_async_remote_copy(
            src_ref=source,
            dst_ref=target.at[pl.ds(j * rows, rows)],
            send_sem=outs.at[0],
            recv_sem=ins.at[j],
            device_id={"seq": place, "fsdp": owner},
            device_id_type=pl.DeviceIdType.MESH,
        )

    own = pltpu.make_async_copy(source, target.at[spot], here.at[0])

    def is_self(s):
        return jnp.logical_and(owner == shard, place == s)

    def comes_from(j):
        return shard // per, (shard % per) * count + j

    def from_self(j):
        seq, fsdp = comes_from(j)
        return jnp.logical_and(seq == place, fsdp == shard)

    def greeting(barrier):
        for j in range(count):
            seq, fsdp = comes_from(j)
            pl.when(jnp.logical_not(from_self(j)))(
                lambda seq=seq, fsdp=fsdp: greet(barrier, {"seq": seq, "fsdp": fsdp})
            )
        return jnp.where(owner == shard, count - 1, count)

    def begin():
        pl.when(owner == shard)(own.start)
        for s in range(count):
            pl.when(jnp.logical_not(is_self(s)))(lambda s=s: copy(s).start())

    def finish():
        pl.when(owner == shard)(own.wait)
        for s in range(count):
            pl.when(jnp.logical_not(is_self(s)))(lambda s=s: copy(s).wait_send())
        for j in range(count):
            pl.when(jnp.logical_not(from_self(j)))(lambda j=j: arrival(j).wait_recv())

    return greeting, begin, nothing, finish


def own_job(sources, targets, scratch):
    (here,) = scratch
    place = lax.axis_index("seq")
    count = lax.axis_size("seq")
    part = targets[0].shape[1]
    copies = []
    for c, target in enumerate(targets):
        for k, source in enumerate(sources):
            start = place * (source.shape[0] // count) + c * part
            spot = pl.ds(pl.multiple_of(start, part), part)
            copies.append(
                pltpu.make_async_copy(
                    source.at[spot], target.at[k], here.at[c * len(sources) + k]
                )
            )

    def begin():
        for copy in copies:
            copy.start()

    def finish():
        for copy in copies:
            copy.wait()

    return no_greeting, begin, nothing, finish


MAKERS = {
    "gather": gather_job,
    "scatter": scatter_job,
    "deal": deal_job,
    "home": home_job,
    "own": own_job,
}


def job_scratch(job):
    kind, *arrays = job
    if kind == "scatter":
        _, rows, width = arrays[0].shape
        halves = pltpu.VMEM((2, rows // 2, width), BF16)
        return [
            pltpu.SemaphoreType.DMA((6,)),
            pltpu.SemaphoreType.DMA((6,)),
            pltpu.SemaphoreType.DMA((4,)),
            halves,
            halves,
            halves,
            pltpu.VMEM((rows, width), BF16),
            halves,
            pltpu.VMEM((rows, width), F32),
        ]
    if kind == "own":
        return [pltpu.SemaphoreType.DMA((CHUNKS * len(arrays),))]
    return [
        pltpu.SemaphoreType.DMA((4,)),
        pltpu.SemaphoreType.DMA((4,)),
        pltpu.SemaphoreType.DMA((1,)),
    ]


def job_results(job):
    kind, *arrays = job
    shape = arrays[0].shape
    if kind == "gather":
        return [jax.ShapeDtypeStruct((4,) + shape, BF16)]
    if kind == "scatter":
        return [jax.ShapeDtypeStruct(shape[1:], F32)]
    if kind == "deal":
        return [jax.ShapeDtypeStruct((shape[0] // 4,) + shape[1:], BF16)]
    if kind == "home":
        return [jax.ShapeDtypeStruct((shape[0] * 4,) + shape[1:], BF16)]
    part = shape[0] // lax.axis_size("seq") // CHUNKS
    return [jax.ShapeDtypeStruct((len(arrays), part) + shape[1:], BF16)] * CHUNKS


def plain_job(job):
    kind, *arrays = job
    seqs = lax.axis_size("seq")
    shards = lax.axis_size("fsdp")
    per = shards // seqs
    ends = [(s, h, s * shards + s * per + h) for s in range(seqs) for h in range(per)]
    if kind == "gather":
        return [lax.all_gather(arrays[0], "seq", axis=0)]
    if kind == "scatter":
        return [lax.psum_scatter(arrays[0], "seq", scatter_dimension=0).astype(F32)]
    if kind == "deal":
        rows = arrays[0].shape[0] // seqs
        total = None
        for j in range(seqs):
            moves = [(end, s * shards + h * seqs + j) for s, h, end in ends]
            got = lax.ppermute(arrays[0][j * rows : (j + 1) * rows], ("seq", "fsdp"), moves)
            total = got if total is None else total + got
        return [total]
    if kind == "home":
        held = []
        for j in range(seqs):
            moves = [(s * shards + h * seqs + j, end) for s, h, end in ends]
            held.append(lax.ppermute(arrays[0], ("seq", "fsdp"), moves))
        return [lax.psum(jnp.concatenate(held, axis=0), "seq")]
    own_rows = arrays[0].shape[0] // seqs
    part = own_rows // CHUNKS
    start = lax.axis_index("seq") * own_rows
    return [
        jnp.stack([lax.dynamic_slice_in_dim(w, start + c * part, part, 0) for w in arrays])
        for c in range(CHUNKS)
    ]


def meet(greetings):
    place = lax.axis_index("seq")
    barrier = pltpu.get_barrier_semaphore()
    for device in (over_one(place), over_two(place)):
        greet(barrier, {"seq": device})
    peers = 2
    for greeting in greetings:
        peers = peers + greeting(barrier)
    pl.semaphore_wait(barrier, peers)


def call(
    body, operands, in_specs, out_shape, out_specs, jobs, number, after=None,
    grid=(), scratch=(), cost=None, name=None,
):
    plain = lax.axis_size("seq") != 4
    results = [v for job in jobs for v in plain_job(job)] if plain else []
    inside = [] if plain else jobs
    extra = [] if after is None else [after]
    job_shapes = [job_scratch(job) for job in inside]
    job_outs = [job_results(job) for job in inside]
    n_in = len(operands)
    n_out = len(out_shape)

    def kernel(*refs):
        refs = list(refs)

        def take(count):
            taken, refs[:] = refs[:count], refs[count:]
            return taken

        ins = take(n_in)
        take(len(extra))
        sources = [take(len(job) - 1) for job in inside]
        outs = take(n_out)
        targets = [take(len(shapes)) for shapes in job_outs]
        held = take(len(scratch))
        phases = [
            MAKERS[job[0]](source, target, take(len(shapes)))
            for job, source, target, shapes in zip(inside, sources, targets, job_shapes)
        ]

        def hook(k):
            if k == 0 and phases:
                meet([phase[0] for phase in phases])
            for phase in phases:
                phase[k + 1]()

        body(hook, ins, outs, held)

    given = {}
    if inside:
        given = {"collective_id": number, "has_side_effects": True}
    arrays = [array for job in inside for array in job[1:]]
    shapes = [shape for shapes in job_outs for shape in shapes]
    made = pl.pallas_call(
        kernel,
        grid=grid,
        out_shape=tuple(out_shape) + tuple(shapes),
        in_specs=list(in_specs) + [ANY] * (len(extra) + len(arrays)),
        out_specs=tuple(out_specs) + (ANY,) * len(shapes),
        scratch_shapes=list(scratch) + [shape for shapes in job_shapes for shape in shapes],
        compiler_params=pltpu.CompilerParams(vmem_limit_bytes=VMEM_LIMIT, **given),
        cost_estimate=cost,
        name=name,
    )(*operands, *extra, *arrays)
    return list(made[:n_out]), list(made[n_out:]) + results


def transfer(jobs, number, after=None):
    if lax.axis_size("seq") != 4:
        return [v for job in jobs for v in plain_job(job)]

    def body(hook, ins, outs, held):
        for k in range(3):
            hook(k)

    return call(body, [], [], [], [], jobs, number, after, name="transfer")[1]


def partner(v):
    lane = lax.broadcasted_iota(jnp.int32, v.shape, 1)
    return jnp.where(lane % HEAD < HEAD // 2, pltpu.roll(v, 96, 1), pltpu.roll(v, 32, 1))


def head_mean(v, ones):
    high = v.astype(BF16)
    rest = (v - high.astype(F32)).astype(BF16)
    return dot(high, ones) + dot(rest, ones)


def true_chunk(place, c, count):
    if count != 4:
        return c
    low = 1 - place % 2 if c % 2 else place % 2
    high = 1 - place // 2 if c // 2 else place // 2
    return low + 2 * high


def prepare_heads(sizes, place, qkv_ref, qg_ref, kg_ref, cos_ref, sin_ref, ones, q_s, k_s, v_s):
    hq, hkv, _ = sizes
    seqs, rows_in, _ = qkv_ref.shape
    for c in range(seqs):
        j = true_chunk(place, c, seqs)
        rows = slice(c * rows_in, (c + 1) * rows_in)
        cos = cos_ref[rows, :]
        sin = sin_ref[rows, :]
        for p in range((hq + hkv) // 2):
            is_query = p < hq // 2
            x = qkv_ref[j, :, p * 128 : (p + 1) * 128].astype(F32)
            gain = qg_ref[...] * HEAD**-0.5 if is_query else kg_ref[...]
            y = x * lax.rsqrt(head_mean(x * x, ones) + EPSILON) * gain
            y = (y * cos + partner(y) * sin).astype(BF16)
            for t in range(2):
                part = y[:, t * HEAD : (t + 1) * HEAD]
                if is_query:
                    q_s[2 * p + t, rows, :] = part
                else:
                    k_s[2 * p - hq + t, rows, :] = part
        for t in range(hkv):
            start = (hq + hkv + t) * HEAD
            v_s[t, rows, :] = qkv_ref[j, :, start : start + HEAD]


def allowed_keys(block, first, keys, length):
    bound = jnp.minimum(first + lax.broadcasted_iota(jnp.int32, (block, 1), 0), length - 1)
    return lax.broadcasted_iota(jnp.int32, (block, keys), 1) <= bound


def attend_kernel(sizes, hook, ins, outs, held):
    len_ref, qkv_ref, qg_ref, kg_ref, cos_ref, sin_ref, ones_ref = ins
    out_ref, lse_ref = outs
    q_s, k_s, v_s, o_s = held
    hook(0)
    hq, hkv, group = sizes
    seqs, rows_in, _ = qkv_ref.shape
    place = lax.axis_index("seq")
    prepare_heads(
        sizes, place, qkv_ref, qg_ref, kg_ref, cos_ref, sin_ref, ones_ref[...], q_s, k_s, v_s
    )
    for i in range(seqs * rows_in // BLOCK):
        keys = (i + 1) * BLOCK
        rows = slice(i * BLOCK, (i + 1) * BLOCK)
        keep = allowed_keys(BLOCK, i * BLOCK, keys, len_ref[0])

        def one_head(h, _):
            kv = h // group
            scores = dot(q_s[h, rows, :], k_s[kv, :keys, :], NT)
            scores = jnp.where(keep, scores, NEGATIVE)
            highest = jnp.max(scores, axis=1, keepdims=True)
            shifted = jnp.exp(scores - highest)
            total = jnp.sum(shifted, axis=1, keepdims=True)
            mixed = dot(shifted.astype(BF16), v_s[kv, :keys, :]) / total
            o_s[h, rows, :] = mixed.astype(BF16)
            lse_ref[h, rows, :] = highest + jnp.log(total)
            return 0

        lax.fori_loop(0, hq, one_head, 0)
        if i == seqs * rows_in // BLOCK - 2:
            hook(1)
    for c in range(seqs):
        j = true_chunk(place, c, seqs)
        rows = slice(c * rows_in, (c + 1) * rows_in)
        for p in range(hq // 2):
            out_ref[j, :, p * 128 : (p + 1) * 128] = jnp.concatenate(
                [o_s[2 * p, rows, :], o_s[2 * p + 1, rows, :]], axis=1
            )
    hook(2)


def attend_back_kernel(sizes, hook, ins, outs, held):
    len_ref, qkv_ref, cot_ref, lse_ref, qg_ref, kg_ref, cos_ref, sin_ref, ones_ref = ins
    dqkv_ref, dgain_ref = outs
    q_s, k_s, v_s, cot_s, dq_s, dk_s, dv_s = held
    hook(0)
    hq, hkv, group = sizes
    seqs, rows_in, _ = qkv_ref.shape
    place = lax.axis_index("seq")
    ones = ones_ref[...]
    prepare_heads(sizes, place, qkv_ref, qg_ref, kg_ref, cos_ref, sin_ref, ones, q_s, k_s, v_s)
    for c in range(seqs):
        j = true_chunk(place, c, seqs)
        for h in range(hq):
            cot_s[h, c * rows_in : (c + 1) * rows_in, :] = cot_ref[
                j, :, h * HEAD : (h + 1) * HEAD
            ]
    dk_s[...] = jnp.zeros_like(dk_s)
    dv_s[...] = jnp.zeros_like(dv_s)
    for i in range(seqs * rows_in // BLOCK):
        keys = (i + 1) * BLOCK
        rows = slice(i * BLOCK, (i + 1) * BLOCK)
        keep = allowed_keys(BLOCK, i * BLOCK, keys, len_ref[0])

        def one_head(h, _):
            kv = h // group
            q = q_s[h, rows, :]
            cot = cot_s[h, rows, :]
            k = k_s[kv, :keys, :]
            scores = jnp.where(keep, dot(q, k, NT), NEGATIVE)
            probs = jnp.exp(scores - lse_ref[h, rows, :])
            prob_cot = dot(cot, v_s[kv, :keys, :], NT)
            inner = jnp.sum(probs * prob_cot, axis=1, keepdims=True)
            score_cot = (probs * (prob_cot - inner)).astype(BF16)
            dq_s[h, rows, :] = dot(score_cot, k) * HEAD**-0.5
            dk_s[kv, :keys, :] += dot(score_cot, q, TN)
            dv_s[kv, :keys, :] += dot(probs.astype(BF16), cot, TN)
            return 0

        lax.fori_loop(0, hq, one_head, 0)
        if i == seqs * rows_in // BLOCK - 2:
            hook(1)
    gain_sums = [jnp.zeros((1, 128), F32), jnp.zeros((1, 128), F32)]
    for c in range(seqs):
        j = true_chunk(place, c, seqs)
        rows = slice(c * rows_in, (c + 1) * rows_in)
        cos = cos_ref[rows, :]
        sin = sin_ref[rows, :]
        for p in range((hq + hkv) // 2):
            is_query = p < hq // 2
            x = qkv_ref[j, :, p * 128 : (p + 1) * 128].astype(F32)
            gain = qg_ref[...] if is_query else kg_ref[...]
            source, first = (dq_s, 2 * p) if is_query else (dk_s, 2 * p - hq)
            turned = jnp.concatenate([source[first, rows, :], source[first + 1, rows, :]], axis=1)
            scale = lax.rsqrt(head_mean(x * x, ones) + EPSILON)
            straight = turned * cos + partner(turned * sin)
            unit = x * scale
            which = 0 if is_query else 1
            gain_sums[which] += jnp.sum(straight * unit, axis=0, keepdims=True)
            pulled = gain * straight
            dx = scale * (pulled - unit * head_mean(unit * pulled, ones))
            dqkv_ref[j, :, p * 128 : (p + 1) * 128] = dx.astype(BF16)
        for p in range(hkv // 2):
            start = (hq + hkv) * HEAD + p * 128
            dqkv_ref[j, :, start : start + 128] = jnp.concatenate(
                [dv_s[2 * p, rows, :], dv_s[2 * p + 1, rows, :]], axis=1
            ).astype(BF16)
    dgain_ref[0:1, :] = gain_sums[0]
    dgain_ref[1:2, :] = gain_sums[1]
    hook(2)


def position_tables(length):
    places = np.arange(length, dtype=np.float32)
    half = HEAD // 2
    freqs = np.float32(ROPE_BASE) ** (-(np.arange(half, dtype=np.float32) * 2.0) / HEAD)
    angles = places[:, None] * freqs.astype(np.float32)[None, :]
    cos = np.cos(angles).astype(np.float32)
    sin = np.sin(angles).astype(np.float32)
    ones = np.kron(np.eye(2), np.ones((HEAD, HEAD)) / HEAD)
    return (
        jnp.asarray(np.concatenate([cos] * 4, axis=1)),
        jnp.asarray(np.concatenate([-sin, sin, -sin, sin], axis=1)),
        jnp.asarray(ones, dtype=BF16),
    )


def attend(sizes, length, qkv, gains, tables, jobs, number, after):
    seqs, rows_in, _ = qkv.shape
    hq, hkv, _ = sizes
    slot = seqs * rows_in
    return call(
        functools.partial(attend_kernel, sizes),
        [length, qkv, *gains, *tables],
        [SMEM] + [VMEM] * 6,
        [
            jax.ShapeDtypeStruct((seqs, rows_in, hq * HEAD), BF16),
            jax.ShapeDtypeStruct((hq, slot, 1), F32),
        ],
        [VMEM, VMEM],
        jobs,
        number,
        after,
        scratch=[
            pltpu.VMEM((hq, slot, HEAD), BF16),
            pltpu.VMEM((hkv, slot, HEAD), BF16),
            pltpu.VMEM((hkv, slot, HEAD), BF16),
            pltpu.VMEM((hq, slot, HEAD), BF16),
        ],
        cost=pl.CostEstimate(
            flops=56 * hq * slot * slot * HEAD, bytes_accessed=1 << 23, transcendentals=0
        ),
        name="attend",
    )


def attend_back(sizes, length, qkv, cot, lse, gains, tables, jobs, number, after):
    seqs, rows_in, width = qkv.shape
    hq, hkv, _ = sizes
    slot = seqs * rows_in
    return call(
        functools.partial(attend_back_kernel, sizes),
        [length, qkv, cot, lse, *gains, *tables],
        [SMEM] + [VMEM] * 8,
        [
            jax.ShapeDtypeStruct((seqs, rows_in, width), BF16),
            jax.ShapeDtypeStruct((2, 128), F32),
        ],
        [VMEM, VMEM],
        jobs,
        number,
        after,
        scratch=[
            pltpu.VMEM((hq, slot, HEAD), BF16),
            pltpu.VMEM((hkv, slot, HEAD), BF16),
            pltpu.VMEM((hkv, slot, HEAD), BF16),
            pltpu.VMEM((hq, slot, HEAD), BF16),
            pltpu.VMEM((hq, slot, HEAD), F32),
            pltpu.VMEM((hkv, slot, HEAD), F32),
            pltpu.VMEM((hkv, slot, HEAD), F32),
        ],
        cost=pl.CostEstimate(
            flops=88 * hq * slot * slot * HEAD, bytes_accessed=1 << 23, transcendentals=0
        ),
        name="attend_back",
    )


def hooked(hook, step, steps, work):
    pl.when(step == 0)(lambda: hook(0))
    pl.when(step == (3 * steps) // 4)(lambda: hook(1))
    work()
    pl.when(step == steps - 1)(lambda: hook(2))


def ffn_kernel(steps, hook, ins, outs, held):
    hooked(hook, pl.program_id(0), steps, lambda: ffn_tile(*ins[:5], ins[5:], *outs))


def ffn_tile(mid_ref, cot_ref, gate_ref, up_ref, down_ref, sums, acts_ref, pull_ref):
    model = mid_ref.shape[-1]
    hidden = acts_ref.shape[-1]
    gate_w = gate_ref[...].reshape(hidden, model)
    up_w = up_ref[...].reshape(hidden, model)
    down_w = down_ref[...].reshape(hidden, model)
    mid = mid_ref[...]
    gate = dot(mid, gate_w, NT)
    up = dot(mid, up_w, NT)
    mids_cot = dot(cot_ref[...], down_w, NT)
    sigmoid = jax.nn.sigmoid(gate)
    active = gate * sigmoid
    gate_cot = (mids_cot * up * sigmoid * (1.0 + gate * (1.0 - sigmoid))).astype(BF16)
    up_cot = (mids_cot * active).astype(BF16)
    acts_ref[0] = gate_cot
    acts_ref[1] = up_cot
    acts_ref[2] = (active * up).astype(BF16)
    pulled = dot(gate_cot, gate_w) + dot(up_cot, up_w)
    for sum_ref in sums:
        pulled = pulled + sum_ref[...]
    pull_ref[...] = pulled.astype(pull_ref.dtype)


def ffn_both(mid, cot, weights, summed, last, jobs, number, after):
    tokens, model = mid.shape
    shards, _, part, _ = weights.shape
    hidden = shards * part
    tile = min(256, tokens)

    def weight_spec(kind):
        return pl.BlockSpec(
            (shards, 1, part, model),
            lambda i: (0, kind, 0, 0),
            pipeline_mode=pl.Buffered(buffer_count=1),
        )

    row_spec = pl.BlockSpec((tile, model), lambda i: (i, 0))
    extra = () if summed is None else (summed,)
    return call(
        functools.partial(ffn_kernel, tokens // tile),
        [mid, cot, weights, weights, weights, *extra],
        [row_spec, row_spec, weight_spec(0), weight_spec(1), weight_spec(2)]
        + [row_spec] * len(extra),
        [
            jax.ShapeDtypeStruct((3, tokens, hidden), BF16),
            jax.ShapeDtypeStruct((tokens, model), BF16 if last else F32),
        ],
        [pl.BlockSpec((3, tile, hidden), lambda i: (0, i, 0)), row_spec],
        jobs,
        number,
        after,
        grid=(tokens // tile,),
        cost=pl.CostEstimate(
            flops=16 * tokens * model * hidden,
            bytes_accessed=4 * tokens * model + 6 * hidden * model,
            transcendentals=0,
        ),
        name="ffn_both",
    )


def ffn_grad_kernel(slots, tiles, hook, ins, outs, held):
    acts = ins[:slots]
    mids = ins[slots : 2 * slots]
    cots = ins[2 * slots :]
    (out_ref,) = outs
    kind = pl.program_id(0)

    def store(others):
        total = dot(acts[0][0], others[0][...], TN)
        for act, other in zip(acts[1:], others[1:]):
            total = total + dot(act[0], other[...], TN)
        out_ref[...] = total.astype(BF16).reshape(out_ref.shape)

    def work():
        pl.when(kind < 2)(lambda: store(mids))
        pl.when(kind == 2)(lambda: store(cots))

    hooked(hook, kind * tiles + pl.program_id(1), 3 * tiles, work)


def ffn_grads(acts, mids, cots, shards, jobs, number, after):
    slots = len(acts)
    _, tokens, hidden = acts[0].shape
    model = mids[0].shape[-1]
    part = hidden // shards
    tile = 256
    per = tile // part
    whole = pl.BlockSpec(
        (tokens, model), lambda k, i: (0, 0), pipeline_mode=pl.Buffered(buffer_count=1)
    )
    return call(
        functools.partial(ffn_grad_kernel, slots, hidden // tile),
        [*acts, *mids, *cots],
        [pl.BlockSpec((1, tokens, tile), lambda k, i: (k, 0, i))] * slots
        + [whole] * (2 * slots),
        [jax.ShapeDtypeStruct((shards, 3, part, model), BF16)],
        [pl.BlockSpec((per, 1, part, model), lambda k, i: (i, k, 0, 0))],
        jobs,
        number,
        after,
        grid=(3, hidden // tile),
        cost=pl.CostEstimate(
            flops=9 * slots * tokens * model * hidden,
            bytes_accessed=4 * slots * tokens * model,
            transcendentals=0,
        ),
        name="ffn_grads",
    )


def ffn_down_kernel(chunks, steps, hook, ins, outs, held):
    acts = ins[:chunks]
    downs = ins[chunks:]
    (out_ref,) = outs

    def work():
        total = None
        for act, down in zip(acts, downs):
            hidden = act.shape[-1]
            term = dot(act[0], down[...].reshape(hidden, down.shape[-1]))
            total = term if total is None else total + term
        out_ref[...] = total.astype(BF16)

    hooked(hook, pl.program_id(0), steps, work)


def ffn_down(acts, weights, jobs, number, after):
    chunks = len(acts)
    _, tokens, hidden = acts[0].shape
    shards, _, part, model = weights[0].shape
    tile = min(256, tokens)
    act_spec = pl.BlockSpec((1, tile, hidden), lambda i: (2, i, 0))
    down_spec = pl.BlockSpec(
        (shards, 1, part, model),
        lambda i: (0, 2, 0, 0),
        pipeline_mode=pl.Buffered(buffer_count=1),
    )
    return call(
        functools.partial(ffn_down_kernel, chunks, tokens // tile),
        [*acts, *weights],
        [act_spec] * chunks + [down_spec] * chunks,
        [jax.ShapeDtypeStruct((tokens, model), BF16)],
        [pl.BlockSpec((tile, model), lambda i: (i, 0))],
        jobs,
        number,
        after,
        grid=(tokens // tile,),
        cost=pl.CostEstimate(
            flops=4 * chunks * tokens * model * hidden,
            bytes_accessed=chunks * hidden * (tokens + model) * 2,
            transcendentals=0,
        ),
        name="ffn_down",
    )


def place_kernel(place_ref, parts_ref, *refs):
    for kind, out_ref in enumerate(refs[-3:]):
        out_ref[0, 0] = parts_ref[0, kind].astype(F32)


def place_parts(place, parts, chunk, held):
    seqs, _, part, model = parts.shape
    out = jax.ShapeDtypeStruct((seqs, CHUNKS, part, model), F32)
    out_spec = pl.BlockSpec(
        (1, 1, part, model), lambda j, at: (jnp.bitwise_xor(at[0], j), chunk, 0, 0)
    )
    return pl.pallas_call(
        place_kernel,
        out_shape=(out,) * 3,
        grid_spec=pltpu.PrefetchScalarGridSpec(
            num_scalar_prefetch=1,
            grid=(seqs,),
            in_specs=[pl.BlockSpec((1, 3, part, model), lambda j, at: (j, 0, 0, 0))]
            + [ANY] * len(held),
            out_specs=(out_spec,) * 3,
        ),
        input_output_aliases={2 + k: k for k in range(len(held))},
        compiler_params=pltpu.CompilerParams(vmem_limit_bytes=VMEM_LIMIT),
        cost_estimate=pl.CostEstimate(
            flops=0, bytes_accessed=18 * seqs * part * model, transcendentals=0
        ),
        name="place_parts",
    )(place, parts, *held)


def place_heads_kernel(place_ref, parts_ref, query_ref, key_ref, value_ref, rest_ref):
    edge = query_ref.shape[1]
    width = key_ref.shape[1]
    part = parts_ref[0].astype(F32)
    query_ref[...] = part[:, :edge]
    key_ref[...] = part[:, edge : edge + width]
    value_ref[...] = part[:, edge + width : edge + 2 * width]
    rest = part[:, edge + 2 * width :]

    @pl.when(pl.program_id(0) == 0)
    def _():
        rest_ref[...] = rest

    @pl.when(pl.program_id(0) > 0)
    def _():
        rest_ref[...] += rest


def place_heads(place, parts, edge, width):
    seqs, rows, total = parts.shape
    rest = total - edge - 2 * width

    def column_spec(size):
        return pl.BlockSpec((rows, size), lambda j, at: (0, jnp.bitwise_xor(at[0], j)))

    return pl.pallas_call(
        place_heads_kernel,
        out_shape=[
            jax.ShapeDtypeStruct((rows, seqs * edge), F32),
            jax.ShapeDtypeStruct((rows, seqs * width), F32),
            jax.ShapeDtypeStruct((rows, seqs * width), F32),
            jax.ShapeDtypeStruct((rows, rest), F32),
        ],
        grid_spec=pltpu.PrefetchScalarGridSpec(
            num_scalar_prefetch=1,
            grid=(seqs,),
            in_specs=[pl.BlockSpec((1, rows, total), lambda j, at: (j, 0, 0))],
            out_specs=[
                column_spec(edge),
                column_spec(width),
                column_spec(width),
                pl.BlockSpec((rows, rest), lambda j, at: (0, 0)),
            ],
        ),
        compiler_params=pltpu.CompilerParams(vmem_limit_bytes=VMEM_LIMIT),
        name="place_heads",
    )(place, parts)


def scale_of(values):
    return lax.rsqrt(jnp.mean(values * values, axis=-1, keepdims=True) + EPSILON)


def normed(values, gain):
    return values * scale_of(values) * gain


def normed_back(values, gain, cot):
    scale = scale_of(values)
    pulled = cot * gain
    mean = jnp.mean(values * pulled, axis=-1, keepdims=True)
    return (
        scale * pulled - values * (scale * scale * scale) * mean,
        jnp.sum(cot * values * scale, axis=0),
    )


def follow(values, earlier):
    return lax.optimization_barrier((values, *earlier))[0]


def own_columns(weight, heads, place):
    width = heads * HEAD
    part = lax.dynamic_slice_in_dim(weight, place * width, width, 1)
    if heads % 2:
        part = jnp.pad(part, ((0, 0), (0, HEAD)))
    return part


def on_device(
    tokens,
    cotangent,
    lengths,
    attn_gain,
    query_weight,
    key_weight,
    value_weight,
    query_gain,
    key_gain,
    out_weight,
    ffn_gain,
    gate_weight,
    up_weight,
    down_weight,
):
    slots, rows, model = tokens.shape
    seqs = lax.axis_size("seq")
    shards = lax.axis_size("fsdp")
    place = lax.axis_index("seq")
    shard = lax.axis_index("fsdp")
    slot_len = rows * seqs
    query_width = query_weight.shape[1]
    kv_width = key_weight.shape[1]
    hq = query_width // seqs // HEAD
    hkv = kv_width // seqs // HEAD
    hkv_held = hkv + hkv % 2
    sizes = (hq, hkv_held, hq // hkv)
    order = (place if seqs == 4 else place * 0).reshape(1)
    tables = position_tables(slot_len)
    gains = (
        jnp.concatenate([query_gain, query_gain]).reshape(1, 2 * HEAD),
        jnp.concatenate([key_gain, key_gain]).reshape(1, 2 * HEAD),
    )

    flat = (slot_len, model)
    chunked = (seqs, rows, model)
    places = place * rows + jnp.arange(rows, dtype=jnp.int32)
    live = (places[None, :] < lengths[:, None]).astype(F32)[..., None]
    inputs = tokens.astype(F32)
    out_cot = cotangent.astype(F32) * live
    out_low = [out_cot[b].astype(BF16) for b in range(slots)]
    normal_in = [normed(inputs[b], attn_gain).astype(BF16) for b in range(slots)]

    qkv_own = jnp.concatenate(
        [
            own_columns(query_weight, hq, place),
            own_columns(key_weight, hkv, place),
            own_columns(value_weight, hkv, place),
        ],
        axis=1,
    )
    qkv_weight = lax.all_gather(qkv_own, "fsdp", axis=0, tiled=True)
    start = [
        ("gather", normal_in[0]),
        ("deal", out_weight),
        ("own", gate_weight, up_weight, down_weight),
    ]
    normal_0, out_own, *ffn_own = transfer(start, 1)
    out_rows = lax.all_gather(out_own, "fsdp", axis=0, tiled=True)
    hidden_own = gate_weight.shape[0] // seqs
    part = hidden_own // CHUNKS
    ffn_weights = [lax.all_gather(own, "fsdp", axis=0) for own in ffn_own]

    def project(full):
        return dot(full.reshape(flat), qkv_weight).astype(BF16).reshape(seqs, rows, -1)

    def leave(mixed):
        return dot(mixed.reshape(slot_len, -1), out_rows).astype(BF16).reshape(chunked)

    def enter_ffn(b, total):
        res = inputs[b] + total
        return res, normed(res, ffn_gain).astype(BF16)

    def heads(b, raw, jobs, number, after):
        return attend(sizes, lengths[b : b + 1], raw, gains, tables, jobs, number, after)

    normal_full = [None] * slots
    cot_full = [None] * slots
    mid_full = [None] * slots
    normal_full[0] = normal_0
    qkv_0 = project(normal_full[0])
    (mixed_0, lse_0), (normal_full[1],) = heads(
        0, qkv_0, [("gather", normal_in[1])], 2, normal_full[0]
    )
    qkv_1 = project(normal_full[1])
    (mixed_1, lse_1), (total_0,) = heads(1, qkv_1, [("scatter", leave(mixed_0))], 3, mixed_0)
    qkv = [qkv_0, qkv_1]
    log_sums = [lse_0, lse_1]
    attended = [v.reshape(slot_len, hq * HEAD) for v in (mixed_0, mixed_1)]
    res_0, mid_0 = enter_ffn(0, total_0)
    mid_full[0], cot_full[0] = [
        v.reshape(flat)
        for v in transfer([("gather", mid_0), ("gather", out_low[0])], 4, mixed_1)
    ]

    acts = [[None] * slots for _ in range(CHUNKS)]
    pulled = [None] * slots

    def ffn_step(b, c, jobs, number, after):
        (acts[c][b], pulled[b]), results = ffn_both(
            mid_full[b], cot_full[b], ffn_weights[c], pulled[b], c == CHUNKS - 1,
            jobs, number, after,
        )
        return results

    def grad_step(c, jobs, number, after):
        (grads,), results = ffn_grads(
            acts[c], mid_full, cot_full, shards, jobs, number, after
        )
        return grads.reshape(shards, 3 * part, model), results

    def leave_ffn(b, jobs, number, after):
        (out,), results = ffn_down(
            [acts[c][b] for c in range(CHUNKS)], ffn_weights, jobs, number, after
        )
        return out.reshape(chunked), results

    total_1, full = ffn_step(
        0, 0, [("scatter", leave(mixed_1)), ("gather", out_low[1])], 5, mid_full[0]
    )
    cot_full[1] = full.reshape(flat)
    res_1, mid_1 = enter_ffn(1, total_1)
    hidden_res = [res_0, res_1]
    (full,) = ffn_step(0, 1, [("gather", mid_1)], 6, acts[0][0])
    mid_full[1] = full.reshape(flat)
    (mid_total_0,) = ffn_step(1, 0, [("scatter", pulled[0].reshape(chunked))], 7, acts[1][0])

    def pull_mid(b, total):
        pull, gain_part = normed_back(hidden_res[b], ffn_gain, total)
        cot = out_cot[b] + pull
        return cot, cot.astype(BF16), gain_part

    res_cot_0, low_0, ffn_gain_0 = pull_mid(0, mid_total_0)
    grads_0, (res_full_0,) = grad_step(0, [("gather", low_0)], 8, acts[0][1])
    ffn_sums = [lax.psum_scatter(grads_0, "fsdp", scatter_dimension=0)]
    out_0, _ = leave_ffn(0, [], 0, grads_0)
    (out_total_0,) = ffn_step(1, 1, [("scatter", out_0)], 9, out_0)
    grads_1, (mid_total_1,) = grad_step(
        1, [("scatter", pulled[1].reshape(chunked))], 10, acts[1][1]
    )
    res_cot_1, low_1, ffn_gain_1 = pull_mid(1, mid_total_1)
    grad_ffn_gain = ffn_gain_0 + ffn_gain_1

    def back(b, full, jobs, number, after):
        attended_cot = dot(full, out_rows, NT).astype(BF16).reshape(seqs, rows, hq * HEAD)
        (cots, gain_part), results = attend_back(
            sizes, lengths[b : b + 1], qkv[b], attended_cot, log_sums[b], gains, tables,
            jobs, number, after,
        )
        return cots.reshape(slot_len, -1), gain_part, results

    def pull_heads(cots):
        return dot(cots, qkv_weight, NT).astype(BF16).reshape(chunked)

    dqkv_0, heads_gain_0, (res_full_1,) = back(
        0, res_full_0.reshape(flat), [("gather", low_1)], 11, grads_1
    )
    ffn_sums.append(
        lax.psum_scatter(follow(grads_1, [*ffn_sums, dqkv_0]), "fsdp", scatter_dimension=0)
    )
    dqkv_1, heads_gain_1, (in_total_0,) = back(
        1, res_full_1.reshape(flat), [("scatter", pull_heads(dqkv_0))], 12, dqkv_0
    )
    head_gain = heads_gain_0 + heads_gain_1
    dqkv = [dqkv_0, dqkv_1]
    res_full = [v.reshape(flat) for v in (res_full_0, res_full_1)]
    out_1, (in_total_1, ffn_parts_0) = leave_ffn(
        1, [("scatter", pull_heads(dqkv_1)), ("gather", ffn_sums[0])], 13, dqkv_1
    )

    grad_tokens = []
    grad_attn_gain = 0.0
    for b, (in_cot, cot) in enumerate(((in_total_0, res_cot_0), (in_total_1, res_cot_1))):
        pull, gain_part = normed_back(inputs[b], attn_gain, in_cot)
        grad_attn_gain = grad_attn_gain + gain_part
        grad_tokens.append((cot + pull).astype(BF16))

    out_grads = sum(dot(attended[b], res_full[b], TN) for b in range(slots)).astype(BF16)
    held = model // shards
    piece = out_grads.shape[0] // shards
    blocks = held // piece
    out_grads = jnp.swapaxes(out_grads.reshape(shards, piece, blocks, model // blocks), 1, 2)
    head_sums = jnp.pad(
        (head_gain[:, :HEAD] + head_gain[:, HEAD:]).reshape(2, shards, HEAD // shards),
        ((0, 0), (0, 0), (0, held - HEAD // shards)),
    ).reshape(2, model)
    gain_columns = jnp.stack(
        [grad_attn_gain, grad_ffn_gain, head_sums[0], head_sums[1]], axis=1
    ).astype(BF16)
    attn_grads = jnp.concatenate(
        [
            sum(dot(normal_full[b].reshape(flat), dqkv[b], TN) for b in range(slots)).astype(BF16),
            jnp.pad(gain_columns, ((0, 0), (0, 124))),
            out_grads.reshape(model, model // blocks),
        ],
        axis=1,
    )
    attn_sums = lax.psum_scatter(
        follow(attn_grads, ffn_sums[1:]), "fsdp", scatter_dimension=0, tiled=True
    )
    out_edge = attn_sums.shape[1] - model // blocks
    out_sums = jnp.swapaxes(
        attn_sums[:, out_edge:].reshape(blocks, piece, model // blocks), 0, 1
    ).reshape(piece, model)

    out_total_1, ffn_parts_1 = transfer(
        [("scatter", out_1), ("gather", ffn_sums[1])], 14, in_total_1
    )
    output = [
        (live[b] * (hidden_res[b] + total)).astype(BF16)
        for b, total in enumerate((out_total_0, out_total_1))
    ]
    ffn_grad = ()
    for c, parts in enumerate((ffn_parts_0, ffn_parts_1)):
        ffn_grad = place_parts(order, parts.reshape(seqs, 3, part, model), c, ffn_grad)
    ffn_grad = [v.reshape(seqs * hidden_own, model) for v in ffn_grad]

    heads_all, grad_out = transfer(
        [("gather", attn_sums[:, :out_edge]), ("home", out_sums)], 15, out_total_1
    )
    edge = hq * HEAD
    width = hkv_held * HEAD
    if hkv == hkv_held:
        grad_query, grad_key, grad_value, gain_sums = place_heads(order, heads_all, edge, width)
    else:
        heads_all = jnp.moveaxis(heads_all, 0, 1).astype(F32)
        last = edge + width
        grad_query = heads_all[..., :edge].reshape(held, query_width)
        grad_key = heads_all[..., edge : edge + hkv * HEAD].reshape(held, kv_width)
        grad_value = heads_all[..., last : last + hkv * HEAD].reshape(held, kv_width)
        gain_sums = jnp.sum(heads_all[..., last + width :], axis=1)

    return (
        jnp.stack(output),
        jnp.stack(grad_tokens),
        gain_sums[:, 0],
        grad_query,
        grad_key,
        grad_value,
        gain_sums[: HEAD // shards, 2],
        gain_sums[: HEAD // shards, 3],
        grad_out.astype(F32),
        gain_sums[:, 1],
        ffn_grad[0],
        ffn_grad[1],
        ffn_grad[2],
    )


def solution(mesh):
    return jax.shard_map(
        on_device,
        mesh=mesh,
        in_specs=(
            P("fsdp", "seq", None),
            P("fsdp", "seq", None),
            P("fsdp"),
            P(),
            P("fsdp", None),
            P("fsdp", None),
            P("fsdp", None),
            P(),
            P(),
            P("fsdp", None),
            P(),
            P("fsdp", None),
            P("fsdp", None),
            P("fsdp", None),
        ),
        out_specs=(
            P("fsdp", "seq", None),
            P("fsdp", "seq", None),
            P("fsdp"),
            P("fsdp", None),
            P("fsdp", None),
            P("fsdp", None),
            P("fsdp"),
            P("fsdp"),
            P("fsdp", None),
            P("fsdp"),
            P("fsdp", None),
            P("fsdp", None),
            P("fsdp", None),
        ),
        check_vma=False,
    )
```

```python
import functools

import jax
import jax.numpy as jnp
import numpy as np
from jax import lax
from jax.experimental import pallas as pl
from jax.experimental.pallas import tpu as pltpu
from jax.sharding import PartitionSpec as P

EPSILON = 1e-05
ROPE_BASE = 1000000.0
NEGATIVE = -1e30
F32 = jnp.float32
BF16 = jnp.bfloat16
NN = (((1,), (0,)), ((), ()))
NT = (((1,), (1,)), ((), ()))
TN = (((0,), (0,)), ((), ()))
SMEM = pl.BlockSpec(memory_space=pltpu.SMEM)
VMEM = pl.BlockSpec(memory_space=pltpu.VMEM)
VMEM_LIMIT = 58 << 20
HEAD = 64
BLOCK = 256
CHUNKS = 2
ANY = pl.BlockSpec(memory_space=pl.ANY)


def dot(a, b, dims=NN):
    return lax.dot_general(a, b, dims, preferred_element_type=F32)


def over_one(place):
    return place + 1 - 2 * (place % 2)


def over_two(place):
    return (place + 2) % 4


def send(source, target, device, out_sem, in_sem):
    return pltpu.make_async_remote_copy(
        src_ref=source,
        dst_ref=target,
        send_sem=out_sem,
        recv_sem=in_sem,
        device_id={"seq": device},
        device_id_type=pl.DeviceIdType.MESH,
    )


def gather_job(sources, targets, scratch):
    (source,) = sources
    (target,) = targets
    outs, ins, here, held = scratch
    place = lax.axis_index("seq")
    one, two = over_one(place), over_two(place)
    half = source.shape[0] // 2
    load = pltpu.make_async_copy(source, held, here.at[0])
    store = pltpu.make_async_copy(held, target.at[0], here.at[1])
    first = send(source, target.at[1], one, outs.at[0], ins.at[0])
    second = send(source, target.at[2], two, outs.at[1], ins.at[1])
    top = pl.ds(0, half)
    low = pl.ds(half, half)
    third = send(target.at[2, top], target.at[3, top], one, outs.at[2], ins.at[2])
    fourth = send(target.at[1, low], target.at[3, low], two, outs.at[3], ins.at[3])

    def begin():
        first.start()
        second.start()
        load.start()

    def middle():
        load.wait()
        store.start()
        second.wait_recv()
        third.start()
        first.wait_recv()
        fourth.start()

    def finish():
        third.wait_recv()
        fourth.wait_recv()
        for copy in (first, second, third, fourth):
            copy.wait_send()
        store.wait()

    return no_greeting, begin, middle, finish


def scatter_job(sources, targets, scratch):
    (parts,) = sources
    (total,) = targets
    outs, ins, here, got_one, got_two, kept, own, last, summed = scratch
    place = lax.axis_index("seq")
    one, two = over_one(place), over_two(place)
    half = parts.shape[1] // 2
    top = pl.ds(0, half)
    low = pl.ds(half, half)
    sends = [
        send(parts.at[3, top], got_one.at[0], one, outs.at[0], ins.at[0]),
        send(parts.at[3, low], got_two.at[0], two, outs.at[1], ins.at[1]),
        send(parts.at[1, top], got_one.at[1], one, outs.at[2], ins.at[2]),
        send(parts.at[2, low], got_two.at[1], two, outs.at[3], ins.at[3]),
        send(kept.at[0], last.at[0], two, outs.at[4], ins.at[4]),
        send(kept.at[1], last.at[1], one, outs.at[5], ins.at[5]),
    ]
    loads = [
        pltpu.make_async_copy(parts.at[2, top], kept.at[0], here.at[0]),
        pltpu.make_async_copy(parts.at[1, low], kept.at[1], here.at[1]),
        pltpu.make_async_copy(parts.at[0], own, here.at[2]),
    ]
    store = pltpu.make_async_copy(summed, total, here.at[3])

    def begin():
        for copy in sends[:4]:
            copy.start()
        for copy in loads:
            copy.start()

    def middle():
        for k, got in enumerate((got_one, got_two)):
            loads[k].wait()
            sends[k].wait_recv()
            kept[k] = (kept[k].astype(F32) + got[0].astype(F32)).astype(BF16)
            sends[4 + k].start()

    def finish():
        loads[2].wait()
        for k, got in enumerate((got_one, got_two)):
            sends[2 + k].wait_recv()
            sends[4 + k].wait_recv()
            rows = slice(k * half, (k + 1) * half)
            summed[rows, :] = (
                own[rows, :].astype(F32) + got[1].astype(F32) + last[k].astype(F32)
            )
        store.start()
        for copy in sends:
            copy.wait_send()
        store.wait()

    return no_greeting, begin, middle, finish


def no_greeting(barrier):
    return 0


def nothing():
    pass


def greet(barrier, device):
    pl.semaphore_signal(
        barrier, inc=1, device_id=device, device_id_type=pl.DeviceIdType.MESH
    )


def deal_job(sources, targets, scratch):
    (source,) = sources
    (target,) = targets
    outs, ins, here = scratch
    rows = target.shape[0]
    count = source.shape[0] // rows
    place = lax.axis_index("seq")
    shard = lax.axis_index("fsdp")
    per = lax.axis_size("fsdp") // count
    part = shard % per
    is_source = shard // per == place
    to_self = jnp.logical_and(is_source, shard // count == part)
    origin = place * per + shard // count

    def copy(j):
        return pltpu.make_async_remote_copy(
            src_ref=source.at[pl.ds(j * rows, rows)],
            dst_ref=target,
            send_sem=outs.at[j],
            recv_sem=ins.at[0],
            device_id={"fsdp": part * count + j},
            device_id_type=pl.DeviceIdType.MESH,
        )

    def local(j):
        return pltpu.make_async_copy(source.at[pl.ds(j * rows, rows)], target, here.at[0])

    def greeting(barrier):
        pl.when(origin != shard)(lambda: greet(barrier, {"fsdp": origin}))
        return jnp.where(is_source, count, 0) - jnp.where(to_self, 1, 0)

    def each(act_remote, act_local):
        for j in range(count):
            mine = part * count + j == shard
            pl.when(jnp.logical_and(is_source, mine))(lambda j=j: act_local(local(j)))
            pl.when(jnp.logical_and(is_source, jnp.logical_not(mine)))(
                lambda j=j: act_remote(copy(j))
            )

    def begin():
        each(lambda c: c.start(), lambda c: c.start())

    def finish():
        each(lambda c: c.wait_send(), lambda c: c.wait())
        pl.when(origin != shard)(lambda: copy(0).wait_recv())

    return greeting, begin, nothing, finish


def home_job(sources, targets, scratch):
    (source,) = sources
    (target,) = targets
    outs, ins, here = scratch
    rows = source.shape[0]
    count = target.shape[0] // rows
    place = lax.axis_index("seq")
    shard = lax.axis_index("fsdp")
    per = lax.axis_size("fsdp") // count
    piece = shard % count
    owner = place * per + shard // count
    spot = pl.ds(pl.multiple_of(piece * rows, rows), rows)

    def copy(s):
        return pltpu.make_async_remote_copy(
            src_ref=source,
            dst_ref=target.at[spot],
            send_sem=outs.at[s],
            recv_sem=ins.at[piece],
            device_id={"seq": s, "fsdp": owner},
            device_id_type=pl.DeviceIdType.MESH,
        )

    def arrival(j):
        return pltpu.make_async_remote_copy(
            src_ref=source,
            dst_ref=target.at[pl.ds(j * rows, rows)],
            send_sem=outs.at[0],
            recv_sem=ins.at[j],
            device_id={"seq": place, "fsdp": owner},
            device_id_type=pl.DeviceIdType.MESH,
        )

    own = pltpu.make_async_copy(source, target.at[spot], here.at[0])

    def is_self(s):
        return jnp.logical_and(owner == shard, place == s)

    def comes_from(j):
        return shard // per, (shard % per) * count + j

    def from_self(j):
        seq, fsdp = comes_from(j)
        return jnp.logical_and(seq == place, fsdp == shard)

    def greeting(barrier):
        for j in range(count):
            seq, fsdp = comes_from(j)
            pl.when(jnp.logical_not(from_self(j)))(
                lambda seq=seq, fsdp=fsdp: greet(barrier, {"seq": seq, "fsdp": fsdp})
            )
        return jnp.where(owner == shard, count - 1, count)

    def begin():
        pl.when(owner == shard)(own.start)
        for s in range(count):
            pl.when(jnp.logical_not(is_self(s)))(lambda s=s: copy(s).start())

    def finish():
        pl.when(owner == shard)(own.wait)
        for s in range(count):
            pl.when(jnp.logical_not(is_self(s)))(lambda s=s: copy(s).wait_send())
        for j in range(count):
            pl.when(jnp.logical_not(from_self(j)))(lambda j=j: arrival(j).wait_recv())

    return greeting, begin, nothing, finish


def own_job(sources, targets, scratch):
    loaded, stored, held = scratch
    place = lax.axis_index("seq")
    count = lax.axis_size("seq")
    part = targets[0].shape[1]
    loads = []
    stores = []
    for c, target in enumerate(targets):
        for k, source in enumerate(sources):
            start = place * (source.shape[0] // count) + c * part
            spot = pl.ds(pl.multiple_of(start, part), part)
            n = c * len(sources) + k
            loads.append(pltpu.make_async_copy(source.at[spot], held.at[n], loaded.at[n]))
            stores.append(pltpu.make_async_copy(held.at[n], target.at[k], stored.at[n]))

    def begin():
        for load in loads:
            load.start()

    def middle():
        for load, store in zip(loads, stores):
            load.wait()
            store.start()

    def finish():
        for store in stores:
            store.wait()

    return no_greeting, begin, middle, finish


MAKERS = {
    "gather": gather_job,
    "scatter": scatter_job,
    "deal": deal_job,
    "home": home_job,
    "own": own_job,
}


def job_scratch(job):
    kind, *arrays = job
    if kind == "scatter":
        _, rows, width = arrays[0].shape
        halves = pltpu.VMEM((2, rows // 2, width), BF16)
        return [
            pltpu.SemaphoreType.DMA((6,)),
            pltpu.SemaphoreType.DMA((6,)),
            pltpu.SemaphoreType.DMA((4,)),
            halves,
            halves,
            halves,
            pltpu.VMEM((rows, width), BF16),
            halves,
            pltpu.VMEM((rows, width), F32),
        ]
    if kind == "own":
        count = CHUNKS * len(arrays)
        rows, width = arrays[0].shape
        part = rows // lax.axis_size("seq") // CHUNKS
        return [
            pltpu.SemaphoreType.DMA((count,)),
            pltpu.SemaphoreType.DMA((count,)),
            pltpu.VMEM((count, part, width), BF16),
        ]
    moves = [
        pltpu.SemaphoreType.DMA((4,)),
        pltpu.SemaphoreType.DMA((4,)),
        pltpu.SemaphoreType.DMA((2,)),
    ]
    return moves + [pltpu.VMEM(arrays[0].shape, BF16)] if kind == "gather" else moves


def job_results(job):
    kind, *arrays = job
    shape = arrays[0].shape
    if kind == "gather":
        return [jax.ShapeDtypeStruct((4,) + shape, BF16)]
    if kind == "scatter":
        return [jax.ShapeDtypeStruct(shape[1:], F32)]
    if kind == "deal":
        return [jax.ShapeDtypeStruct((shape[0] // 4,) + shape[1:], BF16)]
    if kind == "home":
        return [jax.ShapeDtypeStruct((shape[0] * 4,) + shape[1:], BF16)]
    part = shape[0] // lax.axis_size("seq") // CHUNKS
    return [jax.ShapeDtypeStruct((len(arrays), part) + shape[1:], BF16)] * CHUNKS


def plain_job(job):
    kind, *arrays = job
    seqs = lax.axis_size("seq")
    shards = lax.axis_size("fsdp")
    per = shards // seqs
    ends = [(s, h, s * shards + s * per + h) for s in range(seqs) for h in range(per)]
    if kind == "gather":
        return [lax.all_gather(arrays[0], "seq", axis=0)]
    if kind == "scatter":
        return [lax.psum_scatter(arrays[0], "seq", scatter_dimension=0).astype(F32)]
    if kind == "deal":
        rows = arrays[0].shape[0] // seqs
        total = None
        for j in range(seqs):
            moves = [(end, s * shards + h * seqs + j) for s, h, end in ends]
            got = lax.ppermute(arrays[0][j * rows : (j + 1) * rows], ("seq", "fsdp"), moves)
            total = got if total is None else total + got
        return [total]
    if kind == "home":
        held = []
        for j in range(seqs):
            moves = [(s * shards + h * seqs + j, end) for s, h, end in ends]
            held.append(lax.ppermute(arrays[0], ("seq", "fsdp"), moves))
        return [lax.psum(jnp.concatenate(held, axis=0), "seq")]
    own_rows = arrays[0].shape[0] // seqs
    part = own_rows // CHUNKS
    start = lax.axis_index("seq") * own_rows
    return [
        jnp.stack([lax.dynamic_slice_in_dim(w, start + c * part, part, 0) for w in arrays])
        for c in range(CHUNKS)
    ]


def meet(greetings):
    place = lax.axis_index("seq")
    barrier = pltpu.get_barrier_semaphore()
    for device in (over_one(place), over_two(place)):
        greet(barrier, {"seq": device})
    peers = 2
    for greeting in greetings:
        peers = peers + greeting(barrier)
    pl.semaphore_wait(barrier, peers)


def call(
    body, operands, in_specs, out_shape, out_specs, jobs, number, after=None,
    grid=(), scratch=(), cost=None, name=None,
):
    plain = lax.axis_size("seq") != 4
    results = [v for job in jobs for v in plain_job(job)] if plain else []
    inside = [] if plain else jobs
    extra = [] if after is None else [after]
    job_shapes = [job_scratch(job) for job in inside]
    job_outs = [job_results(job) for job in inside]
    n_in = len(operands)
    n_out = len(out_shape)

    def kernel(*refs):
        refs = list(refs)

        def take(count):
            taken, refs[:] = refs[:count], refs[count:]
            return taken

        ins = take(n_in)
        take(len(extra))
        sources = [take(len(job) - 1) for job in inside]
        outs = take(n_out)
        targets = [take(len(shapes)) for shapes in job_outs]
        held = take(len(scratch))
        phases = [
            MAKERS[job[0]](source, target, take(len(shapes)))
            for job, source, target, shapes in zip(inside, sources, targets, job_shapes)
        ]

        def hook(k):
            if k == 0 and phases:
                meet([phase[0] for phase in phases])
            for phase in phases:
                phase[k + 1]()

        body(hook, ins, outs, held)

    given = {}
    if inside:
        given = {"collective_id": number, "has_side_effects": True}
    arrays = [array for job in inside for array in job[1:]]
    shapes = [shape for shapes in job_outs for shape in shapes]
    made = pl.pallas_call(
        kernel,
        grid=grid,
        out_shape=tuple(out_shape) + tuple(shapes),
        in_specs=list(in_specs) + [ANY] * (len(extra) + len(arrays)),
        out_specs=tuple(out_specs) + (ANY,) * len(shapes),
        scratch_shapes=list(scratch) + [shape for shapes in job_shapes for shape in shapes],
        compiler_params=pltpu.CompilerParams(vmem_limit_bytes=VMEM_LIMIT, **given),
        cost_estimate=cost,
        name=name,
    )(*operands, *extra, *arrays)
    return list(made[:n_out]), list(made[n_out:]) + results


def transfer(jobs, number, after=None):
    if lax.axis_size("seq") != 4:
        return [v for job in jobs for v in plain_job(job)]

    def body(hook, ins, outs, held):
        for k in range(3):
            hook(k)

    return call(body, [], [], [], [], jobs, number, after, name="transfer")[1]


def partner(v):
    lane = lax.broadcasted_iota(jnp.int32, v.shape, 1)
    return jnp.where(lane % HEAD < HEAD // 2, pltpu.roll(v, 96, 1), pltpu.roll(v, 32, 1))


def head_mean(v, ones):
    high = v.astype(BF16)
    rest = (v - high.astype(F32)).astype(BF16)
    return dot(high, ones) + dot(rest, ones)


def true_chunk(place, c, count):
    if count != 4:
        return c
    low = 1 - place % 2 if c % 2 else place % 2
    high = 1 - place // 2 if c // 2 else place // 2
    return low + 2 * high


def prepare_heads(sizes, place, qkv_ref, qg_ref, kg_ref, cos_ref, sin_ref, ones, q_s, k_s, v_s):
    hq, hkv, _ = sizes
    seqs, rows_in, _ = qkv_ref.shape
    for c in range(seqs):
        j = true_chunk(place, c, seqs)
        rows = slice(c * rows_in, (c + 1) * rows_in)
        cos = cos_ref[rows, :]
        sin = sin_ref[rows, :]
        for p in range((hq + hkv) // 2):
            is_query = p < hq // 2
            x = qkv_ref[j, :, p * 128 : (p + 1) * 128].astype(F32)
            gain = qg_ref[...] * HEAD**-0.5 if is_query else kg_ref[...]
            y = x * lax.rsqrt(head_mean(x * x, ones) + EPSILON) * gain
            y = (y * cos + partner(y) * sin).astype(BF16)
            for t in range(2):
                part = y[:, t * HEAD : (t + 1) * HEAD]
                if is_query:
                    q_s[2 * p + t, rows, :] = part
                else:
                    k_s[2 * p - hq + t, rows, :] = part
        for t in range(hkv):
            start = (hq + hkv + t) * HEAD
            v_s[t, rows, :] = qkv_ref[j, :, start : start + HEAD]


def allowed_keys(block, first, keys, length):
    bound = jnp.minimum(first + lax.broadcasted_iota(jnp.int32, (block, 1), 0), length - 1)
    return lax.broadcasted_iota(jnp.int32, (block, keys), 1) <= bound


def attend_kernel(sizes, hook, ins, outs, held):
    len_ref, qkv_ref, qg_ref, kg_ref, cos_ref, sin_ref, ones_ref = ins
    out_ref, lse_ref = outs
    q_s, k_s, v_s, o_s = held
    hook(0)
    hq, hkv, group = sizes
    seqs, rows_in, _ = qkv_ref.shape
    place = lax.axis_index("seq")
    prepare_heads(
        sizes, place, qkv_ref, qg_ref, kg_ref, cos_ref, sin_ref, ones_ref[...], q_s, k_s, v_s
    )
    for i in range(seqs * rows_in // BLOCK):
        keys = (i + 1) * BLOCK
        rows = slice(i * BLOCK, (i + 1) * BLOCK)
        keep = allowed_keys(BLOCK, i * BLOCK, keys, len_ref[0])

        def one_head(h, _):
            kv = h // group
            scores = dot(q_s[h, rows, :], k_s[kv, :keys, :], NT)
            scores = jnp.where(keep, scores, NEGATIVE)
            highest = jnp.max(scores, axis=1, keepdims=True)
            shifted = jnp.exp(scores - highest)
            total = jnp.sum(shifted, axis=1, keepdims=True)
            mixed = dot(shifted.astype(BF16), v_s[kv, :keys, :]) / total
            o_s[h, rows, :] = mixed.astype(BF16)
            lse_ref[h, rows, :] = highest + jnp.log(total)
            return 0

        lax.fori_loop(0, hq, one_head, 0)
        if i == seqs * rows_in // BLOCK - 2:
            hook(1)
    for c in range(seqs):
        j = true_chunk(place, c, seqs)
        rows = slice(c * rows_in, (c + 1) * rows_in)
        for p in range(hq // 2):
            out_ref[j, :, p * 128 : (p + 1) * 128] = jnp.concatenate(
                [o_s[2 * p, rows, :], o_s[2 * p + 1, rows, :]], axis=1
            )
    hook(2)


def attend_back_kernel(sizes, hook, ins, outs, held):
    len_ref, qkv_ref, cot_ref, lse_ref, qg_ref, kg_ref, cos_ref, sin_ref, ones_ref = ins
    dqkv_ref, dgain_ref = outs
    q_s, k_s, v_s, cot_s, dq_s, dk_s, dv_s = held
    hook(0)
    hq, hkv, group = sizes
    seqs, rows_in, _ = qkv_ref.shape
    place = lax.axis_index("seq")
    ones = ones_ref[...]
    prepare_heads(sizes, place, qkv_ref, qg_ref, kg_ref, cos_ref, sin_ref, ones, q_s, k_s, v_s)
    for c in range(seqs):
        j = true_chunk(place, c, seqs)
        for h in range(hq):
            cot_s[h, c * rows_in : (c + 1) * rows_in, :] = cot_ref[
                j, :, h * HEAD : (h + 1) * HEAD
            ]
    dk_s[...] = jnp.zeros_like(dk_s)
    dv_s[...] = jnp.zeros_like(dv_s)
    for i in range(seqs * rows_in // BLOCK):
        keys = (i + 1) * BLOCK
        rows = slice(i * BLOCK, (i + 1) * BLOCK)
        keep = allowed_keys(BLOCK, i * BLOCK, keys, len_ref[0])

        def one_head(h, _):
            kv = h // group
            q = q_s[h, rows, :]
            cot = cot_s[h, rows, :]
            k = k_s[kv, :keys, :]
            scores = jnp.where(keep, dot(q, k, NT), NEGATIVE)
            probs = jnp.exp(scores - lse_ref[h, rows, :])
            prob_cot = dot(cot, v_s[kv, :keys, :], NT)
            inner = jnp.sum(probs * prob_cot, axis=1, keepdims=True)
            score_cot = (probs * (prob_cot - inner)).astype(BF16)
            dq_s[h, rows, :] = dot(score_cot, k) * HEAD**-0.5
            dk_s[kv, :keys, :] += dot(score_cot, q, TN)
            dv_s[kv, :keys, :] += dot(probs.astype(BF16), cot, TN)
            return 0

        lax.fori_loop(0, hq, one_head, 0)
        if i == seqs * rows_in // BLOCK - 2:
            hook(1)
    gain_sums = [jnp.zeros((1, 128), F32), jnp.zeros((1, 128), F32)]
    for c in range(seqs):
        j = true_chunk(place, c, seqs)
        rows = slice(c * rows_in, (c + 1) * rows_in)
        cos = cos_ref[rows, :]
        sin = sin_ref[rows, :]
        for p in range((hq + hkv) // 2):
            is_query = p < hq // 2
            x = qkv_ref[j, :, p * 128 : (p + 1) * 128].astype(F32)
            gain = qg_ref[...] if is_query else kg_ref[...]
            source, first = (dq_s, 2 * p) if is_query else (dk_s, 2 * p - hq)
            turned = jnp.concatenate([source[first, rows, :], source[first + 1, rows, :]], axis=1)
            scale = lax.rsqrt(head_mean(x * x, ones) + EPSILON)
            straight = turned * cos + partner(turned * sin)
            unit = x * scale
            which = 0 if is_query else 1
            gain_sums[which] += jnp.sum(straight * unit, axis=0, keepdims=True)
            pulled = gain * straight
            dx = scale * (pulled - unit * head_mean(unit * pulled, ones))
            dqkv_ref[j, :, p * 128 : (p + 1) * 128] = dx.astype(BF16)
        for p in range(hkv // 2):
            start = (hq + hkv) * HEAD + p * 128
            dqkv_ref[j, :, start : start + 128] = jnp.concatenate(
                [dv_s[2 * p, rows, :], dv_s[2 * p + 1, rows, :]], axis=1
            ).astype(BF16)
    dgain_ref[0:1, :] = gain_sums[0]
    dgain_ref[1:2, :] = gain_sums[1]
    hook(2)


def position_tables(length):
    places = np.arange(length, dtype=np.float32)
    half = HEAD // 2
    freqs = np.float32(ROPE_BASE) ** (-(np.arange(half, dtype=np.float32) * 2.0) / HEAD)
    angles = places[:, None] * freqs.astype(np.float32)[None, :]
    cos = np.cos(angles).astype(np.float32)
    sin = np.sin(angles).astype(np.float32)
    ones = np.kron(np.eye(2), np.ones((HEAD, HEAD)) / HEAD)
    return (
        jnp.asarray(np.concatenate([cos] * 4, axis=1)),
        jnp.asarray(np.concatenate([-sin, sin, -sin, sin], axis=1)),
        jnp.asarray(ones, dtype=BF16),
    )


def attend(sizes, length, qkv, gains, tables, jobs, number, after):
    seqs, rows_in, _ = qkv.shape
    hq, hkv, _ = sizes
    slot = seqs * rows_in
    return call(
        functools.partial(attend_kernel, sizes),
        [length, qkv, *gains, *tables],
        [SMEM] + [VMEM] * 6,
        [
            jax.ShapeDtypeStruct((seqs, rows_in, hq * HEAD), BF16),
            jax.ShapeDtypeStruct((hq, slot, 1), F32),
        ],
        [VMEM, VMEM],
        jobs,
        number,
        after,
        scratch=[
            pltpu.VMEM((hq, slot, HEAD), BF16),
            pltpu.VMEM((hkv, slot, HEAD), BF16),
            pltpu.VMEM((hkv, slot, HEAD), BF16),
            pltpu.VMEM((hq, slot, HEAD), BF16),
        ],
        cost=pl.CostEstimate(
            flops=56 * hq * slot * slot * HEAD, bytes_accessed=1 << 23, transcendentals=0
        ),
        name="attend",
    )


def attend_back(sizes, length, qkv, cot, lse, gains, tables, jobs, number, after):
    seqs, rows_in, width = qkv.shape
    hq, hkv, _ = sizes
    slot = seqs * rows_in
    return call(
        functools.partial(attend_back_kernel, sizes),
        [length, qkv, cot, lse, *gains, *tables],
        [SMEM] + [VMEM] * 8,
        [
            jax.ShapeDtypeStruct((seqs, rows_in, width), BF16),
            jax.ShapeDtypeStruct((2, 128), F32),
        ],
        [VMEM, VMEM],
        jobs,
        number,
        after,
        scratch=[
            pltpu.VMEM((hq, slot, HEAD), BF16),
            pltpu.VMEM((hkv, slot, HEAD), BF16),
            pltpu.VMEM((hkv, slot, HEAD), BF16),
            pltpu.VMEM((hq, slot, HEAD), BF16),
            pltpu.VMEM((hq, slot, HEAD), F32),
            pltpu.VMEM((hkv, slot, HEAD), F32),
            pltpu.VMEM((hkv, slot, HEAD), F32),
        ],
        cost=pl.CostEstimate(
            flops=88 * hq * slot * slot * HEAD, bytes_accessed=1 << 23, transcendentals=0
        ),
        name="attend_back",
    )


def hooked(hook, step, steps, work):
    pl.when(step == 0)(lambda: hook(0))
    work(lambda: pl.when(step == (3 * steps) // 5)(lambda: hook(1)))
    pl.when(step == steps - 1)(lambda: hook(2))


def ffn_kernel(steps, hook, ins, outs, held):
    hooked(hook, pl.program_id(0), steps, lambda late: ffn_tile(late, *ins[:5], ins[5:], *outs))


def ffn_tile(late, mid_ref, cot_ref, gate_ref, up_ref, down_ref, sums, acts_ref, pull_ref):
    model = mid_ref.shape[-1]
    hidden = acts_ref.shape[-1]
    gate_w = gate_ref[...].reshape(hidden, model)
    up_w = up_ref[...].reshape(hidden, model)
    down_w = down_ref[...].reshape(hidden, model)
    mid = mid_ref[...]
    gate = dot(mid, gate_w, NT)
    up = dot(mid, up_w, NT)
    mids_cot = dot(cot_ref[...], down_w, NT)
    late()
    sigmoid = jax.nn.sigmoid(gate)
    active = gate * sigmoid
    gate_cot = (mids_cot * up * sigmoid * (1.0 + gate * (1.0 - sigmoid))).astype(BF16)
    up_cot = (mids_cot * active).astype(BF16)
    acts_ref[0] = gate_cot
    acts_ref[1] = up_cot
    acts_ref[2] = (active * up).astype(BF16)
    pulled = dot(gate_cot, gate_w) + dot(up_cot, up_w)
    for sum_ref in sums:
        pulled = pulled + sum_ref[...]
    pull_ref[...] = pulled.astype(pull_ref.dtype)


def ffn_both(mid, cot, weights, summed, last, jobs, number, after):
    tokens, model = mid.shape
    shards, _, part, _ = weights.shape
    hidden = shards * part
    tile = min(256, tokens)

    def weight_spec(kind):
        return pl.BlockSpec(
            (shards, 1, part, model),
            lambda i: (0, kind, 0, 0),
            pipeline_mode=pl.Buffered(buffer_count=1),
        )

    row_spec = pl.BlockSpec((tile, model), lambda i: (i, 0))
    extra = () if summed is None else (summed,)
    return call(
        functools.partial(ffn_kernel, tokens // tile),
        [mid, cot, weights, weights, weights, *extra],
        [row_spec, row_spec, weight_spec(0), weight_spec(1), weight_spec(2)]
        + [row_spec] * len(extra),
        [
            jax.ShapeDtypeStruct((3, tokens, hidden), BF16),
            jax.ShapeDtypeStruct((tokens, model), BF16 if last else F32),
        ],
        [pl.BlockSpec((3, tile, hidden), lambda i: (0, i, 0)), row_spec],
        jobs,
        number,
        after,
        grid=(tokens // tile,),
        cost=pl.CostEstimate(
            flops=16 * tokens * model * hidden,
            bytes_accessed=4 * tokens * model + 6 * hidden * model,
            transcendentals=0,
        ),
        name="ffn_both",
    )


def ffn_grad_kernel(slots, tiles, hook, ins, outs, held):
    acts = ins[:slots]
    mids = ins[slots : 2 * slots]
    cots = ins[2 * slots :]
    (out_ref,) = outs
    kind = pl.program_id(0)

    def store(others):
        total = dot(acts[0][0], others[0][...], TN)
        for act, other in zip(acts[1:], others[1:]):
            total = total + dot(act[0], other[...], TN)
        out_ref[...] = total.astype(BF16).reshape(out_ref.shape)

    def work(late):
        late()
        pl.when(kind < 2)(lambda: store(mids))
        pl.when(kind == 2)(lambda: store(cots))

    hooked(hook, kind * tiles + pl.program_id(1), 3 * tiles, work)


def ffn_grads(acts, mids, cots, shards, jobs, number, after):
    slots = len(acts)
    _, tokens, hidden = acts[0].shape
    model = mids[0].shape[-1]
    part = hidden // shards
    tile = 256
    per = tile // part
    whole = pl.BlockSpec(
        (tokens, model), lambda k, i: (0, 0), pipeline_mode=pl.Buffered(buffer_count=1)
    )
    return call(
        functools.partial(ffn_grad_kernel, slots, hidden // tile),
        [*acts, *mids, *cots],
        [pl.BlockSpec((1, tokens, tile), lambda k, i: (k, 0, i))] * slots
        + [whole] * (2 * slots),
        [jax.ShapeDtypeStruct((shards, 3, part, model), BF16)],
        [pl.BlockSpec((per, 1, part, model), lambda k, i: (i, k, 0, 0))],
        jobs,
        number,
        after,
        grid=(3, hidden // tile),
        cost=pl.CostEstimate(
            flops=9 * slots * tokens * model * hidden,
            bytes_accessed=4 * slots * tokens * model,
            transcendentals=0,
        ),
        name="ffn_grads",
    )


def ffn_down_kernel(chunks, steps, hook, ins, outs, held):
    acts = ins[:chunks]
    downs = ins[chunks:]
    (out_ref,) = outs

    def work(late):
        late()
        total = None
        for act, down in zip(acts, downs):
            hidden = act.shape[-1]
            term = dot(act[0], down[...].reshape(hidden, down.shape[-1]))
            total = term if total is None else total + term
        out_ref[...] = total.astype(BF16)

    hooked(hook, pl.program_id(0), steps, work)


def ffn_down(acts, weights, jobs, number, after):
    chunks = len(acts)
    _, tokens, hidden = acts[0].shape
    shards, _, part, model = weights[0].shape
    tile = min(256, tokens)
    act_spec = pl.BlockSpec((1, tile, hidden), lambda i: (2, i, 0))
    down_spec = pl.BlockSpec(
        (shards, 1, part, model),
        lambda i: (0, 2, 0, 0),
        pipeline_mode=pl.Buffered(buffer_count=1),
    )
    return call(
        functools.partial(ffn_down_kernel, chunks, tokens // tile),
        [*acts, *weights],
        [act_spec] * chunks + [down_spec] * chunks,
        [jax.ShapeDtypeStruct((tokens, model), BF16)],
        [pl.BlockSpec((tile, model), lambda i: (i, 0))],
        jobs,
        number,
        after,
        grid=(tokens // tile,),
        cost=pl.CostEstimate(
            flops=4 * chunks * tokens * model * hidden,
            bytes_accessed=chunks * hidden * (tokens + model) * 2,
            transcendentals=0,
        ),
        name="ffn_down",
    )


def place_kernel(place_ref, parts_ref, *refs):
    for kind, out_ref in enumerate(refs[-3:]):
        out_ref[0, 0] = parts_ref[0, kind].astype(F32)


def place_parts(place, parts, chunk, held):
    seqs, _, part, model = parts.shape
    out = jax.ShapeDtypeStruct((seqs, CHUNKS, part, model), F32)
    out_spec = pl.BlockSpec(
        (1, 1, part, model), lambda j, at: (jnp.bitwise_xor(at[0], j), chunk, 0, 0)
    )
    return pl.pallas_call(
        place_kernel,
        out_shape=(out,) * 3,
        grid_spec=pltpu.PrefetchScalarGridSpec(
            num_scalar_prefetch=1,
            grid=(seqs,),
            in_specs=[pl.BlockSpec((1, 3, part, model), lambda j, at: (j, 0, 0, 0))]
            + [ANY] * len(held),
            out_specs=(out_spec,) * 3,
        ),
        input_output_aliases={2 + k: k for k in range(len(held))},
        compiler_params=pltpu.CompilerParams(vmem_limit_bytes=VMEM_LIMIT),
        cost_estimate=pl.CostEstimate(
            flops=0, bytes_accessed=18 * seqs * part * model, transcendentals=0
        ),
        name="place_parts",
    )(place, parts, *held)


def place_heads_kernel(
    place_ref, parts_ref, query_w_ref, key_w_ref, value_w_ref,
    query_ref, key_ref, value_ref, rest_ref, met_ref,
):
    edge = query_ref.shape[1]
    width = key_ref.shape[1]
    part = parts_ref[0].astype(F32)
    query_ref[...] = part[:, :edge]
    key_ref[...] = part[:, edge : edge + width]
    value_ref[...] = part[:, edge + width : edge + 2 * width]
    rest = part[:, edge + 2 * width :]
    met = jnp.zeros_like(met_ref)
    for grad_ref, weight_ref in (
        (query_ref, query_w_ref),
        (key_ref, key_w_ref),
        (value_ref, value_w_ref),
    ):
        product = grad_ref[...] * weight_ref[...].astype(F32)
        met = met + jnp.sum(product, axis=1, keepdims=True)

    @pl.when(pl.program_id(0) == 0)
    def _():
        rest_ref[...] = rest
        met_ref[...] = met

    @pl.when(pl.program_id(0) > 0)
    def _():
        rest_ref[...] += rest
        met_ref[...] += met


def place_heads(place, parts, edge, width, weights):
    seqs, rows, total = parts.shape
    rest = total - edge - 2 * width

    def column_spec(size):
        return pl.BlockSpec((rows, size), lambda j, at: (0, jnp.bitwise_xor(at[0], j)))

    return pl.pallas_call(
        place_heads_kernel,
        out_shape=[
            jax.ShapeDtypeStruct((rows, seqs * edge), F32),
            jax.ShapeDtypeStruct((rows, seqs * width), F32),
            jax.ShapeDtypeStruct((rows, seqs * width), F32),
            jax.ShapeDtypeStruct((rows, rest), F32),
            jax.ShapeDtypeStruct((rows, 128), F32),
        ],
        grid_spec=pltpu.PrefetchScalarGridSpec(
            num_scalar_prefetch=1,
            grid=(seqs,),
            in_specs=[
                pl.BlockSpec((1, rows, total), lambda j, at: (j, 0, 0)),
                column_spec(edge),
                column_spec(width),
                column_spec(width),
            ],
            out_specs=[
                column_spec(edge),
                column_spec(width),
                column_spec(width),
                pl.BlockSpec((rows, rest), lambda j, at: (0, 0)),
                pl.BlockSpec((rows, 128), lambda j, at: (0, 0)),
            ],
        ),
        compiler_params=pltpu.CompilerParams(vmem_limit_bytes=VMEM_LIMIT),
        name="place_heads",
    )(place, parts, *weights)


def scale_of(values):
    return lax.rsqrt(jnp.mean(values * values, axis=-1, keepdims=True) + EPSILON)


def normed(values, gain):
    return values * scale_of(values) * gain


def normed_back(values, gain, cot):
    scale = scale_of(values)
    pulled = cot * gain
    mean = jnp.mean(values * pulled, axis=-1, keepdims=True)
    return (
        scale * pulled - values * (scale * scale * scale) * mean,
        jnp.sum(cot * values * scale, axis=0),
    )


def follow(values, earlier):
    return lax.optimization_barrier((values, *earlier))[0]


def own_columns(weight, heads, place):
    width = heads * HEAD
    part = lax.dynamic_slice_in_dim(weight, place * width, width, 1)
    if heads % 2:
        part = jnp.pad(part, ((0, 0), (0, HEAD)))
    return part


def on_device(
    tokens,
    cotangent,
    lengths,
    attn_gain,
    query_weight,
    key_weight,
    value_weight,
    query_gain,
    key_gain,
    out_weight,
    ffn_gain,
    gate_weight,
    up_weight,
    down_weight,
):
    slots, rows, model = tokens.shape
    seqs = lax.axis_size("seq")
    shards = lax.axis_size("fsdp")
    place = lax.axis_index("seq")
    shard = lax.axis_index("fsdp")
    slot_len = rows * seqs
    query_width = query_weight.shape[1]
    kv_width = key_weight.shape[1]
    hq = query_width // seqs // HEAD
    hkv = kv_width // seqs // HEAD
    hkv_held = hkv + hkv % 2
    sizes = (hq, hkv_held, hq // hkv)
    order = (place if seqs == 4 else place * 0).reshape(1)
    tables = position_tables(slot_len)
    gains = (
        jnp.concatenate([query_gain, query_gain]).reshape(1, 2 * HEAD),
        jnp.concatenate([key_gain, key_gain]).reshape(1, 2 * HEAD),
    )

    flat = (slot_len, model)
    chunked = (seqs, rows, model)
    places = place * rows + jnp.arange(rows, dtype=jnp.int32)
    live = (places[None, :] < lengths[:, None]).astype(F32)[..., None]
    inputs = tokens.astype(F32)
    out_cot = cotangent.astype(F32) * live
    out_low = [out_cot[b].astype(BF16) for b in range(slots)]
    normal_in = [normed(inputs[b], attn_gain).astype(BF16) for b in range(slots)]

    qkv_own = jnp.concatenate(
        [
            own_columns(query_weight, hq, place),
            own_columns(key_weight, hkv, place),
            own_columns(value_weight, hkv, place),
        ],
        axis=1,
    )
    qkv_weight = lax.all_gather(qkv_own, "fsdp", axis=0, tiled=True)
    start = [
        ("gather", normal_in[0]),
        ("deal", out_weight),
        ("own", gate_weight, up_weight, down_weight),
    ]
    normal_0, out_own, *ffn_own = transfer(start, 1)
    out_rows = lax.all_gather(out_own, "fsdp", axis=0, tiled=True)
    hidden_own = gate_weight.shape[0] // seqs
    part = hidden_own // CHUNKS
    ffn_weights = [lax.all_gather(own, "fsdp", axis=0) for own in ffn_own]

    def project(full):
        return dot(full.reshape(flat), qkv_weight).astype(BF16).reshape(seqs, rows, -1)

    def leave(mixed):
        return dot(mixed.reshape(slot_len, -1), out_rows).astype(BF16).reshape(chunked)

    def enter_ffn(b, total):
        res = inputs[b] + total
        return res, normed(res, ffn_gain).astype(BF16)

    def heads(b, raw, jobs, number, after):
        return attend(sizes, lengths[b : b + 1], raw, gains, tables, jobs, number, after)

    normal_full = [None] * slots
    cot_full = [None] * slots
    mid_full = [None] * slots
    normal_full[0] = normal_0
    qkv_0 = project(normal_full[0])
    (mixed_0, lse_0), (normal_full[1],) = heads(
        0, qkv_0, [("gather", normal_in[1])], 2, normal_full[0]
    )
    qkv_1 = project(normal_full[1])
    (mixed_1, lse_1), (total_0,) = heads(1, qkv_1, [("scatter", leave(mixed_0))], 3, mixed_0)
    qkv = [qkv_0, qkv_1]
    log_sums = [lse_0, lse_1]
    attended = [v.reshape(slot_len, hq * HEAD) for v in (mixed_0, mixed_1)]
    res_0, mid_0 = enter_ffn(0, total_0)
    mid_full[0], cot_full[0] = [
        v.reshape(flat)
        for v in transfer([("gather", mid_0), ("gather", out_low[0])], 4, mixed_1)
    ]

    acts = [[None] * slots for _ in range(CHUNKS)]
    pulled = [None] * slots

    def ffn_step(b, c, jobs, number, after):
        (acts[c][b], pulled[b]), results = ffn_both(
            mid_full[b], cot_full[b], ffn_weights[c], pulled[b], c == CHUNKS - 1,
            jobs, number, after,
        )
        return results

    def grad_step(c, jobs, number, after):
        (grads,), results = ffn_grads(
            acts[c], mid_full, cot_full, shards, jobs, number, after
        )
        return grads.reshape(shards, 3 * part, model), results

    def leave_ffn(b, jobs, number, after):
        (out,), results = ffn_down(
            [acts[c][b] for c in range(CHUNKS)], ffn_weights, jobs, number, after
        )
        return out.reshape(chunked), results

    total_1, full = ffn_step(
        0, 0, [("scatter", leave(mixed_1)), ("gather", out_low[1])], 5, mid_full[0]
    )
    cot_full[1] = full.reshape(flat)
    res_1, mid_1 = enter_ffn(1, total_1)
    hidden_res = [res_0, res_1]
    (full,) = ffn_step(0, 1, [("gather", mid_1)], 6, acts[0][0])
    mid_full[1] = full.reshape(flat)
    (mid_total_0,) = ffn_step(1, 0, [("scatter", pulled[0].reshape(chunked))], 7, acts[1][0])

    def pull_mid(b, total):
        pull, gain_part = normed_back(hidden_res[b], ffn_gain, total)
        cot = out_cot[b] + pull
        return cot, cot.astype(BF16), gain_part

    res_cot_0, low_0, ffn_gain_0 = pull_mid(0, mid_total_0)
    grads_0, (res_full_0,) = grad_step(0, [("gather", low_0)], 8, acts[0][1])
    ffn_sums = [lax.psum_scatter(grads_0, "fsdp", scatter_dimension=0)]
    out_0, _ = leave_ffn(0, [], 0, grads_0)
    (out_total_0,) = ffn_step(1, 1, [("scatter", out_0)], 9, out_0)
    grads_1, (mid_total_1,) = grad_step(
        1, [("scatter", pulled[1].reshape(chunked))], 10, acts[1][1]
    )
    ffn_sums.append(lax.psum_scatter(grads_1, "fsdp", scatter_dimension=0))
    out_1, _ = leave_ffn(1, [], 0, grads_1)
    res_cot_1, low_1, ffn_gain_1 = pull_mid(1, mid_total_1)
    grad_ffn_gain = ffn_gain_0 + ffn_gain_1

    def back(b, full, jobs, number, after):
        attended_cot = dot(full, out_rows, NT).astype(BF16).reshape(seqs, rows, hq * HEAD)
        (cots, gain_part), results = attend_back(
            sizes, lengths[b : b + 1], qkv[b], attended_cot, log_sums[b], gains, tables,
            jobs, number, after,
        )
        return cots.reshape(slot_len, -1), gain_part, results

    def pull_heads(cots):
        return dot(cots, qkv_weight, NT).astype(BF16).reshape(chunked)

    dqkv_0, heads_gain_0, (res_full_1, out_total_1) = back(
        0, res_full_0.reshape(flat), [("gather", low_1), ("scatter", out_1)], 11, out_1
    )
    dqkv_1, heads_gain_1, (in_total_0, ffn_parts_0) = back(
        1,
        res_full_1.reshape(flat),
        [("scatter", pull_heads(dqkv_0)), ("gather", ffn_sums[0])],
        12,
        dqkv_0,
    )
    head_gain = heads_gain_0 + heads_gain_1
    dqkv = [dqkv_0, dqkv_1]
    res_full = [v.reshape(flat) for v in (res_full_0, res_full_1)]
    in_total_1, ffn_parts_1 = transfer(
        [("scatter", pull_heads(dqkv_1)), ("gather", ffn_sums[1])], 13, dqkv_1
    )
    grad_tokens = []
    for b, (in_cot, cot) in enumerate(((in_total_0, res_cot_0), (in_total_1, res_cot_1))):
        pull, _ = normed_back(inputs[b], attn_gain, in_cot)
        grad_tokens.append((cot + pull).astype(BF16))

    out_grads = sum(dot(attended[b], res_full[b], TN) for b in range(slots)).astype(BF16)
    held = model // shards
    piece = out_grads.shape[0] // shards
    blocks = held // piece
    out_grads = jnp.swapaxes(out_grads.reshape(shards, piece, blocks, model // blocks), 1, 2)
    head_sums = jnp.pad(
        (head_gain[:, :HEAD] + head_gain[:, HEAD:]).reshape(2, shards, HEAD // shards),
        ((0, 0), (0, 0), (0, held - HEAD // shards)),
    ).reshape(2, model)
    gain_columns = jnp.stack(
        [grad_ffn_gain, head_sums[0], head_sums[1]], axis=1
    ).astype(BF16)
    attn_grads = jnp.concatenate(
        [
            sum(dot(normal_full[b].reshape(flat), dqkv[b], TN) for b in range(slots)).astype(BF16),
            jnp.pad(gain_columns, ((0, 0), (0, 125))),
            out_grads.reshape(model, model // blocks),
        ],
        axis=1,
    )
    attn_sums = lax.psum_scatter(attn_grads, "fsdp", scatter_dimension=0, tiled=True)
    out_edge = attn_sums.shape[1] - model // blocks
    out_sums = jnp.swapaxes(
        attn_sums[:, out_edge:].reshape(blocks, piece, model // blocks), 0, 1
    ).reshape(piece, model)

    output = [
        (live[b] * (hidden_res[b] + total)).astype(BF16)
        for b, total in enumerate((out_total_0, out_total_1))
    ]
    ffn_grad = ()
    for c, parts in enumerate((ffn_parts_0, ffn_parts_1)):
        ffn_grad = place_parts(order, parts.reshape(seqs, 3, part, model), c, ffn_grad)
    ffn_grad = [v.reshape(seqs * hidden_own, model) for v in ffn_grad]

    heads_all, grad_out = transfer(
        [("gather", attn_sums[:, :out_edge]), ("home", out_sums)], 14, in_total_1
    )
    edge = hq * HEAD
    width = hkv_held * HEAD
    if hkv == hkv_held:
        grad_query, grad_key, grad_value, gain_sums, met = place_heads(
            order, heads_all, edge, width, (query_weight, key_weight, value_weight)
        )
        met = met[:, 0]
    else:
        heads_all = jnp.moveaxis(heads_all, 0, 1).astype(F32)
        last = edge + width
        grad_query = heads_all[..., :edge].reshape(held, query_width)
        grad_key = heads_all[..., edge : edge + hkv * HEAD].reshape(held, kv_width)
        grad_value = heads_all[..., last : last + hkv * HEAD].reshape(held, kv_width)
        gain_sums = jnp.sum(heads_all[..., last + width :], axis=1)
        met = sum(
            jnp.sum(grad * weight.astype(F32), axis=1)
            for grad, weight in (
                (grad_query, query_weight),
                (grad_key, key_weight),
                (grad_value, value_weight),
            )
        )
    grad_attn_gain = met / lax.dynamic_slice_in_dim(attn_gain, shard * held, held, 0)

    return (
        jnp.stack(output),
        jnp.stack(grad_tokens),
        grad_attn_gain,
        grad_query,
        grad_key,
        grad_value,
        gain_sums[: HEAD // shards, 1],
        gain_sums[: HEAD // shards, 2],
        grad_out.astype(F32),
        gain_sums[:, 0],
        ffn_grad[0],
        ffn_grad[1],
        ffn_grad[2],
    )


def solution(mesh):
    return jax.shard_map(
        on_device,
        mesh=mesh,
        in_specs=(
            P("fsdp", "seq", None),
            P("fsdp", "seq", None),
            P("fsdp"),
            P(),
            P("fsdp", None),
            P("fsdp", None),
            P("fsdp", None),
            P(),
            P(),
            P("fsdp", None),
            P(),
            P("fsdp", None),
            P("fsdp", None),
            P("fsdp", None),
        ),
        out_specs=(
            P("fsdp", "seq", None),
            P("fsdp", "seq", None),
            P("fsdp"),
            P("fsdp", None),
            P("fsdp", None),
            P("fsdp", None),
            P("fsdp"),
            P("fsdp"),
            P("fsdp", None),
            P("fsdp"),
            P("fsdp", None),
            P("fsdp", None),
            P("fsdp", None),
        ),
        check_vma=False,
    )
```

```python
import functools

import jax
import jax.numpy as jnp
import numpy as np
from jax import lax
from jax.experimental import pallas as pl
from jax.experimental.pallas import tpu as pltpu
from jax.sharding import PartitionSpec as P

EPSILON = 1e-05
ROPE_BASE = 1000000.0
NEGATIVE = -1e30
F32 = jnp.float32
BF16 = jnp.bfloat16
NN = (((1,), (0,)), ((), ()))
NT = (((1,), (1,)), ((), ()))
TN = (((0,), (0,)), ((), ()))
SMEM = pl.BlockSpec(memory_space=pltpu.SMEM)
VMEM = pl.BlockSpec(memory_space=pltpu.VMEM)
VMEM_LIMIT = 58 << 20
HEAD = 64
BLOCK = 256
CHUNKS = 2
ANY = pl.BlockSpec(memory_space=pl.ANY)


def dot(a, b, dims=NN):
    return lax.dot_general(a, b, dims, preferred_element_type=F32)


def over_one(place):
    return place + 1 - 2 * (place % 2)


def over_two(place):
    return (place + 2) % 4


def send(source, target, device, out_sem, in_sem):
    return pltpu.make_async_remote_copy(
        src_ref=source,
        dst_ref=target,
        send_sem=out_sem,
        recv_sem=in_sem,
        device_id={"seq": device},
        device_id_type=pl.DeviceIdType.MESH,
    )


def gather_job(sources, targets, scratch):
    (source,) = sources
    (target,) = targets
    outs, ins, here, held = scratch
    place = lax.axis_index("seq")
    one, two = over_one(place), over_two(place)
    half = source.shape[0] // 2
    load = pltpu.make_async_copy(source, held, here.at[0])
    store = pltpu.make_async_copy(held, target.at[0], here.at[1])
    first = send(source, target.at[1], one, outs.at[0], ins.at[0])
    second = send(source, target.at[2], two, outs.at[1], ins.at[1])
    top = pl.ds(0, half)
    low = pl.ds(half, half)
    third = send(target.at[2, top], target.at[3, top], one, outs.at[2], ins.at[2])
    fourth = send(target.at[1, low], target.at[3, low], two, outs.at[3], ins.at[3])

    def begin():
        first.start()
        second.start()
        load.start()

    def middle():
        load.wait()
        store.start()
        second.wait_recv()
        third.start()
        first.wait_recv()
        fourth.start()

    def finish():
        third.wait_recv()
        fourth.wait_recv()
        for copy in (first, second, third, fourth):
            copy.wait_send()
        store.wait()

    return no_greeting, begin, middle, finish


def scatter_job(sources, targets, scratch):
    (parts,) = sources
    (total,) = targets
    outs, ins, here, got_one, got_two, kept, own, last, summed = scratch
    place = lax.axis_index("seq")
    one, two = over_one(place), over_two(place)
    half = parts.shape[1] // 2
    top = pl.ds(0, half)
    low = pl.ds(half, half)
    sends = [
        send(parts.at[3, top], got_one.at[0], one, outs.at[0], ins.at[0]),
        send(parts.at[3, low], got_two.at[0], two, outs.at[1], ins.at[1]),
        send(parts.at[1, top], got_one.at[1], one, outs.at[2], ins.at[2]),
        send(parts.at[2, low], got_two.at[1], two, outs.at[3], ins.at[3]),
        send(kept.at[0], last.at[0], two, outs.at[4], ins.at[4]),
        send(kept.at[1], last.at[1], one, outs.at[5], ins.at[5]),
    ]
    loads = [
        pltpu.make_async_copy(parts.at[2, top], kept.at[0], here.at[0]),
        pltpu.make_async_copy(parts.at[1, low], kept.at[1], here.at[1]),
        pltpu.make_async_copy(parts.at[0], own, here.at[2]),
    ]
    store = pltpu.make_async_copy(summed, total, here.at[3])

    def begin():
        for copy in sends[:4]:
            copy.start()
        for copy in loads:
            copy.start()

    def middle():
        for k, got in enumerate((got_one, got_two)):
            loads[k].wait()
            sends[k].wait_recv()
            kept[k] = (kept[k].astype(F32) + got[0].astype(F32)).astype(BF16)
            sends[4 + k].start()

    def finish():
        loads[2].wait()
        for k, got in enumerate((got_one, got_two)):
            sends[2 + k].wait_recv()
            sends[4 + k].wait_recv()
            rows = slice(k * half, (k + 1) * half)
            summed[rows, :] = (
                own[rows, :].astype(F32) + got[1].astype(F32) + last[k].astype(F32)
            )
        store.start()
        for copy in sends:
            copy.wait_send()
        store.wait()

    return no_greeting, begin, middle, finish


def no_greeting(barrier):
    return 0


def nothing():
    pass


def greet(barrier, device):
    pl.semaphore_signal(
        barrier, inc=1, device_id=device, device_id_type=pl.DeviceIdType.MESH
    )


def deal_job(sources, targets, scratch):
    (source,) = sources
    (target,) = targets
    outs, ins, here = scratch
    rows = target.shape[0]
    count = source.shape[0] // rows
    place = lax.axis_index("seq")
    shard = lax.axis_index("fsdp")
    per = lax.axis_size("fsdp") // count
    part = shard % per
    is_source = shard // per == place
    to_self = jnp.logical_and(is_source, shard // count == part)
    origin = place * per + shard // count

    def copy(j):
        return pltpu.make_async_remote_copy(
            src_ref=source.at[pl.ds(j * rows, rows)],
            dst_ref=target,
            send_sem=outs.at[j],
            recv_sem=ins.at[0],
            device_id={"fsdp": part * count + j},
            device_id_type=pl.DeviceIdType.MESH,
        )

    def local(j):
        return pltpu.make_async_copy(source.at[pl.ds(j * rows, rows)], target, here.at[0])

    def greeting(barrier):
        pl.when(origin != shard)(lambda: greet(barrier, {"fsdp": origin}))
        return jnp.where(is_source, count, 0) - jnp.where(to_self, 1, 0)

    def each(act_remote, act_local):
        for j in range(count):
            mine = part * count + j == shard
            pl.when(jnp.logical_and(is_source, mine))(lambda j=j: act_local(local(j)))
            pl.when(jnp.logical_and(is_source, jnp.logical_not(mine)))(
                lambda j=j: act_remote(copy(j))
            )

    def begin():
        each(lambda c: c.start(), lambda c: c.start())

    def finish():
        each(lambda c: c.wait_send(), lambda c: c.wait())
        pl.when(origin != shard)(lambda: copy(0).wait_recv())

    return greeting, begin, nothing, finish


def home_job(sources, targets, scratch):
    (source,) = sources
    (target,) = targets
    outs, ins, here = scratch
    rows = source.shape[0]
    count = target.shape[0] // rows
    place = lax.axis_index("seq")
    shard = lax.axis_index("fsdp")
    per = lax.axis_size("fsdp") // count
    piece = shard % count
    owner = place * per + shard // count
    spot = pl.ds(pl.multiple_of(piece * rows, rows), rows)

    def copy(s):
        return pltpu.make_async_remote_copy(
            src_ref=source,
            dst_ref=target.at[spot],
            send_sem=outs.at[s],
            recv_sem=ins.at[piece],
            device_id={"seq": s, "fsdp": owner},
            device_id_type=pl.DeviceIdType.MESH,
        )

    def arrival(j):
        return pltpu.make_async_remote_copy(
            src_ref=source,
            dst_ref=target.at[pl.ds(j * rows, rows)],
            send_sem=outs.at[0],
            recv_sem=ins.at[j],
            device_id={"seq": place, "fsdp": owner},
            device_id_type=pl.DeviceIdType.MESH,
        )

    own = pltpu.make_async_copy(source, target.at[spot], here.at[0])

    def is_self(s):
        return jnp.logical_and(owner == shard, place == s)

    def comes_from(j):
        return shard // per, (shard % per) * count + j

    def from_self(j):
        seq, fsdp = comes_from(j)
        return jnp.logical_and(seq == place, fsdp == shard)

    def greeting(barrier):
        for j in range(count):
            seq, fsdp = comes_from(j)
            pl.when(jnp.logical_not(from_self(j)))(
                lambda seq=seq, fsdp=fsdp: greet(barrier, {"seq": seq, "fsdp": fsdp})
            )
        return jnp.where(owner == shard, count - 1, count)

    def begin():
        pl.when(owner == shard)(own.start)
        for s in range(count):
            pl.when(jnp.logical_not(is_self(s)))(lambda s=s: copy(s).start())

    def finish():
        pl.when(owner == shard)(own.wait)
        for s in range(count):
            pl.when(jnp.logical_not(is_self(s)))(lambda s=s: copy(s).wait_send())
        for j in range(count):
            pl.when(jnp.logical_not(from_self(j)))(lambda j=j: arrival(j).wait_recv())

    return greeting, begin, nothing, finish


def own_job(sources, targets, scratch):
    loaded, stored, held = scratch
    place = lax.axis_index("seq")
    count = lax.axis_size("seq")
    part = targets[0].shape[1]
    loads = []
    stores = []
    for c, target in enumerate(targets):
        for k, source in enumerate(sources):
            start = place * (source.shape[0] // count) + c * part
            spot = pl.ds(pl.multiple_of(start, part), part)
            n = c * len(sources) + k
            loads.append(pltpu.make_async_copy(source.at[spot], held.at[n], loaded.at[n]))
            stores.append(pltpu.make_async_copy(held.at[n], target.at[k], stored.at[n]))

    def begin():
        for load in loads:
            load.start()

    def middle():
        for load, store in zip(loads, stores):
            load.wait()
            store.start()

    def finish():
        for store in stores:
            store.wait()

    return no_greeting, begin, middle, finish


MAKERS = {
    "gather": gather_job,
    "scatter": scatter_job,
    "deal": deal_job,
    "home": home_job,
    "own": own_job,
}


def job_scratch(job):
    kind, *arrays = job
    if kind == "scatter":
        _, rows, width = arrays[0].shape
        halves = pltpu.VMEM((2, rows // 2, width), BF16)
        return [
            pltpu.SemaphoreType.DMA((6,)),
            pltpu.SemaphoreType.DMA((6,)),
            pltpu.SemaphoreType.DMA((4,)),
            halves,
            halves,
            halves,
            pltpu.VMEM((rows, width), BF16),
            halves,
            pltpu.VMEM((rows, width), F32),
        ]
    if kind == "own":
        count = CHUNKS * len(arrays)
        rows, width = arrays[0].shape
        part = rows // lax.axis_size("seq") // CHUNKS
        return [
            pltpu.SemaphoreType.DMA((count,)),
            pltpu.SemaphoreType.DMA((count,)),
            pltpu.VMEM((count, part, width), BF16),
        ]
    moves = [
        pltpu.SemaphoreType.DMA((4,)),
        pltpu.SemaphoreType.DMA((4,)),
        pltpu.SemaphoreType.DMA((2,)),
    ]
    return moves + [pltpu.VMEM(arrays[0].shape, BF16)] if kind == "gather" else moves


def job_results(job):
    kind, *arrays = job
    shape = arrays[0].shape
    if kind == "gather":
        return [jax.ShapeDtypeStruct((4,) + shape, BF16)]
    if kind == "scatter":
        return [jax.ShapeDtypeStruct(shape[1:], F32)]
    if kind == "deal":
        return [jax.ShapeDtypeStruct((shape[0] // 4,) + shape[1:], BF16)]
    if kind == "home":
        return [jax.ShapeDtypeStruct((shape[0] * 4,) + shape[1:], BF16)]
    part = shape[0] // lax.axis_size("seq") // CHUNKS
    return [jax.ShapeDtypeStruct((len(arrays), part) + shape[1:], BF16)] * CHUNKS


def plain_job(job):
    kind, *arrays = job
    seqs = lax.axis_size("seq")
    shards = lax.axis_size("fsdp")
    per = shards // seqs
    ends = [(s, h, s * shards + s * per + h) for s in range(seqs) for h in range(per)]
    if kind == "gather":
        return [lax.all_gather(arrays[0], "seq", axis=0)]
    if kind == "scatter":
        return [lax.psum_scatter(arrays[0], "seq", scatter_dimension=0).astype(F32)]
    if kind == "deal":
        rows = arrays[0].shape[0] // seqs
        total = None
        for j in range(seqs):
            moves = [(end, s * shards + h * seqs + j) for s, h, end in ends]
            got = lax.ppermute(arrays[0][j * rows : (j + 1) * rows], ("seq", "fsdp"), moves)
            total = got if total is None else total + got
        return [total]
    if kind == "home":
        held = []
        for j in range(seqs):
            moves = [(s * shards + h * seqs + j, end) for s, h, end in ends]
            held.append(lax.ppermute(arrays[0], ("seq", "fsdp"), moves))
        return [lax.psum(jnp.concatenate(held, axis=0), "seq")]
    own_rows = arrays[0].shape[0] // seqs
    part = own_rows // CHUNKS
    start = lax.axis_index("seq") * own_rows
    return [
        jnp.stack([lax.dynamic_slice_in_dim(w, start + c * part, part, 0) for w in arrays])
        for c in range(CHUNKS)
    ]


def meet(greetings):
    place = lax.axis_index("seq")
    barrier = pltpu.get_barrier_semaphore()
    for device in (over_one(place), over_two(place)):
        greet(barrier, {"seq": device})
    peers = 2
    for greeting in greetings:
        peers = peers + greeting(barrier)
    pl.semaphore_wait(barrier, peers)


def call(
    body, operands, in_specs, out_shape, out_specs, jobs, number, after=None,
    grid=(), scratch=(), cost=None, name=None,
):
    plain = lax.axis_size("seq") != 4
    results = [v for job in jobs for v in plain_job(job)] if plain else []
    inside = [] if plain else jobs
    extra = [] if after is None else [after]
    job_shapes = [job_scratch(job) for job in inside]
    job_outs = [job_results(job) for job in inside]
    n_in = len(operands)
    n_out = len(out_shape)

    def kernel(*refs):
        refs = list(refs)

        def take(count):
            taken, refs[:] = refs[:count], refs[count:]
            return taken

        ins = take(n_in)
        take(len(extra))
        sources = [take(len(job) - 1) for job in inside]
        outs = take(n_out)
        targets = [take(len(shapes)) for shapes in job_outs]
        held = take(len(scratch))
        phases = [
            MAKERS[job[0]](source, target, take(len(shapes)))
            for job, source, target, shapes in zip(inside, sources, targets, job_shapes)
        ]

        def hook(k):
            if k == 0 and phases:
                meet([phase[0] for phase in phases])
            for phase in phases:
                phase[k + 1]()

        body(hook, ins, outs, held)

    given = {}
    if inside:
        given = {"collective_id": number, "has_side_effects": True}
    arrays = [array for job in inside for array in job[1:]]
    shapes = [shape for shapes in job_outs for shape in shapes]
    made = pl.pallas_call(
        kernel,
        grid=grid,
        out_shape=tuple(out_shape) + tuple(shapes),
        in_specs=list(in_specs) + [ANY] * (len(extra) + len(arrays)),
        out_specs=tuple(out_specs) + (ANY,) * len(shapes),
        scratch_shapes=list(scratch) + [shape for shapes in job_shapes for shape in shapes],
        compiler_params=pltpu.CompilerParams(vmem_limit_bytes=VMEM_LIMIT, **given),
        cost_estimate=cost,
        name=name,
    )(*operands, *extra, *arrays)
    return list(made[:n_out]), list(made[n_out:]) + results


def transfer(jobs, number, after=None):
    if lax.axis_size("seq") != 4:
        return [v for job in jobs for v in plain_job(job)]

    def body(hook, ins, outs, held):
        for k in range(3):
            hook(k)

    return call(body, [], [], [], [], jobs, number, after, name="transfer")[1]


def partner(v):
    lane = lax.broadcasted_iota(jnp.int32, v.shape, 1)
    return jnp.where(lane % HEAD < HEAD // 2, pltpu.roll(v, 96, 1), pltpu.roll(v, 32, 1))


def head_mean(v, ones):
    high = v.astype(BF16)
    rest = (v - high.astype(F32)).astype(BF16)
    return dot(high, ones) + dot(rest, ones)


def true_chunk(place, c, count):
    if count != 4:
        return c
    low = 1 - place % 2 if c % 2 else place % 2
    high = 1 - place // 2 if c // 2 else place // 2
    return low + 2 * high


def prepare_heads(sizes, place, qkv_ref, qg_ref, kg_ref, cos_ref, sin_ref, ones, q_s, k_s, v_s):
    hq, hkv, _ = sizes
    seqs, rows_in, _ = qkv_ref.shape
    for c in range(seqs):
        j = true_chunk(place, c, seqs)
        rows = slice(c * rows_in, (c + 1) * rows_in)
        cos = cos_ref[rows, :]
        sin = sin_ref[rows, :]
        for p in range((hq + hkv) // 2):
            is_query = p < hq // 2
            x = qkv_ref[j, :, p * 128 : (p + 1) * 128].astype(F32)
            gain = qg_ref[...] * HEAD**-0.5 if is_query else kg_ref[...]
            y = x * lax.rsqrt(head_mean(x * x, ones) + EPSILON) * gain
            y = (y * cos + partner(y) * sin).astype(BF16)
            for t in range(2):
                part = y[:, t * HEAD : (t + 1) * HEAD]
                if is_query:
                    q_s[2 * p + t, rows, :] = part
                else:
                    k_s[2 * p - hq + t, rows, :] = part
        for t in range(hkv):
            start = (hq + hkv + t) * HEAD
            v_s[t, rows, :] = qkv_ref[j, :, start : start + HEAD]


def allowed_keys(block, first, keys, length):
    bound = jnp.minimum(first + lax.broadcasted_iota(jnp.int32, (block, 1), 0), length - 1)
    return lax.broadcasted_iota(jnp.int32, (block, keys), 1) <= bound


def attend_kernel(sizes, hook, ins, outs, held):
    len_ref, normal_ref, weight_ref, qg_ref, kg_ref, cos_ref, sin_ref, ones_ref = ins
    out_ref, lse_ref, qkv_ref = outs
    q_s, k_s, v_s, o_s = held
    hook(0)

    @pl.loop(0, qkv_ref.shape[0])
    def _(j):
        qkv_ref[j] = dot(normal_ref[j], weight_ref[...]).astype(BF16)

    hq, hkv, group = sizes
    seqs, rows_in, _ = qkv_ref.shape
    place = lax.axis_index("seq")
    prepare_heads(
        sizes, place, qkv_ref, qg_ref, kg_ref, cos_ref, sin_ref, ones_ref[...], q_s, k_s, v_s
    )
    for i in range(seqs * rows_in // BLOCK):
        keys = (i + 1) * BLOCK
        rows = slice(i * BLOCK, (i + 1) * BLOCK)
        keep = allowed_keys(BLOCK, i * BLOCK, keys, len_ref[0])

        def one_head(h, _):
            kv = h // group
            scores = dot(q_s[h, rows, :], k_s[kv, :keys, :], NT)
            scores = jnp.where(keep, scores, NEGATIVE)
            highest = jnp.max(scores, axis=1, keepdims=True)
            shifted = jnp.exp(scores - highest)
            total = jnp.sum(shifted, axis=1, keepdims=True)
            mixed = dot(shifted.astype(BF16), v_s[kv, :keys, :]) / total
            o_s[h, rows, :] = mixed.astype(BF16)
            lse_ref[h, rows, :] = highest + jnp.log(total)
            return 0

        lax.fori_loop(0, hq, one_head, 0)
        if i == seqs * rows_in // BLOCK - 2:
            hook(1)
    for c in range(seqs):
        j = true_chunk(place, c, seqs)
        rows = slice(c * rows_in, (c + 1) * rows_in)
        for p in range(hq // 2):
            out_ref[j, :, p * 128 : (p + 1) * 128] = jnp.concatenate(
                [o_s[2 * p, rows, :], o_s[2 * p + 1, rows, :]], axis=1
            )
    hook(2)


def attend_back_kernel(sizes, hook, ins, outs, held):
    (
        len_ref, qkv_ref, res_ref, out_w_ref, qkv_w_ref, lse_ref,
        qg_ref, kg_ref, cos_ref, sin_ref, ones_ref,
    ) = ins
    dqkv_ref, dgain_ref, pull_ref = outs
    q_s, k_s, v_s, cot_s, dq_s, dk_s, dv_s = held
    hook(0)
    hq, hkv, group = sizes
    seqs, rows_in, _ = qkv_ref.shape
    place = lax.axis_index("seq")
    ones = ones_ref[...]
    prepare_heads(sizes, place, qkv_ref, qg_ref, kg_ref, cos_ref, sin_ref, ones, q_s, k_s, v_s)
    for c in range(seqs):
        j = true_chunk(place, c, seqs)
        cots = dot(res_ref[j], out_w_ref[...], NT).astype(BF16)
        for h in range(hq):
            cot_s[h, c * rows_in : (c + 1) * rows_in, :] = cots[:, h * HEAD : (h + 1) * HEAD]
    dk_s[...] = jnp.zeros_like(dk_s)
    dv_s[...] = jnp.zeros_like(dv_s)
    for i in range(seqs * rows_in // BLOCK):
        keys = (i + 1) * BLOCK
        rows = slice(i * BLOCK, (i + 1) * BLOCK)
        keep = allowed_keys(BLOCK, i * BLOCK, keys, len_ref[0])

        def one_head(h, _):
            kv = h // group
            q = q_s[h, rows, :]
            cot = cot_s[h, rows, :]
            k = k_s[kv, :keys, :]
            scores = jnp.where(keep, dot(q, k, NT), NEGATIVE)
            probs = jnp.exp(scores - lse_ref[h, rows, :])
            prob_cot = dot(cot, v_s[kv, :keys, :], NT)
            inner = jnp.sum(probs * prob_cot, axis=1, keepdims=True)
            score_cot = (probs * (prob_cot - inner)).astype(BF16)
            dq_s[h, rows, :] = dot(score_cot, k) * HEAD**-0.5
            dk_s[kv, :keys, :] += dot(score_cot, q, TN)
            dv_s[kv, :keys, :] += dot(probs.astype(BF16), cot, TN)
            return 0

        lax.fori_loop(0, hq, one_head, 0)
        if i == seqs * rows_in // BLOCK - 2:
            hook(1)
    gain_sums = [jnp.zeros((1, 128), F32), jnp.zeros((1, 128), F32)]
    for c in range(seqs):
        j = true_chunk(place, c, seqs)
        rows = slice(c * rows_in, (c + 1) * rows_in)
        cos = cos_ref[rows, :]
        sin = sin_ref[rows, :]
        for p in range((hq + hkv) // 2):
            is_query = p < hq // 2
            x = qkv_ref[j, :, p * 128 : (p + 1) * 128].astype(F32)
            gain = qg_ref[...] if is_query else kg_ref[...]
            source, first = (dq_s, 2 * p) if is_query else (dk_s, 2 * p - hq)
            turned = jnp.concatenate([source[first, rows, :], source[first + 1, rows, :]], axis=1)
            scale = lax.rsqrt(head_mean(x * x, ones) + EPSILON)
            straight = turned * cos + partner(turned * sin)
            unit = x * scale
            which = 0 if is_query else 1
            gain_sums[which] += jnp.sum(straight * unit, axis=0, keepdims=True)
            pulled = gain * straight
            dx = scale * (pulled - unit * head_mean(unit * pulled, ones))
            dqkv_ref[j, :, p * 128 : (p + 1) * 128] = dx.astype(BF16)
        for p in range(hkv // 2):
            start = (hq + hkv) * HEAD + p * 128
            dqkv_ref[j, :, start : start + 128] = jnp.concatenate(
                [dv_s[2 * p, rows, :], dv_s[2 * p + 1, rows, :]], axis=1
            ).astype(BF16)
    dgain_ref[0:1, :] = gain_sums[0]
    dgain_ref[1:2, :] = gain_sums[1]

    @pl.loop(0, seqs)
    def _(j):
        pull_ref[j] = dot(dqkv_ref[j], qkv_w_ref[...], NT).astype(BF16)

    hook(2)


def position_tables(length):
    places = np.arange(length, dtype=np.float32)
    half = HEAD // 2
    freqs = np.float32(ROPE_BASE) ** (-(np.arange(half, dtype=np.float32) * 2.0) / HEAD)
    angles = places[:, None] * freqs.astype(np.float32)[None, :]
    cos = np.cos(angles).astype(np.float32)
    sin = np.sin(angles).astype(np.float32)
    ones = np.kron(np.eye(2), np.ones((HEAD, HEAD)) / HEAD)
    return (
        jnp.asarray(np.concatenate([cos] * 4, axis=1)),
        jnp.asarray(np.concatenate([-sin, sin, -sin, sin], axis=1)),
        jnp.asarray(ones, dtype=BF16),
    )


def attend(sizes, length, normal, weight, gains, tables, jobs, number, after):
    seqs, rows_in, _ = normal.shape
    hq, hkv, _ = sizes
    slot = seqs * rows_in
    return call(
        functools.partial(attend_kernel, sizes),
        [length, normal, weight, *gains, *tables],
        [SMEM] + [VMEM] * 7,
        [
            jax.ShapeDtypeStruct((seqs, rows_in, hq * HEAD), BF16),
            jax.ShapeDtypeStruct((hq, slot, 1), F32),
            jax.ShapeDtypeStruct((seqs, rows_in, weight.shape[1]), BF16),
        ],
        [VMEM, VMEM, VMEM],
        jobs,
        number,
        after,
        scratch=[
            pltpu.VMEM((hq, slot, HEAD), BF16),
            pltpu.VMEM((hkv, slot, HEAD), BF16),
            pltpu.VMEM((hkv, slot, HEAD), BF16),
            pltpu.VMEM((hq, slot, HEAD), BF16),
        ],
        cost=pl.CostEstimate(
            flops=56 * hq * slot * slot * HEAD, bytes_accessed=1 << 23, transcendentals=0
        ),
        name="attend",
    )


def attend_back(
    sizes, length, qkv, res, out_w, qkv_w, lse, gains, tables, jobs, number, after
):
    seqs, rows_in, width = qkv.shape
    hq, hkv, _ = sizes
    slot = seqs * rows_in
    return call(
        functools.partial(attend_back_kernel, sizes),
        [length, qkv, res, out_w, qkv_w, lse, *gains, *tables],
        [SMEM] + [VMEM] * 10,
        [
            jax.ShapeDtypeStruct((seqs, rows_in, width), BF16),
            jax.ShapeDtypeStruct((2, 128), F32),
            jax.ShapeDtypeStruct(res.shape, BF16),
        ],
        [VMEM, VMEM, VMEM],
        jobs,
        number,
        after,
        scratch=[
            pltpu.VMEM((hq, slot, HEAD), BF16),
            pltpu.VMEM((hkv, slot, HEAD), BF16),
            pltpu.VMEM((hkv, slot, HEAD), BF16),
            pltpu.VMEM((hq, slot, HEAD), BF16),
            pltpu.VMEM((hq, slot, HEAD), F32),
            pltpu.VMEM((hkv, slot, HEAD), F32),
            pltpu.VMEM((hkv, slot, HEAD), F32),
        ],
        cost=pl.CostEstimate(
            flops=88 * hq * slot * slot * HEAD, bytes_accessed=1 << 23, transcendentals=0
        ),
        name="attend_back",
    )


def hooked(hook, step, steps, work):
    pl.when(step == 0)(lambda: hook(0))
    work(lambda: pl.when(step == (3 * steps) // 5)(lambda: hook(1)))
    pl.when(step == steps - 1)(lambda: hook(2))


def ffn_kernel(steps, hook, ins, outs, held):
    step = pl.program_id(0)
    weights_ref, loaded = held
    loads = [
        pltpu.make_async_copy(ins[2].at[:, k], weights_ref.at[k], loaded.at[k]) for k in range(3)
    ]

    def first(act):
        pl.when(step == 0)(act)

    def work(late):
        for load in loads:
            first(load.start)
        ffn_tile(late, first, loads, *ins[:2], weights_ref, ins[3:], *outs)

    hooked(hook, step, steps, work)


def ffn_tile(late, first, loads, mid_ref, cot_ref, weights_ref, sums, acts_ref, pull_ref):
    model = mid_ref.shape[-1]
    hidden = acts_ref.shape[-1]
    whole = (hidden, model)
    mid = mid_ref[...]
    first(loads[0].wait)
    gate = dot(mid, weights_ref[0].reshape(whole), NT)
    first(loads[1].wait)
    up = dot(mid, weights_ref[1].reshape(whole), NT)
    first(loads[2].wait)
    mids_cot = dot(cot_ref[...], weights_ref[2].reshape(whole), NT)
    late()
    sigmoid = jax.nn.sigmoid(gate)
    active = gate * sigmoid
    gate_cot = (mids_cot * up * sigmoid * (1.0 + gate * (1.0 - sigmoid))).astype(BF16)
    up_cot = (mids_cot * active).astype(BF16)
    acts_ref[0] = gate_cot
    acts_ref[1] = up_cot
    acts_ref[2] = (active * up).astype(BF16)
    pulled = dot(gate_cot, weights_ref[0].reshape(whole)) + dot(
        up_cot, weights_ref[1].reshape(whole)
    )
    for sum_ref in sums:
        pulled = pulled + sum_ref[...]
    pull_ref[...] = pulled.astype(pull_ref.dtype)


def ffn_both(mid, cot, weights, summed, last, jobs, number, after):
    tokens, model = mid.shape
    shards, _, part, _ = weights.shape
    hidden = shards * part
    tile = min(256, tokens)

    row_spec = pl.BlockSpec((tile, model), lambda i: (i, 0))
    extra = () if summed is None else (summed,)
    return call(
        functools.partial(ffn_kernel, tokens // tile),
        [mid, cot, weights, *extra],
        [row_spec, row_spec, ANY] + [row_spec] * len(extra),
        [
            jax.ShapeDtypeStruct((3, tokens, hidden), BF16),
            jax.ShapeDtypeStruct((tokens, model), BF16 if last else F32),
        ],
        [pl.BlockSpec((3, tile, hidden), lambda i: (0, i, 0)), row_spec],
        jobs,
        number,
        after,
        grid=(tokens // tile,),
        scratch=[
            pltpu.VMEM((3, shards, part, model), BF16),
            pltpu.SemaphoreType.DMA((3,)),
        ],
        cost=pl.CostEstimate(
            flops=16 * tokens * model * hidden,
            bytes_accessed=4 * tokens * model + 6 * hidden * model,
            transcendentals=0,
        ),
        name="ffn_both",
    )


def ffn_grad_kernel(slots, tiles, hook, ins, outs, held):
    acts = ins[:slots]
    others = ins[slots:]
    (out_ref,) = outs
    rows_ref, loaded = held
    kind = pl.program_id(0)
    step = kind * tiles + pl.program_id(1)
    loads = [
        pltpu.make_async_copy(other, rows_ref.at[k], loaded.at[k])
        for k, other in enumerate(others)
    ]

    def store(first):
        total = None
        for k, act in enumerate(acts):
            term = dot(act[0], rows_ref[first + k], TN)
            total = term if total is None else total + term
        out_ref[...] = total.astype(BF16).reshape(out_ref.shape)

    def work(late):
        for k, load in enumerate(loads):
            pl.when(step == 0)(load.start)
        for k, load in enumerate(loads):
            pl.when(step == (0 if k < slots else 2 * tiles))(load.wait)
        late()
        pl.when(kind < 2)(lambda: store(0))
        pl.when(kind == 2)(lambda: store(slots))

    hooked(hook, step, 3 * tiles, work)


def ffn_grads(acts, mids, cots, shards, jobs, number, after):
    slots = len(acts)
    _, tokens, hidden = acts[0].shape
    model = mids[0].shape[-1]
    part = hidden // shards
    tile = 256
    per = tile // part
    return call(
        functools.partial(ffn_grad_kernel, slots, hidden // tile),
        [*acts, *mids, *cots],
        [pl.BlockSpec((1, tokens, tile), lambda k, i: (k, 0, i))] * slots
        + [ANY] * (2 * slots),
        [jax.ShapeDtypeStruct((shards, 3, part, model), BF16)],
        [pl.BlockSpec((per, 1, part, model), lambda k, i: (i, k, 0, 0))],
        jobs,
        number,
        after,
        grid=(3, hidden // tile),
        scratch=[
            pltpu.VMEM((2 * slots, tokens, model), BF16),
            pltpu.SemaphoreType.DMA((2 * slots,)),
        ],
        cost=pl.CostEstimate(
            flops=9 * slots * tokens * model * hidden,
            bytes_accessed=4 * slots * tokens * model,
            transcendentals=0,
        ),
        name="ffn_grads",
    )


def ffn_down_kernel(chunks, steps, hook, ins, outs, held):
    acts = ins[:chunks]
    downs = ins[chunks:]
    (out_ref,) = outs

    def work(late):
        late()
        total = None
        for act, down in zip(acts, downs):
            hidden = act.shape[-1]
            term = dot(act[0], down[...].reshape(hidden, down.shape[-1]))
            total = term if total is None else total + term
        out_ref[...] = total.astype(BF16)

    hooked(hook, pl.program_id(0), steps, work)


def ffn_down(acts, weights, jobs, number, after):
    chunks = len(acts)
    _, tokens, hidden = acts[0].shape
    shards, _, part, model = weights[0].shape
    tile = min(256, tokens)
    act_spec = pl.BlockSpec((1, tile, hidden), lambda i: (2, i, 0))
    down_spec = pl.BlockSpec(
        (shards, 1, part, model),
        lambda i: (0, 2, 0, 0),
        pipeline_mode=pl.Buffered(buffer_count=1),
    )
    return call(
        functools.partial(ffn_down_kernel, chunks, tokens // tile),
        [*acts, *weights],
        [act_spec] * chunks + [down_spec] * chunks,
        [jax.ShapeDtypeStruct((tokens, model), BF16)],
        [pl.BlockSpec((tile, model), lambda i: (i, 0))],
        jobs,
        number,
        after,
        grid=(tokens // tile,),
        cost=pl.CostEstimate(
            flops=4 * chunks * tokens * model * hidden,
            bytes_accessed=chunks * hidden * (tokens + model) * 2,
            transcendentals=0,
        ),
        name="ffn_down",
    )


def place_kernel(place_ref, parts_ref, *refs):
    for kind, out_ref in enumerate(refs[-3:]):
        out_ref[0, 0] = parts_ref[0, kind].astype(F32)


def place_parts(place, parts, chunk, held):
    seqs, _, part, model = parts.shape
    out = jax.ShapeDtypeStruct((seqs, CHUNKS, part, model), F32)
    out_spec = pl.BlockSpec(
        (1, 1, part, model), lambda j, at: (jnp.bitwise_xor(at[0], j), chunk, 0, 0)
    )
    return pl.pallas_call(
        place_kernel,
        out_shape=(out,) * 3,
        grid_spec=pltpu.PrefetchScalarGridSpec(
            num_scalar_prefetch=1,
            grid=(seqs,),
            in_specs=[pl.BlockSpec((1, 3, part, model), lambda j, at: (j, 0, 0, 0))]
            + [ANY] * len(held),
            out_specs=(out_spec,) * 3,
        ),
        input_output_aliases={2 + k: k for k in range(len(held))},
        compiler_params=pltpu.CompilerParams(vmem_limit_bytes=VMEM_LIMIT),
        cost_estimate=pl.CostEstimate(
            flops=0, bytes_accessed=18 * seqs * part * model, transcendentals=0
        ),
        name="place_parts",
    )(place, parts, *held)


def place_heads_kernel(
    place_ref, parts_ref, query_w_ref, key_w_ref, value_w_ref,
    query_ref, key_ref, value_ref, rest_ref, met_ref,
):
    edge = query_ref.shape[1]
    width = key_ref.shape[1]
    part = parts_ref[0].astype(F32)
    query_ref[...] = part[:, :edge]
    key_ref[...] = part[:, edge : edge + width]
    value_ref[...] = part[:, edge + width : edge + 2 * width]
    rest = part[:, edge + 2 * width :]
    met = jnp.zeros_like(met_ref)
    for grad_ref, weight_ref in (
        (query_ref, query_w_ref),
        (key_ref, key_w_ref),
        (value_ref, value_w_ref),
    ):
        product = grad_ref[...] * weight_ref[...].astype(F32)
        met = met + jnp.sum(product, axis=1, keepdims=True)

    @pl.when(pl.program_id(0) == 0)
    def _():
        rest_ref[...] = rest
        met_ref[...] = met

    @pl.when(pl.program_id(0) > 0)
    def _():
        rest_ref[...] += rest
        met_ref[...] += met


def place_heads(place, parts, edge, width, weights):
    seqs, rows, total = parts.shape
    rest = total - edge - 2 * width

    def column_spec(size):
        return pl.BlockSpec((rows, size), lambda j, at: (0, jnp.bitwise_xor(at[0], j)))

    return pl.pallas_call(
        place_heads_kernel,
        out_shape=[
            jax.ShapeDtypeStruct((rows, seqs * edge), F32),
            jax.ShapeDtypeStruct((rows, seqs * width), F32),
            jax.ShapeDtypeStruct((rows, seqs * width), F32),
            jax.ShapeDtypeStruct((rows, rest), F32),
            jax.ShapeDtypeStruct((rows, 128), F32),
        ],
        grid_spec=pltpu.PrefetchScalarGridSpec(
            num_scalar_prefetch=1,
            grid=(seqs,),
            in_specs=[
                pl.BlockSpec((1, rows, total), lambda j, at: (j, 0, 0)),
                column_spec(edge),
                column_spec(width),
                column_spec(width),
            ],
            out_specs=[
                column_spec(edge),
                column_spec(width),
                column_spec(width),
                pl.BlockSpec((rows, rest), lambda j, at: (0, 0)),
                pl.BlockSpec((rows, 128), lambda j, at: (0, 0)),
            ],
        ),
        compiler_params=pltpu.CompilerParams(vmem_limit_bytes=VMEM_LIMIT),
        name="place_heads",
    )(place, parts, *weights)


def scale_of(values):
    return lax.rsqrt(jnp.mean(values * values, axis=-1, keepdims=True) + EPSILON)


def normed(values, gain):
    return values * scale_of(values) * gain


def normed_back(values, gain, cot):
    scale = scale_of(values)
    pulled = cot * gain
    mean = jnp.mean(values * pulled, axis=-1, keepdims=True)
    return (
        scale * pulled - values * (scale * scale * scale) * mean,
        jnp.sum(cot * values * scale, axis=0),
    )


def follow(values, earlier):
    return lax.optimization_barrier((values, *earlier))[0]


def own_columns(weight, heads, place):
    width = heads * HEAD
    part = lax.dynamic_slice_in_dim(weight, place * width, width, 1)
    if heads % 2:
        part = jnp.pad(part, ((0, 0), (0, HEAD)))
    return part


def on_device(
    tokens,
    cotangent,
    lengths,
    attn_gain,
    query_weight,
    key_weight,
    value_weight,
    query_gain,
    key_gain,
    out_weight,
    ffn_gain,
    gate_weight,
    up_weight,
    down_weight,
):
    slots, rows, model = tokens.shape
    seqs = lax.axis_size("seq")
    shards = lax.axis_size("fsdp")
    place = lax.axis_index("seq")
    shard = lax.axis_index("fsdp")
    slot_len = rows * seqs
    query_width = query_weight.shape[1]
    kv_width = key_weight.shape[1]
    hq = query_width // seqs // HEAD
    hkv = kv_width // seqs // HEAD
    hkv_held = hkv + hkv % 2
    sizes = (hq, hkv_held, hq // hkv)
    order = (place if seqs == 4 else place * 0).reshape(1)
    tables = position_tables(slot_len)
    gains = (
        jnp.concatenate([query_gain, query_gain]).reshape(1, 2 * HEAD),
        jnp.concatenate([key_gain, key_gain]).reshape(1, 2 * HEAD),
    )

    flat = (slot_len, model)
    chunked = (seqs, rows, model)
    places = place * rows + jnp.arange(rows, dtype=jnp.int32)
    live = (places[None, :] < lengths[:, None]).astype(F32)[..., None]
    inputs = tokens.astype(F32)
    out_cot = cotangent.astype(F32) * live
    out_low = [out_cot[b].astype(BF16) for b in range(slots)]
    normal_in = [normed(inputs[b], attn_gain).astype(BF16) for b in range(slots)]

    qkv_own = jnp.concatenate(
        [
            own_columns(query_weight, hq, place),
            own_columns(key_weight, hkv, place),
            own_columns(value_weight, hkv, place),
        ],
        axis=1,
    )
    qkv_weight = lax.all_gather(qkv_own, "fsdp", axis=0, tiled=True)
    start = [
        ("gather", normal_in[0]),
        ("deal", out_weight),
        ("own", gate_weight, up_weight, down_weight),
    ]
    normal_0, out_own, *ffn_own = transfer(start, 1)
    out_rows = lax.all_gather(out_own, "fsdp", axis=0, tiled=True)
    hidden_own = gate_weight.shape[0] // seqs
    part = hidden_own // CHUNKS
    ffn_weights = [lax.all_gather(own, "fsdp", axis=0) for own in ffn_own]

    def leave(mixed):
        return dot(mixed.reshape(slot_len, -1), out_rows).astype(BF16).reshape(chunked)

    def enter_ffn(b, total):
        res = inputs[b] + total
        return res, normed(res, ffn_gain).astype(BF16)

    def heads(b, jobs, number, after):
        return attend(
            sizes, lengths[b : b + 1], normal_full[b], qkv_weight, gains, tables,
            jobs, number, after,
        )

    normal_full = [None] * slots
    cot_full = [None] * slots
    mid_full = [None] * slots
    normal_full[0] = normal_0
    (mixed_0, lse_0, qkv_0), (normal_full[1],) = heads(
        0, [("gather", normal_in[1])], 2, normal_full[0]
    )
    (mixed_1, lse_1, qkv_1), (total_0,) = heads(1, [("scatter", leave(mixed_0))], 3, mixed_0)
    qkv = [qkv_0, qkv_1]
    log_sums = [lse_0, lse_1]
    attended = [v.reshape(slot_len, hq * HEAD) for v in (mixed_0, mixed_1)]
    res_0, mid_0 = enter_ffn(0, total_0)
    mid_full[0], cot_full[0] = [
        v.reshape(flat)
        for v in transfer([("gather", mid_0), ("gather", out_low[0])], 4, mixed_1)
    ]

    acts = [[None] * slots for _ in range(CHUNKS)]
    pulled = [None] * slots

    def ffn_step(b, c, jobs, number, after):
        (acts[c][b], pulled[b]), results = ffn_both(
            mid_full[b], cot_full[b], ffn_weights[c], pulled[b], c == CHUNKS - 1,
            jobs, number, after,
        )
        return results

    def grad_step(c, jobs, number, after):
        (grads,), results = ffn_grads(
            acts[c], mid_full, cot_full, shards, jobs, number, after
        )
        return grads.reshape(shards, 3 * part, model), results

    def leave_ffn(b, jobs, number, after):
        (out,), results = ffn_down(
            [acts[c][b] for c in range(CHUNKS)], ffn_weights, jobs, number, after
        )
        return out.reshape(chunked), results

    total_1, full = ffn_step(
        0, 0, [("scatter", leave(mixed_1)), ("gather", out_low[1])], 5, mid_full[0]
    )
    cot_full[1] = full.reshape(flat)
    res_1, mid_1 = enter_ffn(1, total_1)
    hidden_res = [res_0, res_1]
    (full,) = ffn_step(0, 1, [("gather", mid_1)], 6, acts[0][0])
    mid_full[1] = full.reshape(flat)
    (mid_total_0,) = ffn_step(1, 0, [("scatter", pulled[0].reshape(chunked))], 7, acts[1][0])

    def pull_mid(b, total):
        pull, gain_part = normed_back(hidden_res[b], ffn_gain, total)
        cot = out_cot[b] + pull
        return cot, cot.astype(BF16), gain_part

    res_cot_0, low_0, ffn_gain_0 = pull_mid(0, mid_total_0)
    grads_0, (res_full_0,) = grad_step(0, [("gather", low_0)], 8, acts[0][1])
    ffn_sums = [lax.psum_scatter(grads_0, "fsdp", scatter_dimension=0)]
    out_0, _ = leave_ffn(0, [], 0, grads_0)
    (out_total_0,) = ffn_step(1, 1, [("scatter", out_0)], 9, out_0)
    grads_1, (mid_total_1,) = grad_step(
        1, [("scatter", pulled[1].reshape(chunked))], 10, acts[1][1]
    )
    ffn_sums.append(
        lax.psum_scatter(grads_1, "fsdp", scatter_dimension=0)
    )
    out_1, _ = leave_ffn(1, [], 0, grads_1)
    res_cot_1, low_1, ffn_gain_1 = pull_mid(1, mid_total_1)
    grad_ffn_gain = ffn_gain_0 + ffn_gain_1

    def back(b, full, jobs, number, after):
        return attend_back(
            sizes, lengths[b : b + 1], qkv[b], full, out_rows, qkv_weight, log_sums[b],
            gains, tables, jobs, number, after,
        )

    (dqkv_0, heads_gain_0, pull_0), (res_full_1, out_total_1) = back(
        0, res_full_0, [("gather", low_1), ("scatter", out_1)], 11, out_1
    )
    res_full = [v.reshape(flat) for v in (res_full_0, res_full_1)]
    out_grads = sum(dot(attended[b], res_full[b], TN) for b in range(slots)).astype(BF16)
    (dqkv_1, heads_gain_1, pull_1), (in_total_0, ffn_parts_0) = back(
        1, res_full_1, [("scatter", pull_0), ("gather", ffn_sums[0])], 12, out_grads
    )
    out_sums = lax.psum_scatter(
        follow(out_grads, [ffn_sums[1], dqkv_1]), "fsdp", scatter_dimension=0, tiled=True
    )
    head_gain = heads_gain_0 + heads_gain_1
    dqkv = [v.reshape(slot_len, -1) for v in (dqkv_0, dqkv_1)]
    held = model // shards
    head_sums = jnp.pad(
        (head_gain[:, :HEAD] + head_gain[:, HEAD:]).reshape(2, shards, HEAD // shards),
        ((0, 0), (0, 0), (0, held - HEAD // shards)),
    ).reshape(2, model)
    gain_columns = jnp.stack([grad_ffn_gain, head_sums[0], head_sums[1]], axis=1).astype(BF16)
    qkv_grads = jnp.concatenate(
        [
            sum(dot(normal_full[b].reshape(flat), dqkv[b], TN) for b in range(slots)).astype(BF16),
            jnp.pad(gain_columns, ((0, 0), (0, 125))),
        ],
        axis=1,
    )
    in_total_1, ffn_parts_1, grad_out = transfer(
        [("scatter", pull_1), ("gather", ffn_sums[1]), ("home", out_sums)], 13, qkv_grads
    )
    qkv_sums = lax.psum_scatter(qkv_grads, "fsdp", scatter_dimension=0, tiled=True)
    (heads_all,) = transfer([("gather", qkv_sums)], 14, in_total_1)
    grad_tokens = []
    for b, (in_cot, cot) in enumerate(((in_total_0, res_cot_0), (in_total_1, res_cot_1))):
        pull, _ = normed_back(inputs[b], attn_gain, in_cot)
        grad_tokens.append((cot + pull).astype(BF16))
    output = [
        (live[b] * (hidden_res[b] + total)).astype(BF16)
        for b, total in enumerate((out_total_0, out_total_1))
    ]
    ffn_grad = ()
    for c, parts in enumerate((ffn_parts_0, ffn_parts_1)):
        ffn_grad = place_parts(order, parts.reshape(seqs, 3, part, model), c, ffn_grad)
    ffn_grad = [v.reshape(seqs * hidden_own, model) for v in ffn_grad]

    edge = hq * HEAD
    width = hkv_held * HEAD
    if hkv == hkv_held:
        grad_query, grad_key, grad_value, gain_sums, met = place_heads(
            order, heads_all, edge, width, (query_weight, key_weight, value_weight)
        )
        met = met[:, 0]
    else:
        heads_all = jnp.moveaxis(heads_all, 0, 1).astype(F32)
        last = edge + width
        grad_query = heads_all[..., :edge].reshape(held, query_width)
        grad_key = heads_all[..., edge : edge + hkv * HEAD].reshape(held, kv_width)
        grad_value = heads_all[..., last : last + hkv * HEAD].reshape(held, kv_width)
        gain_sums = jnp.sum(heads_all[..., last + width :], axis=1)
        met = sum(
            jnp.sum(grad * weight.astype(F32), axis=1)
            for grad, weight in (
                (grad_query, query_weight),
                (grad_key, key_weight),
                (grad_value, value_weight),
            )
        )
    grad_attn_gain = met / lax.dynamic_slice_in_dim(attn_gain, shard * held, held, 0)

    return (
        jnp.stack(output),
        jnp.stack(grad_tokens),
        grad_attn_gain,
        grad_query,
        grad_key,
        grad_value,
        gain_sums[: HEAD // shards, 1],
        gain_sums[: HEAD // shards, 2],
        grad_out.astype(F32),
        gain_sums[:, 0],
        ffn_grad[0],
        ffn_grad[1],
        ffn_grad[2],
    )


def solution(mesh):
    return jax.shard_map(
        on_device,
        mesh=mesh,
        in_specs=(
            P("fsdp", "seq", None),
            P("fsdp", "seq", None),
            P("fsdp"),
            P(),
            P("fsdp", None),
            P("fsdp", None),
            P("fsdp", None),
            P(),
            P(),
            P("fsdp", None),
            P(),
            P("fsdp", None),
            P("fsdp", None),
            P("fsdp", None),
        ),
        out_specs=(
            P("fsdp", "seq", None),
            P("fsdp", "seq", None),
            P("fsdp"),
            P("fsdp", None),
            P("fsdp", None),
            P("fsdp", None),
            P("fsdp"),
            P("fsdp"),
            P("fsdp", None),
            P("fsdp"),
            P("fsdp", None),
            P("fsdp", None),
            P("fsdp", None),
        ),
        check_vma=False,
    )
```

```python
import functools

import jax
import jax.numpy as jnp
import numpy as np
from jax import lax
from jax.experimental import pallas as pl
from jax.experimental.pallas import tpu as pltpu
from jax.sharding import PartitionSpec as P

EPSILON = 1e-05
ROPE_BASE = 1000000.0
NEGATIVE = -1e30
F32 = jnp.float32
BF16 = jnp.bfloat16
NN = (((1,), (0,)), ((), ()))
NT = (((1,), (1,)), ((), ()))
TN = (((0,), (0,)), ((), ()))
SMEM = pl.BlockSpec(memory_space=pltpu.SMEM)
VMEM = pl.BlockSpec(memory_space=pltpu.VMEM)
VMEM_LIMIT = 58 << 20
HEAD = 64
BLOCK = 256
CHUNKS = 2
ANY = pl.BlockSpec(memory_space=pl.ANY)


def dot(a, b, dims=NN):
    return lax.dot_general(a, b, dims, preferred_element_type=F32)


def over_one(place):
    return place + 1 - 2 * (place % 2)


def over_two(place):
    return (place + 2) % 4


def send(source, target, device, out_sem, in_sem):
    return pltpu.make_async_remote_copy(
        src_ref=source,
        dst_ref=target,
        send_sem=out_sem,
        recv_sem=in_sem,
        device_id={"seq": device},
        device_id_type=pl.DeviceIdType.MESH,
    )


def gather_job(sources, targets, scratch):
    (source,) = sources
    (target,) = targets
    outs, ins, here, held = scratch
    place = lax.axis_index("seq")
    one, two = over_one(place), over_two(place)
    half = source.shape[0] // 2
    load = pltpu.make_async_copy(source, held, here.at[0])
    store = pltpu.make_async_copy(held, target.at[0], here.at[1])
    first = send(source, target.at[1], one, outs.at[0], ins.at[0])
    second = send(source, target.at[2], two, outs.at[1], ins.at[1])
    top = pl.ds(0, half)
    low = pl.ds(half, half)
    third = send(target.at[2, top], target.at[3, top], one, outs.at[2], ins.at[2])
    fourth = send(target.at[1, low], target.at[3, low], two, outs.at[3], ins.at[3])

    def begin():
        first.start()
        second.start()
        load.start()

    def middle():
        load.wait()
        store.start()
        second.wait_recv()
        third.start()
        first.wait_recv()
        fourth.start()

    def finish():
        third.wait_recv()
        fourth.wait_recv()
        for copy in (first, second, third, fourth):
            copy.wait_send()
        store.wait()

    return no_greeting, begin, middle, finish


def scatter_job(sources, targets, scratch):
    (parts,) = sources
    (total,) = targets
    outs, ins, here, got_one, got_two, kept, own, last, summed = scratch
    place = lax.axis_index("seq")
    one, two = over_one(place), over_two(place)
    half = parts.shape[1] // 2
    top = pl.ds(0, half)
    low = pl.ds(half, half)
    sends = [
        send(parts.at[3, top], got_one.at[0], one, outs.at[0], ins.at[0]),
        send(parts.at[3, low], got_two.at[0], two, outs.at[1], ins.at[1]),
        send(parts.at[1, top], got_one.at[1], one, outs.at[2], ins.at[2]),
        send(parts.at[2, low], got_two.at[1], two, outs.at[3], ins.at[3]),
        send(kept.at[0], last.at[0], two, outs.at[4], ins.at[4]),
        send(kept.at[1], last.at[1], one, outs.at[5], ins.at[5]),
    ]
    loads = [
        pltpu.make_async_copy(parts.at[2, top], kept.at[0], here.at[0]),
        pltpu.make_async_copy(parts.at[1, low], kept.at[1], here.at[1]),
        pltpu.make_async_copy(parts.at[0], own, here.at[2]),
    ]
    store = pltpu.make_async_copy(summed, total, here.at[3])

    def begin():
        for copy in sends[:4]:
            copy.start()
        for copy in loads:
            copy.start()

    def middle():
        for k, got in enumerate((got_one, got_two)):
            loads[k].wait()
            sends[k].wait_recv()
            kept[k] = (kept[k].astype(F32) + got[0].astype(F32)).astype(BF16)
            sends[4 + k].start()

    def finish():
        loads[2].wait()
        for k, got in enumerate((got_one, got_two)):
            sends[2 + k].wait_recv()
            sends[4 + k].wait_recv()
            rows = slice(k * half, (k + 1) * half)
            summed[rows, :] = (
                own[rows, :].astype(F32) + got[1].astype(F32) + last[k].astype(F32)
            )
        store.start()
        for copy in sends:
            copy.wait_send()
        store.wait()

    return no_greeting, begin, middle, finish


def no_greeting(barrier):
    return 0


def nothing():
    pass


def greet(barrier, device):
    pl.semaphore_signal(
        barrier, inc=1, device_id=device, device_id_type=pl.DeviceIdType.MESH
    )


def deal_job(sources, targets, scratch):
    (source,) = sources
    (target,) = targets
    outs, ins, here = scratch
    rows = target.shape[0]
    count = source.shape[0] // rows
    place = lax.axis_index("seq")
    shard = lax.axis_index("fsdp")
    per = lax.axis_size("fsdp") // count
    part = shard % per
    is_source = shard // per == place
    to_self = jnp.logical_and(is_source, shard // count == part)
    origin = place * per + shard // count

    def copy(j):
        return pltpu.make_async_remote_copy(
            src_ref=source.at[pl.ds(j * rows, rows)],
            dst_ref=target,
            send_sem=outs.at[j],
            recv_sem=ins.at[0],
            device_id={"fsdp": part * count + j},
            device_id_type=pl.DeviceIdType.MESH,
        )

    def local(j):
        return pltpu.make_async_copy(source.at[pl.ds(j * rows, rows)], target, here.at[0])

    def greeting(barrier):
        pl.when(origin != shard)(lambda: greet(barrier, {"fsdp": origin}))
        return jnp.where(is_source, count, 0) - jnp.where(to_self, 1, 0)

    def each(act_remote, act_local):
        for j in range(count):
            mine = part * count + j == shard
            pl.when(jnp.logical_and(is_source, mine))(lambda j=j: act_local(local(j)))
            pl.when(jnp.logical_and(is_source, jnp.logical_not(mine)))(
                lambda j=j: act_remote(copy(j))
            )

    def begin():
        each(lambda c: c.start(), lambda c: c.start())

    def finish():
        each(lambda c: c.wait_send(), lambda c: c.wait())
        pl.when(origin != shard)(lambda: copy(0).wait_recv())

    return greeting, begin, nothing, finish


def swap_job(sources, targets, scratch):
    (source,) = sources
    (target,) = targets
    outs, ins, here = scratch
    count, rows, _ = source.shape
    place = lax.axis_index("seq")
    shard = lax.axis_index("fsdp")
    per = lax.axis_size("fsdp") // count
    piece = shard % count
    spot = pl.ds(pl.multiple_of(piece * rows, rows), rows)

    def owner(j):
        return true_chunk(place, j, count) * per + shard // count

    def copy(j):
        return pltpu.make_async_remote_copy(
            src_ref=source.at[j],
            dst_ref=target.at[spot],
            send_sem=outs.at[j],
            recv_sem=ins.at[piece],
            device_id={"fsdp": owner(j)},
            device_id_type=pl.DeviceIdType.MESH,
        )

    def arrival(p):
        return pltpu.make_async_remote_copy(
            src_ref=source.at[0],
            dst_ref=target.at[pl.ds(p * rows, rows)],
            send_sem=outs.at[0],
            recv_sem=ins.at[p],
            device_id={"fsdp": owner(0)},
            device_id_type=pl.DeviceIdType.MESH,
        )

    def local(j):
        return pltpu.make_async_copy(source.at[j], target.at[spot], here.at[0])

    def origin(p):
        return (shard % per) * count + p

    def each(act_remote, act_local):
        for j in range(count):
            pl.when(owner(j) != shard)(lambda j=j: act_remote(copy(j)))
            pl.when(owner(j) == shard)(lambda j=j: act_local(local(j)))

    def greeting(barrier):
        for p in range(count):
            pl.when(origin(p) != shard)(lambda p=p: greet(barrier, {"fsdp": origin(p)}))
        return jnp.where(shard % per == shard // count, count - 1, count)

    def begin():
        each(lambda c: c.start(), lambda c: c.start())

    def finish():
        each(lambda c: c.wait_send(), lambda c: c.wait())
        for p in range(count):
            pl.when(origin(p) != shard)(lambda p=p: arrival(p).wait_recv())

    return greeting, begin, nothing, finish


def own_job(sources, targets, scratch):
    loaded, stored, held = scratch
    place = lax.axis_index("seq")
    count = lax.axis_size("seq")
    part = targets[0].shape[1]
    loads = []
    stores = []
    for c, target in enumerate(targets):
        for k, source in enumerate(sources):
            start = place * (source.shape[0] // count) + c * part
            spot = pl.ds(pl.multiple_of(start, part), part)
            n = c * len(sources) + k
            loads.append(pltpu.make_async_copy(source.at[spot], held.at[n], loaded.at[n]))
            stores.append(pltpu.make_async_copy(held.at[n], target.at[k], stored.at[n]))

    def begin():
        for load in loads:
            load.start()

    def middle():
        for load, store in zip(loads, stores):
            load.wait()
            store.start()

    def finish():
        for store in stores:
            store.wait()

    return no_greeting, begin, middle, finish


MAKERS = {
    "gather": gather_job,
    "scatter": scatter_job,
    "deal": deal_job,
    "swap": swap_job,
    "own": own_job,
}


def job_scratch(job):
    kind, *arrays = job
    if kind == "scatter":
        _, rows, width = arrays[0].shape
        halves = pltpu.VMEM((2, rows // 2, width), BF16)
        return [
            pltpu.SemaphoreType.DMA((6,)),
            pltpu.SemaphoreType.DMA((6,)),
            pltpu.SemaphoreType.DMA((4,)),
            halves,
            halves,
            halves,
            pltpu.VMEM((rows, width), BF16),
            halves,
            pltpu.VMEM((rows, width), F32),
        ]
    if kind == "own":
        count = CHUNKS * len(arrays)
        rows, width = arrays[0].shape
        part = rows // lax.axis_size("seq") // CHUNKS
        return [
            pltpu.SemaphoreType.DMA((count,)),
            pltpu.SemaphoreType.DMA((count,)),
            pltpu.VMEM((count, part, width), BF16),
        ]
    moves = [
        pltpu.SemaphoreType.DMA((4,)),
        pltpu.SemaphoreType.DMA((4,)),
        pltpu.SemaphoreType.DMA((2,)),
    ]
    return moves + [pltpu.VMEM(arrays[0].shape, BF16)] if kind == "gather" else moves


def job_results(job):
    kind, *arrays = job
    shape = arrays[0].shape
    if kind == "gather":
        return [jax.ShapeDtypeStruct((4,) + shape, BF16)]
    if kind == "scatter":
        return [jax.ShapeDtypeStruct(shape[1:], F32)]
    if kind == "deal":
        return [jax.ShapeDtypeStruct((shape[0] // 4,) + shape[1:], BF16)]
    if kind == "swap":
        return [jax.ShapeDtypeStruct((shape[0] * shape[1], shape[2]), BF16)]
    part = shape[0] // lax.axis_size("seq") // CHUNKS
    return [jax.ShapeDtypeStruct((len(arrays), part) + shape[1:], BF16)] * CHUNKS


def plain_job(job):
    kind, *arrays = job
    seqs = lax.axis_size("seq")
    shards = lax.axis_size("fsdp")
    per = shards // seqs
    ends = [(s, h, s * shards + s * per + h) for s in range(seqs) for h in range(per)]
    if kind == "gather":
        return [lax.all_gather(arrays[0], "seq", axis=0)]
    if kind == "scatter":
        return [lax.psum_scatter(arrays[0], "seq", scatter_dimension=0).astype(F32)]
    if kind == "deal":
        rows = arrays[0].shape[0] // seqs
        total = None
        for j in range(seqs):
            moves = [(end, s * shards + h * seqs + j) for s, h, end in ends]
            got = lax.ppermute(arrays[0][j * rows : (j + 1) * rows], ("seq", "fsdp"), moves)
            total = got if total is None else total + got
        return [total]
    if kind == "swap":
        total = None
        for q in range(seqs):
            for p in range(seqs):
                moves = [
                    (s * shards + h * seqs + p, s * shards + q * per + h)
                    for s in range(seqs)
                    for h in range(per)
                ]
                got = lax.ppermute(arrays[0][q], ("seq", "fsdp"), moves)
                rows = got.shape[0]
                got = jnp.pad(got, ((p * rows, (seqs - 1 - p) * rows), (0, 0)))
                total = got if total is None else total + got
        return [total]
    own_rows = arrays[0].shape[0] // seqs
    part = own_rows // CHUNKS
    start = lax.axis_index("seq") * own_rows
    return [
        jnp.stack([lax.dynamic_slice_in_dim(w, start + c * part, part, 0) for w in arrays])
        for c in range(CHUNKS)
    ]


def meet(greetings):
    place = lax.axis_index("seq")
    barrier = pltpu.get_barrier_semaphore()
    for device in (over_one(place), over_two(place)):
        greet(barrier, {"seq": device})
    peers = 2
    for greeting in greetings:
        peers = peers + greeting(barrier)
    pl.semaphore_wait(barrier, peers)


def call(
    body, operands, in_specs, out_shape, out_specs, jobs, number, after=None,
    grid=(), scratch=(), cost=None, name=None, late=(),
):
    plain = lax.axis_size("seq") != 4
    results = [v for job in jobs for v in plain_job(job)] if plain else []
    inside = [] if plain else jobs
    extra = [] if after is None else [after]
    job_shapes = [job_scratch(job) for job in inside]
    job_outs = [job_results(job) for job in inside]
    n_in = len(operands)
    n_out = len(out_shape)

    def kernel(*refs):
        refs = list(refs)

        def take(count):
            taken, refs[:] = refs[:count], refs[count:]
            return taken

        ins = take(n_in)
        take(len(extra))
        sources = [take(len(job) - 1) for job in inside]
        outs = take(n_out)
        targets = [take(len(shapes)) for shapes in job_outs]
        held = take(len(scratch))
        loaded = take(len(late))
        marks = take(1) if late else []
        loads = [
            pltpu.make_async_copy(ins[n], ref, marks[0].at[k])
            for k, (n, ref) in enumerate(zip(late, loaded))
        ]
        for n, ref in zip(late, loaded):
            ins[n] = ref
        phases = [
            MAKERS[job[0]](source, target, take(len(shapes)))
            for job, source, target, shapes in zip(inside, sources, targets, job_shapes)
        ]

        def hook(k):
            if k == 0 and phases:
                meet([phase[0] for phase in phases])
            for phase in phases:
                phase[k + 1]()
            if k == 0:
                for load in loads:
                    load.start()
                for load in loads:
                    load.wait()

        body(hook, ins, outs, held)

    given = {}
    if inside:
        given = {"collective_id": number, "has_side_effects": True}
    arrays = [array for job in inside for array in job[1:]]
    in_specs = [ANY if n in late else spec for n, spec in enumerate(in_specs)]
    late_shapes = [pltpu.VMEM(operands[n].shape, operands[n].dtype) for n in late]
    if late:
        late_shapes.append(pltpu.SemaphoreType.DMA((len(late),)))
    shapes = [shape for shapes in job_outs for shape in shapes]
    made = pl.pallas_call(
        kernel,
        grid=grid,
        out_shape=tuple(out_shape) + tuple(shapes),
        in_specs=list(in_specs) + [ANY] * (len(extra) + len(arrays)),
        out_specs=tuple(out_specs) + (ANY,) * len(shapes),
        scratch_shapes=list(scratch)
        + late_shapes
        + [shape for shapes in job_shapes for shape in shapes],
        compiler_params=pltpu.CompilerParams(vmem_limit_bytes=VMEM_LIMIT, **given),
        cost_estimate=cost,
        name=name,
    )(*operands, *extra, *arrays)
    return list(made[:n_out]), list(made[n_out:]) + results


def transfer(jobs, number, after=None):
    if lax.axis_size("seq") != 4:
        return [v for job in jobs for v in plain_job(job)]

    def body(hook, ins, outs, held):
        for k in range(3):
            hook(k)

    return call(body, [], [], [], [], jobs, number, after, name="transfer")[1]


def partner(v):
    lane = lax.broadcasted_iota(jnp.int32, v.shape, 1)
    return jnp.where(lane % HEAD < HEAD // 2, pltpu.roll(v, 96, 1), pltpu.roll(v, 32, 1))


def head_mean(v, ones):
    high = v.astype(BF16)
    rest = (v - high.astype(F32)).astype(BF16)
    return dot(high, ones) + dot(rest, ones)


def true_chunk(place, c, count):
    if count != 4:
        return c
    low = 1 - place % 2 if c % 2 else place % 2
    high = 1 - place // 2 if c // 2 else place // 2
    return low + 2 * high


def prepare_heads(sizes, place, qkv_ref, qg_ref, kg_ref, cos_ref, sin_ref, ones, q_s, k_s, v_s):
    hq, hkv, _ = sizes
    seqs, rows_in, _ = qkv_ref.shape
    for c in range(seqs):
        j = true_chunk(place, c, seqs)
        rows = slice(c * rows_in, (c + 1) * rows_in)
        cos = cos_ref[rows, :]
        sin = sin_ref[rows, :]
        for p in range((hq + hkv) // 2):
            is_query = p < hq // 2
            x = qkv_ref[j, :, p * 128 : (p + 1) * 128].astype(F32)
            gain = qg_ref[...] * HEAD**-0.5 if is_query else kg_ref[...]
            y = x * lax.rsqrt(head_mean(x * x, ones) + EPSILON) * gain
            y = (y * cos + partner(y) * sin).astype(BF16)
            for t in range(2):
                part = y[:, t * HEAD : (t + 1) * HEAD]
                if is_query:
                    q_s[2 * p + t, rows, :] = part
                else:
                    k_s[2 * p - hq + t, rows, :] = part
        for t in range(hkv):
            start = (hq + hkv + t) * HEAD
            v_s[t, rows, :] = qkv_ref[j, :, start : start + HEAD]


def allowed_keys(block, first, keys, length):
    bound = jnp.minimum(first + lax.broadcasted_iota(jnp.int32, (block, 1), 0), length - 1)
    return lax.broadcasted_iota(jnp.int32, (block, keys), 1) <= bound


def attend_kernel(sizes, hook, ins, outs, held):
    len_ref, normal_ref, weight_ref, qg_ref, kg_ref, cos_ref, sin_ref, ones_ref = ins
    out_ref, lse_ref, qkv_ref = outs
    q_s, k_s, v_s, o_s = held
    hook(0)

    @pl.loop(0, qkv_ref.shape[0])
    def _(j):
        qkv_ref[j] = dot(normal_ref[j], weight_ref[...]).astype(BF16)

    hq, hkv, group = sizes
    seqs, rows_in, _ = qkv_ref.shape
    place = lax.axis_index("seq")
    prepare_heads(
        sizes, place, qkv_ref, qg_ref, kg_ref, cos_ref, sin_ref, ones_ref[...], q_s, k_s, v_s
    )
    for i in range(seqs * rows_in // BLOCK):
        keys = (i + 1) * BLOCK
        rows = slice(i * BLOCK, (i + 1) * BLOCK)
        keep = allowed_keys(BLOCK, i * BLOCK, keys, len_ref[0])

        def one_head(h, _):
            kv = h // group
            scores = dot(q_s[h, rows, :], k_s[kv, :keys, :], NT)
            scores = jnp.where(keep, scores, NEGATIVE)
            highest = jnp.max(scores, axis=1, keepdims=True)
            shifted = jnp.exp(scores - highest)
            total = jnp.sum(shifted, axis=1, keepdims=True)
            mixed = dot(shifted.astype(BF16), v_s[kv, :keys, :]) / total
            o_s[h, rows, :] = mixed.astype(BF16)
            lse_ref[h, rows, :] = highest + jnp.log(total)
            return 0

        lax.fori_loop(0, hq, one_head, 0)
        if i == seqs * rows_in // BLOCK - 2:
            hook(1)
    for c in range(seqs):
        j = true_chunk(place, c, seqs)
        rows = slice(c * rows_in, (c + 1) * rows_in)
        for p in range(hq // 2):
            out_ref[j, :, p * 128 : (p + 1) * 128] = jnp.concatenate(
                [o_s[2 * p, rows, :], o_s[2 * p + 1, rows, :]], axis=1
            )
    hook(2)


def attend_back_kernel(sizes, hook, ins, outs, held):
    (
        len_ref, qkv_ref, res_ref, out_w_ref, qkv_w_ref, lse_ref,
        qg_ref, kg_ref, cos_ref, sin_ref, ones_ref,
    ) = ins
    dqkv_ref, dgain_ref, pull_ref = outs
    q_s, k_s, v_s, cot_s, dq_s, dk_s, dv_s = held
    hook(0)
    hq, hkv, group = sizes
    seqs, rows_in, _ = qkv_ref.shape
    place = lax.axis_index("seq")
    ones = ones_ref[...]
    prepare_heads(sizes, place, qkv_ref, qg_ref, kg_ref, cos_ref, sin_ref, ones, q_s, k_s, v_s)
    for c in range(seqs):
        j = true_chunk(place, c, seqs)
        cots = dot(res_ref[j], out_w_ref[...], NT).astype(BF16)
        for h in range(hq):
            cot_s[h, c * rows_in : (c + 1) * rows_in, :] = cots[:, h * HEAD : (h + 1) * HEAD]
    dk_s[...] = jnp.zeros_like(dk_s)
    dv_s[...] = jnp.zeros_like(dv_s)
    for i in range(seqs * rows_in // BLOCK):
        keys = (i + 1) * BLOCK
        rows = slice(i * BLOCK, (i + 1) * BLOCK)
        keep = allowed_keys(BLOCK, i * BLOCK, keys, len_ref[0])

        def one_head(h, _):
            kv = h // group
            q = q_s[h, rows, :]
            cot = cot_s[h, rows, :]
            k = k_s[kv, :keys, :]
            scores = jnp.where(keep, dot(q, k, NT), NEGATIVE)
            probs = jnp.exp(scores - lse_ref[h, rows, :])
            prob_cot = dot(cot, v_s[kv, :keys, :], NT)
            inner = jnp.sum(probs * prob_cot, axis=1, keepdims=True)
            score_cot = (probs * (prob_cot - inner)).astype(BF16)
            dq_s[h, rows, :] = dot(score_cot, k) * HEAD**-0.5
            dk_s[kv, :keys, :] += dot(score_cot, q, TN)
            dv_s[kv, :keys, :] += dot(probs.astype(BF16), cot, TN)
            return 0

        lax.fori_loop(0, hq, one_head, 0)
        if i == seqs * rows_in // BLOCK - 2:
            hook(1)
    gain_sums = [jnp.zeros((1, 128), F32), jnp.zeros((1, 128), F32)]
    for c in range(seqs):
        j = true_chunk(place, c, seqs)
        rows = slice(c * rows_in, (c + 1) * rows_in)
        cos = cos_ref[rows, :]
        sin = sin_ref[rows, :]
        for p in range((hq + hkv) // 2):
            is_query = p < hq // 2
            x = qkv_ref[j, :, p * 128 : (p + 1) * 128].astype(F32)
            gain = qg_ref[...] if is_query else kg_ref[...]
            source, first = (dq_s, 2 * p) if is_query else (dk_s, 2 * p - hq)
            turned = jnp.concatenate([source[first, rows, :], source[first + 1, rows, :]], axis=1)
            scale = lax.rsqrt(head_mean(x * x, ones) + EPSILON)
            straight = turned * cos + partner(turned * sin)
            unit = x * scale
            which = 0 if is_query else 1
            gain_sums[which] += jnp.sum(straight * unit, axis=0, keepdims=True)
            pulled = gain * straight
            dx = scale * (pulled - unit * head_mean(unit * pulled, ones))
            dqkv_ref[j, :, p * 128 : (p + 1) * 128] = dx.astype(BF16)
        for p in range(hkv // 2):
            start = (hq + hkv) * HEAD + p * 128
            dqkv_ref[j, :, start : start + 128] = jnp.concatenate(
                [dv_s[2 * p, rows, :], dv_s[2 * p + 1, rows, :]], axis=1
            ).astype(BF16)
    dgain_ref[0:1, :] = gain_sums[0]
    dgain_ref[1:2, :] = gain_sums[1]

    @pl.loop(0, seqs)
    def _(j):
        pull_ref[j] = dot(dqkv_ref[j], qkv_w_ref[...], NT).astype(BF16)

    hook(2)


def position_tables(length):
    places = np.arange(length, dtype=np.float32)
    half = HEAD // 2
    freqs = np.float32(ROPE_BASE) ** (-(np.arange(half, dtype=np.float32) * 2.0) / HEAD)
    angles = places[:, None] * freqs.astype(np.float32)[None, :]
    cos = np.cos(angles).astype(np.float32)
    sin = np.sin(angles).astype(np.float32)
    ones = np.kron(np.eye(2), np.ones((HEAD, HEAD)) / HEAD)
    return (
        jnp.asarray(np.concatenate([cos] * 4, axis=1)),
        jnp.asarray(np.concatenate([-sin, sin, -sin, sin], axis=1)),
        jnp.asarray(ones, dtype=BF16),
    )


def attend(sizes, length, normal, weight, gains, tables, jobs, number, after):
    seqs, rows_in, _ = normal.shape
    hq, hkv, _ = sizes
    slot = seqs * rows_in
    return call(
        functools.partial(attend_kernel, sizes),
        [length, normal, weight, *gains, *tables],
        [SMEM] + [VMEM] * 7,
        [
            jax.ShapeDtypeStruct((seqs, rows_in, hq * HEAD), BF16),
            jax.ShapeDtypeStruct((hq, slot, 1), F32),
            jax.ShapeDtypeStruct((seqs, rows_in, weight.shape[1]), BF16),
        ],
        [VMEM, VMEM, VMEM],
        jobs,
        number,
        after,
        scratch=[
            pltpu.VMEM((hq, slot, HEAD), BF16),
            pltpu.VMEM((hkv, slot, HEAD), BF16),
            pltpu.VMEM((hkv, slot, HEAD), BF16),
            pltpu.VMEM((hq, slot, HEAD), BF16),
        ],
        cost=pl.CostEstimate(
            flops=56 * hq * slot * slot * HEAD, bytes_accessed=1 << 23, transcendentals=0
        ),
        name="attend",
        late=(1, 2),
    )


def attend_back(
    sizes, length, qkv, res, out_w, qkv_w, lse, gains, tables, jobs, number, after
):
    seqs, rows_in, width = qkv.shape
    hq, hkv, _ = sizes
    slot = seqs * rows_in
    return call(
        functools.partial(attend_back_kernel, sizes),
        [length, qkv, res, out_w, qkv_w, lse, *gains, *tables],
        [SMEM] + [VMEM] * 10,
        [
            jax.ShapeDtypeStruct((seqs, rows_in, width), BF16),
            jax.ShapeDtypeStruct((2, 128), F32),
            jax.ShapeDtypeStruct(res.shape, BF16),
        ],
        [VMEM, VMEM, VMEM],
        jobs,
        number,
        after,
        scratch=[
            pltpu.VMEM((hq, slot, HEAD), BF16),
            pltpu.VMEM((hkv, slot, HEAD), BF16),
            pltpu.VMEM((hkv, slot, HEAD), BF16),
            pltpu.VMEM((hq, slot, HEAD), BF16),
            pltpu.VMEM((hq, slot, HEAD), F32),
            pltpu.VMEM((hkv, slot, HEAD), F32),
            pltpu.VMEM((hkv, slot, HEAD), F32),
        ],
        cost=pl.CostEstimate(
            flops=88 * hq * slot * slot * HEAD, bytes_accessed=1 << 23, transcendentals=0
        ),
        name="attend_back",
        late=(1, 2, 3, 4, 5),
    )


def hooked(hook, step, steps, work):
    pl.when(step == 0)(lambda: hook(0))
    work(lambda: pl.when(step == (3 * steps) // 5)(lambda: hook(1)))
    pl.when(step == steps - 1)(lambda: hook(2))


def ffn_kernel(steps, hook, ins, outs, held):
    step = pl.program_id(0)
    weights_ref, loaded = held
    loads = [
        pltpu.make_async_copy(ins[2].at[:, k], weights_ref.at[k], loaded.at[k]) for k in range(3)
    ]

    def first(act):
        pl.when(step == 0)(act)

    def work(late):
        for load in loads:
            first(load.start)
        ffn_tile(late, first, loads, *ins[:2], weights_ref, ins[3:], *outs)

    hooked(hook, step, steps, work)


def ffn_tile(late, first, loads, mid_ref, cot_ref, weights_ref, sums, acts_ref, pull_ref):
    model = mid_ref.shape[-1]
    hidden = acts_ref.shape[-1]
    whole = (hidden, model)
    mid = mid_ref[...]
    first(loads[0].wait)
    gate = dot(mid, weights_ref[0].reshape(whole), NT)
    first(loads[1].wait)
    up = dot(mid, weights_ref[1].reshape(whole), NT)
    first(loads[2].wait)
    mids_cot = dot(cot_ref[...], weights_ref[2].reshape(whole), NT)
    late()
    sigmoid = jax.nn.sigmoid(gate)
    active = gate * sigmoid
    gate_cot = (mids_cot * up * sigmoid * (1.0 + gate * (1.0 - sigmoid))).astype(BF16)
    up_cot = (mids_cot * active).astype(BF16)
    acts_ref[0] = gate_cot
    acts_ref[1] = up_cot
    acts_ref[2] = (active * up).astype(BF16)
    pulled = dot(gate_cot, weights_ref[0].reshape(whole)) + dot(
        up_cot, weights_ref[1].reshape(whole)
    )
    for sum_ref in sums:
        pulled = pulled + sum_ref[...]
    pull_ref[...] = pulled.astype(pull_ref.dtype)


def ffn_both(mid, cot, weights, summed, last, jobs, number, after):
    tokens, model = mid.shape
    shards, _, part, _ = weights.shape
    hidden = shards * part
    tile = min(256, tokens)

    row_spec = pl.BlockSpec((tile, model), lambda i: (i, 0))
    extra = () if summed is None else (summed,)
    return call(
        functools.partial(ffn_kernel, tokens // tile),
        [mid, cot, weights, *extra],
        [row_spec, row_spec, ANY] + [row_spec] * len(extra),
        [
            jax.ShapeDtypeStruct((3, tokens, hidden), BF16),
            jax.ShapeDtypeStruct((tokens, model), BF16 if last else F32),
        ],
        [pl.BlockSpec((3, tile, hidden), lambda i: (0, i, 0)), row_spec],
        jobs,
        number,
        after,
        grid=(tokens // tile,),
        scratch=[
            pltpu.VMEM((3, shards, part, model), BF16),
            pltpu.SemaphoreType.DMA((3,)),
        ],
        cost=pl.CostEstimate(
            flops=16 * tokens * model * hidden,
            bytes_accessed=4 * tokens * model + 6 * hidden * model,
            transcendentals=0,
        ),
        name="ffn_both",
    )


def ffn_grad_kernel(slots, tiles, hook, ins, outs, held):
    acts = ins[:slots]
    others = ins[slots:]
    (out_ref,) = outs
    rows_ref, loaded = held
    kind = pl.program_id(0)
    step = kind * tiles + pl.program_id(1)
    loads = [
        pltpu.make_async_copy(other, rows_ref.at[k], loaded.at[k])
        for k, other in enumerate(others)
    ]

    def store(first):
        total = None
        for k, act in enumerate(acts):
            term = dot(act[0], rows_ref[first + k], TN)
            total = term if total is None else total + term
        out_ref[...] = total.astype(BF16).reshape(out_ref.shape)

    def work(late):
        for k, load in enumerate(loads):
            pl.when(step == 0)(load.start)
        for k, load in enumerate(loads):
            pl.when(step == (0 if k < slots else 2 * tiles))(load.wait)
        late()
        pl.when(kind < 2)(lambda: store(0))
        pl.when(kind == 2)(lambda: store(slots))

    hooked(hook, step, 3 * tiles, work)


def ffn_grads(acts, mids, cots, shards, jobs, number, after):
    slots = len(acts)
    _, tokens, hidden = acts[0].shape
    model = mids[0].shape[-1]
    part = hidden // shards
    tile = 256
    per = tile // part
    return call(
        functools.partial(ffn_grad_kernel, slots, hidden // tile),
        [*acts, *mids, *cots],
        [pl.BlockSpec((1, tokens, tile), lambda k, i: (k, 0, i))] * slots
        + [ANY] * (2 * slots),
        [jax.ShapeDtypeStruct((shards, 3, part, model), BF16)],
        [pl.BlockSpec((per, 1, part, model), lambda k, i: (i, k, 0, 0))],
        jobs,
        number,
        after,
        grid=(3, hidden // tile),
        scratch=[
            pltpu.VMEM((2 * slots, tokens, model), BF16),
            pltpu.SemaphoreType.DMA((2 * slots,)),
        ],
        cost=pl.CostEstimate(
            flops=9 * slots * tokens * model * hidden,
            bytes_accessed=4 * slots * tokens * model,
            transcendentals=0,
        ),
        name="ffn_grads",
    )


def ffn_down_kernel(chunks, steps, hook, ins, outs, held):
    acts = ins[:chunks]
    downs = ins[chunks:]
    (out_ref,) = outs

    def work(late):
        late()
        total = None
        for act, down in zip(acts, downs):
            hidden = act.shape[-1]
            term = dot(act[0], down[...].reshape(hidden, down.shape[-1]))
            total = term if total is None else total + term
        out_ref[...] = total.astype(BF16)

    hooked(hook, pl.program_id(0), steps, work)


def ffn_down(acts, weights, jobs, number, after):
    chunks = len(acts)
    _, tokens, hidden = acts[0].shape
    shards, _, part, model = weights[0].shape
    tile = min(256, tokens)
    act_spec = pl.BlockSpec((1, tile, hidden), lambda i: (2, i, 0))
    down_spec = pl.BlockSpec(
        (shards, 1, part, model),
        lambda i: (0, 2, 0, 0),
        pipeline_mode=pl.Buffered(buffer_count=1),
    )
    return call(
        functools.partial(ffn_down_kernel, chunks, tokens // tile),
        [*acts, *weights],
        [act_spec] * chunks + [down_spec] * chunks,
        [jax.ShapeDtypeStruct((tokens, model), BF16)],
        [pl.BlockSpec((tile, model), lambda i: (i, 0))],
        jobs,
        number,
        after,
        grid=(tokens // tile,),
        cost=pl.CostEstimate(
            flops=4 * chunks * tokens * model * hidden,
            bytes_accessed=chunks * hidden * (tokens + model) * 2,
            transcendentals=0,
        ),
        name="ffn_down",
    )


def place_kernel(place_ref, parts_ref, *refs):
    for kind, out_ref in enumerate(refs[-3:]):
        out_ref[0, 0] = parts_ref[0, kind].astype(F32)


def place_parts(place, parts, chunk, held):
    seqs, _, part, model = parts.shape
    out = jax.ShapeDtypeStruct((seqs, CHUNKS, part, model), F32)
    out_spec = pl.BlockSpec(
        (1, 1, part, model), lambda j, at: (jnp.bitwise_xor(at[0], j), chunk, 0, 0)
    )
    return pl.pallas_call(
        place_kernel,
        out_shape=(out,) * 3,
        grid_spec=pltpu.PrefetchScalarGridSpec(
            num_scalar_prefetch=1,
            grid=(seqs,),
            in_specs=[pl.BlockSpec((1, 3, part, model), lambda j, at: (j, 0, 0, 0))]
            + [ANY] * len(held),
            out_specs=(out_spec,) * 3,
        ),
        input_output_aliases={2 + k: k for k in range(len(held))},
        compiler_params=pltpu.CompilerParams(vmem_limit_bytes=VMEM_LIMIT),
        cost_estimate=pl.CostEstimate(
            flops=0, bytes_accessed=18 * seqs * part * model, transcendentals=0
        ),
        name="place_parts",
    )(place, parts, *held)


def place_heads_kernel(
    place_ref, parts_ref, query_w_ref, key_w_ref, value_w_ref,
    query_ref, key_ref, value_ref, rest_ref, met_ref,
):
    edge = query_ref.shape[1]
    width = key_ref.shape[1]
    part = parts_ref[0].astype(F32)
    query_ref[...] = part[:, :edge]
    key_ref[...] = part[:, edge : edge + width]
    value_ref[...] = part[:, edge + width : edge + 2 * width]
    rest = part[:, edge + 2 * width :]
    met = jnp.zeros_like(met_ref)
    for grad_ref, weight_ref in (
        (query_ref, query_w_ref),
        (key_ref, key_w_ref),
        (value_ref, value_w_ref),
    ):
        product = grad_ref[...] * weight_ref[...].astype(F32)
        met = met + jnp.sum(product, axis=1, keepdims=True)

    @pl.when(pl.program_id(0) == 0)
    def _():
        rest_ref[...] = rest
        met_ref[...] = met

    @pl.when(pl.program_id(0) > 0)
    def _():
        rest_ref[...] += rest
        met_ref[...] += met


def place_heads(place, parts, edge, width, weights):
    seqs, rows, total = parts.shape
    rest = total - edge - 2 * width

    def column_spec(size):
        return pl.BlockSpec((rows, size), lambda j, at: (0, jnp.bitwise_xor(at[0], j)))

    return pl.pallas_call(
        place_heads_kernel,
        out_shape=[
            jax.ShapeDtypeStruct((rows, seqs * edge), F32),
            jax.ShapeDtypeStruct((rows, seqs * width), F32),
            jax.ShapeDtypeStruct((rows, seqs * width), F32),
            jax.ShapeDtypeStruct((rows, rest), F32),
            jax.ShapeDtypeStruct((rows, 128), F32),
        ],
        grid_spec=pltpu.PrefetchScalarGridSpec(
            num_scalar_prefetch=1,
            grid=(seqs,),
            in_specs=[
                pl.BlockSpec((1, rows, total), lambda j, at: (j, 0, 0)),
                column_spec(edge),
                column_spec(width),
                column_spec(width),
            ],
            out_specs=[
                column_spec(edge),
                column_spec(width),
                column_spec(width),
                pl.BlockSpec((rows, rest), lambda j, at: (0, 0)),
                pl.BlockSpec((rows, 128), lambda j, at: (0, 0)),
            ],
        ),
        compiler_params=pltpu.CompilerParams(vmem_limit_bytes=VMEM_LIMIT),
        name="place_heads",
    )(place, parts, *weights)


def scale_of(values):
    return lax.rsqrt(jnp.mean(values * values, axis=-1, keepdims=True) + EPSILON)


def normed(values, gain):
    return values * scale_of(values) * gain


def normed_back(values, gain, cot):
    scale = scale_of(values)
    pulled = cot * gain
    mean = jnp.mean(values * pulled, axis=-1, keepdims=True)
    return (
        scale * pulled - values * (scale * scale * scale) * mean,
        jnp.sum(cot * values * scale, axis=0),
    )


def follow(values, earlier):
    return lax.optimization_barrier((values, *earlier))[0]


def own_columns(weight, heads, place):
    width = heads * HEAD
    part = lax.dynamic_slice_in_dim(weight, place * width, width, 1)
    if heads % 2:
        part = jnp.pad(part, ((0, 0), (0, HEAD)))
    return part


def on_device(
    tokens,
    cotangent,
    lengths,
    attn_gain,
    query_weight,
    key_weight,
    value_weight,
    query_gain,
    key_gain,
    out_weight,
    ffn_gain,
    gate_weight,
    up_weight,
    down_weight,
):
    slots, rows, model = tokens.shape
    seqs = lax.axis_size("seq")
    shards = lax.axis_size("fsdp")
    place = lax.axis_index("seq")
    shard = lax.axis_index("fsdp")
    slot_len = rows * seqs
    query_width = query_weight.shape[1]
    kv_width = key_weight.shape[1]
    hq = query_width // seqs // HEAD
    hkv = kv_width // seqs // HEAD
    hkv_held = hkv + hkv % 2
    sizes = (hq, hkv_held, hq // hkv)
    order = (place if seqs == 4 else place * 0).reshape(1)
    tables = position_tables(slot_len)
    gains = (
        jnp.concatenate([query_gain, query_gain]).reshape(1, 2 * HEAD),
        jnp.concatenate([key_gain, key_gain]).reshape(1, 2 * HEAD),
    )

    flat = (slot_len, model)
    chunked = (seqs, rows, model)
    places = place * rows + jnp.arange(rows, dtype=jnp.int32)
    live = (places[None, :] < lengths[:, None]).astype(F32)[..., None]
    inputs = tokens.astype(F32)
    out_cot = cotangent.astype(F32) * live
    out_low = [out_cot[b].astype(BF16) for b in range(slots)]
    normal_in = [normed(inputs[b], attn_gain).astype(BF16) for b in range(slots)]

    qkv_own = jnp.concatenate(
        [
            own_columns(query_weight, hq, place),
            own_columns(key_weight, hkv, place),
            own_columns(value_weight, hkv, place),
        ],
        axis=1,
    )
    qkv_weight = lax.all_gather(qkv_own, "fsdp", axis=0, tiled=True)
    start = [
        ("gather", normal_in[0]),
        ("deal", out_weight),
        ("own", gate_weight, up_weight, down_weight),
    ]
    normal_0, out_own, *ffn_own = transfer(start, 1)
    out_rows = lax.all_gather(out_own, "fsdp", axis=0, tiled=True)
    hidden_own = gate_weight.shape[0] // seqs
    part = hidden_own // CHUNKS
    ffn_weights = [lax.all_gather(own, "fsdp", axis=0) for own in ffn_own]

    def leave(mixed):
        return dot(mixed.reshape(slot_len, -1), out_rows).astype(BF16).reshape(chunked)

    def enter_ffn(b, total):
        res = inputs[b] + total
        return res, normed(res, ffn_gain).astype(BF16)

    def heads(b, jobs, number, after):
        return attend(
            sizes, lengths[b : b + 1], normal_full[b], qkv_weight, gains, tables,
            jobs, number, after,
        )

    normal_full = [None] * slots
    cot_full = [None] * slots
    mid_full = [None] * slots
    normal_full[0] = normal_0
    (mixed_0, lse_0, qkv_0), (normal_full[1],) = heads(
        0, [("gather", normal_in[1])], 2, normal_full[0]
    )
    (mixed_1, lse_1, qkv_1), (total_0,) = heads(1, [("scatter", leave(mixed_0))], 3, mixed_0)
    qkv = [qkv_0, qkv_1]
    log_sums = [lse_0, lse_1]
    attended = [v.reshape(slot_len, hq * HEAD) for v in (mixed_0, mixed_1)]
    res_0, mid_0 = enter_ffn(0, total_0)
    mid_full[0], cot_full[0] = [
        v.reshape(flat)
        for v in transfer([("gather", mid_0), ("gather", out_low[0])], 4, mixed_1)
    ]

    acts = [[None] * slots for _ in range(CHUNKS)]
    pulled = [None] * slots

    def ffn_step(b, c, jobs, number, after):
        (acts[c][b], pulled[b]), results = ffn_both(
            mid_full[b], cot_full[b], ffn_weights[c], pulled[b], c == CHUNKS - 1,
            jobs, number, after,
        )
        return results

    def grad_step(c, jobs, number, after):
        (grads,), results = ffn_grads(
            acts[c], mid_full, cot_full, shards, jobs, number, after
        )
        return grads.reshape(shards, 3 * part, model), results

    def leave_ffn(b, jobs, number, after):
        (out,), results = ffn_down(
            [acts[c][b] for c in range(CHUNKS)], ffn_weights, jobs, number, after
        )
        return out.reshape(chunked), results

    total_1, full = ffn_step(
        0, 0, [("scatter", leave(mixed_1)), ("gather", out_low[1])], 5, mid_full[0]
    )
    cot_full[1] = full.reshape(flat)
    res_1, mid_1 = enter_ffn(1, total_1)
    hidden_res = [res_0, res_1]
    (full,) = ffn_step(0, 1, [("gather", mid_1)], 6, acts[0][0])
    mid_full[1] = full.reshape(flat)
    (mid_total_0,) = ffn_step(1, 0, [("scatter", pulled[0].reshape(chunked))], 7, acts[1][0])

    def pull_mid(b, total):
        pull, gain_part = normed_back(hidden_res[b], ffn_gain, total)
        cot = out_cot[b] + pull
        return cot, cot.astype(BF16), gain_part

    res_cot_0, low_0, ffn_gain_0 = pull_mid(0, mid_total_0)
    grads_0, (res_full_0,) = grad_step(0, [("gather", low_0)], 8, acts[0][1])
    ffn_sums = [lax.psum_scatter(grads_0, "fsdp", scatter_dimension=0)]
    out_0, _ = leave_ffn(0, [], 0, grads_0)
    (out_total_0,) = ffn_step(1, 1, [("scatter", out_0)], 9, out_0)
    grads_1, (mid_total_1,) = grad_step(
        1, [("scatter", pulled[1].reshape(chunked))], 10, acts[1][1]
    )
    ffn_sums.append(
        lax.psum_scatter(grads_1, "fsdp", scatter_dimension=0)
    )
    res_cot_1, low_1, ffn_gain_1 = pull_mid(1, mid_total_1)
    grad_ffn_gain = ffn_gain_0 + ffn_gain_1

    def back(b, full, jobs, number, after):
        return attend_back(
            sizes, lengths[b : b + 1], qkv[b], full, out_rows, qkv_weight, log_sums[b],
            gains, tables, jobs, number, after,
        )

    (dqkv_0, heads_gain_0, pull_0), (res_full_1,) = back(
        0, res_full_0, [("gather", low_1)], 11, grads_1
    )
    res_full = [v.reshape(flat) for v in (res_full_0, res_full_1)]
    out_grads = sum(dot(attended[b], res_full[b], TN) for b in range(slots)).astype(BF16)
    (dqkv_1, heads_gain_1, pull_1), (in_total_0, ffn_parts_0) = back(
        1, res_full_1, [("scatter", pull_0), ("gather", ffn_sums[0])], 12, out_grads
    )
    head_gain = heads_gain_0 + heads_gain_1
    dqkv = [v.reshape(slot_len, -1) for v in (dqkv_0, dqkv_1)]
    held = model // shards
    piece = out_grads.shape[0] // shards
    blocks = held // piece
    out_grads = jnp.swapaxes(out_grads.reshape(shards, piece, blocks, model // blocks), 1, 2)
    head_sums = jnp.pad(
        (head_gain[:, :HEAD] + head_gain[:, HEAD:]).reshape(2, shards, HEAD // shards),
        ((0, 0), (0, 0), (0, held - HEAD // shards)),
    ).reshape(2, model)
    gain_columns = jnp.stack([grad_ffn_gain, head_sums[0], head_sums[1]], axis=1).astype(BF16)
    attn_grads = jnp.concatenate(
        [
            sum(dot(normal_full[b].reshape(flat), dqkv[b], TN) for b in range(slots)).astype(BF16),
            jnp.pad(gain_columns, ((0, 0), (0, 125))),
            out_grads.reshape(model, model // blocks),
        ],
        axis=1,
    )
    attn_sums = lax.psum_scatter(attn_grads, "fsdp", scatter_dimension=0, tiled=True)
    out_1, (in_total_1, ffn_parts_1) = leave_ffn(
        1, [("scatter", pull_1), ("gather", ffn_sums[1])], 13, attn_grads
    )
    (heads_all,) = transfer([("gather", attn_sums)], 14, out_1)
    out_edge = attn_sums.shape[1] - model // blocks
    out_pieces = jnp.swapaxes(
        heads_all[..., out_edge:].reshape(seqs, blocks, piece, model // blocks), 1, 2
    ).reshape(seqs, piece, model)
    grad_out, out_total_1 = transfer([("swap", out_pieces), ("scatter", out_1)], 15, out_1)
    grad_tokens = []
    for b, (in_cot, cot) in enumerate(((in_total_0, res_cot_0), (in_total_1, res_cot_1))):
        pull, _ = normed_back(inputs[b], attn_gain, in_cot)
        grad_tokens.append((cot + pull).astype(BF16))
    output = [
        (live[b] * (hidden_res[b] + total)).astype(BF16)
        for b, total in enumerate((out_total_0, out_total_1))
    ]
    ffn_grad = ()
    for c, parts in enumerate((ffn_parts_0, ffn_parts_1)):
        ffn_grad = place_parts(order, parts.reshape(seqs, 3, part, model), c, ffn_grad)
    ffn_grad = [v.reshape(seqs * hidden_own, model) for v in ffn_grad]

    edge = hq * HEAD
    width = hkv_held * HEAD
    if hkv == hkv_held:
        grad_query, grad_key, grad_value, gain_sums, met = place_heads(
            order, heads_all[..., :out_edge], edge, width, (query_weight, key_weight, value_weight)
        )
        met = met[:, 0]
    else:
        heads_all = jnp.moveaxis(heads_all[..., :out_edge], 0, 1).astype(F32)
        last = edge + width
        grad_query = heads_all[..., :edge].reshape(held, query_width)
        grad_key = heads_all[..., edge : edge + hkv * HEAD].reshape(held, kv_width)
        grad_value = heads_all[..., last : last + hkv * HEAD].reshape(held, kv_width)
        gain_sums = jnp.sum(heads_all[..., last + width :], axis=1)
        met = sum(
            jnp.sum(grad * weight.astype(F32), axis=1)
            for grad, weight in (
                (grad_query, query_weight),
                (grad_key, key_weight),
                (grad_value, value_weight),
            )
        )
    grad_attn_gain = met / lax.dynamic_slice_in_dim(attn_gain, shard * held, held, 0)

    return (
        jnp.stack(output),
        jnp.stack(grad_tokens),
        grad_attn_gain,
        grad_query,
        grad_key,
        grad_value,
        gain_sums[: HEAD // shards, 1],
        gain_sums[: HEAD // shards, 2],
        grad_out.astype(F32),
        gain_sums[:, 0],
        ffn_grad[0],
        ffn_grad[1],
        ffn_grad[2],
    )


def solution(mesh):
    return jax.shard_map(
        on_device,
        mesh=mesh,
        in_specs=(
            P("fsdp", "seq", None),
            P("fsdp", "seq", None),
            P("fsdp"),
            P(),
            P("fsdp", None),
            P("fsdp", None),
            P("fsdp", None),
            P(),
            P(),
            P("fsdp", None),
            P(),
            P("fsdp", None),
            P("fsdp", None),
            P("fsdp", None),
        ),
        out_specs=(
            P("fsdp", "seq", None),
            P("fsdp", "seq", None),
            P("fsdp"),
            P("fsdp", None),
            P("fsdp", None),
            P("fsdp", None),
            P("fsdp"),
            P("fsdp"),
            P("fsdp", None),
            P("fsdp"),
            P("fsdp", None),
            P("fsdp", None),
            P("fsdp", None),
        ),
        check_vma=False,
    )
```

```python
import functools

import jax
import jax.numpy as jnp
import numpy as np
from jax import lax
from jax.experimental import pallas as pl
from jax.experimental.pallas import tpu as pltpu
from jax.sharding import PartitionSpec as P

EPSILON = 1e-05
ROPE_BASE = 1000000.0
NEGATIVE = -1e30
F32 = jnp.float32
BF16 = jnp.bfloat16
NN = (((1,), (0,)), ((), ()))
NT = (((1,), (1,)), ((), ()))
TN = (((0,), (0,)), ((), ()))
SMEM = pl.BlockSpec(memory_space=pltpu.SMEM)
VMEM = pl.BlockSpec(memory_space=pltpu.VMEM)
VMEM_LIMIT = 58 << 20
HEAD = 64
BLOCK = 256
CHUNKS = 2
ANY = pl.BlockSpec(memory_space=pl.ANY)


def dot(a, b, dims=NN):
    return lax.dot_general(a, b, dims, preferred_element_type=F32)


def over_one(place):
    return place + 1 - 2 * (place % 2)


def over_two(place):
    return (place + 2) % 4


def send(source, target, device, out_sem, in_sem):
    return pltpu.make_async_remote_copy(
        src_ref=source,
        dst_ref=target,
        send_sem=out_sem,
        recv_sem=in_sem,
        device_id={"seq": device},
        device_id_type=pl.DeviceIdType.MESH,
    )


def gather_job(sources, targets, scratch):
    (source,) = sources
    (target,) = targets
    outs, ins, here, held = scratch
    place = lax.axis_index("seq")
    one, two = over_one(place), over_two(place)
    half = source.shape[0] // 2
    load = pltpu.make_async_copy(source, held, here.at[0])
    store = pltpu.make_async_copy(held, target.at[0], here.at[1])
    first = send(source, target.at[1], one, outs.at[0], ins.at[0])
    second = send(source, target.at[2], two, outs.at[1], ins.at[1])
    top = pl.ds(0, half)
    low = pl.ds(half, half)
    third = send(target.at[2, top], target.at[3, top], one, outs.at[2], ins.at[2])
    fourth = send(target.at[1, low], target.at[3, low], two, outs.at[3], ins.at[3])

    def begin():
        first.start()
        second.start()
        load.start()

    def middle():
        load.wait()
        store.start()
        second.wait_recv()
        third.start()
        first.wait_recv()
        fourth.start()

    def finish():
        third.wait_recv()
        fourth.wait_recv()
        for copy in (first, second, third, fourth):
            copy.wait_send()
        store.wait()

    return no_greeting, begin, middle, finish


def scatter_job(sources, targets, scratch):
    (parts,) = sources
    (total,) = targets
    outs, ins, here, got_one, got_two, kept, own, last, summed = scratch
    place = lax.axis_index("seq")
    one, two = over_one(place), over_two(place)
    half = parts.shape[1] // 2
    top = pl.ds(0, half)
    low = pl.ds(half, half)
    sends = [
        send(parts.at[3, top], got_one.at[0], one, outs.at[0], ins.at[0]),
        send(parts.at[3, low], got_two.at[0], two, outs.at[1], ins.at[1]),
        send(parts.at[1, top], got_one.at[1], one, outs.at[2], ins.at[2]),
        send(parts.at[2, low], got_two.at[1], two, outs.at[3], ins.at[3]),
        send(kept.at[0], last.at[0], two, outs.at[4], ins.at[4]),
        send(kept.at[1], last.at[1], one, outs.at[5], ins.at[5]),
    ]
    loads = [
        pltpu.make_async_copy(parts.at[2, top], kept.at[0], here.at[0]),
        pltpu.make_async_copy(parts.at[1, low], kept.at[1], here.at[1]),
        pltpu.make_async_copy(parts.at[0], own, here.at[2]),
    ]
    store = pltpu.make_async_copy(summed, total, here.at[3])

    def begin():
        for copy in sends[:4]:
            copy.start()
        for copy in loads:
            copy.start()

    def middle():
        for k, got in enumerate((got_one, got_two)):
            loads[k].wait()
            sends[k].wait_recv()
            kept[k] = (kept[k].astype(F32) + got[0].astype(F32)).astype(BF16)
            sends[4 + k].start()

    def finish():
        loads[2].wait()
        for k, got in enumerate((got_one, got_two)):
            sends[2 + k].wait_recv()
            sends[4 + k].wait_recv()
            rows = slice(k * half, (k + 1) * half)
            summed[rows, :] = (
                own[rows, :].astype(F32) + got[1].astype(F32) + last[k].astype(F32)
            )
        store.start()
        for copy in sends:
            copy.wait_send()
        store.wait()

    return no_greeting, begin, middle, finish


def no_greeting(barrier):
    return 0


def nothing():
    pass


def greet(barrier, device):
    pl.semaphore_signal(
        barrier, inc=1, device_id=device, device_id_type=pl.DeviceIdType.MESH
    )


def deal_job(sources, targets, scratch):
    (source,) = sources
    (target,) = targets
    outs, ins, here = scratch
    rows = target.shape[0]
    count = source.shape[0] // rows
    place = lax.axis_index("seq")
    shard = lax.axis_index("fsdp")
    per = lax.axis_size("fsdp") // count
    part = shard % per
    is_source = shard // per == place
    to_self = jnp.logical_and(is_source, shard // count == part)
    origin = place * per + shard // count

    def copy(j):
        return pltpu.make_async_remote_copy(
            src_ref=source.at[pl.ds(j * rows, rows)],
            dst_ref=target,
            send_sem=outs.at[j],
            recv_sem=ins.at[0],
            device_id={"fsdp": part * count + j},
            device_id_type=pl.DeviceIdType.MESH,
        )

    def local(j):
        return pltpu.make_async_copy(source.at[pl.ds(j * rows, rows)], target, here.at[0])

    def greeting(barrier):
        pl.when(origin != shard)(lambda: greet(barrier, {"fsdp": origin}))
        return jnp.where(is_source, count, 0) - jnp.where(to_self, 1, 0)

    def each(act_remote, act_local):
        for j in range(count):
            mine = part * count + j == shard
            pl.when(jnp.logical_and(is_source, mine))(lambda j=j: act_local(local(j)))
            pl.when(jnp.logical_and(is_source, jnp.logical_not(mine)))(
                lambda j=j: act_remote(copy(j))
            )

    def begin():
        each(lambda c: c.start(), lambda c: c.start())

    def finish():
        each(lambda c: c.wait_send(), lambda c: c.wait())
        pl.when(origin != shard)(lambda: copy(0).wait_recv())

    return greeting, begin, nothing, finish


def spread_job(sources, targets, scratch):
    (source,) = sources
    gathered, target = targets
    *first, z_outs, z_ins, z_here = scratch
    _, begin_gather, middle_gather, finish_gather = gather_job(sources, [gathered], first)
    count = gathered.shape[0]
    place = lax.axis_index("seq")
    shard = lax.axis_index("fsdp")
    per = lax.axis_size("fsdp") // count
    piece = shard % count

    def owner(j):
        return true_chunk(place, j, count) * per + shard // count

    def chunk(j):
        return gathered.at[j] if j else source

    def copy(j):
        return pltpu.make_async_remote_copy(
            src_ref=chunk(j),
            dst_ref=target.at[piece],
            send_sem=z_outs.at[j],
            recv_sem=z_ins.at[piece],
            device_id={"fsdp": owner(j)},
            device_id_type=pl.DeviceIdType.MESH,
        )

    def arrival(p):
        return pltpu.make_async_remote_copy(
            src_ref=source,
            dst_ref=target.at[p],
            send_sem=z_outs.at[0],
            recv_sem=z_ins.at[p],
            device_id={"fsdp": owner(0)},
            device_id_type=pl.DeviceIdType.MESH,
        )

    def local(j):
        return pltpu.make_async_copy(chunk(j), target.at[piece], z_here.at[0])

    def origin(p):
        return (shard % per) * count + p

    def start(j):
        pl.when(owner(j) != shard)(lambda: copy(j).start())
        pl.when(owner(j) == shard)(lambda: local(j).start())

    def greeting(barrier):
        for p in range(count):
            pl.when(origin(p) != shard)(lambda p=p: greet(barrier, {"fsdp": origin(p)}))
        return jnp.where(shard % per == shard // count, count - 1, count)

    def begin():
        begin_gather()
        start(0)

    def middle():
        middle_gather()
        start(1)
        start(2)

    def finish():
        finish_gather()
        start(3)
        for j in range(count):
            pl.when(owner(j) != shard)(lambda j=j: copy(j).wait_send())
            pl.when(owner(j) == shard)(lambda j=j: local(j).wait())
        for p in range(count):
            pl.when(origin(p) != shard)(lambda p=p: arrival(p).wait_recv())

    return greeting, begin, middle, finish


def own_job(sources, targets, scratch):
    loaded, stored, held = scratch
    place = lax.axis_index("seq")
    count = lax.axis_size("seq")
    part = targets[0].shape[1]
    loads = []
    stores = []
    for c, target in enumerate(targets):
        for k, source in enumerate(sources):
            start = place * (source.shape[0] // count) + c * part
            spot = pl.ds(pl.multiple_of(start, part), part)
            n = c * len(sources) + k
            loads.append(pltpu.make_async_copy(source.at[spot], held.at[n], loaded.at[n]))
            stores.append(pltpu.make_async_copy(held.at[n], target.at[k], stored.at[n]))

    def begin():
        for load in loads:
            load.start()

    def middle():
        for load, store in zip(loads, stores):
            load.wait()
            store.start()

    def finish():
        for store in stores:
            store.wait()

    return no_greeting, begin, middle, finish


MAKERS = {
    "gather": gather_job,
    "scatter": scatter_job,
    "deal": deal_job,
    "spread": spread_job,
    "own": own_job,
}


def job_scratch(job):
    kind, *arrays = job
    if kind == "scatter":
        _, rows, width = arrays[0].shape
        halves = pltpu.VMEM((2, rows // 2, width), BF16)
        return [
            pltpu.SemaphoreType.DMA((6,)),
            pltpu.SemaphoreType.DMA((6,)),
            pltpu.SemaphoreType.DMA((4,)),
            halves,
            halves,
            halves,
            pltpu.VMEM((rows, width), BF16),
            halves,
            pltpu.VMEM((rows, width), F32),
        ]
    if kind == "own":
        count = CHUNKS * len(arrays)
        rows, width = arrays[0].shape
        part = rows // lax.axis_size("seq") // CHUNKS
        return [
            pltpu.SemaphoreType.DMA((count,)),
            pltpu.SemaphoreType.DMA((count,)),
            pltpu.VMEM((count, part, width), BF16),
        ]
    moves = [
        pltpu.SemaphoreType.DMA((4,)),
        pltpu.SemaphoreType.DMA((4,)),
        pltpu.SemaphoreType.DMA((2,)),
    ]
    if kind == "deal":
        return moves
    moves.append(pltpu.VMEM(arrays[0].shape, BF16))
    if kind == "spread":
        moves += [
            pltpu.SemaphoreType.DMA((4,)),
            pltpu.SemaphoreType.DMA((4,)),
            pltpu.SemaphoreType.DMA((1,)),
        ]
    return moves


def job_results(job):
    kind, *arrays = job
    shape = arrays[0].shape
    if kind == "gather":
        return [jax.ShapeDtypeStruct((4,) + shape, BF16)]
    if kind == "scatter":
        return [jax.ShapeDtypeStruct(shape[1:], F32)]
    if kind == "deal":
        return [jax.ShapeDtypeStruct((shape[0] // 4,) + shape[1:], BF16)]
    if kind == "spread":
        return [jax.ShapeDtypeStruct((4,) + shape, BF16)] * 2
    part = shape[0] // lax.axis_size("seq") // CHUNKS
    return [jax.ShapeDtypeStruct((len(arrays), part) + shape[1:], BF16)] * CHUNKS


def plain_job(job):
    kind, *arrays = job
    seqs = lax.axis_size("seq")
    shards = lax.axis_size("fsdp")
    per = shards // seqs
    ends = [(s, h, s * shards + s * per + h) for s in range(seqs) for h in range(per)]
    if kind == "gather":
        return [lax.all_gather(arrays[0], "seq", axis=0)]
    if kind == "scatter":
        return [lax.psum_scatter(arrays[0], "seq", scatter_dimension=0).astype(F32)]
    if kind == "deal":
        rows = arrays[0].shape[0] // seqs
        total = None
        for j in range(seqs):
            moves = [(end, s * shards + h * seqs + j) for s, h, end in ends]
            got = lax.ppermute(arrays[0][j * rows : (j + 1) * rows], ("seq", "fsdp"), moves)
            total = got if total is None else total + got
        return [total]
    if kind == "spread":
        gathered = lax.all_gather(arrays[0], "seq", axis=0)
        pieces = []
        for p in range(seqs):
            total = None
            for q in range(seqs):
                moves = [
                    (s * shards + h * seqs + p, s * shards + q * per + h)
                    for s in range(seqs)
                    for h in range(per)
                ]
                got = lax.ppermute(gathered[q], ("seq", "fsdp"), moves)
                total = got if total is None else total + got
            pieces.append(total)
        return [gathered, jnp.stack(pieces)]
    own_rows = arrays[0].shape[0] // seqs
    part = own_rows // CHUNKS
    start = lax.axis_index("seq") * own_rows
    return [
        jnp.stack([lax.dynamic_slice_in_dim(w, start + c * part, part, 0) for w in arrays])
        for c in range(CHUNKS)
    ]


def meet(greetings):
    place = lax.axis_index("seq")
    barrier = pltpu.get_barrier_semaphore()
    for device in (over_one(place), over_two(place)):
        greet(barrier, {"seq": device})
    peers = 2
    for greeting in greetings:
        peers = peers + greeting(barrier)
    pl.semaphore_wait(barrier, peers)


def call(
    body, operands, in_specs, out_shape, out_specs, jobs, number, after=None,
    grid=(), scratch=(), cost=None, name=None, late=(),
):
    plain = lax.axis_size("seq") != 4
    results = [v for job in jobs for v in plain_job(job)] if plain else []
    inside = [] if plain else jobs
    extra = [] if after is None else [after]
    job_shapes = [job_scratch(job) for job in inside]
    job_outs = [job_results(job) for job in inside]
    n_in = len(operands)
    n_out = len(out_shape)

    def kernel(*refs):
        refs = list(refs)

        def take(count):
            taken, refs[:] = refs[:count], refs[count:]
            return taken

        ins = take(n_in)
        take(len(extra))
        sources = [take(len(job) - 1) for job in inside]
        outs = take(n_out)
        targets = [take(len(shapes)) for shapes in job_outs]
        held = take(len(scratch))
        loaded = take(len(late))
        marks = take(1) if late else []
        loads = [
            pltpu.make_async_copy(ins[n], ref, marks[0].at[k])
            for k, (n, ref) in enumerate(zip(late, loaded))
        ]
        for n, ref in zip(late, loaded):
            ins[n] = ref
        phases = [
            MAKERS[job[0]](source, target, take(len(shapes)))
            for job, source, target, shapes in zip(inside, sources, targets, job_shapes)
        ]

        def hook(k):
            if k == 0 and phases:
                meet([phase[0] for phase in phases])
            for phase in phases:
                phase[k + 1]()
            if k == 0:
                for load in loads:
                    load.start()
                for load in loads:
                    load.wait()

        body(hook, ins, outs, held)

    given = {}
    if inside:
        given = {"collective_id": number, "has_side_effects": True}
    arrays = [array for job in inside for array in job[1:]]
    in_specs = [ANY if n in late else spec for n, spec in enumerate(in_specs)]
    late_shapes = [pltpu.VMEM(operands[n].shape, operands[n].dtype) for n in late]
    if late:
        late_shapes.append(pltpu.SemaphoreType.DMA((len(late),)))
    shapes = [shape for shapes in job_outs for shape in shapes]
    made = pl.pallas_call(
        kernel,
        grid=grid,
        out_shape=tuple(out_shape) + tuple(shapes),
        in_specs=list(in_specs) + [ANY] * (len(extra) + len(arrays)),
        out_specs=tuple(out_specs) + (ANY,) * len(shapes),
        scratch_shapes=list(scratch)
        + late_shapes
        + [shape for shapes in job_shapes for shape in shapes],
        compiler_params=pltpu.CompilerParams(vmem_limit_bytes=VMEM_LIMIT, **given),
        cost_estimate=cost,
        name=name,
    )(*operands, *extra, *arrays)
    return list(made[:n_out]), list(made[n_out:]) + results


def transfer(jobs, number, after=None):
    if lax.axis_size("seq") != 4:
        return [v for job in jobs for v in plain_job(job)]

    def body(hook, ins, outs, held):
        for k in range(3):
            hook(k)

    return call(body, [], [], [], [], jobs, number, after, name="transfer")[1]


def partner(v):
    lane = lax.broadcasted_iota(jnp.int32, v.shape, 1)
    return jnp.where(lane % HEAD < HEAD // 2, pltpu.roll(v, 96, 1), pltpu.roll(v, 32, 1))


def head_mean(v, ones):
    high = v.astype(BF16)
    rest = (v - high.astype(F32)).astype(BF16)
    return dot(high, ones) + dot(rest, ones)


def true_chunk(place, c, count):
    if count != 4:
        return c
    low = 1 - place % 2 if c % 2 else place % 2
    high = 1 - place // 2 if c // 2 else place // 2
    return low + 2 * high


def prepare_heads(sizes, place, qkv_ref, qg_ref, kg_ref, cos_ref, sin_ref, ones, q_s, k_s, v_s):
    hq, hkv, _ = sizes
    seqs, rows_in, _ = qkv_ref.shape
    for c in range(seqs):
        j = true_chunk(place, c, seqs)
        rows = slice(c * rows_in, (c + 1) * rows_in)
        cos = cos_ref[rows, :]
        sin = sin_ref[rows, :]
        for p in range((hq + hkv) // 2):
            is_query = p < hq // 2
            x = qkv_ref[j, :, p * 128 : (p + 1) * 128].astype(F32)
            gain = qg_ref[...] * HEAD**-0.5 if is_query else kg_ref[...]
            y = x * lax.rsqrt(head_mean(x * x, ones) + EPSILON) * gain
            y = (y * cos + partner(y) * sin).astype(BF16)
            for t in range(2):
                part = y[:, t * HEAD : (t + 1) * HEAD]
                if is_query:
                    q_s[2 * p + t, rows, :] = part
                else:
                    k_s[2 * p - hq + t, rows, :] = part
        for t in range(hkv):
            start = (hq + hkv + t) * HEAD
            v_s[t, rows, :] = qkv_ref[j, :, start : start + HEAD]


def allowed_keys(block, first, keys, length):
    bound = jnp.minimum(first + lax.broadcasted_iota(jnp.int32, (block, 1), 0), length - 1)
    return lax.broadcasted_iota(jnp.int32, (block, keys), 1) <= bound


def attend_kernel(sizes, hook, ins, outs, held):
    len_ref, normal_ref, weight_ref, qg_ref, kg_ref, cos_ref, sin_ref, ones_ref = ins
    out_ref, lse_ref, qkv_ref = outs
    q_s, k_s, v_s, o_s = held
    hook(0)

    @pl.loop(0, qkv_ref.shape[0])
    def _(j):
        qkv_ref[j] = dot(normal_ref[j], weight_ref[...]).astype(BF16)

    hq, hkv, group = sizes
    seqs, rows_in, _ = qkv_ref.shape
    place = lax.axis_index("seq")
    prepare_heads(
        sizes, place, qkv_ref, qg_ref, kg_ref, cos_ref, sin_ref, ones_ref[...], q_s, k_s, v_s
    )
    for i in range(seqs * rows_in // BLOCK):
        keys = (i + 1) * BLOCK
        rows = slice(i * BLOCK, (i + 1) * BLOCK)
        keep = allowed_keys(BLOCK, i * BLOCK, keys, len_ref[0])

        def one_head(h, _):
            kv = h // group
            scores = dot(q_s[h, rows, :], k_s[kv, :keys, :], NT)
            scores = jnp.where(keep, scores, NEGATIVE)
            highest = jnp.max(scores, axis=1, keepdims=True)
            shifted = jnp.exp(scores - highest)
            total = jnp.sum(shifted, axis=1, keepdims=True)
            mixed = dot(shifted.astype(BF16), v_s[kv, :keys, :]) / total
            o_s[h, rows, :] = mixed.astype(BF16)
            lse_ref[h, rows, :] = highest + jnp.log(total)
            return 0

        lax.fori_loop(0, hq, one_head, 0, unroll=min(4, hq))
        if i == seqs * rows_in // BLOCK - 2:
            hook(1)
    for c in range(seqs):
        j = true_chunk(place, c, seqs)
        rows = slice(c * rows_in, (c + 1) * rows_in)
        for p in range(hq // 2):
            out_ref[j, :, p * 128 : (p + 1) * 128] = jnp.concatenate(
                [o_s[2 * p, rows, :], o_s[2 * p + 1, rows, :]], axis=1
            )
    hook(2)


def attend_back_kernel(sizes, hook, ins, outs, held):
    (
        len_ref, qkv_ref, res_ref, out_w_ref, qkv_w_ref, lse_ref,
        qg_ref, kg_ref, cos_ref, sin_ref, ones_ref,
    ) = ins
    dqkv_ref, dgain_ref, pull_ref = outs
    q_s, k_s, v_s, cot_s, dq_s, dk_s, dv_s = held
    hook(0)
    hq, hkv, group = sizes
    seqs, rows_in, _ = qkv_ref.shape
    place = lax.axis_index("seq")
    ones = ones_ref[...]
    prepare_heads(sizes, place, qkv_ref, qg_ref, kg_ref, cos_ref, sin_ref, ones, q_s, k_s, v_s)
    for c in range(seqs):
        j = true_chunk(place, c, seqs)
        cots = dot(res_ref[j], out_w_ref[...], NT).astype(BF16)
        for h in range(hq):
            cot_s[h, c * rows_in : (c + 1) * rows_in, :] = cots[:, h * HEAD : (h + 1) * HEAD]
    dk_s[...] = jnp.zeros_like(dk_s)
    dv_s[...] = jnp.zeros_like(dv_s)
    for i in range(seqs * rows_in // BLOCK):
        keys = (i + 1) * BLOCK
        rows = slice(i * BLOCK, (i + 1) * BLOCK)
        keep = allowed_keys(BLOCK, i * BLOCK, keys, len_ref[0])

        def one_head(h, _):
            kv = h // group
            q = q_s[h, rows, :]
            cot = cot_s[h, rows, :]
            k = k_s[kv, :keys, :]
            scores = jnp.where(keep, dot(q, k, NT), NEGATIVE)
            probs = jnp.exp(scores - lse_ref[h, rows, :])
            prob_cot = dot(cot, v_s[kv, :keys, :], NT)
            inner = jnp.sum(probs * prob_cot, axis=1, keepdims=True)
            score_cot = (probs * (prob_cot - inner)).astype(BF16)
            dq_s[h, rows, :] = dot(score_cot, k) * HEAD**-0.5
            dk_s[kv, :keys, :] += dot(score_cot, q, TN)
            dv_s[kv, :keys, :] += dot(probs.astype(BF16), cot, TN)
            return 0

        lax.fori_loop(0, hq, one_head, 0, unroll=min(4, hq))
        if i == seqs * rows_in // BLOCK - 2:
            hook(1)
    gain_sums = [jnp.zeros((1, 128), F32), jnp.zeros((1, 128), F32)]
    for c in range(seqs):
        j = true_chunk(place, c, seqs)
        rows = slice(c * rows_in, (c + 1) * rows_in)
        cos = cos_ref[rows, :]
        sin = sin_ref[rows, :]
        for p in range((hq + hkv) // 2):
            is_query = p < hq // 2
            x = qkv_ref[j, :, p * 128 : (p + 1) * 128].astype(F32)
            gain = qg_ref[...] if is_query else kg_ref[...]
            source, first = (dq_s, 2 * p) if is_query else (dk_s, 2 * p - hq)
            turned = jnp.concatenate([source[first, rows, :], source[first + 1, rows, :]], axis=1)
            scale = lax.rsqrt(head_mean(x * x, ones) + EPSILON)
            straight = turned * cos + partner(turned * sin)
            unit = x * scale
            which = 0 if is_query else 1
            gain_sums[which] += jnp.sum(straight * unit, axis=0, keepdims=True)
            pulled = gain * straight
            dx = scale * (pulled - unit * head_mean(unit * pulled, ones))
            dqkv_ref[j, :, p * 128 : (p + 1) * 128] = dx.astype(BF16)
        for p in range(hkv // 2):
            start = (hq + hkv) * HEAD + p * 128
            dqkv_ref[j, :, start : start + 128] = jnp.concatenate(
                [dv_s[2 * p, rows, :], dv_s[2 * p + 1, rows, :]], axis=1
            ).astype(BF16)
    dgain_ref[0:1, :] = gain_sums[0]
    dgain_ref[1:2, :] = gain_sums[1]

    @pl.loop(0, seqs)
    def _(j):
        pull_ref[j] = dot(dqkv_ref[j], qkv_w_ref[...], NT).astype(BF16)

    hook(2)


def position_tables(length):
    places = np.arange(length, dtype=np.float32)
    half = HEAD // 2
    freqs = np.float32(ROPE_BASE) ** (-(np.arange(half, dtype=np.float32) * 2.0) / HEAD)
    angles = places[:, None] * freqs.astype(np.float32)[None, :]
    cos = np.cos(angles).astype(np.float32)
    sin = np.sin(angles).astype(np.float32)
    ones = np.kron(np.eye(2), np.ones((HEAD, HEAD)) / HEAD)
    return (
        jnp.asarray(np.concatenate([cos] * 4, axis=1)),
        jnp.asarray(np.concatenate([-sin, sin, -sin, sin], axis=1)),
        jnp.asarray(ones, dtype=BF16),
    )


def attend(sizes, length, normal, weight, gains, tables, jobs, number, after):
    seqs, rows_in, _ = normal.shape
    hq, hkv, _ = sizes
    slot = seqs * rows_in
    return call(
        functools.partial(attend_kernel, sizes),
        [length, normal, weight, *gains, *tables],
        [SMEM] + [VMEM] * 7,
        [
            jax.ShapeDtypeStruct((seqs, rows_in, hq * HEAD), BF16),
            jax.ShapeDtypeStruct((hq, slot, 1), F32),
            jax.ShapeDtypeStruct((seqs, rows_in, weight.shape[1]), BF16),
        ],
        [VMEM, VMEM, VMEM],
        jobs,
        number,
        after,
        scratch=[
            pltpu.VMEM((hq, slot, HEAD), BF16),
            pltpu.VMEM((hkv, slot, HEAD), BF16),
            pltpu.VMEM((hkv, slot, HEAD), BF16),
            pltpu.VMEM((hq, slot, HEAD), BF16),
        ],
        cost=pl.CostEstimate(
            flops=56 * hq * slot * slot * HEAD, bytes_accessed=1 << 23, transcendentals=0
        ),
        name="attend",
        late=(1, 2),
    )


def attend_back(
    sizes, length, qkv, res, out_w, qkv_w, lse, gains, tables, jobs, number, after
):
    seqs, rows_in, width = qkv.shape
    hq, hkv, _ = sizes
    slot = seqs * rows_in
    return call(
        functools.partial(attend_back_kernel, sizes),
        [length, qkv, res, out_w, qkv_w, lse, *gains, *tables],
        [SMEM] + [VMEM] * 10,
        [
            jax.ShapeDtypeStruct((seqs, rows_in, width), BF16),
            jax.ShapeDtypeStruct((2, 128), F32),
            jax.ShapeDtypeStruct(res.shape, BF16),
        ],
        [VMEM, VMEM, VMEM],
        jobs,
        number,
        after,
        scratch=[
            pltpu.VMEM((hq, slot, HEAD), BF16),
            pltpu.VMEM((hkv, slot, HEAD), BF16),
            pltpu.VMEM((hkv, slot, HEAD), BF16),
            pltpu.VMEM((hq, slot, HEAD), BF16),
            pltpu.VMEM((hq, slot, HEAD), F32),
            pltpu.VMEM((hkv, slot, HEAD), F32),
            pltpu.VMEM((hkv, slot, HEAD), F32),
        ],
        cost=pl.CostEstimate(
            flops=88 * hq * slot * slot * HEAD, bytes_accessed=1 << 23, transcendentals=0
        ),
        name="attend_back",
        late=(1, 2, 3, 4, 5),
    )


def hooked(hook, step, steps, work):
    pl.when(step == 0)(lambda: hook(0))
    work(lambda: pl.when(step == (3 * steps) // 5)(lambda: hook(1)))
    pl.when(step == steps - 1)(lambda: hook(2))


def ffn_kernel(steps, hook, ins, outs, held):
    step = pl.program_id(0)
    weights_ref, loaded = held
    loads = [
        pltpu.make_async_copy(ins[2].at[:, k], weights_ref.at[k], loaded.at[k]) for k in range(3)
    ]

    def first(act):
        pl.when(step == 0)(act)

    def work(late):
        for load in loads:
            first(load.start)
        ffn_tile(late, first, loads, *ins[:2], weights_ref, ins[3:], *outs)

    hooked(hook, step, steps, work)


def ffn_tile(late, first, loads, mid_ref, cot_ref, weights_ref, sums, acts_ref, pull_ref):
    model = mid_ref.shape[-1]
    hidden = acts_ref.shape[-1]
    whole = (hidden, model)
    mid = mid_ref[...]
    first(loads[0].wait)
    gate = dot(mid, weights_ref[0].reshape(whole), NT)
    first(loads[1].wait)
    up = dot(mid, weights_ref[1].reshape(whole), NT)
    first(loads[2].wait)
    mids_cot = dot(cot_ref[...], weights_ref[2].reshape(whole), NT)
    late()
    sigmoid = jax.nn.sigmoid(gate)
    active = gate * sigmoid
    gate_cot = (mids_cot * up * sigmoid * (1.0 + gate * (1.0 - sigmoid))).astype(BF16)
    up_cot = (mids_cot * active).astype(BF16)
    acts_ref[0] = gate_cot
    acts_ref[1] = up_cot
    acts_ref[2] = (active * up).astype(BF16)
    pulled = dot(gate_cot, weights_ref[0].reshape(whole)) + dot(
        up_cot, weights_ref[1].reshape(whole)
    )
    for sum_ref in sums:
        pulled = pulled + sum_ref[...]
    pull_ref[...] = pulled.astype(pull_ref.dtype)


def ffn_both(mid, cot, weights, summed, last, jobs, number, after):
    tokens, model = mid.shape
    shards, _, part, _ = weights.shape
    hidden = shards * part
    tile = min(256, tokens)

    row_spec = pl.BlockSpec((tile, model), lambda i: (i, 0))
    extra = () if summed is None else (summed,)
    return call(
        functools.partial(ffn_kernel, tokens // tile),
        [mid, cot, weights, *extra],
        [row_spec, row_spec, ANY] + [row_spec] * len(extra),
        [
            jax.ShapeDtypeStruct((3, tokens, hidden), BF16),
            jax.ShapeDtypeStruct((tokens, model), BF16 if last else F32),
        ],
        [pl.BlockSpec((3, tile, hidden), lambda i: (0, i, 0)), row_spec],
        jobs,
        number,
        after,
        grid=(tokens // tile,),
        scratch=[
            pltpu.VMEM((3, shards, part, model), BF16),
            pltpu.SemaphoreType.DMA((3,)),
        ],
        cost=pl.CostEstimate(
            flops=16 * tokens * model * hidden,
            bytes_accessed=4 * tokens * model + 6 * hidden * model,
            transcendentals=0,
        ),
        name="ffn_both",
    )


def ffn_grad_kernel(slots, tiles, hook, ins, outs, held):
    acts = ins[:slots]
    others = ins[slots:]
    (out_ref,) = outs
    rows_ref, loaded = held
    kind = pl.program_id(0)
    step = kind * tiles + pl.program_id(1)
    loads = [
        pltpu.make_async_copy(other, rows_ref.at[k], loaded.at[k])
        for k, other in enumerate(others)
    ]

    def store(first):
        total = None
        for k, act in enumerate(acts):
            term = dot(act[0], rows_ref[first + k], TN)
            total = term if total is None else total + term
        out_ref[...] = total.astype(BF16).reshape(out_ref.shape)

    def work(late):
        for k, load in enumerate(loads):
            pl.when(step == 0)(load.start)
        for k, load in enumerate(loads):
            pl.when(step == (0 if k < slots else 2 * tiles))(load.wait)
        late()
        pl.when(kind < 2)(lambda: store(0))
        pl.when(kind == 2)(lambda: store(slots))

    hooked(hook, step, 3 * tiles, work)


def ffn_grads(acts, mids, cots, shards, jobs, number, after):
    slots = len(acts)
    _, tokens, hidden = acts[0].shape
    model = mids[0].shape[-1]
    part = hidden // shards
    tile = 256
    per = tile // part
    return call(
        functools.partial(ffn_grad_kernel, slots, hidden // tile),
        [*acts, *mids, *cots],
        [pl.BlockSpec((1, tokens, tile), lambda k, i: (k, 0, i))] * slots
        + [ANY] * (2 * slots),
        [jax.ShapeDtypeStruct((shards, 3, part, model), BF16)],
        [pl.BlockSpec((per, 1, part, model), lambda k, i: (i, k, 0, 0))],
        jobs,
        number,
        after,
        grid=(3, hidden // tile),
        scratch=[
            pltpu.VMEM((2 * slots, tokens, model), BF16),
            pltpu.SemaphoreType.DMA((2 * slots,)),
        ],
        cost=pl.CostEstimate(
            flops=9 * slots * tokens * model * hidden,
            bytes_accessed=4 * slots * tokens * model,
            transcendentals=0,
        ),
        name="ffn_grads",
    )


def ffn_down_kernel(chunks, steps, hook, ins, outs, held):
    acts = ins[:chunks]
    downs = ins[chunks:]
    (out_ref,) = outs

    def work(late):
        late()
        total = None
        for act, down in zip(acts, downs):
            hidden = act.shape[-1]
            term = dot(act[0], down[...].reshape(hidden, down.shape[-1]))
            total = term if total is None else total + term
        out_ref[...] = total.astype(BF16)

    hooked(hook, pl.program_id(0), steps, work)


def ffn_down(acts, weights, jobs, number, after):
    chunks = len(acts)
    _, tokens, hidden = acts[0].shape
    shards, _, part, model = weights[0].shape
    tile = min(256, tokens)
    act_spec = pl.BlockSpec((1, tile, hidden), lambda i: (2, i, 0))
    down_spec = pl.BlockSpec(
        (shards, 1, part, model),
        lambda i: (0, 2, 0, 0),
        pipeline_mode=pl.Buffered(buffer_count=1),
    )
    return call(
        functools.partial(ffn_down_kernel, chunks, tokens // tile),
        [*acts, *weights],
        [act_spec] * chunks + [down_spec] * chunks,
        [jax.ShapeDtypeStruct((tokens, model), BF16)],
        [pl.BlockSpec((tile, model), lambda i: (i, 0))],
        jobs,
        number,
        after,
        grid=(tokens // tile,),
        cost=pl.CostEstimate(
            flops=4 * chunks * tokens * model * hidden,
            bytes_accessed=chunks * hidden * (tokens + model) * 2,
            transcendentals=0,
        ),
        name="ffn_down",
    )


def place_kernel(place_ref, parts_ref, *refs):
    for kind, out_ref in enumerate(refs[-3:]):
        out_ref[0, 0] = parts_ref[0, kind].astype(F32)


def place_parts(place, parts, chunk, held):
    seqs, _, part, model = parts.shape
    out = jax.ShapeDtypeStruct((seqs, CHUNKS, part, model), F32)
    out_spec = pl.BlockSpec(
        (1, 1, part, model), lambda j, at: (jnp.bitwise_xor(at[0], j), chunk, 0, 0)
    )
    return pl.pallas_call(
        place_kernel,
        out_shape=(out,) * 3,
        grid_spec=pltpu.PrefetchScalarGridSpec(
            num_scalar_prefetch=1,
            grid=(seqs,),
            in_specs=[pl.BlockSpec((1, 3, part, model), lambda j, at: (j, 0, 0, 0))]
            + [ANY] * len(held),
            out_specs=(out_spec,) * 3,
        ),
        input_output_aliases={2 + k: k for k in range(len(held))},
        compiler_params=pltpu.CompilerParams(vmem_limit_bytes=VMEM_LIMIT),
        cost_estimate=pl.CostEstimate(
            flops=0, bytes_accessed=18 * seqs * part * model, transcendentals=0
        ),
        name="place_parts",
    )(place, parts, *held)


def place_heads_kernel(
    place_ref, parts_ref, query_w_ref, key_w_ref, value_w_ref,
    query_ref, key_ref, value_ref, rest_ref, met_ref,
):
    edge = query_ref.shape[1]
    width = key_ref.shape[1]
    part = parts_ref[0].astype(F32)
    query_ref[...] = part[:, :edge]
    key_ref[...] = part[:, edge : edge + width]
    value_ref[...] = part[:, edge + width : edge + 2 * width]
    rest = part[:, edge + 2 * width :]
    met = jnp.zeros_like(met_ref)
    for grad_ref, weight_ref in (
        (query_ref, query_w_ref),
        (key_ref, key_w_ref),
        (value_ref, value_w_ref),
    ):
        product = grad_ref[...] * weight_ref[...].astype(F32)
        met = met + jnp.sum(product, axis=1, keepdims=True)

    @pl.when(pl.program_id(0) == 0)
    def _():
        rest_ref[...] = rest
        met_ref[...] = met

    @pl.when(pl.program_id(0) > 0)
    def _():
        rest_ref[...] += rest
        met_ref[...] += met


def place_heads(place, parts, edge, width, weights):
    seqs, rows, total = parts.shape
    rest = total - edge - 2 * width

    def column_spec(size):
        return pl.BlockSpec((rows, size), lambda j, at: (0, jnp.bitwise_xor(at[0], j)))

    return pl.pallas_call(
        place_heads_kernel,
        out_shape=[
            jax.ShapeDtypeStruct((rows, seqs * edge), F32),
            jax.ShapeDtypeStruct((rows, seqs * width), F32),
            jax.ShapeDtypeStruct((rows, seqs * width), F32),
            jax.ShapeDtypeStruct((rows, rest), F32),
            jax.ShapeDtypeStruct((rows, 128), F32),
        ],
        grid_spec=pltpu.PrefetchScalarGridSpec(
            num_scalar_prefetch=1,
            grid=(seqs,),
            in_specs=[
                pl.BlockSpec((1, rows, total), lambda j, at: (j, 0, 0)),
                column_spec(edge),
                column_spec(width),
                column_spec(width),
            ],
            out_specs=[
                column_spec(edge),
                column_spec(width),
                column_spec(width),
                pl.BlockSpec((rows, rest), lambda j, at: (0, 0)),
                pl.BlockSpec((rows, 128), lambda j, at: (0, 0)),
            ],
        ),
        compiler_params=pltpu.CompilerParams(vmem_limit_bytes=VMEM_LIMIT),
        name="place_heads",
    )(place, parts, *weights)


def scale_of(values):
    return lax.rsqrt(jnp.mean(values * values, axis=-1, keepdims=True) + EPSILON)


def normed(values, gain):
    return values * scale_of(values) * gain


def normed_back(values, gain, cot):
    scale = scale_of(values)
    pulled = cot * gain
    mean = jnp.mean(values * pulled, axis=-1, keepdims=True)
    return (
        scale * pulled - values * (scale * scale * scale) * mean,
        jnp.sum(cot * values * scale, axis=0),
    )


def follow(values, earlier):
    return lax.optimization_barrier((values, *earlier))[0]


def own_columns(weight, heads, place):
    width = heads * HEAD
    part = lax.dynamic_slice_in_dim(weight, place * width, width, 1)
    if heads % 2:
        part = jnp.pad(part, ((0, 0), (0, HEAD)))
    return part


def on_device(
    tokens,
    cotangent,
    lengths,
    attn_gain,
    query_weight,
    key_weight,
    value_weight,
    query_gain,
    key_gain,
    out_weight,
    ffn_gain,
    gate_weight,
    up_weight,
    down_weight,
):
    slots, rows, model = tokens.shape
    seqs = lax.axis_size("seq")
    shards = lax.axis_size("fsdp")
    place = lax.axis_index("seq")
    shard = lax.axis_index("fsdp")
    slot_len = rows * seqs
    query_width = query_weight.shape[1]
    kv_width = key_weight.shape[1]
    hq = query_width // seqs // HEAD
    hkv = kv_width // seqs // HEAD
    hkv_held = hkv + hkv % 2
    sizes = (hq, hkv_held, hq // hkv)
    order = (place if seqs == 4 else place * 0).reshape(1)
    tables = position_tables(slot_len)
    gains = (
        jnp.concatenate([query_gain, query_gain]).reshape(1, 2 * HEAD),
        jnp.concatenate([key_gain, key_gain]).reshape(1, 2 * HEAD),
    )

    flat = (slot_len, model)
    chunked = (seqs, rows, model)
    places = place * rows + jnp.arange(rows, dtype=jnp.int32)
    live = (places[None, :] < lengths[:, None]).astype(F32)[..., None]
    inputs = tokens.astype(F32)
    out_cot = cotangent.astype(F32) * live
    out_low = [out_cot[b].astype(BF16) for b in range(slots)]
    normal_in = [normed(inputs[b], attn_gain).astype(BF16) for b in range(slots)]

    qkv_own = jnp.concatenate(
        [
            own_columns(query_weight, hq, place),
            own_columns(key_weight, hkv, place),
            own_columns(value_weight, hkv, place),
        ],
        axis=1,
    )
    qkv_weight = lax.all_gather(qkv_own, "fsdp", axis=0, tiled=True)
    start = [
        ("gather", normal_in[0]),
        ("deal", out_weight),
        ("own", gate_weight, up_weight, down_weight),
    ]
    normal_0, out_own, *ffn_own = transfer(start, 1)
    out_rows = lax.all_gather(out_own, "fsdp", axis=0, tiled=True)
    hidden_own = gate_weight.shape[0] // seqs
    part = hidden_own // CHUNKS
    ffn_weights = [lax.all_gather(own, "fsdp", axis=0) for own in ffn_own]

    def leave(mixed):
        return dot(mixed.reshape(slot_len, -1), out_rows).astype(BF16).reshape(chunked)

    def enter_ffn(b, total):
        res = inputs[b] + total
        return res, normed(res, ffn_gain).astype(BF16)

    def heads(b, jobs, number, after):
        return attend(
            sizes, lengths[b : b + 1], normal_full[b], qkv_weight, gains, tables,
            jobs, number, after,
        )

    normal_full = [None] * slots
    cot_full = [None] * slots
    mid_full = [None] * slots
    normal_full[0] = normal_0
    (mixed_0, lse_0, qkv_0), (normal_full[1],) = heads(
        0, [("gather", normal_in[1])], 2, normal_full[0]
    )
    (mixed_1, lse_1, qkv_1), (total_0,) = heads(1, [("scatter", leave(mixed_0))], 3, mixed_0)
    qkv = [qkv_0, qkv_1]
    log_sums = [lse_0, lse_1]
    attended = [v.reshape(slot_len, hq * HEAD) for v in (mixed_0, mixed_1)]
    res_0, mid_0 = enter_ffn(0, total_0)
    mid_full[0], cot_full[0] = [
        v.reshape(flat)
        for v in transfer([("gather", mid_0), ("gather", out_low[0])], 4, mixed_1)
    ]

    acts = [[None] * slots for _ in range(CHUNKS)]
    pulled = [None] * slots

    def ffn_step(b, c, jobs, number, after):
        (acts[c][b], pulled[b]), results = ffn_both(
            mid_full[b], cot_full[b], ffn_weights[c], pulled[b], c == CHUNKS - 1,
            jobs, number, after,
        )
        return results

    def grad_step(c, jobs, number, after):
        (grads,), results = ffn_grads(
            acts[c], mid_full, cot_full, shards, jobs, number, after
        )
        return grads.reshape(shards, 3 * part, model), results

    def leave_ffn(b, jobs, number, after):
        (out,), results = ffn_down(
            [acts[c][b] for c in range(CHUNKS)], ffn_weights, jobs, number, after
        )
        return out.reshape(chunked), results

    total_1, full = ffn_step(
        0, 0, [("scatter", leave(mixed_1)), ("gather", out_low[1])], 5, mid_full[0]
    )
    cot_full[1] = full.reshape(flat)
    res_1, mid_1 = enter_ffn(1, total_1)
    hidden_res = [res_0, res_1]
    (full,) = ffn_step(0, 1, [("gather", mid_1)], 6, acts[0][0])
    mid_full[1] = full.reshape(flat)
    (mid_total_0,) = ffn_step(1, 0, [("scatter", pulled[0].reshape(chunked))], 7, acts[1][0])

    def pull_mid(b, total):
        pull, gain_part = normed_back(hidden_res[b], ffn_gain, total)
        cot = out_cot[b] + pull
        return cot, cot.astype(BF16), gain_part

    res_cot_0, low_0, ffn_gain_0 = pull_mid(0, mid_total_0)
    grads_0, (res_full_0,) = grad_step(0, [("gather", low_0)], 8, acts[0][1])
    ffn_sums = [lax.psum_scatter(grads_0, "fsdp", scatter_dimension=0)]
    out_0, _ = leave_ffn(0, [], 0, grads_0)
    (out_total_0,) = ffn_step(1, 1, [("scatter", out_0)], 9, out_0)
    grads_1, (mid_total_1,) = grad_step(
        1, [("scatter", pulled[1].reshape(chunked))], 10, acts[1][1]
    )
    ffn_sums.append(
        lax.psum_scatter(grads_1, "fsdp", scatter_dimension=0)
    )
    res_cot_1, low_1, ffn_gain_1 = pull_mid(1, mid_total_1)
    grad_ffn_gain = ffn_gain_0 + ffn_gain_1

    def back(b, full, jobs, number, after):
        return attend_back(
            sizes, lengths[b : b + 1], qkv[b], full, out_rows, qkv_weight, log_sums[b],
            gains, tables, jobs, number, after,
        )

    (dqkv_0, heads_gain_0, pull_0), (res_full_1,) = back(
        0, res_full_0, [("gather", low_1)], 11, grads_1
    )
    res_full = [v.reshape(flat) for v in (res_full_0, res_full_1)]
    out_grads = sum(dot(attended[b], res_full[b], TN) for b in range(slots)).astype(BF16)
    (dqkv_1, heads_gain_1, pull_1), (in_total_0, ffn_parts_0) = back(
        1, res_full_1, [("scatter", pull_0), ("gather", ffn_sums[0])], 12, out_grads
    )
    head_gain = heads_gain_0 + heads_gain_1
    dqkv = [v.reshape(slot_len, -1) for v in (dqkv_0, dqkv_1)]
    held = model // shards
    piece = out_grads.shape[0] // shards
    blocks = held // piece
    out_grads = jnp.swapaxes(out_grads.reshape(shards, piece, blocks, model // blocks), 1, 2)
    head_sums = jnp.pad(
        (head_gain[:, :HEAD] + head_gain[:, HEAD:]).reshape(2, shards, HEAD // shards),
        ((0, 0), (0, 0), (0, held - HEAD // shards)),
    ).reshape(2, model)
    gain_columns = jnp.stack([grad_ffn_gain, head_sums[0], head_sums[1]], axis=1).astype(BF16)
    attn_grads = jnp.concatenate(
        [
            sum(dot(normal_full[b].reshape(flat), dqkv[b], TN) for b in range(slots)).astype(BF16),
            jnp.pad(gain_columns, ((0, 0), (0, 125))),
            out_grads.reshape(model, model // blocks),
        ],
        axis=1,
    )
    attn_sums = lax.psum_scatter(attn_grads, "fsdp", scatter_dimension=0, tiled=True)
    out_1, (in_total_1,) = leave_ffn(1, [("scatter", pull_1)], 13, attn_grads)
    (out_total_1,) = transfer([("scatter", out_1)], 14, in_total_1)
    ffn_parts_1 = lax.all_gather(follow(ffn_sums[1], [attn_sums, in_total_1]), "seq", axis=0)
    out_edge = attn_sums.shape[1] - model // blocks
    heads_all, _, out_parts = transfer(
        [("gather", attn_sums[:, :out_edge]), ("spread", attn_sums[:, out_edge:])],
        15,
        out_total_1,
    )
    grad_out = jnp.swapaxes(
        out_parts.reshape(seqs, blocks, piece, model // blocks), 1, 2
    ).reshape(held, model)
    grad_tokens = []
    for b, (in_cot, cot) in enumerate(((in_total_0, res_cot_0), (in_total_1, res_cot_1))):
        pull, _ = normed_back(inputs[b], attn_gain, in_cot)
        grad_tokens.append((cot + pull).astype(BF16))
    output = [
        (live[b] * (hidden_res[b] + total)).astype(BF16)
        for b, total in enumerate((out_total_0, out_total_1))
    ]
    ffn_grad = ()
    for c, parts in enumerate((ffn_parts_0, ffn_parts_1)):
        ffn_grad = place_parts(order * (1 - c), parts.reshape(seqs, 3, part, model), c, ffn_grad)
    ffn_grad = [v.reshape(seqs * hidden_own, model) for v in ffn_grad]

    edge = hq * HEAD
    width = hkv_held * HEAD
    if hkv == hkv_held:
        grad_query, grad_key, grad_value, gain_sums, met = place_heads(
            order, heads_all, edge, width, (query_weight, key_weight, value_weight)
        )
        met = met[:, 0]
    else:
        heads_all = jnp.moveaxis(heads_all, 0, 1).astype(F32)
        last = edge + width
        grad_query = heads_all[..., :edge].reshape(held, query_width)
        grad_key = heads_all[..., edge : edge + hkv * HEAD].reshape(held, kv_width)
        grad_value = heads_all[..., last : last + hkv * HEAD].reshape(held, kv_width)
        gain_sums = jnp.sum(heads_all[..., last + width :], axis=1)
        met = sum(
            jnp.sum(grad * weight.astype(F32), axis=1)
            for grad, weight in (
                (grad_query, query_weight),
                (grad_key, key_weight),
                (grad_value, value_weight),
            )
        )
    grad_attn_gain = met / lax.dynamic_slice_in_dim(attn_gain, shard * held, held, 0)

    return (
        jnp.stack(output),
        jnp.stack(grad_tokens),
        grad_attn_gain,
        grad_query,
        grad_key,
        grad_value,
        gain_sums[: HEAD // shards, 1],
        gain_sums[: HEAD // shards, 2],
        grad_out.astype(F32),
        gain_sums[:, 0],
        ffn_grad[0],
        ffn_grad[1],
        ffn_grad[2],
    )


def solution(mesh):
    return jax.shard_map(
        on_device,
        mesh=mesh,
        in_specs=(
            P("fsdp", "seq", None),
            P("fsdp", "seq", None),
            P("fsdp"),
            P(),
            P("fsdp", None),
            P("fsdp", None),
            P("fsdp", None),
            P(),
            P(),
            P("fsdp", None),
            P(),
            P("fsdp", None),
            P("fsdp", None),
            P("fsdp", None),
        ),
        out_specs=(
            P("fsdp", "seq", None),
            P("fsdp", "seq", None),
            P("fsdp"),
            P("fsdp", None),
            P("fsdp", None),
            P("fsdp", None),
            P("fsdp"),
            P("fsdp"),
            P("fsdp", None),
            P("fsdp"),
            P("fsdp", None),
            P("fsdp", None),
            P("fsdp", None),
        ),
        check_vma=False,
    )
```

```python
import functools

import jax
import jax.numpy as jnp
import numpy as np
from jax import lax
from jax.experimental import pallas as pl
from jax.experimental.pallas import tpu as pltpu
from jax.sharding import PartitionSpec as P

EPSILON = 1e-05
ROPE_BASE = 1000000.0
NEGATIVE = -1e30
F32 = jnp.float32
BF16 = jnp.bfloat16
NN = (((1,), (0,)), ((), ()))
NT = (((1,), (1,)), ((), ()))
TN = (((0,), (0,)), ((), ()))
SMEM = pl.BlockSpec(memory_space=pltpu.SMEM)
VMEM = pl.BlockSpec(memory_space=pltpu.VMEM)
VMEM_LIMIT = 58 << 20
HEAD = 64
BLOCK = 256
CHUNKS = 2
ANY = pl.BlockSpec(memory_space=pl.ANY)


def dot(a, b, dims=NN):
    return lax.dot_general(a, b, dims, preferred_element_type=F32)


def over_one(place):
    return place + 1 - 2 * (place % 2)


def over_two(place):
    return (place + 2) % 4


def send(source, target, device, out_sem, in_sem):
    return pltpu.make_async_remote_copy(
        src_ref=source,
        dst_ref=target,
        send_sem=out_sem,
        recv_sem=in_sem,
        device_id={"seq": device},
        device_id_type=pl.DeviceIdType.MESH,
    )


def gather_job(sources, targets, scratch):
    (source,) = sources
    (target,) = targets
    outs, ins, here, held = scratch
    place = lax.axis_index("seq")
    one, two = over_one(place), over_two(place)
    half = source.shape[0] // 2
    load = pltpu.make_async_copy(source, held, here.at[0])
    store = pltpu.make_async_copy(held, target.at[0], here.at[1])
    first = send(source, target.at[1], one, outs.at[0], ins.at[0])
    second = send(source, target.at[2], two, outs.at[1], ins.at[1])
    top = pl.ds(0, half)
    low = pl.ds(half, half)
    third = send(target.at[2, top], target.at[3, top], one, outs.at[2], ins.at[2])
    fourth = send(target.at[1, low], target.at[3, low], two, outs.at[3], ins.at[3])

    def begin():
        first.start()
        second.start()
        load.start()

    def middle():
        load.wait()
        store.start()
        second.wait_recv()
        third.start()
        first.wait_recv()
        fourth.start()

    def finish():
        third.wait_recv()
        fourth.wait_recv()
        for copy in (first, second, third, fourth):
            copy.wait_send()
        store.wait()

    return no_greeting, begin, middle, finish


def scatter_job(sources, targets, scratch):
    (parts,) = sources
    (total,) = targets
    outs, ins, here, got_one, got_two, kept, own, last, summed = scratch
    place = lax.axis_index("seq")
    one, two = over_one(place), over_two(place)
    half = parts.shape[1] // 2
    top = pl.ds(0, half)
    low = pl.ds(half, half)
    sends = [
        send(parts.at[3, top], got_one.at[0], one, outs.at[0], ins.at[0]),
        send(parts.at[3, low], got_two.at[0], two, outs.at[1], ins.at[1]),
        send(parts.at[1, top], got_one.at[1], one, outs.at[2], ins.at[2]),
        send(parts.at[2, low], got_two.at[1], two, outs.at[3], ins.at[3]),
        send(kept.at[0], last.at[0], two, outs.at[4], ins.at[4]),
        send(kept.at[1], last.at[1], one, outs.at[5], ins.at[5]),
    ]
    loads = [
        pltpu.make_async_copy(parts.at[2, top], kept.at[0], here.at[0]),
        pltpu.make_async_copy(parts.at[1, low], kept.at[1], here.at[1]),
        pltpu.make_async_copy(parts.at[0], own, here.at[2]),
    ]
    store = pltpu.make_async_copy(summed, total, here.at[3])

    def begin():
        for copy in sends[:4]:
            copy.start()
        for copy in loads:
            copy.start()

    def middle():
        for k, got in enumerate((got_one, got_two)):
            loads[k].wait()
            sends[k].wait_recv()
            kept[k] = (kept[k].astype(F32) + got[0].astype(F32)).astype(BF16)
            sends[4 + k].start()

    def finish():
        loads[2].wait()
        for k, got in enumerate((got_one, got_two)):
            sends[2 + k].wait_recv()
            sends[4 + k].wait_recv()
            rows = slice(k * half, (k + 1) * half)
            summed[rows, :] = (
                own[rows, :].astype(F32) + got[1].astype(F32) + last[k].astype(F32)
            )
        store.start()
        for copy in sends:
            copy.wait_send()
        store.wait()

    return no_greeting, begin, middle, finish


def no_greeting(barrier):
    return 0


def nothing():
    pass


def greet(barrier, device):
    pl.semaphore_signal(
        barrier, inc=1, device_id=device, device_id_type=pl.DeviceIdType.MESH
    )


def deal_job(sources, targets, scratch):
    (source,) = sources
    (target,) = targets
    outs, ins, here = scratch
    rows = target.shape[0]
    count = source.shape[0] // rows
    place = lax.axis_index("seq")
    shard = lax.axis_index("fsdp")
    per = lax.axis_size("fsdp") // count
    part = shard % per
    is_source = shard // per == place
    to_self = jnp.logical_and(is_source, shard // count == part)
    origin = place * per + shard // count

    def copy(j):
        return pltpu.make_async_remote_copy(
            src_ref=source.at[pl.ds(j * rows, rows)],
            dst_ref=target,
            send_sem=outs.at[j],
            recv_sem=ins.at[0],
            device_id={"fsdp": part * count + j},
            device_id_type=pl.DeviceIdType.MESH,
        )

    def local(j):
        return pltpu.make_async_copy(source.at[pl.ds(j * rows, rows)], target, here.at[0])

    def greeting(barrier):
        pl.when(origin != shard)(lambda: greet(barrier, {"fsdp": origin}))
        return jnp.where(is_source, count, 0) - jnp.where(to_self, 1, 0)

    def each(act_remote, act_local):
        for j in range(count):
            mine = part * count + j == shard
            pl.when(jnp.logical_and(is_source, mine))(lambda j=j: act_local(local(j)))
            pl.when(jnp.logical_and(is_source, jnp.logical_not(mine)))(
                lambda j=j: act_remote(copy(j))
            )

    def begin():
        each(lambda c: c.start(), lambda c: c.start())

    def finish():
        each(lambda c: c.wait_send(), lambda c: c.wait())
        pl.when(origin != shard)(lambda: copy(0).wait_recv())

    return greeting, begin, nothing, finish


def line_job(sources, targets, scratch):
    (source,) = sources
    (target,) = targets
    far_out, far_in, near_out, near_in, here = scratch
    shards = target.shape[0]
    steps = shards // 2
    shard = lax.axis_index("fsdp")
    near = shard + 1 - 2 * (shard % 2)

    def away(start, k):
        return (start + 2 * k) % shards

    def send_line(origin, spot, device, out_sem, in_sem):
        return pltpu.make_async_remote_copy(
            src_ref=origin,
            dst_ref=target.at[spot],
            send_sem=out_sem,
            recv_sem=in_sem,
            device_id={"fsdp": device},
            device_id_type=pl.DeviceIdType.MESH,
        )

    own = pltpu.make_async_copy(source, target.at[shard], here.at[0])
    far = [
        send_line(source, shard, away(shard, k), far_out.at[k - 1], far_in.at[k - 1])
        for k in range(1, steps)
    ]
    far_came = [
        send_line(
            source, away(shard, steps - k), away(shard, k), far_out.at[k - 1], far_in.at[k - 1]
        )
        for k in range(1, steps)
    ]
    held = [shard] + [away(shard, steps - k) for k in range(1, steps)]
    close = [
        send_line(target.at[spot] if k else source, spot, near, near_out.at[k], near_in.at[k])
        for k, spot in enumerate(held)
    ]
    close_came = [
        send_line(source, away(near, steps - k) if k else near, near, near_out.at[k], near_in.at[k])
        for k in range(steps)
    ]

    def greeting(barrier):
        for k in range(1, steps):
            greet(barrier, {"fsdp": away(shard, k)})
        greet(barrier, {"fsdp": near})
        return steps

    def begin():
        own.start()
        for copy in far:
            copy.start()
        close[0].start()

    def finish():
        for k in range(1, steps):
            far_came[k - 1].wait_recv()
            close[k].start()
        for copy in close_came:
            copy.wait_recv()
        for copy in far + close:
            copy.wait_send()
        own.wait()

    return greeting, begin, nothing, finish


def spread_job(sources, targets, scratch):
    (source,) = sources
    gathered, target = targets
    *first, z_outs, z_ins, z_here = scratch
    _, begin_gather, middle_gather, finish_gather = gather_job(sources, [gathered], first)
    count = gathered.shape[0]
    place = lax.axis_index("seq")
    shard = lax.axis_index("fsdp")
    per = lax.axis_size("fsdp") // count
    piece = shard % count

    def owner(j):
        return true_chunk(place, j, count) * per + shard // count

    def chunk(j):
        return gathered.at[j] if j else source

    def copy(j):
        return pltpu.make_async_remote_copy(
            src_ref=chunk(j),
            dst_ref=target.at[piece],
            send_sem=z_outs.at[j],
            recv_sem=z_ins.at[piece],
            device_id={"fsdp": owner(j)},
            device_id_type=pl.DeviceIdType.MESH,
        )

    def arrival(p):
        return pltpu.make_async_remote_copy(
            src_ref=source,
            dst_ref=target.at[p],
            send_sem=z_outs.at[0],
            recv_sem=z_ins.at[p],
            device_id={"fsdp": owner(0)},
            device_id_type=pl.DeviceIdType.MESH,
        )

    def local(j):
        return pltpu.make_async_copy(chunk(j), target.at[piece], z_here.at[0])

    def origin(p):
        return (shard % per) * count + p

    def start(j):
        pl.when(owner(j) != shard)(lambda: copy(j).start())
        pl.when(owner(j) == shard)(lambda: local(j).start())

    def greeting(barrier):
        for p in range(count):
            pl.when(origin(p) != shard)(lambda p=p: greet(barrier, {"fsdp": origin(p)}))
        return jnp.where(shard % per == shard // count, count - 1, count)

    def begin():
        begin_gather()
        start(0)

    def middle():
        middle_gather()
        start(1)
        start(2)

    def finish():
        finish_gather()
        start(3)
        for j in range(count):
            pl.when(owner(j) != shard)(lambda j=j: copy(j).wait_send())
            pl.when(owner(j) == shard)(lambda j=j: local(j).wait())
        for p in range(count):
            pl.when(origin(p) != shard)(lambda p=p: arrival(p).wait_recv())

    return greeting, begin, middle, finish


def own_job(sources, targets, scratch):
    loaded, stored, held = scratch
    place = lax.axis_index("seq")
    count = lax.axis_size("seq")
    part = targets[0].shape[1]
    loads = []
    stores = []
    for c, target in enumerate(targets):
        for k, source in enumerate(sources):
            start = place * (source.shape[0] // count) + c * part
            spot = pl.ds(pl.multiple_of(start, part), part)
            n = c * len(sources) + k
            loads.append(pltpu.make_async_copy(source.at[spot], held.at[n], loaded.at[n]))
            stores.append(pltpu.make_async_copy(held.at[n], target.at[k], stored.at[n]))

    def begin():
        for load in loads:
            load.start()

    def middle():
        for load, store in zip(loads, stores):
            load.wait()
            store.start()

    def finish():
        for store in stores:
            store.wait()

    return no_greeting, begin, middle, finish


MAKERS = {
    "gather": gather_job,
    "scatter": scatter_job,
    "deal": deal_job,
    "spread": spread_job,
    "line": line_job,
    "own": own_job,
}


def job_scratch(job):
    kind, *arrays = job
    if kind == "scatter":
        _, rows, width = arrays[0].shape
        halves = pltpu.VMEM((2, rows // 2, width), BF16)
        return [
            pltpu.SemaphoreType.DMA((6,)),
            pltpu.SemaphoreType.DMA((6,)),
            pltpu.SemaphoreType.DMA((4,)),
            halves,
            halves,
            halves,
            pltpu.VMEM((rows, width), BF16),
            halves,
            pltpu.VMEM((rows, width), F32),
        ]
    if kind == "own":
        count = CHUNKS * len(arrays)
        rows, width = arrays[0].shape
        part = rows // lax.axis_size("seq") // CHUNKS
        return [
            pltpu.SemaphoreType.DMA((count,)),
            pltpu.SemaphoreType.DMA((count,)),
            pltpu.VMEM((count, part, width), BF16),
        ]
    moves = [
        pltpu.SemaphoreType.DMA((4,)),
        pltpu.SemaphoreType.DMA((4,)),
        pltpu.SemaphoreType.DMA((2,)),
    ]
    if kind == "deal":
        return moves
    if kind == "line":
        steps = lax.axis_size("fsdp") // 2
        return [pltpu.SemaphoreType.DMA((steps,))] * 4 + [pltpu.SemaphoreType.DMA((1,))]
    moves.append(pltpu.VMEM(arrays[0].shape, BF16))
    if kind == "spread":
        moves += [
            pltpu.SemaphoreType.DMA((4,)),
            pltpu.SemaphoreType.DMA((4,)),
            pltpu.SemaphoreType.DMA((1,)),
        ]
    return moves


def job_results(job):
    kind, *arrays = job
    shape = arrays[0].shape
    if kind == "gather":
        return [jax.ShapeDtypeStruct((4,) + shape, BF16)]
    if kind == "scatter":
        return [jax.ShapeDtypeStruct(shape[1:], F32)]
    if kind == "deal":
        return [jax.ShapeDtypeStruct((shape[0] // 4,) + shape[1:], BF16)]
    if kind == "spread":
        return [jax.ShapeDtypeStruct((4,) + shape, BF16)] * 2
    if kind == "line":
        return [jax.ShapeDtypeStruct((lax.axis_size("fsdp"),) + shape, BF16)]
    part = shape[0] // lax.axis_size("seq") // CHUNKS
    return [jax.ShapeDtypeStruct((len(arrays), part) + shape[1:], BF16)] * CHUNKS


def plain_job(job):
    kind, *arrays = job
    seqs = lax.axis_size("seq")
    shards = lax.axis_size("fsdp")
    per = shards // seqs
    ends = [(s, h, s * shards + s * per + h) for s in range(seqs) for h in range(per)]
    if kind == "gather":
        return [lax.all_gather(arrays[0], "seq", axis=0)]
    if kind == "scatter":
        return [lax.psum_scatter(arrays[0], "seq", scatter_dimension=0).astype(F32)]
    if kind == "deal":
        rows = arrays[0].shape[0] // seqs
        total = None
        for j in range(seqs):
            moves = [(end, s * shards + h * seqs + j) for s, h, end in ends]
            got = lax.ppermute(arrays[0][j * rows : (j + 1) * rows], ("seq", "fsdp"), moves)
            total = got if total is None else total + got
        return [total]
    if kind == "line":
        return [lax.all_gather(arrays[0], "fsdp", axis=0)]
    if kind == "spread":
        gathered = lax.all_gather(arrays[0], "seq", axis=0)
        pieces = []
        for p in range(seqs):
            total = None
            for q in range(seqs):
                moves = [
                    (s * shards + h * seqs + p, s * shards + q * per + h)
                    for s in range(seqs)
                    for h in range(per)
                ]
                got = lax.ppermute(gathered[q], ("seq", "fsdp"), moves)
                total = got if total is None else total + got
            pieces.append(total)
        return [gathered, jnp.stack(pieces)]
    own_rows = arrays[0].shape[0] // seqs
    part = own_rows // CHUNKS
    start = lax.axis_index("seq") * own_rows
    return [
        jnp.stack([lax.dynamic_slice_in_dim(w, start + c * part, part, 0) for w in arrays])
        for c in range(CHUNKS)
    ]


def meet(greetings):
    place = lax.axis_index("seq")
    barrier = pltpu.get_barrier_semaphore()
    for device in (over_one(place), over_two(place)):
        greet(barrier, {"seq": device})
    peers = 2
    for greeting in greetings:
        peers = peers + greeting(barrier)
    pl.semaphore_wait(barrier, peers)


def call(
    body, operands, in_specs, out_shape, out_specs, jobs, number, after=None,
    grid=(), scratch=(), cost=None, name=None, late=(),
):
    plain = lax.axis_size("seq") != 4
    results = [v for job in jobs for v in plain_job(job)] if plain else []
    inside = [] if plain else jobs
    extra = [] if after is None else [after]
    job_shapes = [job_scratch(job) for job in inside]
    job_outs = [job_results(job) for job in inside]
    n_in = len(operands)
    n_out = len(out_shape)

    def kernel(*refs):
        refs = list(refs)

        def take(count):
            taken, refs[:] = refs[:count], refs[count:]
            return taken

        ins = take(n_in)
        take(len(extra))
        sources = [take(len(job) - 1) for job in inside]
        outs = take(n_out)
        targets = [take(len(shapes)) for shapes in job_outs]
        held = take(len(scratch))
        loaded = take(len(late))
        marks = take(1) if late else []
        loads = [
            pltpu.make_async_copy(ins[n], ref, marks[0].at[k])
            for k, (n, ref) in enumerate(zip(late, loaded))
        ]
        for n, ref in zip(late, loaded):
            ins[n] = ref
        phases = [
            MAKERS[job[0]](source, target, take(len(shapes)))
            for job, source, target, shapes in zip(inside, sources, targets, job_shapes)
        ]

        def hook(k):
            if k == 0 and phases:
                meet([phase[0] for phase in phases])
            for phase in phases:
                phase[k + 1]()
            if k == 0:
                for load in loads:
                    load.start()
                for load in loads:
                    load.wait()

        body(hook, ins, outs, held)

    given = {}
    if inside:
        given = {"collective_id": number, "has_side_effects": True}
    arrays = [array for job in inside for array in job[1:]]
    in_specs = [ANY if n in late else spec for n, spec in enumerate(in_specs)]
    late_shapes = [pltpu.VMEM(operands[n].shape, operands[n].dtype) for n in late]
    if late:
        late_shapes.append(pltpu.SemaphoreType.DMA((len(late),)))
    shapes = [shape for shapes in job_outs for shape in shapes]
    made = pl.pallas_call(
        kernel,
        grid=grid,
        out_shape=tuple(out_shape) + tuple(shapes),
        in_specs=list(in_specs) + [ANY] * (len(extra) + len(arrays)),
        out_specs=tuple(out_specs) + (ANY,) * len(shapes),
        scratch_shapes=list(scratch)
        + late_shapes
        + [shape for shapes in job_shapes for shape in shapes],
        compiler_params=pltpu.CompilerParams(vmem_limit_bytes=VMEM_LIMIT, **given),
        cost_estimate=cost,
        name=name,
    )(*operands, *extra, *arrays)
    return list(made[:n_out]), list(made[n_out:]) + results


def transfer(jobs, number, after=None):
    if lax.axis_size("seq") != 4:
        return [v for job in jobs for v in plain_job(job)]

    def body(hook, ins, outs, held):
        for k in range(3):
            hook(k)

    return call(body, [], [], [], [], jobs, number, after, name="transfer")[1]


def partner(v):
    lane = lax.broadcasted_iota(jnp.int32, v.shape, 1)
    return jnp.where(lane % HEAD < HEAD // 2, pltpu.roll(v, 96, 1), pltpu.roll(v, 32, 1))


def head_mean(v, ones):
    high = v.astype(BF16)
    rest = (v - high.astype(F32)).astype(BF16)
    return dot(high, ones) + dot(rest, ones)


def true_chunk(place, c, count):
    if count != 4:
        return c
    low = 1 - place % 2 if c % 2 else place % 2
    high = 1 - place // 2 if c // 2 else place // 2
    return low + 2 * high


def prepare_heads(sizes, place, qkv_ref, qg_ref, kg_ref, cos_ref, sin_ref, ones, q_s, k_s, v_s):
    hq, hkv, _ = sizes
    seqs, rows_in, _ = qkv_ref.shape
    for c in range(seqs):
        j = true_chunk(place, c, seqs)
        rows = slice(c * rows_in, (c + 1) * rows_in)
        cos = cos_ref[rows, :]
        sin = sin_ref[rows, :]
        for p in range((hq + hkv) // 2):
            is_query = p < hq // 2
            x = qkv_ref[j, :, p * 128 : (p + 1) * 128].astype(F32)
            gain = qg_ref[...] * HEAD**-0.5 if is_query else kg_ref[...]
            y = x * lax.rsqrt(head_mean(x * x, ones) + EPSILON) * gain
            y = (y * cos + partner(y) * sin).astype(BF16)
            for t in range(2):
                part = y[:, t * HEAD : (t + 1) * HEAD]
                if is_query:
                    q_s[2 * p + t, rows, :] = part
                else:
                    k_s[2 * p - hq + t, rows, :] = part
        for t in range(hkv):
            start = (hq + hkv + t) * HEAD
            v_s[t, rows, :] = qkv_ref[j, :, start : start + HEAD]


def allowed_keys(block, first, keys, length):
    bound = jnp.minimum(first + lax.broadcasted_iota(jnp.int32, (block, 1), 0), length - 1)
    return lax.broadcasted_iota(jnp.int32, (block, keys), 1) <= bound


def attend_kernel(sizes, hook, ins, outs, held):
    len_ref, normal_ref, weight_ref, qg_ref, kg_ref, cos_ref, sin_ref, ones_ref = ins
    out_ref, lse_ref, qkv_ref = outs
    q_s, k_s, v_s, o_s = held
    hook(0)

    @pl.loop(0, qkv_ref.shape[0])
    def _(j):
        qkv_ref[j] = dot(normal_ref[j], weight_ref[...]).astype(BF16)

    hq, hkv, group = sizes
    seqs, rows_in, _ = qkv_ref.shape
    place = lax.axis_index("seq")
    prepare_heads(
        sizes, place, qkv_ref, qg_ref, kg_ref, cos_ref, sin_ref, ones_ref[...], q_s, k_s, v_s
    )
    for i in range(seqs * rows_in // BLOCK):
        keys = (i + 1) * BLOCK
        rows = slice(i * BLOCK, (i + 1) * BLOCK)
        keep = allowed_keys(BLOCK, i * BLOCK, keys, len_ref[0])

        def one_head(h, _):
            kv = h // group
            scores = dot(q_s[h, rows, :], k_s[kv, :keys, :], NT)
            scores = jnp.where(keep, scores, NEGATIVE)
            highest = jnp.max(scores, axis=1, keepdims=True)
            shifted = jnp.exp(scores - highest)
            total = jnp.sum(shifted, axis=1, keepdims=True)
            mixed = dot(shifted.astype(BF16), v_s[kv, :keys, :]) / total
            o_s[h, rows, :] = mixed.astype(BF16)
            lse_ref[h, rows, :] = highest + jnp.log(total)
            return 0

        lax.fori_loop(0, hq, one_head, 0, unroll=min(4, hq))
        if i == seqs * rows_in // BLOCK - 2:
            hook(1)
    for c in range(seqs):
        j = true_chunk(place, c, seqs)
        rows = slice(c * rows_in, (c + 1) * rows_in)
        for p in range(hq // 2):
            out_ref[j, :, p * 128 : (p + 1) * 128] = jnp.concatenate(
                [o_s[2 * p, rows, :], o_s[2 * p + 1, rows, :]], axis=1
            )
    hook(2)


def attend_back_kernel(sizes, hook, ins, outs, held):
    (
        len_ref, qkv_ref, res_ref, out_w_ref, qkv_w_ref, lse_ref,
        qg_ref, kg_ref, cos_ref, sin_ref, ones_ref,
    ) = ins
    dqkv_ref, dgain_ref, pull_ref = outs
    q_s, k_s, v_s, cot_s, dq_s, dk_s, dv_s = held
    hook(0)
    hq, hkv, group = sizes
    seqs, rows_in, _ = qkv_ref.shape
    place = lax.axis_index("seq")
    ones = ones_ref[...]
    prepare_heads(sizes, place, qkv_ref, qg_ref, kg_ref, cos_ref, sin_ref, ones, q_s, k_s, v_s)
    for c in range(seqs):
        j = true_chunk(place, c, seqs)
        cots = dot(res_ref[j], out_w_ref[...], NT).astype(BF16)
        for h in range(hq):
            cot_s[h, c * rows_in : (c + 1) * rows_in, :] = cots[:, h * HEAD : (h + 1) * HEAD]
    dk_s[...] = jnp.zeros_like(dk_s)
    dv_s[...] = jnp.zeros_like(dv_s)
    for i in range(seqs * rows_in // BLOCK):
        keys = (i + 1) * BLOCK
        rows = slice(i * BLOCK, (i + 1) * BLOCK)
        keep = allowed_keys(BLOCK, i * BLOCK, keys, len_ref[0])

        def one_head(h, _):
            kv = h // group
            q = q_s[h, rows, :]
            cot = cot_s[h, rows, :]
            k = k_s[kv, :keys, :]
            scores = jnp.where(keep, dot(q, k, NT), NEGATIVE)
            probs = jnp.exp(scores - lse_ref[h, rows, :])
            prob_cot = dot(cot, v_s[kv, :keys, :], NT)
            inner = jnp.sum(probs * prob_cot, axis=1, keepdims=True)
            score_cot = (probs * (prob_cot - inner)).astype(BF16)
            dq_s[h, rows, :] = dot(score_cot, k) * HEAD**-0.5
            dk_s[kv, :keys, :] += dot(score_cot, q, TN)
            dv_s[kv, :keys, :] += dot(probs.astype(BF16), cot, TN)
            return 0

        lax.fori_loop(0, hq, one_head, 0, unroll=min(4, hq))
        if i == seqs * rows_in // BLOCK - 2:
            hook(1)
    gain_sums = [jnp.zeros((1, 128), F32), jnp.zeros((1, 128), F32)]
    for c in range(seqs):
        j = true_chunk(place, c, seqs)
        rows = slice(c * rows_in, (c + 1) * rows_in)
        cos = cos_ref[rows, :]
        sin = sin_ref[rows, :]
        for p in range((hq + hkv) // 2):
            is_query = p < hq // 2
            x = qkv_ref[j, :, p * 128 : (p + 1) * 128].astype(F32)
            gain = qg_ref[...] if is_query else kg_ref[...]
            source, first = (dq_s, 2 * p) if is_query else (dk_s, 2 * p - hq)
            turned = jnp.concatenate([source[first, rows, :], source[first + 1, rows, :]], axis=1)
            scale = lax.rsqrt(head_mean(x * x, ones) + EPSILON)
            straight = turned * cos + partner(turned * sin)
            unit = x * scale
            which = 0 if is_query else 1
            gain_sums[which] += jnp.sum(straight * unit, axis=0, keepdims=True)
            pulled = gain * straight
            dx = scale * (pulled - unit * head_mean(unit * pulled, ones))
            dqkv_ref[j, :, p * 128 : (p + 1) * 128] = dx.astype(BF16)
        for p in range(hkv // 2):
            start = (hq + hkv) * HEAD + p * 128
            dqkv_ref[j, :, start : start + 128] = jnp.concatenate(
                [dv_s[2 * p, rows, :], dv_s[2 * p + 1, rows, :]], axis=1
            ).astype(BF16)
    dgain_ref[0:1, :] = gain_sums[0]
    dgain_ref[1:2, :] = gain_sums[1]

    @pl.loop(0, seqs)
    def _(j):
        pull_ref[j] = dot(dqkv_ref[j], qkv_w_ref[...], NT).astype(BF16)

    hook(2)


def position_tables(length):
    places = np.arange(length, dtype=np.float32)
    half = HEAD // 2
    freqs = np.float32(ROPE_BASE) ** (-(np.arange(half, dtype=np.float32) * 2.0) / HEAD)
    angles = places[:, None] * freqs.astype(np.float32)[None, :]
    cos = np.cos(angles).astype(np.float32)
    sin = np.sin(angles).astype(np.float32)
    ones = np.kron(np.eye(2), np.ones((HEAD, HEAD)) / HEAD)
    return (
        jnp.asarray(np.concatenate([cos] * 4, axis=1)),
        jnp.asarray(np.concatenate([-sin, sin, -sin, sin], axis=1)),
        jnp.asarray(ones, dtype=BF16),
    )


def attend(sizes, length, normal, weight, gains, tables, jobs, number, after):
    seqs, rows_in, _ = normal.shape
    hq, hkv, _ = sizes
    slot = seqs * rows_in
    return call(
        functools.partial(attend_kernel, sizes),
        [length, normal, weight, *gains, *tables],
        [SMEM] + [VMEM] * 7,
        [
            jax.ShapeDtypeStruct((seqs, rows_in, hq * HEAD), BF16),
            jax.ShapeDtypeStruct((hq, slot, 1), F32),
            jax.ShapeDtypeStruct((seqs, rows_in, weight.shape[1]), BF16),
        ],
        [VMEM, VMEM, VMEM],
        jobs,
        number,
        after,
        scratch=[
            pltpu.VMEM((hq, slot, HEAD), BF16),
            pltpu.VMEM((hkv, slot, HEAD), BF16),
            pltpu.VMEM((hkv, slot, HEAD), BF16),
            pltpu.VMEM((hq, slot, HEAD), BF16),
        ],
        cost=pl.CostEstimate(
            flops=56 * hq * slot * slot * HEAD, bytes_accessed=1 << 23, transcendentals=0
        ),
        name="attend",
        late=(1, 2),
    )


def attend_back(
    sizes, length, qkv, res, out_w, qkv_w, lse, gains, tables, jobs, number, after
):
    seqs, rows_in, width = qkv.shape
    hq, hkv, _ = sizes
    slot = seqs * rows_in
    return call(
        functools.partial(attend_back_kernel, sizes),
        [length, qkv, res, out_w, qkv_w, lse, *gains, *tables],
        [SMEM] + [VMEM] * 10,
        [
            jax.ShapeDtypeStruct((seqs, rows_in, width), BF16),
            jax.ShapeDtypeStruct((2, 128), F32),
            jax.ShapeDtypeStruct(res.shape, BF16),
        ],
        [VMEM, VMEM, VMEM],
        jobs,
        number,
        after,
        scratch=[
            pltpu.VMEM((hq, slot, HEAD), BF16),
            pltpu.VMEM((hkv, slot, HEAD), BF16),
            pltpu.VMEM((hkv, slot, HEAD), BF16),
            pltpu.VMEM((hq, slot, HEAD), BF16),
            pltpu.VMEM((hq, slot, HEAD), F32),
            pltpu.VMEM((hkv, slot, HEAD), F32),
            pltpu.VMEM((hkv, slot, HEAD), F32),
        ],
        cost=pl.CostEstimate(
            flops=88 * hq * slot * slot * HEAD, bytes_accessed=1 << 23, transcendentals=0
        ),
        name="attend_back",
        late=(1, 2, 3, 4, 5),
    )


def hooked(hook, step, steps, work):
    pl.when(step == 0)(lambda: hook(0))
    work(lambda: pl.when(step == (3 * steps) // 5)(lambda: hook(1)))
    pl.when(step == steps - 1)(lambda: hook(2))


def ffn_kernel(steps, hook, ins, outs, held):
    step = pl.program_id(0)
    weights_ref, loaded = held
    loads = [
        pltpu.make_async_copy(ins[2].at[:, k], weights_ref.at[k], loaded.at[k]) for k in range(3)
    ]

    def first(act):
        pl.when(step == 0)(act)

    def work(late):
        for load in loads:
            first(load.start)
        ffn_tile(late, first, loads, *ins[:2], weights_ref, ins[3:], *outs)

    hooked(hook, step, steps, work)


def ffn_tile(late, first, loads, mid_ref, cot_ref, weights_ref, sums, acts_ref, pull_ref):
    model = mid_ref.shape[-1]
    hidden = acts_ref.shape[-1]
    whole = (hidden, model)
    mid = mid_ref[...]
    first(loads[0].wait)
    gate = dot(mid, weights_ref[0].reshape(whole), NT)
    first(loads[1].wait)
    up = dot(mid, weights_ref[1].reshape(whole), NT)
    first(loads[2].wait)
    mids_cot = dot(cot_ref[...], weights_ref[2].reshape(whole), NT)
    late()
    sigmoid = jax.nn.sigmoid(gate)
    active = gate * sigmoid
    gate_cot = (mids_cot * up * sigmoid * (1.0 + gate * (1.0 - sigmoid))).astype(BF16)
    up_cot = (mids_cot * active).astype(BF16)
    acts_ref[0] = gate_cot
    acts_ref[1] = up_cot
    acts_ref[2] = (active * up).astype(BF16)
    pulled = dot(gate_cot, weights_ref[0].reshape(whole)) + dot(
        up_cot, weights_ref[1].reshape(whole)
    )
    for sum_ref in sums:
        pulled = pulled + sum_ref[...]
    pull_ref[...] = pulled.astype(pull_ref.dtype)


def ffn_both(mid, cot, weights, summed, last, jobs, number, after):
    tokens, model = mid.shape
    shards, _, part, _ = weights.shape
    hidden = shards * part
    tile = min(256, tokens)

    row_spec = pl.BlockSpec((tile, model), lambda i: (i, 0))
    extra = () if summed is None else (summed,)
    return call(
        functools.partial(ffn_kernel, tokens // tile),
        [mid, cot, weights, *extra],
        [row_spec, row_spec, ANY] + [row_spec] * len(extra),
        [
            jax.ShapeDtypeStruct((3, tokens, hidden), BF16),
            jax.ShapeDtypeStruct((tokens, model), BF16 if last else F32),
        ],
        [pl.BlockSpec((3, tile, hidden), lambda i: (0, i, 0)), row_spec],
        jobs,
        number,
        after,
        grid=(tokens // tile,),
        scratch=[
            pltpu.VMEM((3, shards, part, model), BF16),
            pltpu.SemaphoreType.DMA((3,)),
        ],
        cost=pl.CostEstimate(
            flops=16 * tokens * model * hidden,
            bytes_accessed=4 * tokens * model + 6 * hidden * model,
            transcendentals=0,
        ),
        name="ffn_both",
    )


def ffn_grad_kernel(slots, tiles, hook, ins, outs, held):
    acts = ins[:slots]
    others = ins[slots:]
    (out_ref,) = outs
    rows_ref, loaded = held
    kind = pl.program_id(0)
    step = kind * tiles + pl.program_id(1)
    loads = [
        pltpu.make_async_copy(other, rows_ref.at[k], loaded.at[k])
        for k, other in enumerate(others)
    ]

    def store(first):
        total = None
        for k, act in enumerate(acts):
            term = dot(act[0], rows_ref[first + k], TN)
            total = term if total is None else total + term
        out_ref[...] = total.astype(BF16).reshape(out_ref.shape)

    def work(late):
        for k, load in enumerate(loads):
            pl.when(step == 0)(load.start)
        for k, load in enumerate(loads):
            pl.when(step == (0 if k < slots else 2 * tiles))(load.wait)
        late()
        pl.when(kind < 2)(lambda: store(0))
        pl.when(kind == 2)(lambda: store(slots))

    hooked(hook, step, 3 * tiles, work)


def ffn_grads(acts, mids, cots, shards, jobs, number, after):
    slots = len(acts)
    _, tokens, hidden = acts[0].shape
    model = mids[0].shape[-1]
    part = hidden // shards
    tile = 256
    per = tile // part
    return call(
        functools.partial(ffn_grad_kernel, slots, hidden // tile),
        [*acts, *mids, *cots],
        [pl.BlockSpec((1, tokens, tile), lambda k, i: (k, 0, i))] * slots
        + [ANY] * (2 * slots),
        [jax.ShapeDtypeStruct((shards, 3, part, model), BF16)],
        [pl.BlockSpec((per, 1, part, model), lambda k, i: (i, k, 0, 0))],
        jobs,
        number,
        after,
        grid=(3, hidden // tile),
        scratch=[
            pltpu.VMEM((2 * slots, tokens, model), BF16),
            pltpu.SemaphoreType.DMA((2 * slots,)),
        ],
        cost=pl.CostEstimate(
            flops=9 * slots * tokens * model * hidden,
            bytes_accessed=4 * slots * tokens * model,
            transcendentals=0,
        ),
        name="ffn_grads",
    )


def ffn_down_kernel(chunks, steps, hook, ins, outs, held):
    acts = ins[:chunks]
    downs = ins[chunks:]
    (out_ref,) = outs

    def work(late):
        late()
        total = None
        for act, down in zip(acts, downs):
            hidden = act.shape[-1]
            term = dot(act[0], down[...].reshape(hidden, down.shape[-1]))
            total = term if total is None else total + term
        out_ref[...] = total.astype(BF16)

    hooked(hook, pl.program_id(0), steps, work)


def ffn_down(acts, weights, jobs, number, after, true_order=False):
    chunks = len(acts)
    _, tokens, hidden = acts[0].shape
    shards, _, part, model = weights[0].shape
    tile = min(256, tokens)
    def spot(i):
        if not true_order or lax.axis_size("seq") != 4:
            return i
        place = lax.axis_index("seq")
        low = (place % 2 + i % 2) % 2
        high = (place // 2 + i // 2) % 2
        return low + 2 * high

    act_spec = pl.BlockSpec((1, tile, hidden), lambda i: (2, i, 0))
    down_spec = pl.BlockSpec(
        (shards, 1, part, model),
        lambda i: (0, 2, 0, 0),
        pipeline_mode=pl.Buffered(buffer_count=1),
    )
    return call(
        functools.partial(ffn_down_kernel, chunks, tokens // tile),
        [*acts, *weights],
        [act_spec] * chunks + [down_spec] * chunks,
        [jax.ShapeDtypeStruct((tokens, model), BF16)],
        [pl.BlockSpec((tile, model), lambda i: (spot(i), 0))],
        jobs,
        number,
        after,
        grid=(tokens // tile,),
        cost=pl.CostEstimate(
            flops=4 * chunks * tokens * model * hidden,
            bytes_accessed=chunks * hidden * (tokens + model) * 2,
            transcendentals=0,
        ),
        name="ffn_down",
    )


def place_kernel(place_ref, parts_ref, *refs):
    for kind, out_ref in enumerate(refs[-3:]):
        out_ref[0, 0] = parts_ref[0, kind].astype(F32)


def place_parts(place, parts, chunk, held):
    seqs, _, part, model = parts.shape
    out = jax.ShapeDtypeStruct((seqs, CHUNKS, part, model), F32)
    out_spec = pl.BlockSpec(
        (1, 1, part, model), lambda j, at: (jnp.bitwise_xor(at[0], j), chunk, 0, 0)
    )
    return pl.pallas_call(
        place_kernel,
        out_shape=(out,) * 3,
        grid_spec=pltpu.PrefetchScalarGridSpec(
            num_scalar_prefetch=1,
            grid=(seqs,),
            in_specs=[pl.BlockSpec((1, 3, part, model), lambda j, at: (j, 0, 0, 0))]
            + [ANY] * len(held),
            out_specs=(out_spec,) * 3,
        ),
        input_output_aliases={2 + k: k for k in range(len(held))},
        compiler_params=pltpu.CompilerParams(vmem_limit_bytes=VMEM_LIMIT),
        cost_estimate=pl.CostEstimate(
            flops=0, bytes_accessed=18 * seqs * part * model, transcendentals=0
        ),
        name="place_parts",
    )(place, parts, *held)


def place_heads_kernel(
    place_ref, parts_ref, query_w_ref, key_w_ref, value_w_ref,
    query_ref, key_ref, value_ref, rest_ref, met_ref,
):
    edge = query_ref.shape[1]
    width = key_ref.shape[1]
    part = parts_ref[0].astype(F32)
    query_ref[...] = part[:, :edge]
    key_ref[...] = part[:, edge : edge + width]
    value_ref[...] = part[:, edge + width : edge + 2 * width]
    rest = part[:, edge + 2 * width :]
    met = jnp.zeros_like(met_ref)
    for grad_ref, weight_ref in (
        (query_ref, query_w_ref),
        (key_ref, key_w_ref),
        (value_ref, value_w_ref),
    ):
        product = grad_ref[...] * weight_ref[...].astype(F32)
        met = met + jnp.sum(product, axis=1, keepdims=True)

    @pl.when(pl.program_id(0) == 0)
    def _():
        rest_ref[...] = rest
        met_ref[...] = met

    @pl.when(pl.program_id(0) > 0)
    def _():
        rest_ref[...] += rest
        met_ref[...] += met


def place_heads(place, parts, edge, width, weights):
    seqs, rows, total = parts.shape
    rest = total - edge - 2 * width

    def column_spec(size):
        return pl.BlockSpec((rows, size), lambda j, at: (0, jnp.bitwise_xor(at[0], j)))

    return pl.pallas_call(
        place_heads_kernel,
        out_shape=[
            jax.ShapeDtypeStruct((rows, seqs * edge), F32),
            jax.ShapeDtypeStruct((rows, seqs * width), F32),
            jax.ShapeDtypeStruct((rows, seqs * width), F32),
            jax.ShapeDtypeStruct((rows, rest), F32),
            jax.ShapeDtypeStruct((rows, 128), F32),
        ],
        grid_spec=pltpu.PrefetchScalarGridSpec(
            num_scalar_prefetch=1,
            grid=(seqs,),
            in_specs=[
                pl.BlockSpec((1, rows, total), lambda j, at: (j, 0, 0)),
                column_spec(edge),
                column_spec(width),
                column_spec(width),
            ],
            out_specs=[
                column_spec(edge),
                column_spec(width),
                column_spec(width),
                pl.BlockSpec((rows, rest), lambda j, at: (0, 0)),
                pl.BlockSpec((rows, 128), lambda j, at: (0, 0)),
            ],
        ),
        compiler_params=pltpu.CompilerParams(vmem_limit_bytes=VMEM_LIMIT),
        name="place_heads",
    )(place, parts, *weights)


def scale_of(values):
    return lax.rsqrt(jnp.mean(values * values, axis=-1, keepdims=True) + EPSILON)


def normed(values, gain):
    return values * scale_of(values) * gain


def normed_back(values, gain, cot):
    scale = scale_of(values)
    pulled = cot * gain
    mean = jnp.mean(values * pulled, axis=-1, keepdims=True)
    return (
        scale * pulled - values * (scale * scale * scale) * mean,
        jnp.sum(cot * values * scale, axis=0),
    )


def follow(values, earlier):
    return lax.optimization_barrier((values, *earlier))[0]


def own_columns(weight, heads, place):
    width = heads * HEAD
    part = lax.dynamic_slice_in_dim(weight, place * width, width, 1)
    if heads % 2:
        part = jnp.pad(part, ((0, 0), (0, HEAD)))
    return part


def on_device(
    tokens,
    cotangent,
    lengths,
    attn_gain,
    query_weight,
    key_weight,
    value_weight,
    query_gain,
    key_gain,
    out_weight,
    ffn_gain,
    gate_weight,
    up_weight,
    down_weight,
):
    slots, rows, model = tokens.shape
    seqs = lax.axis_size("seq")
    shards = lax.axis_size("fsdp")
    place = lax.axis_index("seq")
    shard = lax.axis_index("fsdp")
    slot_len = rows * seqs
    query_width = query_weight.shape[1]
    kv_width = key_weight.shape[1]
    hq = query_width // seqs // HEAD
    hkv = kv_width // seqs // HEAD
    hkv_held = hkv + hkv % 2
    sizes = (hq, hkv_held, hq // hkv)
    order = (place if seqs == 4 else place * 0).reshape(1)
    tables = position_tables(slot_len)
    gains = (
        jnp.concatenate([query_gain, query_gain]).reshape(1, 2 * HEAD),
        jnp.concatenate([key_gain, key_gain]).reshape(1, 2 * HEAD),
    )

    flat = (slot_len, model)
    chunked = (seqs, rows, model)
    places = place * rows + jnp.arange(rows, dtype=jnp.int32)
    live = (places[None, :] < lengths[:, None]).astype(F32)[..., None]
    inputs = tokens.astype(F32)
    out_cot = cotangent.astype(F32) * live
    out_low = [out_cot[b].astype(BF16) for b in range(slots)]
    normal_in = [normed(inputs[b], attn_gain).astype(BF16) for b in range(slots)]

    qkv_own = jnp.concatenate(
        [
            own_columns(query_weight, hq, place),
            own_columns(key_weight, hkv, place),
            own_columns(value_weight, hkv, place),
        ],
        axis=1,
    )
    qkv_weight = lax.all_gather(qkv_own, "fsdp", axis=0, tiled=True)
    start = [
        ("gather", normal_in[0]),
        ("deal", out_weight),
        ("own", gate_weight, up_weight, down_weight),
    ]
    normal_0, out_own, *ffn_own = transfer(start, 1)
    hidden_own = gate_weight.shape[0] // seqs
    part = hidden_own // CHUNKS
    ffn_weights = [lax.all_gather(own, "fsdp", axis=0) for own in ffn_own]

    def leave(mixed):
        return dot(mixed.reshape(slot_len, -1), out_rows).astype(BF16).reshape(chunked)

    def enter_ffn(b, total):
        res = inputs[b] + total
        return res, normed(res, ffn_gain).astype(BF16)

    def heads(b, jobs, number, after):
        return attend(
            sizes, lengths[b : b + 1], normal_full[b], qkv_weight, gains, tables,
            jobs, number, after,
        )

    normal_full = [None] * slots
    cot_full = [None] * slots
    mid_full = [None] * slots
    normal_full[0] = normal_0
    (mixed_0, lse_0, qkv_0), (normal_full[1], out_rows) = heads(
        0, [("gather", normal_in[1]), ("line", out_own)], 2, normal_full[0]
    )
    out_rows = out_rows.reshape(-1, model)
    (mixed_1, lse_1, qkv_1), (total_0,) = heads(1, [("scatter", leave(mixed_0))], 3, mixed_0)
    qkv = [qkv_0, qkv_1]
    log_sums = [lse_0, lse_1]
    attended = [v.reshape(slot_len, hq * HEAD) for v in (mixed_0, mixed_1)]
    res_0, mid_0 = enter_ffn(0, total_0)
    mid_full[0], cot_full[0] = [
        v.reshape(flat)
        for v in transfer([("gather", mid_0), ("gather", out_low[0])], 4, mixed_1)
    ]

    acts = [[None] * slots for _ in range(CHUNKS)]
    pulled = [None] * slots

    def ffn_step(b, c, jobs, number, after):
        (acts[c][b], pulled[b]), results = ffn_both(
            mid_full[b], cot_full[b], ffn_weights[c], pulled[b], c == CHUNKS - 1,
            jobs, number, after,
        )
        return results

    def grad_step(c, jobs, number, after):
        (grads,), results = ffn_grads(
            acts[c], mid_full, cot_full, shards, jobs, number, after
        )
        return grads.reshape(shards, 3 * part, model), results

    def leave_ffn(b, jobs, number, after, true_order=False):
        (out,), results = ffn_down(
            [acts[c][b] for c in range(CHUNKS)], ffn_weights, jobs, number, after, true_order
        )
        return out.reshape(chunked), results

    total_1, full = ffn_step(
        0, 0, [("scatter", leave(mixed_1)), ("gather", out_low[1])], 5, mid_full[0]
    )
    cot_full[1] = full.reshape(flat)
    res_1, mid_1 = enter_ffn(1, total_1)
    hidden_res = [res_0, res_1]
    (full,) = ffn_step(0, 1, [("gather", mid_1)], 6, acts[0][0])
    mid_full[1] = full.reshape(flat)
    (mid_total_0,) = ffn_step(1, 0, [("scatter", pulled[0].reshape(chunked))], 7, acts[1][0])

    def pull_mid(b, total):
        pull, gain_part = normed_back(hidden_res[b], ffn_gain, total)
        cot = out_cot[b] + pull
        return cot, cot.astype(BF16), gain_part

    res_cot_0, low_0, ffn_gain_0 = pull_mid(0, mid_total_0)
    grads_0, (res_full_0,) = grad_step(0, [("gather", low_0)], 8, acts[0][1])
    ffn_sums = [lax.psum_scatter(grads_0, "fsdp", scatter_dimension=0)]
    out_0, _ = leave_ffn(0, [], 0, grads_0)
    (out_total_0,) = ffn_step(1, 1, [("scatter", out_0)], 9, out_0)
    grads_1, (mid_total_1,) = grad_step(
        1, [("scatter", pulled[1].reshape(chunked))], 10, acts[1][1]
    )
    ffn_sums.append(
        lax.psum_scatter(grads_1, "fsdp", scatter_dimension=0)
    )
    res_cot_1, low_1, ffn_gain_1 = pull_mid(1, mid_total_1)
    grad_ffn_gain = ffn_gain_0 + ffn_gain_1

    def back(b, full, jobs, number, after):
        return attend_back(
            sizes, lengths[b : b + 1], qkv[b], full, out_rows, qkv_weight, log_sums[b],
            gains, tables, jobs, number, after,
        )

    (dqkv_0, heads_gain_0, pull_0), (res_full_1,) = back(
        0, res_full_0, [("gather", low_1)], 11, grads_1
    )
    res_full = [v.reshape(flat) for v in (res_full_0, res_full_1)]
    out_grads = sum(dot(attended[b], res_full[b], TN) for b in range(slots)).astype(BF16)
    (dqkv_1, heads_gain_1, pull_1), (in_total_0, ffn_parts_0) = back(
        1, res_full_1, [("scatter", pull_0), ("gather", ffn_sums[0])], 12, out_grads
    )
    head_gain = heads_gain_0 + heads_gain_1
    dqkv = [v.reshape(slot_len, -1) for v in (dqkv_0, dqkv_1)]
    held = model // shards
    piece = out_grads.shape[0] // shards
    blocks = held // piece
    out_grads = jnp.swapaxes(out_grads.reshape(shards, piece, blocks, model // blocks), 1, 2)
    head_sums = jnp.pad(
        (head_gain[:, :HEAD] + head_gain[:, HEAD:]).reshape(2, shards, HEAD // shards),
        ((0, 0), (0, 0), (0, held - HEAD // shards)),
    ).reshape(2, model)
    gain_columns = jnp.stack([grad_ffn_gain, head_sums[0], head_sums[1]], axis=1).astype(BF16)
    attn_grads = jnp.concatenate(
        [
            sum(dot(normal_full[b].reshape(flat), dqkv[b], TN) for b in range(slots)).astype(BF16),
            jnp.pad(gain_columns, ((0, 0), (0, 125))),
            out_grads.reshape(model, model // blocks),
        ],
        axis=1,
    )
    attn_sums = lax.psum_scatter(attn_grads, "fsdp", scatter_dimension=0, tiled=True)
    out_1, (in_total_1, ffn_parts_1) = leave_ffn(
        1, [("scatter", pull_1), ("gather", ffn_sums[1])], 13, attn_grads, True
    )
    out_total_1 = lax.psum_scatter(
        follow(out_1, [attn_sums]), "seq", scatter_dimension=0
    ).astype(F32)
    out_edge = attn_sums.shape[1] - model // blocks
    heads_all, _, out_parts = transfer(
        [("gather", attn_sums[:, :out_edge]), ("spread", attn_sums[:, out_edge:])],
        14,
        in_total_1,
    )
    grad_out = jnp.swapaxes(
        out_parts.reshape(seqs, blocks, piece, model // blocks), 1, 2
    ).reshape(held, model)
    grad_tokens = []
    for b, (in_cot, cot) in enumerate(((in_total_0, res_cot_0), (in_total_1, res_cot_1))):
        pull, _ = normed_back(inputs[b], attn_gain, in_cot)
        grad_tokens.append((cot + pull).astype(BF16))
    output = [
        (live[b] * (hidden_res[b] + total)).astype(BF16)
        for b, total in enumerate((out_total_0, out_total_1))
    ]
    ffn_grad = ()
    for c, parts in enumerate((ffn_parts_0, ffn_parts_1)):
        ffn_grad = place_parts(order, parts.reshape(seqs, 3, part, model), c, ffn_grad)
    ffn_grad = [v.reshape(seqs * hidden_own, model) for v in ffn_grad]

    edge = hq * HEAD
    width = hkv_held * HEAD
    if hkv == hkv_held:
        grad_query, grad_key, grad_value, gain_sums, met = place_heads(
            order, heads_all, edge, width, (query_weight, key_weight, value_weight)
        )
        met = met[:, 0]
    else:
        heads_all = jnp.moveaxis(heads_all, 0, 1).astype(F32)
        last = edge + width
        grad_query = heads_all[..., :edge].reshape(held, query_width)
        grad_key = heads_all[..., edge : edge + hkv * HEAD].reshape(held, kv_width)
        grad_value = heads_all[..., last : last + hkv * HEAD].reshape(held, kv_width)
        gain_sums = jnp.sum(heads_all[..., last + width :], axis=1)
        met = sum(
            jnp.sum(grad * weight.astype(F32), axis=1)
            for grad, weight in (
                (grad_query, query_weight),
                (grad_key, key_weight),
                (grad_value, value_weight),
            )
        )
    grad_attn_gain = met / lax.dynamic_slice_in_dim(attn_gain, shard * held, held, 0)

    return (
        jnp.stack(output),
        jnp.stack(grad_tokens),
        grad_attn_gain,
        grad_query,
        grad_key,
        grad_value,
        gain_sums[: HEAD // shards, 1],
        gain_sums[: HEAD // shards, 2],
        grad_out.astype(F32),
        gain_sums[:, 0],
        ffn_grad[0],
        ffn_grad[1],
        ffn_grad[2],
    )


def solution(mesh):
    return jax.shard_map(
        on_device,
        mesh=mesh,
        in_specs=(
            P("fsdp", "seq", None),
            P("fsdp", "seq", None),
            P("fsdp"),
            P(),
            P("fsdp", None),
            P("fsdp", None),
            P("fsdp", None),
            P(),
            P(),
            P("fsdp", None),
            P(),
            P("fsdp", None),
            P("fsdp", None),
            P("fsdp", None),
        ),
        out_specs=(
            P("fsdp", "seq", None),
            P("fsdp", "seq", None),
            P("fsdp"),
            P("fsdp", None),
            P("fsdp", None),
            P("fsdp", None),
            P("fsdp"),
            P("fsdp"),
            P("fsdp", None),
            P("fsdp"),
            P("fsdp", None),
            P("fsdp", None),
            P("fsdp", None),
        ),
        check_vma=False,
    )
```

```python
import functools

import jax
import jax.numpy as jnp
import numpy as np
from jax import lax
from jax.experimental import pallas as pl
from jax.experimental.pallas import tpu as pltpu
from jax.sharding import PartitionSpec as P

EPSILON = 1e-05
ROPE_BASE = 1000000.0
NEGATIVE = -1e30
F32 = jnp.float32
BF16 = jnp.bfloat16
NN = (((1,), (0,)), ((), ()))
NT = (((1,), (1,)), ((), ()))
TN = (((0,), (0,)), ((), ()))
SMEM = pl.BlockSpec(memory_space=pltpu.SMEM)
VMEM = pl.BlockSpec(memory_space=pltpu.VMEM)
VMEM_LIMIT = 58 << 20
HEAD = 64
BLOCK = 256
CHUNKS = 2
ANY = pl.BlockSpec(memory_space=pl.ANY)


def dot(a, b, dims=NN):
    return lax.dot_general(a, b, dims, preferred_element_type=F32)


def over_one(place):
    return place + 1 - 2 * (place % 2)


def over_two(place):
    return (place + 2) % 4


def send(source, target, device, out_sem, in_sem):
    return pltpu.make_async_remote_copy(
        src_ref=source,
        dst_ref=target,
        send_sem=out_sem,
        recv_sem=in_sem,
        device_id={"seq": device},
        device_id_type=pl.DeviceIdType.MESH,
    )


def gather_job(sources, targets, scratch):
    (source,) = sources
    (target,) = targets
    outs, ins, here, held = scratch
    place = lax.axis_index("seq")
    one, two = over_one(place), over_two(place)
    half = source.shape[0] // 2
    load = pltpu.make_async_copy(source, held, here.at[0])
    store = pltpu.make_async_copy(held, target.at[0], here.at[1])
    first = send(source, target.at[1], one, outs.at[0], ins.at[0])
    second = send(source, target.at[2], two, outs.at[1], ins.at[1])
    top = pl.ds(0, half)
    low = pl.ds(half, half)
    third = send(target.at[2, top], target.at[3, top], one, outs.at[2], ins.at[2])
    fourth = send(target.at[1, low], target.at[3, low], two, outs.at[3], ins.at[3])

    def begin():
        first.start()
        second.start()
        load.start()

    def middle():
        load.wait()
        store.start()
        second.wait_recv()
        third.start()
        first.wait_recv()
        fourth.start()

    def finish():
        third.wait_recv()
        fourth.wait_recv()
        for copy in (first, second, third, fourth):
            copy.wait_send()
        store.wait()

    return no_greeting, begin, middle, finish


def scatter_job(sources, targets, scratch):
    (parts,) = sources
    (total,) = targets
    outs, ins, here, got_one, got_two, kept, own, last, summed = scratch
    place = lax.axis_index("seq")
    one, two = over_one(place), over_two(place)
    half = parts.shape[1] // 2
    top = pl.ds(0, half)
    low = pl.ds(half, half)
    sends = [
        send(parts.at[3, top], got_one.at[0], one, outs.at[0], ins.at[0]),
        send(parts.at[3, low], got_two.at[0], two, outs.at[1], ins.at[1]),
        send(parts.at[1, top], got_one.at[1], one, outs.at[2], ins.at[2]),
        send(parts.at[2, low], got_two.at[1], two, outs.at[3], ins.at[3]),
        send(kept.at[0], last.at[0], two, outs.at[4], ins.at[4]),
        send(kept.at[1], last.at[1], one, outs.at[5], ins.at[5]),
    ]
    loads = [
        pltpu.make_async_copy(parts.at[2, top], kept.at[0], here.at[0]),
        pltpu.make_async_copy(parts.at[1, low], kept.at[1], here.at[1]),
        pltpu.make_async_copy(parts.at[0], own, here.at[2]),
    ]
    store = pltpu.make_async_copy(summed, total, here.at[3])

    def begin():
        for copy in sends[:4]:
            copy.start()
        for copy in loads:
            copy.start()

    def middle():
        for k, got in enumerate((got_one, got_two)):
            loads[k].wait()
            sends[k].wait_recv()
            kept[k] = (kept[k].astype(F32) + got[0].astype(F32)).astype(BF16)
            sends[4 + k].start()

    def finish():
        loads[2].wait()
        for k, got in enumerate((got_one, got_two)):
            sends[2 + k].wait_recv()
            sends[4 + k].wait_recv()
            rows = slice(k * half, (k + 1) * half)
            summed[rows, :] = (
                own[rows, :].astype(F32) + got[1].astype(F32) + last[k].astype(F32)
            )
        store.start()
        for copy in sends:
            copy.wait_send()
        store.wait()

    return no_greeting, begin, middle, finish


def no_greeting(barrier):
    return 0


def nothing():
    pass


def greet(barrier, device):
    pl.semaphore_signal(
        barrier, inc=1, device_id=device, device_id_type=pl.DeviceIdType.MESH
    )


def deal_job(sources, targets, scratch):
    (source,) = sources
    (target,) = targets
    outs, ins, here = scratch
    rows = target.shape[0]
    count = source.shape[0] // rows
    place = lax.axis_index("seq")
    shard = lax.axis_index("fsdp")
    per = lax.axis_size("fsdp") // count
    part = shard % per
    is_source = shard // per == place
    to_self = jnp.logical_and(is_source, shard // count == part)
    origin = place * per + shard // count

    def copy(j):
        return pltpu.make_async_remote_copy(
            src_ref=source.at[pl.ds(j * rows, rows)],
            dst_ref=target,
            send_sem=outs.at[j],
            recv_sem=ins.at[0],
            device_id={"fsdp": part * count + j},
            device_id_type=pl.DeviceIdType.MESH,
        )

    def local(j):
        return pltpu.make_async_copy(source.at[pl.ds(j * rows, rows)], target, here.at[0])

    def greeting(barrier):
        pl.when(origin != shard)(lambda: greet(barrier, {"fsdp": origin}))
        return jnp.where(is_source, count, 0) - jnp.where(to_self, 1, 0)

    def each(act_remote, act_local):
        for j in range(count):
            mine = part * count + j == shard
            pl.when(jnp.logical_and(is_source, mine))(lambda j=j: act_local(local(j)))
            pl.when(jnp.logical_and(is_source, jnp.logical_not(mine)))(
                lambda j=j: act_remote(copy(j))
            )

    def begin():
        each(lambda c: c.start(), lambda c: c.start())

    def finish():
        each(lambda c: c.wait_send(), lambda c: c.wait())
        pl.when(origin != shard)(lambda: copy(0).wait_recv())

    return greeting, begin, nothing, finish


def line_job(sources, targets, scratch):
    (source,) = sources
    (target,) = targets
    far_out, far_in, near_out, near_in, here = scratch
    shards = target.shape[0]
    steps = shards // 2
    shard = lax.axis_index("fsdp")
    near = shard + 1 - 2 * (shard % 2)

    def away(start, k):
        return (start + 2 * k) % shards

    def send_line(origin, spot, device, out_sem, in_sem):
        return pltpu.make_async_remote_copy(
            src_ref=origin,
            dst_ref=target.at[spot],
            send_sem=out_sem,
            recv_sem=in_sem,
            device_id={"fsdp": device},
            device_id_type=pl.DeviceIdType.MESH,
        )

    own = pltpu.make_async_copy(source, target.at[shard], here.at[0])
    far = [
        send_line(source, shard, away(shard, k), far_out.at[k - 1], far_in.at[k - 1])
        for k in range(1, steps)
    ]
    far_came = [
        send_line(
            source, away(shard, steps - k), away(shard, k), far_out.at[k - 1], far_in.at[k - 1]
        )
        for k in range(1, steps)
    ]
    held = [shard] + [away(shard, steps - k) for k in range(1, steps)]
    close = [
        send_line(target.at[spot] if k else source, spot, near, near_out.at[k], near_in.at[k])
        for k, spot in enumerate(held)
    ]
    close_came = [
        send_line(source, away(near, steps - k) if k else near, near, near_out.at[k], near_in.at[k])
        for k in range(steps)
    ]

    def greeting(barrier):
        for k in range(1, steps):
            greet(barrier, {"fsdp": away(shard, k)})
        greet(barrier, {"fsdp": near})
        return steps

    def begin():
        own.start()
        for copy in far:
            copy.start()
        close[0].start()

    def finish():
        for k in range(1, steps):
            far_came[k - 1].wait_recv()
            close[k].start()
        for copy in close_came:
            copy.wait_recv()
        for copy in far + close:
            copy.wait_send()
        own.wait()

    return greeting, begin, nothing, finish


def spread_job(sources, targets, scratch):
    (source,) = sources
    gathered, target = targets
    *first, z_outs, z_ins, z_here = scratch
    _, begin_gather, middle_gather, finish_gather = gather_job(sources, [gathered], first)
    count = gathered.shape[0]
    place = lax.axis_index("seq")
    shard = lax.axis_index("fsdp")
    per = lax.axis_size("fsdp") // count
    piece = shard % count

    def owner(j):
        return true_chunk(place, j, count) * per + shard // count

    def chunk(j):
        return gathered.at[j] if j else source

    def copy(j):
        return pltpu.make_async_remote_copy(
            src_ref=chunk(j),
            dst_ref=target.at[piece],
            send_sem=z_outs.at[j],
            recv_sem=z_ins.at[piece],
            device_id={"fsdp": owner(j)},
            device_id_type=pl.DeviceIdType.MESH,
        )

    def arrival(p):
        return pltpu.make_async_remote_copy(
            src_ref=source,
            dst_ref=target.at[p],
            send_sem=z_outs.at[0],
            recv_sem=z_ins.at[p],
            device_id={"fsdp": owner(0)},
            device_id_type=pl.DeviceIdType.MESH,
        )

    def local(j):
        return pltpu.make_async_copy(chunk(j), target.at[piece], z_here.at[0])

    def origin(p):
        return (shard % per) * count + p

    def start(j):
        pl.when(owner(j) != shard)(lambda: copy(j).start())
        pl.when(owner(j) == shard)(lambda: local(j).start())

    def greeting(barrier):
        for p in range(count):
            pl.when(origin(p) != shard)(lambda p=p: greet(barrier, {"fsdp": origin(p)}))
        return jnp.where(shard % per == shard // count, count - 1, count)

    def begin():
        begin_gather()
        start(0)

    def middle():
        middle_gather()
        start(1)
        start(2)

    def finish():
        finish_gather()
        start(3)
        for j in range(count):
            pl.when(owner(j) != shard)(lambda j=j: copy(j).wait_send())
            pl.when(owner(j) == shard)(lambda j=j: local(j).wait())
        for p in range(count):
            pl.when(origin(p) != shard)(lambda p=p: arrival(p).wait_recv())

    return greeting, begin, middle, finish


def own_job(sources, targets, scratch):
    loaded, stored, held = scratch
    place = lax.axis_index("seq")
    count = lax.axis_size("seq")
    part = targets[0].shape[1]
    loads = []
    stores = []
    for c, target in enumerate(targets):
        for k, source in enumerate(sources):
            start = place * (source.shape[0] // count) + c * part
            spot = pl.ds(pl.multiple_of(start, part), part)
            n = c * len(sources) + k
            loads.append(pltpu.make_async_copy(source.at[spot], held.at[n], loaded.at[n]))
            stores.append(pltpu.make_async_copy(held.at[n], target.at[k], stored.at[n]))

    def begin():
        for load in loads:
            load.start()

    def middle():
        for load, store in zip(loads, stores):
            load.wait()
            store.start()

    def finish():
        for store in stores:
            store.wait()

    return no_greeting, begin, middle, finish


MAKERS = {
    "gather": gather_job,
    "scatter": scatter_job,
    "deal": deal_job,
    "spread": spread_job,
    "line": line_job,
    "own": own_job,
}


def job_scratch(job):
    kind, *arrays = job
    if kind == "scatter":
        _, rows, width = arrays[0].shape
        halves = pltpu.VMEM((2, rows // 2, width), BF16)
        return [
            pltpu.SemaphoreType.DMA((6,)),
            pltpu.SemaphoreType.DMA((6,)),
            pltpu.SemaphoreType.DMA((4,)),
            halves,
            halves,
            halves,
            pltpu.VMEM((rows, width), BF16),
            halves,
            pltpu.VMEM((rows, width), F32),
        ]
    if kind == "own":
        count = CHUNKS * len(arrays)
        rows, width = arrays[0].shape
        part = rows // lax.axis_size("seq") // CHUNKS
        return [
            pltpu.SemaphoreType.DMA((count,)),
            pltpu.SemaphoreType.DMA((count,)),
            pltpu.VMEM((count, part, width), BF16),
        ]
    moves = [
        pltpu.SemaphoreType.DMA((4,)),
        pltpu.SemaphoreType.DMA((4,)),
        pltpu.SemaphoreType.DMA((2,)),
    ]
    if kind == "deal":
        return moves
    if kind == "line":
        steps = lax.axis_size("fsdp") // 2
        return [pltpu.SemaphoreType.DMA((steps,))] * 4 + [pltpu.SemaphoreType.DMA((1,))]
    moves.append(pltpu.VMEM(arrays[0].shape, BF16))
    if kind == "spread":
        moves += [
            pltpu.SemaphoreType.DMA((4,)),
            pltpu.SemaphoreType.DMA((4,)),
            pltpu.SemaphoreType.DMA((1,)),
        ]
    return moves


def job_results(job):
    kind, *arrays = job
    shape = arrays[0].shape
    if kind == "gather":
        return [jax.ShapeDtypeStruct((4,) + shape, BF16)]
    if kind == "scatter":
        return [jax.ShapeDtypeStruct(shape[1:], F32)]
    if kind == "deal":
        return [jax.ShapeDtypeStruct((shape[0] // 4,) + shape[1:], BF16)]
    if kind == "spread":
        return [jax.ShapeDtypeStruct((4,) + shape, BF16)] * 2
    if kind == "line":
        return [jax.ShapeDtypeStruct((lax.axis_size("fsdp"),) + shape, BF16)]
    part = shape[0] // lax.axis_size("seq") // CHUNKS
    return [jax.ShapeDtypeStruct((len(arrays), part) + shape[1:], BF16)] * CHUNKS


def plain_job(job):
    kind, *arrays = job
    seqs = lax.axis_size("seq")
    shards = lax.axis_size("fsdp")
    per = shards // seqs
    ends = [(s, h, s * shards + s * per + h) for s in range(seqs) for h in range(per)]
    if kind == "gather":
        return [lax.all_gather(arrays[0], "seq", axis=0)]
    if kind == "scatter":
        return [lax.psum_scatter(arrays[0], "seq", scatter_dimension=0).astype(F32)]
    if kind == "deal":
        rows = arrays[0].shape[0] // seqs
        total = None
        for j in range(seqs):
            moves = [(end, s * shards + h * seqs + j) for s, h, end in ends]
            got = lax.ppermute(arrays[0][j * rows : (j + 1) * rows], ("seq", "fsdp"), moves)
            total = got if total is None else total + got
        return [total]
    if kind == "line":
        return [lax.all_gather(arrays[0], "fsdp", axis=0)]
    if kind == "spread":
        gathered = lax.all_gather(arrays[0], "seq", axis=0)
        pieces = []
        for p in range(seqs):
            total = None
            for q in range(seqs):
                moves = [
                    (s * shards + h * seqs + p, s * shards + q * per + h)
                    for s in range(seqs)
                    for h in range(per)
                ]
                got = lax.ppermute(gathered[q], ("seq", "fsdp"), moves)
                total = got if total is None else total + got
            pieces.append(total)
        return [gathered, jnp.stack(pieces)]
    own_rows = arrays[0].shape[0] // seqs
    part = own_rows // CHUNKS
    start = lax.axis_index("seq") * own_rows
    return [
        jnp.stack([lax.dynamic_slice_in_dim(w, start + c * part, part, 0) for w in arrays])
        for c in range(CHUNKS)
    ]


def meet(greetings):
    place = lax.axis_index("seq")
    barrier = pltpu.get_barrier_semaphore()
    for device in (over_one(place), over_two(place)):
        greet(barrier, {"seq": device})
    peers = 2
    for greeting in greetings:
        peers = peers + greeting(barrier)
    pl.semaphore_wait(barrier, peers)


def call(
    body, operands, in_specs, out_shape, out_specs, jobs, number, after=None,
    grid=(), scratch=(), cost=None, name=None, late=(),
):
    plain = lax.axis_size("seq") != 4
    results = [v for job in jobs for v in plain_job(job)] if plain else []
    inside = [] if plain else jobs
    extra = [] if after is None else [after]
    job_shapes = [job_scratch(job) for job in inside]
    job_outs = [job_results(job) for job in inside]
    n_in = len(operands)
    n_out = len(out_shape)

    def kernel(*refs):
        refs = list(refs)

        def take(count):
            taken, refs[:] = refs[:count], refs[count:]
            return taken

        ins = take(n_in)
        take(len(extra))
        sources = [take(len(job) - 1) for job in inside]
        outs = take(n_out)
        targets = [take(len(shapes)) for shapes in job_outs]
        held = take(len(scratch))
        loaded = take(len(late))
        marks = take(1) if late else []
        loads = [
            pltpu.make_async_copy(ins[n], ref, marks[0].at[k])
            for k, (n, ref) in enumerate(zip(late, loaded))
        ]
        for n, ref in zip(late, loaded):
            ins[n] = ref
        phases = [
            MAKERS[job[0]](source, target, take(len(shapes)))
            for job, source, target, shapes in zip(inside, sources, targets, job_shapes)
        ]

        def hook(k):
            if k == 0 and phases:
                meet([phase[0] for phase in phases])
            for phase in phases:
                phase[k + 1]()
            if k == 0:
                for load in loads:
                    load.start()
                for load in loads:
                    load.wait()

        body(hook, ins, outs, held)

    given = {}
    if inside:
        given = {"collective_id": number, "has_side_effects": True}
    arrays = [array for job in inside for array in job[1:]]
    in_specs = [ANY if n in late else spec for n, spec in enumerate(in_specs)]
    late_shapes = [pltpu.VMEM(operands[n].shape, operands[n].dtype) for n in late]
    if late:
        late_shapes.append(pltpu.SemaphoreType.DMA((len(late),)))
    shapes = [shape for shapes in job_outs for shape in shapes]
    made = pl.pallas_call(
        kernel,
        grid=grid,
        out_shape=tuple(out_shape) + tuple(shapes),
        in_specs=list(in_specs) + [ANY] * (len(extra) + len(arrays)),
        out_specs=tuple(out_specs) + (ANY,) * len(shapes),
        scratch_shapes=list(scratch)
        + late_shapes
        + [shape for shapes in job_shapes for shape in shapes],
        compiler_params=pltpu.CompilerParams(vmem_limit_bytes=VMEM_LIMIT, **given),
        cost_estimate=cost,
        name=name,
    )(*operands, *extra, *arrays)
    return list(made[:n_out]), list(made[n_out:]) + results


def transfer(jobs, number, after=None):
    if lax.axis_size("seq") != 4:
        return [v for job in jobs for v in plain_job(job)]

    def body(hook, ins, outs, held):
        for k in range(3):
            hook(k)

    return call(body, [], [], [], [], jobs, number, after, name="transfer")[1]


def partner(v):
    lane = lax.broadcasted_iota(jnp.int32, v.shape, 1)
    return jnp.where(lane % HEAD < HEAD // 2, pltpu.roll(v, 96, 1), pltpu.roll(v, 32, 1))


def head_mean(v, ones):
    high = v.astype(BF16)
    rest = (v - high.astype(F32)).astype(BF16)
    return dot(high, ones) + dot(rest, ones)


def true_chunk(place, c, count):
    if count != 4:
        return c
    low = 1 - place % 2 if c % 2 else place % 2
    high = 1 - place // 2 if c // 2 else place // 2
    return low + 2 * high


def prepare_heads(sizes, place, qkv_ref, qg_ref, kg_ref, cos_ref, sin_ref, ones, q_s, k_s, v_s):
    hq, hkv, _ = sizes
    seqs, rows_in, _ = qkv_ref.shape
    for c in range(seqs):
        j = true_chunk(place, c, seqs)
        rows = slice(c * rows_in, (c + 1) * rows_in)
        cos = cos_ref[rows, :]
        sin = sin_ref[rows, :]
        for p in range((hq + hkv) // 2):
            is_query = p < hq // 2
            x = qkv_ref[j, :, p * 128 : (p + 1) * 128].astype(F32)
            gain = qg_ref[...] * HEAD**-0.5 if is_query else kg_ref[...]
            y = x * lax.rsqrt(head_mean(x * x, ones) + EPSILON) * gain
            y = (y * cos + partner(y) * sin).astype(BF16)
            for t in range(2):
                part = y[:, t * HEAD : (t + 1) * HEAD]
                if is_query:
                    q_s[2 * p + t, rows, :] = part
                else:
                    k_s[2 * p - hq + t, rows, :] = part
        for t in range(hkv):
            start = (hq + hkv + t) * HEAD
            v_s[t, rows, :] = qkv_ref[j, :, start : start + HEAD]


def allowed_keys(block, first, keys, length):
    bound = jnp.minimum(first + lax.broadcasted_iota(jnp.int32, (block, 1), 0), length - 1)
    return lax.broadcasted_iota(jnp.int32, (block, keys), 1) <= bound


def attend_kernel(sizes, hook, ins, outs, held):
    len_ref, normal_ref, weight_ref, qg_ref, kg_ref, cos_ref, sin_ref, ones_ref = ins
    out_ref, lse_ref, qkv_ref = outs
    q_s, k_s, v_s, o_s = held
    hook(0)

    @pl.loop(0, qkv_ref.shape[0])
    def _(j):
        qkv_ref[j] = dot(normal_ref[j], weight_ref[...]).astype(BF16)

    hq, hkv, group = sizes
    seqs, rows_in, _ = qkv_ref.shape
    place = lax.axis_index("seq")
    prepare_heads(
        sizes, place, qkv_ref, qg_ref, kg_ref, cos_ref, sin_ref, ones_ref[...], q_s, k_s, v_s
    )
    for i in range(seqs * rows_in // BLOCK):
        keys = (i + 1) * BLOCK
        rows = slice(i * BLOCK, (i + 1) * BLOCK)
        keep = allowed_keys(BLOCK, i * BLOCK, keys, len_ref[0])

        def one_head(h, _):
            kv = h // group
            scores = dot(q_s[h, rows, :], k_s[kv, :keys, :], NT)
            scores = jnp.where(keep, scores, NEGATIVE)
            highest = jnp.max(scores, axis=1, keepdims=True)
            shifted = jnp.exp(scores - highest)
            total = jnp.sum(shifted, axis=1, keepdims=True)
            mixed = dot(shifted.astype(BF16), v_s[kv, :keys, :]) / total
            o_s[h, rows, :] = mixed.astype(BF16)
            lse_ref[h, rows, :] = highest + jnp.log(total)
            return 0

        lax.fori_loop(0, hq, one_head, 0, unroll=min(4, hq))
        if i == seqs * rows_in // BLOCK - 2:
            hook(1)
    for c in range(seqs):
        j = true_chunk(place, c, seqs)
        rows = slice(c * rows_in, (c + 1) * rows_in)
        for p in range(hq // 2):
            out_ref[j, :, p * 128 : (p + 1) * 128] = jnp.concatenate(
                [o_s[2 * p, rows, :], o_s[2 * p + 1, rows, :]], axis=1
            )
    hook(2)


def out_weight_grads(grads_ref, shards, slots):
    width = slots[0][0].shape[-1]
    model = slots[0][1].shape[-1]
    tile = min(256, width)
    piece = width // shards
    held = model // shards
    blocks = held // piece
    columns = model // blocks
    for t in range(width // tile):
        total = None
        for mixed_ref, res_ref in slots:
            rows = mixed_ref.shape[0] * mixed_ref.shape[1]
            mixed = mixed_ref[:, :, t * tile : (t + 1) * tile].reshape(rows, tile)
            term = dot(mixed, res_ref[...].reshape(rows, model), TN)
            total = term if total is None else total + term
        total = total.astype(BF16)
        for p in range(tile // piece):
            first = (t * (tile // piece) + p) * held
            for c in range(blocks):
                grads_ref[first + c * piece : first + (c + 1) * piece, :] = total[
                    p * piece : (p + 1) * piece, c * columns : (c + 1) * columns
                ]


def attend_back_kernel(sizes, shards, hook, ins, outs, held):
    (
        len_ref, qkv_ref, res_ref, out_w_ref, qkv_w_ref, lse_ref,
        qg_ref, kg_ref, cos_ref, sin_ref, ones_ref, *others,
    ) = ins
    dqkv_ref, dgain_ref, pull_ref, *out_grads = outs
    q_s, k_s, v_s, cot_s, dq_s, dk_s, dv_s = held
    hook(0)
    hq, hkv, group = sizes
    seqs, rows_in, _ = qkv_ref.shape
    place = lax.axis_index("seq")
    ones = ones_ref[...]
    prepare_heads(sizes, place, qkv_ref, qg_ref, kg_ref, cos_ref, sin_ref, ones, q_s, k_s, v_s)
    for c in range(seqs):
        j = true_chunk(place, c, seqs)
        cots = dot(res_ref[j], out_w_ref[...], NT).astype(BF16)
        for h in range(hq):
            cot_s[h, c * rows_in : (c + 1) * rows_in, :] = cots[:, h * HEAD : (h + 1) * HEAD]
    dk_s[...] = jnp.zeros_like(dk_s)
    dv_s[...] = jnp.zeros_like(dv_s)
    for i in range(seqs * rows_in // BLOCK):
        keys = (i + 1) * BLOCK
        rows = slice(i * BLOCK, (i + 1) * BLOCK)
        keep = allowed_keys(BLOCK, i * BLOCK, keys, len_ref[0])

        def one_head(h, _):
            kv = h // group
            q = q_s[h, rows, :]
            cot = cot_s[h, rows, :]
            k = k_s[kv, :keys, :]
            scores = jnp.where(keep, dot(q, k, NT), NEGATIVE)
            probs = jnp.exp(scores - lse_ref[h, rows, :])
            prob_cot = dot(cot, v_s[kv, :keys, :], NT)
            inner = jnp.sum(probs * prob_cot, axis=1, keepdims=True)
            score_cot = (probs * (prob_cot - inner)).astype(BF16)
            dq_s[h, rows, :] = dot(score_cot, k) * HEAD**-0.5
            dk_s[kv, :keys, :] += dot(score_cot, q, TN)
            dv_s[kv, :keys, :] += dot(probs.astype(BF16), cot, TN)
            return 0

        lax.fori_loop(0, hq, one_head, 0, unroll=min(4, hq))
        if i == seqs * rows_in // BLOCK - 2:
            for grads_ref in out_grads:
                before_ref, here_ref, res_before_ref = others
                out_weight_grads(
                    grads_ref, shards, ((before_ref, res_before_ref), (here_ref, res_ref))
                )
            hook(1)
    gain_sums = [jnp.zeros((1, 128), F32), jnp.zeros((1, 128), F32)]
    for c in range(seqs):
        j = true_chunk(place, c, seqs)
        rows = slice(c * rows_in, (c + 1) * rows_in)
        cos = cos_ref[rows, :]
        sin = sin_ref[rows, :]
        for p in range((hq + hkv) // 2):
            is_query = p < hq // 2
            x = qkv_ref[j, :, p * 128 : (p + 1) * 128].astype(F32)
            gain = qg_ref[...] if is_query else kg_ref[...]
            source, first = (dq_s, 2 * p) if is_query else (dk_s, 2 * p - hq)
            turned = jnp.concatenate([source[first, rows, :], source[first + 1, rows, :]], axis=1)
            scale = lax.rsqrt(head_mean(x * x, ones) + EPSILON)
            straight = turned * cos + partner(turned * sin)
            unit = x * scale
            which = 0 if is_query else 1
            gain_sums[which] += jnp.sum(straight * unit, axis=0, keepdims=True)
            pulled = gain * straight
            dx = scale * (pulled - unit * head_mean(unit * pulled, ones))
            dqkv_ref[j, :, p * 128 : (p + 1) * 128] = dx.astype(BF16)
        for p in range(hkv // 2):
            start = (hq + hkv) * HEAD + p * 128
            dqkv_ref[j, :, start : start + 128] = jnp.concatenate(
                [dv_s[2 * p, rows, :], dv_s[2 * p + 1, rows, :]], axis=1
            ).astype(BF16)
    dgain_ref[0:1, :] = gain_sums[0]
    dgain_ref[1:2, :] = gain_sums[1]

    @pl.loop(0, seqs)
    def _(j):
        pull_ref[j] = dot(dqkv_ref[j], qkv_w_ref[...], NT).astype(BF16)

    hook(2)


def position_tables(length):
    places = np.arange(length, dtype=np.float32)
    half = HEAD // 2
    freqs = np.float32(ROPE_BASE) ** (-(np.arange(half, dtype=np.float32) * 2.0) / HEAD)
    angles = places[:, None] * freqs.astype(np.float32)[None, :]
    cos = np.cos(angles).astype(np.float32)
    sin = np.sin(angles).astype(np.float32)
    ones = np.kron(np.eye(2), np.ones((HEAD, HEAD)) / HEAD)
    return (
        jnp.asarray(np.concatenate([cos] * 4, axis=1)),
        jnp.asarray(np.concatenate([-sin, sin, -sin, sin], axis=1)),
        jnp.asarray(ones, dtype=BF16),
    )


def attend(sizes, length, normal, weight, gains, tables, jobs, number, after):
    seqs, rows_in, _ = normal.shape
    hq, hkv, _ = sizes
    slot = seqs * rows_in
    return call(
        functools.partial(attend_kernel, sizes),
        [length, normal, weight, *gains, *tables],
        [SMEM] + [VMEM] * 7,
        [
            jax.ShapeDtypeStruct((seqs, rows_in, hq * HEAD), BF16),
            jax.ShapeDtypeStruct((hq, slot, 1), F32),
            jax.ShapeDtypeStruct((seqs, rows_in, weight.shape[1]), BF16),
        ],
        [VMEM, VMEM, VMEM],
        jobs,
        number,
        after,
        scratch=[
            pltpu.VMEM((hq, slot, HEAD), BF16),
            pltpu.VMEM((hkv, slot, HEAD), BF16),
            pltpu.VMEM((hkv, slot, HEAD), BF16),
            pltpu.VMEM((hq, slot, HEAD), BF16),
        ],
        cost=pl.CostEstimate(
            flops=56 * hq * slot * slot * HEAD, bytes_accessed=1 << 23, transcendentals=0
        ),
        name="attend",
        late=(1, 2),
    )


def attend_back(
    sizes, length, qkv, res, out_w, qkv_w, lse, gains, tables, jobs, number, after, others=()
):
    seqs, rows_in, width = qkv.shape
    hq, hkv, _ = sizes
    slot = seqs * rows_in
    shards = lax.axis_size("fsdp")
    model = res.shape[-1]
    columns = hq * HEAD // shards * model // (model // shards)
    return call(
        functools.partial(attend_back_kernel, sizes, shards),
        [length, qkv, res, out_w, qkv_w, lse, *gains, *tables, *others],
        [SMEM] + [VMEM] * (10 + len(others)),
        [
            jax.ShapeDtypeStruct((seqs, rows_in, width), BF16),
            jax.ShapeDtypeStruct((2, 128), F32),
            jax.ShapeDtypeStruct(res.shape, BF16),
        ]
        + [jax.ShapeDtypeStruct((model, columns), BF16)] * bool(others),
        [VMEM, VMEM, VMEM] + [VMEM] * bool(others),
        jobs,
        number,
        after,
        scratch=[
            pltpu.VMEM((hq, slot, HEAD), BF16),
            pltpu.VMEM((hkv, slot, HEAD), BF16),
            pltpu.VMEM((hkv, slot, HEAD), BF16),
            pltpu.VMEM((hq, slot, HEAD), BF16),
            pltpu.VMEM((hq, slot, HEAD), F32),
            pltpu.VMEM((hkv, slot, HEAD), F32),
            pltpu.VMEM((hkv, slot, HEAD), F32),
        ],
        cost=pl.CostEstimate(
            flops=88 * hq * slot * slot * HEAD, bytes_accessed=1 << 23, transcendentals=0
        ),
        name="attend_back",
        late=(1, 2, 3, 4, 5) + tuple(range(11, 11 + len(others))),
    )


def hooked(hook, step, steps, work):
    pl.when(step == 0)(lambda: hook(0))
    work(lambda: pl.when(step == (3 * steps) // 5)(lambda: hook(1)))
    pl.when(step == steps - 1)(lambda: hook(2))


def ffn_kernel(steps, hook, ins, outs, held):
    step = pl.program_id(0)
    weights_ref, loaded = held
    loads = [
        pltpu.make_async_copy(ins[2].at[:, k], weights_ref.at[k], loaded.at[k]) for k in range(3)
    ]

    def first(act):
        pl.when(step == 0)(act)

    def work(late):
        for load in loads:
            first(load.start)
        ffn_tile(late, first, loads, *ins[:2], weights_ref, ins[3:], *outs)

    hooked(hook, step, steps, work)


def ffn_tile(late, first, loads, mid_ref, cot_ref, weights_ref, sums, acts_ref, pull_ref):
    model = mid_ref.shape[-1]
    hidden = acts_ref.shape[-1]
    whole = (hidden, model)
    mid = mid_ref[...]
    first(loads[0].wait)
    gate = dot(mid, weights_ref[0].reshape(whole), NT)
    first(loads[1].wait)
    up = dot(mid, weights_ref[1].reshape(whole), NT)
    first(loads[2].wait)
    mids_cot = dot(cot_ref[...], weights_ref[2].reshape(whole), NT)
    late()
    sigmoid = jax.nn.sigmoid(gate)
    active = gate * sigmoid
    gate_cot = (mids_cot * up * sigmoid * (1.0 + gate * (1.0 - sigmoid))).astype(BF16)
    up_cot = (mids_cot * active).astype(BF16)
    acts_ref[0] = gate_cot
    acts_ref[1] = up_cot
    acts_ref[2] = (active * up).astype(BF16)
    pulled = dot(gate_cot, weights_ref[0].reshape(whole)) + dot(
        up_cot, weights_ref[1].reshape(whole)
    )
    for sum_ref in sums:
        pulled = pulled + sum_ref[...]
    pull_ref[...] = pulled.astype(pull_ref.dtype)


def ffn_both(mid, cot, weights, summed, last, jobs, number, after):
    tokens, model = mid.shape
    shards, _, part, _ = weights.shape
    hidden = shards * part
    tile = min(256, tokens)

    row_spec = pl.BlockSpec((tile, model), lambda i: (i, 0))
    extra = () if summed is None else (summed,)
    return call(
        functools.partial(ffn_kernel, tokens // tile),
        [mid, cot, weights, *extra],
        [row_spec, row_spec, ANY] + [row_spec] * len(extra),
        [
            jax.ShapeDtypeStruct((3, tokens, hidden), BF16),
            jax.ShapeDtypeStruct((tokens, model), BF16 if last else F32),
        ],
        [pl.BlockSpec((3, tile, hidden), lambda i: (0, i, 0)), row_spec],
        jobs,
        number,
        after,
        grid=(tokens // tile,),
        scratch=[
            pltpu.VMEM((3, shards, part, model), BF16),
            pltpu.SemaphoreType.DMA((3,)),
        ],
        cost=pl.CostEstimate(
            flops=16 * tokens * model * hidden,
            bytes_accessed=4 * tokens * model + 6 * hidden * model,
            transcendentals=0,
        ),
        name="ffn_both",
    )


def ffn_grad_kernel(slots, tiles, hook, ins, outs, held):
    acts = ins[:slots]
    others = ins[slots:]
    (out_ref,) = outs
    rows_ref, loaded = held
    kind = pl.program_id(0)
    step = kind * tiles + pl.program_id(1)
    loads = [
        pltpu.make_async_copy(other, rows_ref.at[k], loaded.at[k])
        for k, other in enumerate(others)
    ]

    def store(first):
        total = None
        for k, act in enumerate(acts):
            term = dot(act[0], rows_ref[first + k], TN)
            total = term if total is None else total + term
        out_ref[...] = total.astype(BF16).reshape(out_ref.shape)

    def work(late):
        for k, load in enumerate(loads):
            pl.when(step == 0)(load.start)
        for k, load in enumerate(loads):
            pl.when(step == (0 if k < slots else 2 * tiles))(load.wait)
        late()
        pl.when(kind < 2)(lambda: store(0))
        pl.when(kind == 2)(lambda: store(slots))

    hooked(hook, step, 3 * tiles, work)


def ffn_grads(acts, mids, cots, shards, jobs, number, after):
    slots = len(acts)
    _, tokens, hidden = acts[0].shape
    model = mids[0].shape[-1]
    part = hidden // shards
    tile = 256
    per = tile // part
    return call(
        functools.partial(ffn_grad_kernel, slots, hidden // tile),
        [*acts, *mids, *cots],
        [pl.BlockSpec((1, tokens, tile), lambda k, i: (k, 0, i))] * slots
        + [ANY] * (2 * slots),
        [jax.ShapeDtypeStruct((shards, 3, part, model), BF16)],
        [pl.BlockSpec((per, 1, part, model), lambda k, i: (i, k, 0, 0))],
        jobs,
        number,
        after,
        grid=(3, hidden // tile),
        scratch=[
            pltpu.VMEM((2 * slots, tokens, model), BF16),
            pltpu.SemaphoreType.DMA((2 * slots,)),
        ],
        cost=pl.CostEstimate(
            flops=9 * slots * tokens * model * hidden,
            bytes_accessed=4 * slots * tokens * model,
            transcendentals=0,
        ),
        name="ffn_grads",
    )


def ffn_down_kernel(chunks, steps, hook, ins, outs, held):
    acts = ins[:chunks]
    downs = ins[chunks:]
    (out_ref,) = outs

    def work(late):
        late()
        total = None
        for act, down in zip(acts, downs):
            hidden = act.shape[-1]
            term = dot(act[0], down[...].reshape(hidden, down.shape[-1]))
            total = term if total is None else total + term
        out_ref[...] = total.astype(BF16)

    hooked(hook, pl.program_id(0), steps, work)


def ffn_down(acts, weights, jobs, number, after, true_order=False):
    chunks = len(acts)
    _, tokens, hidden = acts[0].shape
    shards, _, part, model = weights[0].shape
    tile = min(256, tokens)
    def spot(i):
        if not true_order or lax.axis_size("seq") != 4:
            return i
        place = lax.axis_index("seq")
        low = (place % 2 + i % 2) % 2
        high = (place // 2 + i // 2) % 2
        return low + 2 * high

    act_spec = pl.BlockSpec((1, tile, hidden), lambda i: (2, i, 0))
    down_spec = pl.BlockSpec(
        (shards, 1, part, model),
        lambda i: (0, 2, 0, 0),
        pipeline_mode=pl.Buffered(buffer_count=1),
    )
    return call(
        functools.partial(ffn_down_kernel, chunks, tokens // tile),
        [*acts, *weights],
        [act_spec] * chunks + [down_spec] * chunks,
        [jax.ShapeDtypeStruct((tokens, model), BF16)],
        [pl.BlockSpec((tile, model), lambda i: (spot(i), 0))],
        jobs,
        number,
        after,
        grid=(tokens // tile,),
        cost=pl.CostEstimate(
            flops=4 * chunks * tokens * model * hidden,
            bytes_accessed=chunks * hidden * (tokens + model) * 2,
            transcendentals=0,
        ),
        name="ffn_down",
    )


def place_kernel(place_ref, parts_ref, *refs):
    for kind, out_ref in enumerate(refs[-3:]):
        out_ref[0, 0] = parts_ref[0, kind].astype(F32)


def place_parts(place, parts, chunk, held):
    seqs, _, part, model = parts.shape
    out = jax.ShapeDtypeStruct((seqs, CHUNKS, part, model), F32)
    out_spec = pl.BlockSpec(
        (1, 1, part, model), lambda j, at: (jnp.bitwise_xor(at[0], j), chunk, 0, 0)
    )
    return pl.pallas_call(
        place_kernel,
        out_shape=(out,) * 3,
        grid_spec=pltpu.PrefetchScalarGridSpec(
            num_scalar_prefetch=1,
            grid=(seqs,),
            in_specs=[pl.BlockSpec((1, 3, part, model), lambda j, at: (j, 0, 0, 0))]
            + [ANY] * len(held),
            out_specs=(out_spec,) * 3,
        ),
        input_output_aliases={2 + k: k for k in range(len(held))},
        compiler_params=pltpu.CompilerParams(vmem_limit_bytes=VMEM_LIMIT),
        cost_estimate=pl.CostEstimate(
            flops=0, bytes_accessed=18 * seqs * part * model, transcendentals=0
        ),
        name="place_parts",
    )(place, parts, *held)


def place_heads_kernel(
    place_ref, parts_ref, query_w_ref, key_w_ref, value_w_ref,
    query_ref, key_ref, value_ref, rest_ref, met_ref,
):
    edge = query_ref.shape[1]
    width = key_ref.shape[1]
    part = parts_ref[0].astype(F32)
    query_ref[...] = part[:, :edge]
    key_ref[...] = part[:, edge : edge + width]
    value_ref[...] = part[:, edge + width : edge + 2 * width]
    rest = part[:, edge + 2 * width :]
    met = jnp.zeros_like(met_ref)
    for grad_ref, weight_ref in (
        (query_ref, query_w_ref),
        (key_ref, key_w_ref),
        (value_ref, value_w_ref),
    ):
        product = grad_ref[...] * weight_ref[...].astype(F32)
        met = met + jnp.sum(product, axis=1, keepdims=True)

    @pl.when(pl.program_id(0) == 0)
    def _():
        rest_ref[...] = rest
        met_ref[...] = met

    @pl.when(pl.program_id(0) > 0)
    def _():
        rest_ref[...] += rest
        met_ref[...] += met


def place_heads(place, parts, edge, width, weights):
    seqs, rows, total = parts.shape
    rest = total - edge - 2 * width

    def column_spec(size):
        return pl.BlockSpec((rows, size), lambda j, at: (0, jnp.bitwise_xor(at[0], j)))

    return pl.pallas_call(
        place_heads_kernel,
        out_shape=[
            jax.ShapeDtypeStruct((rows, seqs * edge), F32),
            jax.ShapeDtypeStruct((rows, seqs * width), F32),
            jax.ShapeDtypeStruct((rows, seqs * width), F32),
            jax.ShapeDtypeStruct((rows, rest), F32),
            jax.ShapeDtypeStruct((rows, 128), F32),
        ],
        grid_spec=pltpu.PrefetchScalarGridSpec(
            num_scalar_prefetch=1,
            grid=(seqs,),
            in_specs=[
                pl.BlockSpec((1, rows, total), lambda j, at: (j, 0, 0)),
                column_spec(edge),
                column_spec(width),
                column_spec(width),
            ],
            out_specs=[
                column_spec(edge),
                column_spec(width),
                column_spec(width),
                pl.BlockSpec((rows, rest), lambda j, at: (0, 0)),
                pl.BlockSpec((rows, 128), lambda j, at: (0, 0)),
            ],
        ),
        compiler_params=pltpu.CompilerParams(vmem_limit_bytes=VMEM_LIMIT),
        name="place_heads",
    )(place, parts, *weights)


def scale_of(values):
    return lax.rsqrt(jnp.mean(values * values, axis=-1, keepdims=True) + EPSILON)


def normed(values, gain):
    return values * scale_of(values) * gain


def normed_back(values, gain, cot):
    scale = scale_of(values)
    pulled = cot * gain
    mean = jnp.mean(values * pulled, axis=-1, keepdims=True)
    return (
        scale * pulled - values * (scale * scale * scale) * mean,
        jnp.sum(cot * values * scale, axis=0),
    )


def follow(values, earlier):
    return lax.optimization_barrier((values, *earlier))[0]


def own_columns(weight, heads, place):
    width = heads * HEAD
    part = lax.dynamic_slice_in_dim(weight, place * width, width, 1)
    if heads % 2:
        part = jnp.pad(part, ((0, 0), (0, HEAD)))
    return part


def on_device(
    tokens,
    cotangent,
    lengths,
    attn_gain,
    query_weight,
    key_weight,
    value_weight,
    query_gain,
    key_gain,
    out_weight,
    ffn_gain,
    gate_weight,
    up_weight,
    down_weight,
):
    slots, rows, model = tokens.shape
    seqs = lax.axis_size("seq")
    shards = lax.axis_size("fsdp")
    place = lax.axis_index("seq")
    shard = lax.axis_index("fsdp")
    slot_len = rows * seqs
    query_width = query_weight.shape[1]
    kv_width = key_weight.shape[1]
    hq = query_width // seqs // HEAD
    hkv = kv_width // seqs // HEAD
    hkv_held = hkv + hkv % 2
    sizes = (hq, hkv_held, hq // hkv)
    order = (place if seqs == 4 else place * 0).reshape(1)
    tables = position_tables(slot_len)
    gains = (
        jnp.concatenate([query_gain, query_gain]).reshape(1, 2 * HEAD),
        jnp.concatenate([key_gain, key_gain]).reshape(1, 2 * HEAD),
    )

    flat = (slot_len, model)
    chunked = (seqs, rows, model)
    places = place * rows + jnp.arange(rows, dtype=jnp.int32)
    live = (places[None, :] < lengths[:, None]).astype(F32)[..., None]
    inputs = tokens.astype(F32)
    out_cot = cotangent.astype(F32) * live
    out_low = [out_cot[b].astype(BF16) for b in range(slots)]
    normal_in = [normed(inputs[b], attn_gain).astype(BF16) for b in range(slots)]

    qkv_own = jnp.concatenate(
        [
            own_columns(query_weight, hq, place),
            own_columns(key_weight, hkv, place),
            own_columns(value_weight, hkv, place),
        ],
        axis=1,
    )
    start = [
        ("gather", normal_in[0]),
        ("deal", out_weight),
        ("own", gate_weight, up_weight, down_weight),
        ("line", qkv_own),
    ]
    normal_0, out_own, *ffn_own, qkv_weight = transfer(start, 1)
    qkv_weight = qkv_weight.reshape(model, -1)
    hidden_own = gate_weight.shape[0] // seqs
    part = hidden_own // CHUNKS
    ffn_weights = [lax.all_gather(own, "fsdp", axis=0) for own in ffn_own]

    def leave(mixed):
        return dot(mixed.reshape(slot_len, -1), out_rows).astype(BF16).reshape(chunked)

    def enter_ffn(b, total):
        res = inputs[b] + total
        return res, normed(res, ffn_gain).astype(BF16)

    def heads(b, jobs, number, after):
        return attend(
            sizes, lengths[b : b + 1], normal_full[b], qkv_weight, gains, tables,
            jobs, number, after,
        )

    normal_full = [None] * slots
    cot_full = [None] * slots
    mid_full = [None] * slots
    normal_full[0] = normal_0
    (mixed_0, lse_0, qkv_0), (normal_full[1], out_rows) = heads(
        0, [("gather", normal_in[1]), ("line", out_own)], 2, normal_full[0]
    )
    out_rows = out_rows.reshape(-1, model)
    (mixed_1, lse_1, qkv_1), (total_0,) = heads(1, [("scatter", leave(mixed_0))], 3, mixed_0)
    qkv = [qkv_0, qkv_1]
    log_sums = [lse_0, lse_1]
    res_0, mid_0 = enter_ffn(0, total_0)
    mid_full[0], cot_full[0] = [
        v.reshape(flat)
        for v in transfer([("gather", mid_0), ("gather", out_low[0])], 4, mixed_1)
    ]

    acts = [[None] * slots for _ in range(CHUNKS)]
    pulled = [None] * slots

    def ffn_step(b, c, jobs, number, after):
        (acts[c][b], pulled[b]), results = ffn_both(
            mid_full[b], cot_full[b], ffn_weights[c], pulled[b], c == CHUNKS - 1,
            jobs, number, after,
        )
        return results

    def grad_step(c, jobs, number, after):
        (grads,), results = ffn_grads(
            acts[c], mid_full, cot_full, shards, jobs, number, after
        )
        return grads.reshape(shards, 3 * part, model), results

    def leave_ffn(b, jobs, number, after, true_order=False):
        (out,), results = ffn_down(
            [acts[c][b] for c in range(CHUNKS)], ffn_weights, jobs, number, after, true_order
        )
        return out.reshape(chunked), results

    total_1, full = ffn_step(
        0, 0, [("scatter", leave(mixed_1)), ("gather", out_low[1])], 5, mid_full[0]
    )
    cot_full[1] = full.reshape(flat)
    res_1, mid_1 = enter_ffn(1, total_1)
    hidden_res = [res_0, res_1]
    (full,) = ffn_step(0, 1, [("gather", mid_1)], 6, acts[0][0])
    mid_full[1] = full.reshape(flat)
    (mid_total_0,) = ffn_step(1, 0, [("scatter", pulled[0].reshape(chunked))], 7, acts[1][0])

    def pull_mid(b, total):
        pull, gain_part = normed_back(hidden_res[b], ffn_gain, total)
        cot = out_cot[b] + pull
        return cot, cot.astype(BF16), gain_part

    res_cot_0, low_0, ffn_gain_0 = pull_mid(0, mid_total_0)
    grads_0, (res_full_0,) = grad_step(0, [("gather", low_0)], 8, acts[0][1])
    ffn_sums = [lax.psum_scatter(grads_0, "fsdp", scatter_dimension=0)]
    out_0, _ = leave_ffn(0, [], 0, grads_0)
    (out_total_0,) = ffn_step(1, 1, [("scatter", out_0)], 9, out_0)
    grads_1, (mid_total_1,) = grad_step(
        1, [("scatter", pulled[1].reshape(chunked))], 10, acts[1][1]
    )
    ffn_sums.append(
        lax.psum_scatter(grads_1, "fsdp", scatter_dimension=0)
    )
    res_cot_1, low_1, ffn_gain_1 = pull_mid(1, mid_total_1)
    grad_ffn_gain = ffn_gain_0 + ffn_gain_1

    def back(b, full, jobs, number, after, others=()):
        return attend_back(
            sizes, lengths[b : b + 1], qkv[b], full, out_rows, qkv_weight, log_sums[b],
            gains, tables, jobs, number, after, others,
        )

    (dqkv_0, heads_gain_0, pull_0), (res_full_1,) = back(
        0, res_full_0, [("gather", low_1)], 11, grads_1
    )
    (dqkv_1, heads_gain_1, pull_1, out_grads), (in_total_0, ffn_parts_0) = back(
        1,
        res_full_1,
        [("scatter", pull_0), ("gather", ffn_sums[0])],
        12,
        dqkv_0,
        (mixed_0, mixed_1, res_full_0),
    )
    head_gain = heads_gain_0 + heads_gain_1
    dqkv = [v.reshape(slot_len, -1) for v in (dqkv_0, dqkv_1)]
    held = model // shards
    piece = hq * HEAD // shards
    blocks = held // piece
    head_sums = jnp.pad(
        (head_gain[:, :HEAD] + head_gain[:, HEAD:]).reshape(2, shards, HEAD // shards),
        ((0, 0), (0, 0), (0, held - HEAD // shards)),
    ).reshape(2, model)
    gain_columns = jnp.stack([grad_ffn_gain, head_sums[0], head_sums[1]], axis=1).astype(BF16)
    attn_grads = jnp.concatenate(
        [
            sum(dot(normal_full[b].reshape(flat), dqkv[b], TN) for b in range(slots)).astype(BF16),
            jnp.pad(gain_columns, ((0, 0), (0, 125))),
            out_grads,
        ],
        axis=1,
    )
    attn_sums = lax.psum_scatter(attn_grads, "fsdp", scatter_dimension=0, tiled=True)
    out_1, (in_total_1, ffn_parts_1) = leave_ffn(
        1, [("scatter", pull_1), ("gather", ffn_sums[1])], 13, attn_grads, True
    )
    out_total_1 = lax.psum_scatter(
        follow(out_1, [attn_sums]), "seq", scatter_dimension=0
    ).astype(F32)
    out_edge = attn_sums.shape[1] - model // blocks
    heads_all, _, out_parts = transfer(
        [("gather", attn_sums[:, :out_edge]), ("spread", attn_sums[:, out_edge:])],
        14,
        in_total_1,
    )
    grad_out = jnp.swapaxes(
        out_parts.reshape(seqs, blocks, piece, model // blocks), 1, 2
    ).reshape(held, model)
    grad_tokens = []
    for b, (in_cot, cot) in enumerate(((in_total_0, res_cot_0), (in_total_1, res_cot_1))):
        pull, _ = normed_back(inputs[b], attn_gain, in_cot)
        grad_tokens.append((cot + pull).astype(BF16))
    output = [
        (live[b] * (hidden_res[b] + total)).astype(BF16)
        for b, total in enumerate((out_total_0, out_total_1))
    ]
    ffn_grad = ()
    for c, parts in enumerate((ffn_parts_0, ffn_parts_1)):
        ffn_grad = place_parts(order, parts.reshape(seqs, 3, part, model), c, ffn_grad)
    ffn_grad = [v.reshape(seqs * hidden_own, model) for v in ffn_grad]

    edge = hq * HEAD
    width = hkv_held * HEAD
    if hkv == hkv_held:
        grad_query, grad_key, grad_value, gain_sums, met = place_heads(
            order, heads_all, edge, width, (query_weight, key_weight, value_weight)
        )
        met = met[:, 0]
    else:
        heads_all = jnp.moveaxis(heads_all, 0, 1).astype(F32)
        last = edge + width
        grad_query = heads_all[..., :edge].reshape(held, query_width)
        grad_key = heads_all[..., edge : edge + hkv * HEAD].reshape(held, kv_width)
        grad_value = heads_all[..., last : last + hkv * HEAD].reshape(held, kv_width)
        gain_sums = jnp.sum(heads_all[..., last + width :], axis=1)
        met = sum(
            jnp.sum(grad * weight.astype(F32), axis=1)
            for grad, weight in (
                (grad_query, query_weight),
                (grad_key, key_weight),
                (grad_value, value_weight),
            )
        )
    grad_attn_gain = met / lax.dynamic_slice_in_dim(attn_gain, shard * held, held, 0)

    return (
        jnp.stack(output),
        jnp.stack(grad_tokens),
        grad_attn_gain,
        grad_query,
        grad_key,
        grad_value,
        gain_sums[: HEAD // shards, 1],
        gain_sums[: HEAD // shards, 2],
        grad_out.astype(F32),
        gain_sums[:, 0],
        ffn_grad[0],
        ffn_grad[1],
        ffn_grad[2],
    )


def solution(mesh):
    return jax.shard_map(
        on_device,
        mesh=mesh,
        in_specs=(
            P("fsdp", "seq", None),
            P("fsdp", "seq", None),
            P("fsdp"),
            P(),
            P("fsdp", None),
            P("fsdp", None),
            P("fsdp", None),
            P(),
            P(),
            P("fsdp", None),
            P(),
            P("fsdp", None),
            P("fsdp", None),
            P("fsdp", None),
        ),
        out_specs=(
            P("fsdp", "seq", None),
            P("fsdp", "seq", None),
            P("fsdp"),
            P("fsdp", None),
            P("fsdp", None),
            P("fsdp", None),
            P("fsdp"),
            P("fsdp"),
            P("fsdp", None),
            P("fsdp"),
            P("fsdp", None),
            P("fsdp", None),
            P("fsdp", None),
        ),
        check_vma=False,
    )
```

```python
import functools

import jax
import jax.numpy as jnp
import numpy as np
from jax import lax
from jax.experimental import pallas as pl
from jax.experimental.pallas import tpu as pltpu
from jax.sharding import PartitionSpec as P

EPSILON = 1e-05
ROPE_BASE = 1000000.0
NEGATIVE = -1e30
F32 = jnp.float32
BF16 = jnp.bfloat16
NN = (((1,), (0,)), ((), ()))
NT = (((1,), (1,)), ((), ()))
TN = (((0,), (0,)), ((), ()))
SMEM = pl.BlockSpec(memory_space=pltpu.SMEM)
VMEM = pl.BlockSpec(memory_space=pltpu.VMEM)
VMEM_LIMIT = 58 << 20
HEAD = 64
BLOCK = 256
CHUNKS = 2
ANY = pl.BlockSpec(memory_space=pl.ANY)


def dot(a, b, dims=NN):
    return lax.dot_general(a, b, dims, preferred_element_type=F32)


def over_one(place):
    return place + 1 - 2 * (place % 2)


def over_two(place):
    return (place + 2) % 4


def send(source, target, device, out_sem, in_sem):
    return pltpu.make_async_remote_copy(
        src_ref=source,
        dst_ref=target,
        send_sem=out_sem,
        recv_sem=in_sem,
        device_id={"seq": device},
        device_id_type=pl.DeviceIdType.MESH,
    )


def gather_job(sources, targets, scratch):
    (source,) = sources
    (target,) = targets
    outs, ins, here, held = scratch
    place = lax.axis_index("seq")
    one, two = over_one(place), over_two(place)
    half = source.shape[0] // 2
    load = pltpu.make_async_copy(source, held, here.at[0])
    store = pltpu.make_async_copy(held, target.at[0], here.at[1])
    first = send(source, target.at[1], one, outs.at[0], ins.at[0])
    second = send(source, target.at[2], two, outs.at[1], ins.at[1])
    top = pl.ds(0, half)
    low = pl.ds(half, half)
    third = send(target.at[2, top], target.at[3, top], one, outs.at[2], ins.at[2])
    fourth = send(target.at[1, low], target.at[3, low], two, outs.at[3], ins.at[3])

    def begin():
        first.start()
        second.start()
        load.start()

    def middle():
        load.wait()
        store.start()
        second.wait_recv()
        third.start()
        first.wait_recv()
        fourth.start()

    def finish():
        third.wait_recv()
        fourth.wait_recv()
        for copy in (first, second, third, fourth):
            copy.wait_send()
        store.wait()

    return no_greeting, begin, middle, finish


def scatter_job(sources, targets, scratch):
    (parts,) = sources
    (total,) = targets
    outs, ins, here, got_one, got_two, kept, own, last, summed = scratch
    place = lax.axis_index("seq")
    one, two = over_one(place), over_two(place)
    half = parts.shape[1] // 2
    top = pl.ds(0, half)
    low = pl.ds(half, half)
    sends = [
        send(parts.at[3, top], got_one.at[0], one, outs.at[0], ins.at[0]),
        send(parts.at[3, low], got_two.at[0], two, outs.at[1], ins.at[1]),
        send(parts.at[1, top], got_one.at[1], one, outs.at[2], ins.at[2]),
        send(parts.at[2, low], got_two.at[1], two, outs.at[3], ins.at[3]),
        send(kept.at[0], last.at[0], two, outs.at[4], ins.at[4]),
        send(kept.at[1], last.at[1], one, outs.at[5], ins.at[5]),
    ]
    loads = [
        pltpu.make_async_copy(parts.at[2, top], kept.at[0], here.at[0]),
        pltpu.make_async_copy(parts.at[1, low], kept.at[1], here.at[1]),
        pltpu.make_async_copy(parts.at[0], own, here.at[2]),
    ]
    store = pltpu.make_async_copy(summed, total, here.at[3])

    def begin():
        for copy in sends[:4]:
            copy.start()
        for copy in loads:
            copy.start()

    def middle():
        for k, got in enumerate((got_one, got_two)):
            loads[k].wait()
            sends[k].wait_recv()
            kept[k] = (kept[k].astype(F32) + got[0].astype(F32)).astype(BF16)
            sends[4 + k].start()

    def finish():
        loads[2].wait()
        for k, got in enumerate((got_one, got_two)):
            sends[2 + k].wait_recv()
            sends[4 + k].wait_recv()
            rows = slice(k * half, (k + 1) * half)
            summed[rows, :] = (
                own[rows, :].astype(F32) + got[1].astype(F32) + last[k].astype(F32)
            )
        store.start()
        for copy in sends:
            copy.wait_send()
        store.wait()

    return no_greeting, begin, middle, finish


def no_greeting(barrier):
    return 0


def nothing():
    pass


def greet(barrier, device):
    pl.semaphore_signal(
        barrier, inc=1, device_id=device, device_id_type=pl.DeviceIdType.MESH
    )


def deal_job(sources, targets, scratch):
    (source,) = sources
    (target,) = targets
    outs, ins, here = scratch
    rows = target.shape[0]
    count = source.shape[0] // rows
    place = lax.axis_index("seq")
    shard = lax.axis_index("fsdp")
    per = lax.axis_size("fsdp") // count
    part = shard % per
    is_source = shard // per == place
    to_self = jnp.logical_and(is_source, shard // count == part)
    origin = place * per + shard // count

    def copy(j):
        return pltpu.make_async_remote_copy(
            src_ref=source.at[pl.ds(j * rows, rows)],
            dst_ref=target,
            send_sem=outs.at[j],
            recv_sem=ins.at[0],
            device_id={"fsdp": part * count + j},
            device_id_type=pl.DeviceIdType.MESH,
        )

    def local(j):
        return pltpu.make_async_copy(source.at[pl.ds(j * rows, rows)], target, here.at[0])

    def greeting(barrier):
        pl.when(origin != shard)(lambda: greet(barrier, {"fsdp": origin}))
        return jnp.where(is_source, count, 0) - jnp.where(to_self, 1, 0)

    def each(act_remote, act_local):
        for j in range(count):
            mine = part * count + j == shard
            pl.when(jnp.logical_and(is_source, mine))(lambda j=j: act_local(local(j)))
            pl.when(jnp.logical_and(is_source, jnp.logical_not(mine)))(
                lambda j=j: act_remote(copy(j))
            )

    def begin():
        each(lambda c: c.start(), lambda c: c.start())

    def finish():
        each(lambda c: c.wait_send(), lambda c: c.wait())
        pl.when(origin != shard)(lambda: copy(0).wait_recv())

    return greeting, begin, nothing, finish


def line_job(sources, targets, scratch):
    (source,) = sources
    (target,) = targets
    far_out, far_in, near_out, near_in, here = scratch
    shards = target.shape[0]
    steps = shards // 2
    shard = lax.axis_index("fsdp")
    near = shard + 1 - 2 * (shard % 2)

    def away(start, k):
        return (start + 2 * k) % shards

    def send_line(origin, spot, device, out_sem, in_sem):
        return pltpu.make_async_remote_copy(
            src_ref=origin,
            dst_ref=target.at[spot],
            send_sem=out_sem,
            recv_sem=in_sem,
            device_id={"fsdp": device},
            device_id_type=pl.DeviceIdType.MESH,
        )

    own = pltpu.make_async_copy(source, target.at[shard], here.at[0])
    far = [
        send_line(source, shard, away(shard, k), far_out.at[k - 1], far_in.at[k - 1])
        for k in range(1, steps)
    ]
    far_came = [
        send_line(
            source, away(shard, steps - k), away(shard, k), far_out.at[k - 1], far_in.at[k - 1]
        )
        for k in range(1, steps)
    ]
    held = [shard] + [away(shard, steps - k) for k in range(1, steps)]
    close = [
        send_line(target.at[spot] if k else source, spot, near, near_out.at[k], near_in.at[k])
        for k, spot in enumerate(held)
    ]
    close_came = [
        send_line(source, away(near, steps - k) if k else near, near, near_out.at[k], near_in.at[k])
        for k in range(steps)
    ]

    def greeting(barrier):
        for k in range(1, steps):
            greet(barrier, {"fsdp": away(shard, k)})
        greet(barrier, {"fsdp": near})
        return steps

    def begin():
        own.start()
        for copy in far:
            copy.start()
        close[0].start()

    def finish():
        for k in range(1, steps):
            far_came[k - 1].wait_recv()
            close[k].start()
        for copy in close_came:
            copy.wait_recv()
        for copy in far + close:
            copy.wait_send()
        own.wait()

    return greeting, begin, nothing, finish


def spread_job(sources, targets, scratch):
    (source,) = sources
    gathered, target = targets
    *first, z_outs, z_ins, z_here = scratch
    _, begin_gather, middle_gather, finish_gather = gather_job(sources, [gathered], first)
    count = gathered.shape[0]
    place = lax.axis_index("seq")
    shard = lax.axis_index("fsdp")
    per = lax.axis_size("fsdp") // count
    piece = shard % count

    def owner(j):
        return true_chunk(place, j, count) * per + shard // count

    def chunk(j):
        return gathered.at[j] if j else source

    def copy(j):
        return pltpu.make_async_remote_copy(
            src_ref=chunk(j),
            dst_ref=target.at[piece],
            send_sem=z_outs.at[j],
            recv_sem=z_ins.at[piece],
            device_id={"fsdp": owner(j)},
            device_id_type=pl.DeviceIdType.MESH,
        )

    def arrival(p):
        return pltpu.make_async_remote_copy(
            src_ref=source,
            dst_ref=target.at[p],
            send_sem=z_outs.at[0],
            recv_sem=z_ins.at[p],
            device_id={"fsdp": owner(0)},
            device_id_type=pl.DeviceIdType.MESH,
        )

    def local(j):
        return pltpu.make_async_copy(chunk(j), target.at[piece], z_here.at[0])

    def origin(p):
        return (shard % per) * count + p

    def start(j):
        pl.when(owner(j) != shard)(lambda: copy(j).start())
        pl.when(owner(j) == shard)(lambda: local(j).start())

    def greeting(barrier):
        for p in range(count):
            pl.when(origin(p) != shard)(lambda p=p: greet(barrier, {"fsdp": origin(p)}))
        return jnp.where(shard % per == shard // count, count - 1, count)

    def begin():
        begin_gather()
        start(0)

    def middle():
        middle_gather()
        start(1)
        start(2)

    def finish():
        finish_gather()
        start(3)
        for j in range(count):
            pl.when(owner(j) != shard)(lambda j=j: copy(j).wait_send())
            pl.when(owner(j) == shard)(lambda j=j: local(j).wait())
        for p in range(count):
            pl.when(origin(p) != shard)(lambda p=p: arrival(p).wait_recv())

    return greeting, begin, middle, finish


def own_job(sources, targets, scratch):
    loaded, stored, held = scratch
    place = lax.axis_index("seq")
    count = lax.axis_size("seq")
    part = targets[0].shape[1]
    loads = []
    stores = []
    for c, target in enumerate(targets):
        for k, source in enumerate(sources):
            start = place * (source.shape[0] // count) + c * part
            spot = pl.ds(pl.multiple_of(start, part), part)
            n = c * len(sources) + k
            loads.append(pltpu.make_async_copy(source.at[spot], held.at[n], loaded.at[n]))
            stores.append(pltpu.make_async_copy(held.at[n], target.at[k], stored.at[n]))

    def begin():
        for load in loads:
            load.start()

    def middle():
        for load, store in zip(loads, stores):
            load.wait()
            store.start()

    def finish():
        for store in stores:
            store.wait()

    return no_greeting, begin, middle, finish


MAKERS = {
    "gather": gather_job,
    "scatter": scatter_job,
    "deal": deal_job,
    "spread": spread_job,
    "line": line_job,
    "own": own_job,
}


def job_scratch(job):
    kind, *arrays = job
    if kind == "scatter":
        _, rows, width = arrays[0].shape
        halves = pltpu.VMEM((2, rows // 2, width), BF16)
        return [
            pltpu.SemaphoreType.DMA((6,)),
            pltpu.SemaphoreType.DMA((6,)),
            pltpu.SemaphoreType.DMA((4,)),
            halves,
            halves,
            halves,
            pltpu.VMEM((rows, width), BF16),
            halves,
            pltpu.VMEM((rows, width), F32),
        ]
    if kind == "own":
        count = CHUNKS * len(arrays)
        rows, width = arrays[0].shape
        part = rows // lax.axis_size("seq") // CHUNKS
        return [
            pltpu.SemaphoreType.DMA((count,)),
            pltpu.SemaphoreType.DMA((count,)),
            pltpu.VMEM((count, part, width), BF16),
        ]
    moves = [
        pltpu.SemaphoreType.DMA((4,)),
        pltpu.SemaphoreType.DMA((4,)),
        pltpu.SemaphoreType.DMA((2,)),
    ]
    if kind == "deal":
        return moves
    if kind == "line":
        steps = lax.axis_size("fsdp") // 2
        return [pltpu.SemaphoreType.DMA((steps,))] * 4 + [pltpu.SemaphoreType.DMA((1,))]
    moves.append(pltpu.VMEM(arrays[0].shape, BF16))
    if kind == "spread":
        moves += [
            pltpu.SemaphoreType.DMA((4,)),
            pltpu.SemaphoreType.DMA((4,)),
            pltpu.SemaphoreType.DMA((1,)),
        ]
    return moves


def job_results(job):
    kind, *arrays = job
    shape = arrays[0].shape
    if kind == "gather":
        return [jax.ShapeDtypeStruct((4,) + shape, BF16)]
    if kind == "scatter":
        return [jax.ShapeDtypeStruct(shape[1:], F32)]
    if kind == "deal":
        return [jax.ShapeDtypeStruct((shape[0] // 4,) + shape[1:], BF16)]
    if kind == "spread":
        return [jax.ShapeDtypeStruct((4,) + shape, BF16)] * 2
    if kind == "line":
        return [jax.ShapeDtypeStruct((lax.axis_size("fsdp"),) + shape, BF16)]
    part = shape[0] // lax.axis_size("seq") // CHUNKS
    return [jax.ShapeDtypeStruct((len(arrays), part) + shape[1:], BF16)] * CHUNKS


def plain_job(job):
    kind, *arrays = job
    seqs = lax.axis_size("seq")
    shards = lax.axis_size("fsdp")
    per = shards // seqs
    ends = [(s, h, s * shards + s * per + h) for s in range(seqs) for h in range(per)]
    if kind == "gather":
        return [lax.all_gather(arrays[0], "seq", axis=0)]
    if kind == "scatter":
        return [lax.psum_scatter(arrays[0], "seq", scatter_dimension=0).astype(F32)]
    if kind == "deal":
        rows = arrays[0].shape[0] // seqs
        total = None
        for j in range(seqs):
            moves = [(end, s * shards + h * seqs + j) for s, h, end in ends]
            got = lax.ppermute(arrays[0][j * rows : (j + 1) * rows], ("seq", "fsdp"), moves)
            total = got if total is None else total + got
        return [total]
    if kind == "line":
        return [lax.all_gather(arrays[0], "fsdp", axis=0)]
    if kind == "spread":
        gathered = lax.all_gather(arrays[0], "seq", axis=0)
        pieces = []
        for p in range(seqs):
            total = None
            for q in range(seqs):
                moves = [
                    (s * shards + h * seqs + p, s * shards + q * per + h)
                    for s in range(seqs)
                    for h in range(per)
                ]
                got = lax.ppermute(gathered[q], ("seq", "fsdp"), moves)
                total = got if total is None else total + got
            pieces.append(total)
        return [gathered, jnp.stack(pieces)]
    own_rows = arrays[0].shape[0] // seqs
    part = own_rows // CHUNKS
    start = lax.axis_index("seq") * own_rows
    return [
        jnp.stack([lax.dynamic_slice_in_dim(w, start + c * part, part, 0) for w in arrays])
        for c in range(CHUNKS)
    ]


def meet(greetings):
    place = lax.axis_index("seq")
    barrier = pltpu.get_barrier_semaphore()
    for device in (over_one(place), over_two(place)):
        greet(barrier, {"seq": device})
    peers = 2
    for greeting in greetings:
        peers = peers + greeting(barrier)
    pl.semaphore_wait(barrier, peers)


def call(
    body, operands, in_specs, out_shape, out_specs, jobs, number, after=None,
    grid=(), scratch=(), cost=None, name=None, late=(),
):
    plain = lax.axis_size("seq") != 4
    results = [v for job in jobs for v in plain_job(job)] if plain else []
    inside = [] if plain else jobs
    extra = [] if after is None else [after]
    job_shapes = [job_scratch(job) for job in inside]
    job_outs = [job_results(job) for job in inside]
    n_in = len(operands)
    n_out = len(out_shape)

    def kernel(*refs):
        refs = list(refs)

        def take(count):
            taken, refs[:] = refs[:count], refs[count:]
            return taken

        ins = take(n_in)
        take(len(extra))
        sources = [take(len(job) - 1) for job in inside]
        outs = take(n_out)
        targets = [take(len(shapes)) for shapes in job_outs]
        held = take(len(scratch))
        loaded = take(len(late))
        marks = take(1) if late else []
        loads = [
            pltpu.make_async_copy(ins[n], ref, marks[0].at[k])
            for k, (n, ref) in enumerate(zip(late, loaded))
        ]
        for n, ref in zip(late, loaded):
            ins[n] = ref
        phases = [
            MAKERS[job[0]](source, target, take(len(shapes)))
            for job, source, target, shapes in zip(inside, sources, targets, job_shapes)
        ]

        def hook(k):
            if k == 0 and phases:
                meet([phase[0] for phase in phases])
            for phase in phases:
                phase[k + 1]()
            if k == 0:
                for load in loads:
                    load.start()
                for load in loads:
                    load.wait()

        body(hook, ins, outs, held)

    given = {}
    if inside:
        given = {"collective_id": number, "has_side_effects": True}
    arrays = [array for job in inside for array in job[1:]]
    in_specs = [ANY if n in late else spec for n, spec in enumerate(in_specs)]
    late_shapes = [pltpu.VMEM(operands[n].shape, operands[n].dtype) for n in late]
    if late:
        late_shapes.append(pltpu.SemaphoreType.DMA((len(late),)))
    shapes = [shape for shapes in job_outs for shape in shapes]
    made = pl.pallas_call(
        kernel,
        grid=grid,
        out_shape=tuple(out_shape) + tuple(shapes),
        in_specs=list(in_specs) + [ANY] * (len(extra) + len(arrays)),
        out_specs=tuple(out_specs) + (ANY,) * len(shapes),
        scratch_shapes=list(scratch)
        + late_shapes
        + [shape for shapes in job_shapes for shape in shapes],
        compiler_params=pltpu.CompilerParams(vmem_limit_bytes=VMEM_LIMIT, **given),
        cost_estimate=cost,
        name=name,
    )(*operands, *extra, *arrays)
    return list(made[:n_out]), list(made[n_out:]) + results


def transfer(jobs, number, after=None):
    if lax.axis_size("seq") != 4:
        return [v for job in jobs for v in plain_job(job)]

    def body(hook, ins, outs, held):
        for k in range(3):
            hook(k)

    return call(body, [], [], [], [], jobs, number, after, name="transfer")[1]


def partner(v):
    lane = lax.broadcasted_iota(jnp.int32, v.shape, 1)
    return jnp.where(lane % HEAD < HEAD // 2, pltpu.roll(v, 96, 1), pltpu.roll(v, 32, 1))


def head_mean(v, ones):
    high = v.astype(BF16)
    rest = (v - high.astype(F32)).astype(BF16)
    return dot(high, ones) + dot(rest, ones)


def true_chunk(place, c, count):
    if count != 4:
        return c
    low = 1 - place % 2 if c % 2 else place % 2
    high = 1 - place // 2 if c // 2 else place // 2
    return low + 2 * high


def prepare_heads(sizes, place, qkv_ref, qg_ref, kg_ref, cos_ref, sin_ref, ones, q_s, k_s, v_s):
    hq, hkv, _ = sizes
    seqs, rows_in, _ = qkv_ref.shape
    for c in range(seqs):
        j = true_chunk(place, c, seqs)
        rows = slice(c * rows_in, (c + 1) * rows_in)
        cos = cos_ref[rows, :]
        sin = sin_ref[rows, :]
        for p in range((hq + hkv) // 2):
            is_query = p < hq // 2
            x = qkv_ref[j, :, p * 128 : (p + 1) * 128].astype(F32)
            gain = qg_ref[...] * HEAD**-0.5 if is_query else kg_ref[...]
            y = x * lax.rsqrt(head_mean(x * x, ones) + EPSILON) * gain
            y = (y * cos + partner(y) * sin).astype(BF16)
            for t in range(2):
                part = y[:, t * HEAD : (t + 1) * HEAD]
                if is_query:
                    q_s[2 * p + t, rows, :] = part
                else:
                    k_s[2 * p - hq + t, rows, :] = part
        for t in range(hkv):
            start = (hq + hkv + t) * HEAD
            v_s[t, rows, :] = qkv_ref[j, :, start : start + HEAD]


def allowed_keys(block, first, keys, length):
    bound = jnp.minimum(first + lax.broadcasted_iota(jnp.int32, (block, 1), 0), length - 1)
    return lax.broadcasted_iota(jnp.int32, (block, keys), 1) <= bound


def attend_kernel(sizes, hook, ins, outs, held):
    len_ref, normal_ref, weight_ref, qg_ref, kg_ref, cos_ref, sin_ref, ones_ref, *out_w = ins
    out_ref, lse_ref, qkv_ref, *left = outs
    q_s, k_s, v_s, o_s = held
    hook(0)

    @pl.loop(0, qkv_ref.shape[0])
    def _(j):
        qkv_ref[j] = dot(normal_ref[j], weight_ref[...]).astype(BF16)

    hq, hkv, group = sizes
    seqs, rows_in, _ = qkv_ref.shape
    place = lax.axis_index("seq")
    prepare_heads(
        sizes, place, qkv_ref, qg_ref, kg_ref, cos_ref, sin_ref, ones_ref[...], q_s, k_s, v_s
    )
    for i in range(seqs * rows_in // BLOCK):
        keys = (i + 1) * BLOCK
        rows = slice(i * BLOCK, (i + 1) * BLOCK)
        keep = allowed_keys(BLOCK, i * BLOCK, keys, len_ref[0])

        def one_head(h, _):
            kv = h // group
            scores = dot(q_s[h, rows, :], k_s[kv, :keys, :], NT)
            scores = jnp.where(keep, scores, NEGATIVE)
            highest = jnp.max(scores, axis=1, keepdims=True)
            shifted = jnp.exp(scores - highest)
            total = jnp.sum(shifted, axis=1, keepdims=True)
            mixed = dot(shifted.astype(BF16), v_s[kv, :keys, :]) / total
            o_s[h, rows, :] = mixed.astype(BF16)
            lse_ref[h, rows, :] = highest + jnp.log(total)
            return 0

        lax.fori_loop(0, hq, one_head, 0, unroll=min(4, hq))
        if i == seqs * rows_in // BLOCK - 2:
            hook(1)
    for c in range(seqs):
        j = true_chunk(place, c, seqs)
        rows = slice(c * rows_in, (c + 1) * rows_in)
        for p in range(hq // 2):
            out_ref[j, :, p * 128 : (p + 1) * 128] = jnp.concatenate(
                [o_s[2 * p, rows, :], o_s[2 * p + 1, rows, :]], axis=1
            )
    for out_w_ref, left_ref in zip(out_w, left):
        for j in range(seqs):
            left_ref[j] = dot(out_ref[j], out_w_ref[...]).astype(BF16)
    hook(2)


def out_weight_grads(grads_ref, shards, slots):
    width = slots[0][0].shape[-1]
    model = slots[0][1].shape[-1]
    tile = min(256, width)
    piece = width // shards
    held = model // shards
    blocks = held // piece
    columns = model // blocks
    for t in range(width // tile):
        total = None
        for mixed_ref, res_ref in slots:
            rows = mixed_ref.shape[0] * mixed_ref.shape[1]
            mixed = mixed_ref[:, :, t * tile : (t + 1) * tile].reshape(rows, tile)
            term = dot(mixed, res_ref[...].reshape(rows, model), TN)
            total = term if total is None else total + term
        total = total.astype(BF16)
        for p in range(tile // piece):
            first = (t * (tile // piece) + p) * held
            for c in range(blocks):
                grads_ref[first + c * piece : first + (c + 1) * piece, :] = total[
                    p * piece : (p + 1) * piece, c * columns : (c + 1) * columns
                ]


def attend_back_kernel(sizes, shards, hook, ins, outs, held):
    (
        len_ref, qkv_ref, res_ref, out_w_ref, qkv_w_ref, lse_ref,
        qg_ref, kg_ref, cos_ref, sin_ref, ones_ref, *others,
    ) = ins
    dqkv_ref, dgain_ref, pull_ref, *out_grads = outs
    q_s, k_s, v_s, cot_s, dq_s, dk_s, dv_s = held
    hook(0)
    hq, hkv, group = sizes
    seqs, rows_in, _ = qkv_ref.shape
    place = lax.axis_index("seq")
    ones = ones_ref[...]
    prepare_heads(sizes, place, qkv_ref, qg_ref, kg_ref, cos_ref, sin_ref, ones, q_s, k_s, v_s)
    for c in range(seqs):
        j = true_chunk(place, c, seqs)
        cots = dot(res_ref[j], out_w_ref[...], NT).astype(BF16)
        for h in range(hq):
            cot_s[h, c * rows_in : (c + 1) * rows_in, :] = cots[:, h * HEAD : (h + 1) * HEAD]
    dk_s[...] = jnp.zeros_like(dk_s)
    dv_s[...] = jnp.zeros_like(dv_s)
    for i in range(seqs * rows_in // BLOCK):
        keys = (i + 1) * BLOCK
        rows = slice(i * BLOCK, (i + 1) * BLOCK)
        keep = allowed_keys(BLOCK, i * BLOCK, keys, len_ref[0])

        def one_head(h, _):
            kv = h // group
            q = q_s[h, rows, :]
            cot = cot_s[h, rows, :]
            k = k_s[kv, :keys, :]
            scores = jnp.where(keep, dot(q, k, NT), NEGATIVE)
            probs = jnp.exp(scores - lse_ref[h, rows, :])
            prob_cot = dot(cot, v_s[kv, :keys, :], NT)
            inner = jnp.sum(probs * prob_cot, axis=1, keepdims=True)
            score_cot = (probs * (prob_cot - inner)).astype(BF16)
            dq_s[h, rows, :] = dot(score_cot, k) * HEAD**-0.5
            dk_s[kv, :keys, :] += dot(score_cot, q, TN)
            dv_s[kv, :keys, :] += dot(probs.astype(BF16), cot, TN)
            return 0

        lax.fori_loop(0, hq, one_head, 0, unroll=min(4, hq))
        if i == seqs * rows_in // BLOCK - 2:
            for grads_ref in out_grads:
                before_ref, here_ref, res_before_ref = others
                out_weight_grads(
                    grads_ref, shards, ((before_ref, res_before_ref), (here_ref, res_ref))
                )
            hook(1)
    gain_sums = [jnp.zeros((1, 128), F32), jnp.zeros((1, 128), F32)]
    for c in range(seqs):
        j = true_chunk(place, c, seqs)
        rows = slice(c * rows_in, (c + 1) * rows_in)
        cos = cos_ref[rows, :]
        sin = sin_ref[rows, :]
        for p in range((hq + hkv) // 2):
            is_query = p < hq // 2
            x = qkv_ref[j, :, p * 128 : (p + 1) * 128].astype(F32)
            gain = qg_ref[...] if is_query else kg_ref[...]
            source, first = (dq_s, 2 * p) if is_query else (dk_s, 2 * p - hq)
            turned = jnp.concatenate([source[first, rows, :], source[first + 1, rows, :]], axis=1)
            scale = lax.rsqrt(head_mean(x * x, ones) + EPSILON)
            straight = turned * cos + partner(turned * sin)
            unit = x * scale
            which = 0 if is_query else 1
            gain_sums[which] += jnp.sum(straight * unit, axis=0, keepdims=True)
            pulled = gain * straight
            dx = scale * (pulled - unit * head_mean(unit * pulled, ones))
            dqkv_ref[j, :, p * 128 : (p + 1) * 128] = dx.astype(BF16)
        for p in range(hkv // 2):
            start = (hq + hkv) * HEAD + p * 128
            dqkv_ref[j, :, start : start + 128] = jnp.concatenate(
                [dv_s[2 * p, rows, :], dv_s[2 * p + 1, rows, :]], axis=1
            ).astype(BF16)
    dgain_ref[0:1, :] = gain_sums[0]
    dgain_ref[1:2, :] = gain_sums[1]

    @pl.loop(0, seqs)
    def _(j):
        pull_ref[j] = dot(dqkv_ref[j], qkv_w_ref[...], NT).astype(BF16)

    hook(2)


def position_tables(length):
    places = np.arange(length, dtype=np.float32)
    half = HEAD // 2
    freqs = np.float32(ROPE_BASE) ** (-(np.arange(half, dtype=np.float32) * 2.0) / HEAD)
    angles = places[:, None] * freqs.astype(np.float32)[None, :]
    cos = np.cos(angles).astype(np.float32)
    sin = np.sin(angles).astype(np.float32)
    ones = np.kron(np.eye(2), np.ones((HEAD, HEAD)) / HEAD)
    return (
        jnp.asarray(np.concatenate([cos] * 4, axis=1)),
        jnp.asarray(np.concatenate([-sin, sin, -sin, sin], axis=1)),
        jnp.asarray(ones, dtype=BF16),
    )


def attend(sizes, length, normal, weight, gains, tables, jobs, number, after, out_w=()):
    seqs, rows_in, _ = normal.shape
    hq, hkv, _ = sizes
    slot = seqs * rows_in
    return call(
        functools.partial(attend_kernel, sizes),
        [length, normal, weight, *gains, *tables, *out_w],
        [SMEM] + [VMEM] * (7 + len(out_w)),
        [
            jax.ShapeDtypeStruct((seqs, rows_in, hq * HEAD), BF16),
            jax.ShapeDtypeStruct((hq, slot, 1), F32),
            jax.ShapeDtypeStruct((seqs, rows_in, weight.shape[1]), BF16),
        ]
        + [jax.ShapeDtypeStruct(normal.shape, BF16)] * len(out_w),
        [VMEM] * (3 + len(out_w)),
        jobs,
        number,
        after,
        scratch=[
            pltpu.VMEM((hq, slot, HEAD), BF16),
            pltpu.VMEM((hkv, slot, HEAD), BF16),
            pltpu.VMEM((hkv, slot, HEAD), BF16),
            pltpu.VMEM((hq, slot, HEAD), BF16),
        ],
        cost=pl.CostEstimate(
            flops=56 * hq * slot * slot * HEAD, bytes_accessed=1 << 23, transcendentals=0
        ),
        name="attend",
        late=(1, 2) + tuple(range(8, 8 + len(out_w))),
    )


def attend_back(
    sizes, length, qkv, res, out_w, qkv_w, lse, gains, tables, jobs, number, after, others=()
):
    seqs, rows_in, width = qkv.shape
    hq, hkv, _ = sizes
    slot = seqs * rows_in
    shards = lax.axis_size("fsdp")
    model = res.shape[-1]
    columns = hq * HEAD // shards * model // (model // shards)
    return call(
        functools.partial(attend_back_kernel, sizes, shards),
        [length, qkv, res, out_w, qkv_w, lse, *gains, *tables, *others],
        [SMEM] + [VMEM] * (10 + len(others)),
        [
            jax.ShapeDtypeStruct((seqs, rows_in, width), BF16),
            jax.ShapeDtypeStruct((2, 128), F32),
            jax.ShapeDtypeStruct(res.shape, BF16),
        ]
        + [jax.ShapeDtypeStruct((model, columns), BF16)] * bool(others),
        [VMEM, VMEM, VMEM] + [VMEM] * bool(others),
        jobs,
        number,
        after,
        scratch=[
            pltpu.VMEM((hq, slot, HEAD), BF16),
            pltpu.VMEM((hkv, slot, HEAD), BF16),
            pltpu.VMEM((hkv, slot, HEAD), BF16),
            pltpu.VMEM((hq, slot, HEAD), BF16),
            pltpu.VMEM((hq, slot, HEAD), F32),
            pltpu.VMEM((hkv, slot, HEAD), F32),
            pltpu.VMEM((hkv, slot, HEAD), F32),
        ],
        cost=pl.CostEstimate(
            flops=88 * hq * slot * slot * HEAD, bytes_accessed=1 << 23, transcendentals=0
        ),
        name="attend_back",
        late=(1, 2, 3, 4, 5) + tuple(range(11, 11 + len(others))),
    )


def hooked(hook, step, steps, work):
    pl.when(step == 0)(lambda: hook(0))
    work(lambda: pl.when(step == (3 * steps) // 5)(lambda: hook(1)))
    pl.when(step == steps - 1)(lambda: hook(2))


def ffn_kernel(steps, hook, ins, outs, held):
    step = pl.program_id(0)
    weights_ref, loaded = held
    loads = [
        pltpu.make_async_copy(ins[2].at[:, k], weights_ref.at[k], loaded.at[k]) for k in range(3)
    ]

    def first(act):
        pl.when(step == 0)(act)

    def work(late):
        for load in loads:
            first(load.start)
        ffn_tile(late, first, loads, *ins[:2], weights_ref, ins[3:], *outs)

    hooked(hook, step, steps, work)


def ffn_tile(late, first, loads, mid_ref, cot_ref, weights_ref, sums, acts_ref, pull_ref):
    model = mid_ref.shape[-1]
    hidden = acts_ref.shape[-1]
    whole = (hidden, model)
    mid = mid_ref[...]
    first(loads[0].wait)
    gate = dot(mid, weights_ref[0].reshape(whole), NT)
    first(loads[1].wait)
    up = dot(mid, weights_ref[1].reshape(whole), NT)
    first(loads[2].wait)
    mids_cot = dot(cot_ref[...], weights_ref[2].reshape(whole), NT)
    late()
    sigmoid = jax.nn.sigmoid(gate)
    active = gate * sigmoid
    gate_cot = (mids_cot * up * sigmoid * (1.0 + gate * (1.0 - sigmoid))).astype(BF16)
    up_cot = (mids_cot * active).astype(BF16)
    acts_ref[0] = gate_cot
    acts_ref[1] = up_cot
    acts_ref[2] = (active * up).astype(BF16)
    pulled = dot(gate_cot, weights_ref[0].reshape(whole)) + dot(
        up_cot, weights_ref[1].reshape(whole)
    )
    for sum_ref in sums:
        pulled = pulled + sum_ref[...]
    pull_ref[...] = pulled.astype(pull_ref.dtype)


def ffn_both(mid, cot, weights, summed, last, jobs, number, after):
    tokens, model = mid.shape
    shards, _, part, _ = weights.shape
    hidden = shards * part
    tile = min(256, tokens)

    row_spec = pl.BlockSpec((tile, model), lambda i: (i, 0))
    extra = () if summed is None else (summed,)
    return call(
        functools.partial(ffn_kernel, tokens // tile),
        [mid, cot, weights, *extra],
        [row_spec, row_spec, ANY] + [row_spec] * len(extra),
        [
            jax.ShapeDtypeStruct((3, tokens, hidden), BF16),
            jax.ShapeDtypeStruct((tokens, model), BF16 if last else F32),
        ],
        [pl.BlockSpec((3, tile, hidden), lambda i: (0, i, 0)), row_spec],
        jobs,
        number,
        after,
        grid=(tokens // tile,),
        scratch=[
            pltpu.VMEM((3, shards, part, model), BF16),
            pltpu.SemaphoreType.DMA((3,)),
        ],
        cost=pl.CostEstimate(
            flops=16 * tokens * model * hidden,
            bytes_accessed=4 * tokens * model + 6 * hidden * model,
            transcendentals=0,
        ),
        name="ffn_both",
    )


def ffn_grad_kernel(slots, tiles, hook, ins, outs, held):
    acts = ins[:slots]
    others = ins[slots:]
    (out_ref,) = outs
    rows_ref, loaded = held
    kind = pl.program_id(0)
    step = kind * tiles + pl.program_id(1)
    loads = [
        pltpu.make_async_copy(other, rows_ref.at[k], loaded.at[k])
        for k, other in enumerate(others)
    ]

    def store(first):
        total = None
        for k, act in enumerate(acts):
            term = dot(act[0], rows_ref[first + k], TN)
            total = term if total is None else total + term
        out_ref[...] = total.astype(BF16).reshape(out_ref.shape)

    def work(late):
        for k, load in enumerate(loads):
            pl.when(step == 0)(load.start)
        for k, load in enumerate(loads):
            pl.when(step == (0 if k < slots else 2 * tiles))(load.wait)
        late()
        pl.when(kind < 2)(lambda: store(0))
        pl.when(kind == 2)(lambda: store(slots))

    hooked(hook, step, 3 * tiles, work)


def ffn_grads(acts, mids, cots, shards, jobs, number, after):
    slots = len(acts)
    _, tokens, hidden = acts[0].shape
    model = mids[0].shape[-1]
    part = hidden // shards
    tile = 256
    per = tile // part
    return call(
        functools.partial(ffn_grad_kernel, slots, hidden // tile),
        [*acts, *mids, *cots],
        [pl.BlockSpec((1, tokens, tile), lambda k, i: (k, 0, i))] * slots
        + [ANY] * (2 * slots),
        [jax.ShapeDtypeStruct((shards, 3, part, model), BF16)],
        [pl.BlockSpec((per, 1, part, model), lambda k, i: (i, k, 0, 0))],
        jobs,
        number,
        after,
        grid=(3, hidden // tile),
        scratch=[
            pltpu.VMEM((2 * slots, tokens, model), BF16),
            pltpu.SemaphoreType.DMA((2 * slots,)),
        ],
        cost=pl.CostEstimate(
            flops=9 * slots * tokens * model * hidden,
            bytes_accessed=4 * slots * tokens * model,
            transcendentals=0,
        ),
        name="ffn_grads",
    )


def ffn_down_kernel(chunks, steps, hook, ins, outs, held):
    acts = ins[:chunks]
    downs = ins[chunks:]
    (out_ref,) = outs

    def work(late):
        late()
        total = None
        for act, down in zip(acts, downs):
            hidden = act.shape[-1]
            term = dot(act[0], down[...].reshape(hidden, down.shape[-1]))
            total = term if total is None else total + term
        out_ref[...] = total.astype(BF16)

    hooked(hook, pl.program_id(0), steps, work)


def ffn_down(acts, weights, jobs, number, after, true_order=False):
    chunks = len(acts)
    _, tokens, hidden = acts[0].shape
    shards, _, part, model = weights[0].shape
    tile = min(256, tokens)
    def spot(i):
        if not true_order or lax.axis_size("seq") != 4:
            return i
        place = lax.axis_index("seq")
        low = (place % 2 + i % 2) % 2
        high = (place // 2 + i // 2) % 2
        return low + 2 * high

    act_spec = pl.BlockSpec((1, tile, hidden), lambda i: (2, i, 0))
    down_spec = pl.BlockSpec(
        (shards, 1, part, model),
        lambda i: (0, 2, 0, 0),
        pipeline_mode=pl.Buffered(buffer_count=1),
    )
    return call(
        functools.partial(ffn_down_kernel, chunks, tokens // tile),
        [*acts, *weights],
        [act_spec] * chunks + [down_spec] * chunks,
        [jax.ShapeDtypeStruct((tokens, model), BF16)],
        [pl.BlockSpec((tile, model), lambda i: (spot(i), 0))],
        jobs,
        number,
        after,
        grid=(tokens // tile,),
        cost=pl.CostEstimate(
            flops=4 * chunks * tokens * model * hidden,
            bytes_accessed=chunks * hidden * (tokens + model) * 2,
            transcendentals=0,
        ),
        name="ffn_down",
    )


def place_kernel(place_ref, parts_ref, *refs):
    for kind, out_ref in enumerate(refs[-3:]):
        out_ref[0, 0] = parts_ref[0, kind].astype(F32)


def place_parts(place, parts, chunk, held):
    seqs, _, part, model = parts.shape
    out = jax.ShapeDtypeStruct((seqs, CHUNKS, part, model), F32)
    out_spec = pl.BlockSpec(
        (1, 1, part, model), lambda j, at: (jnp.bitwise_xor(at[0], j), chunk, 0, 0)
    )
    return pl.pallas_call(
        place_kernel,
        out_shape=(out,) * 3,
        grid_spec=pltpu.PrefetchScalarGridSpec(
            num_scalar_prefetch=1,
            grid=(seqs,),
            in_specs=[pl.BlockSpec((1, 3, part, model), lambda j, at: (j, 0, 0, 0))]
            + [ANY] * len(held),
            out_specs=(out_spec,) * 3,
        ),
        input_output_aliases={2 + k: k for k in range(len(held))},
        compiler_params=pltpu.CompilerParams(vmem_limit_bytes=VMEM_LIMIT),
        cost_estimate=pl.CostEstimate(
            flops=0, bytes_accessed=18 * seqs * part * model, transcendentals=0
        ),
        name="place_parts",
    )(place, parts, *held)


def place_heads_kernel(
    place_ref, parts_ref, query_w_ref, key_w_ref, value_w_ref,
    query_ref, key_ref, value_ref, rest_ref, met_ref,
):
    edge = query_ref.shape[1]
    width = key_ref.shape[1]
    part = parts_ref[0].astype(F32)
    query_ref[...] = part[:, :edge]
    key_ref[...] = part[:, edge : edge + width]
    value_ref[...] = part[:, edge + width : edge + 2 * width]
    rest = part[:, edge + 2 * width :]
    met = jnp.zeros_like(met_ref)
    for grad_ref, weight_ref in (
        (query_ref, query_w_ref),
        (key_ref, key_w_ref),
        (value_ref, value_w_ref),
    ):
        product = grad_ref[...] * weight_ref[...].astype(F32)
        met = met + jnp.sum(product, axis=1, keepdims=True)

    @pl.when(pl.program_id(0) == 0)
    def _():
        rest_ref[...] = rest
        met_ref[...] = met

    @pl.when(pl.program_id(0) > 0)
    def _():
        rest_ref[...] += rest
        met_ref[...] += met


def place_heads(place, parts, edge, width, weights):
    seqs, rows, total = parts.shape
    rest = total - edge - 2 * width

    def column_spec(size):
        return pl.BlockSpec((rows, size), lambda j, at: (0, jnp.bitwise_xor(at[0], j)))

    return pl.pallas_call(
        place_heads_kernel,
        out_shape=[
            jax.ShapeDtypeStruct((rows, seqs * edge), F32),
            jax.ShapeDtypeStruct((rows, seqs * width), F32),
            jax.ShapeDtypeStruct((rows, seqs * width), F32),
            jax.ShapeDtypeStruct((rows, rest), F32),
            jax.ShapeDtypeStruct((rows, 128), F32),
        ],
        grid_spec=pltpu.PrefetchScalarGridSpec(
            num_scalar_prefetch=1,
            grid=(seqs,),
            in_specs=[
                pl.BlockSpec((1, rows, total), lambda j, at: (j, 0, 0)),
                column_spec(edge),
                column_spec(width),
                column_spec(width),
            ],
            out_specs=[
                column_spec(edge),
                column_spec(width),
                column_spec(width),
                pl.BlockSpec((rows, rest), lambda j, at: (0, 0)),
                pl.BlockSpec((rows, 128), lambda j, at: (0, 0)),
            ],
        ),
        compiler_params=pltpu.CompilerParams(vmem_limit_bytes=VMEM_LIMIT),
        name="place_heads",
    )(place, parts, *weights)


def scale_of(values):
    return lax.rsqrt(jnp.mean(values * values, axis=-1, keepdims=True) + EPSILON)


def normed(values, gain):
    return values * scale_of(values) * gain


def normed_back(values, gain, cot):
    scale = scale_of(values)
    pulled = cot * gain
    mean = jnp.mean(values * pulled, axis=-1, keepdims=True)
    return (
        scale * pulled - values * (scale * scale * scale) * mean,
        jnp.sum(cot * values * scale, axis=0),
    )


def follow(values, earlier):
    return lax.optimization_barrier((values, *earlier))[0]


def own_columns(weight, heads, place):
    width = heads * HEAD
    part = lax.dynamic_slice_in_dim(weight, place * width, width, 1)
    if heads % 2:
        part = jnp.pad(part, ((0, 0), (0, HEAD)))
    return part


def on_device(
    tokens,
    cotangent,
    lengths,
    attn_gain,
    query_weight,
    key_weight,
    value_weight,
    query_gain,
    key_gain,
    out_weight,
    ffn_gain,
    gate_weight,
    up_weight,
    down_weight,
):
    slots, rows, model = tokens.shape
    seqs = lax.axis_size("seq")
    shards = lax.axis_size("fsdp")
    place = lax.axis_index("seq")
    shard = lax.axis_index("fsdp")
    slot_len = rows * seqs
    query_width = query_weight.shape[1]
    kv_width = key_weight.shape[1]
    hq = query_width // seqs // HEAD
    hkv = kv_width // seqs // HEAD
    hkv_held = hkv + hkv % 2
    sizes = (hq, hkv_held, hq // hkv)
    order = (place if seqs == 4 else place * 0).reshape(1)
    tables = position_tables(slot_len)
    gains = (
        jnp.concatenate([query_gain, query_gain]).reshape(1, 2 * HEAD),
        jnp.concatenate([key_gain, key_gain]).reshape(1, 2 * HEAD),
    )

    flat = (slot_len, model)
    chunked = (seqs, rows, model)
    places = place * rows + jnp.arange(rows, dtype=jnp.int32)
    live = (places[None, :] < lengths[:, None]).astype(F32)[..., None]
    inputs = tokens.astype(F32)
    out_cot = cotangent.astype(F32) * live
    out_low = [out_cot[b].astype(BF16) for b in range(slots)]
    normal_in = [normed(inputs[b], attn_gain).astype(BF16) for b in range(slots)]

    qkv_own = jnp.concatenate(
        [
            own_columns(query_weight, hq, place),
            own_columns(key_weight, hkv, place),
            own_columns(value_weight, hkv, place),
        ],
        axis=1,
    )
    qkv_weight = lax.all_gather(qkv_own, "fsdp", axis=0, tiled=True)
    start = [
        ("gather", normal_in[0]),
        ("deal", out_weight),
        ("own", gate_weight, up_weight, down_weight),
    ]
    normal_0, out_own, *ffn_own = transfer(start, 1)
    hidden_own = gate_weight.shape[0] // seqs
    part = hidden_own // CHUNKS
    ffn_weights = [lax.all_gather(own, "fsdp", axis=0) for own in ffn_own]

    def leave(mixed):
        return dot(mixed.reshape(slot_len, -1), out_rows).astype(BF16).reshape(chunked)

    def enter_ffn(b, total):
        res = inputs[b] + total
        return res, normed(res, ffn_gain).astype(BF16)

    def heads(b, jobs, number, after, out_w=()):
        return attend(
            sizes, lengths[b : b + 1], normal_full[b].reshape(chunked), qkv_weight, gains, tables,
            jobs, number, after, out_w,
        )

    normal_full = [None] * slots
    cot_full = [None] * slots
    mid_full = [None] * slots
    normal_full[0] = normal_0
    (mixed_0, lse_0, qkv_0), (normal_full[1], out_rows) = heads(
        0, [("gather", normal_in[1]), ("line", out_own)], 2, normal_full[0]
    )
    out_rows = out_rows.reshape(-1, model)
    (mixed_1, lse_1, qkv_1, left_1), (total_0,) = heads(
        1, [("scatter", leave(mixed_0))], 3, mixed_0, (out_rows,)
    )
    qkv = [qkv_0, qkv_1]
    log_sums = [lse_0, lse_1]
    res_0, mid_0 = enter_ffn(0, total_0)
    mid_full[0], cot_full[0] = [
        v.reshape(flat)
        for v in transfer([("gather", mid_0), ("gather", out_low[0])], 4, mixed_1)
    ]

    acts = [[None] * slots for _ in range(CHUNKS)]
    pulled = [None] * slots

    def ffn_step(b, c, jobs, number, after):
        (acts[c][b], pulled[b]), results = ffn_both(
            mid_full[b], cot_full[b], ffn_weights[c], pulled[b], c == CHUNKS - 1,
            jobs, number, after,
        )
        return results

    def grad_step(c, jobs, number, after):
        (grads,), results = ffn_grads(
            acts[c], mid_full, cot_full, shards, jobs, number, after
        )
        return grads.reshape(shards, 3 * part, model), results

    def leave_ffn(b, jobs, number, after, true_order=False):
        (out,), results = ffn_down(
            [acts[c][b] for c in range(CHUNKS)], ffn_weights, jobs, number, after, true_order
        )
        return out.reshape(chunked), results

    total_1, full = ffn_step(
        0, 0, [("scatter", left_1), ("gather", out_low[1])], 5, mid_full[0]
    )
    cot_full[1] = full.reshape(flat)
    res_1, mid_1 = enter_ffn(1, total_1)
    hidden_res = [res_0, res_1]
    (full,) = ffn_step(0, 1, [("gather", mid_1)], 6, acts[0][0])
    mid_full[1] = full.reshape(flat)
    (mid_total_0,) = ffn_step(1, 0, [("scatter", pulled[0].reshape(chunked))], 7, acts[1][0])

    def pull_mid(b, total):
        pull, gain_part = normed_back(hidden_res[b], ffn_gain, total)
        cot = out_cot[b] + pull
        return cot, cot.astype(BF16), gain_part

    res_cot_0, low_0, ffn_gain_0 = pull_mid(0, mid_total_0)
    grads_0, (res_full_0,) = grad_step(0, [("gather", low_0)], 8, acts[0][1])
    ffn_sums = [lax.psum_scatter(grads_0, "fsdp", scatter_dimension=0)]
    out_0, _ = leave_ffn(0, [], 0, grads_0)
    (out_total_0,) = ffn_step(1, 1, [("scatter", out_0)], 9, out_0)
    grads_1, (mid_total_1,) = grad_step(
        1, [("scatter", pulled[1].reshape(chunked))], 10, acts[1][1]
    )
    ffn_sums.append(
        lax.psum_scatter(grads_1, "fsdp", scatter_dimension=0)
    )
    res_cot_1, low_1, ffn_gain_1 = pull_mid(1, mid_total_1)
    grad_ffn_gain = ffn_gain_0 + ffn_gain_1

    def back(b, full, jobs, number, after, others=()):
        return attend_back(
            sizes, lengths[b : b + 1], qkv[b], full, out_rows, qkv_weight, log_sums[b],
            gains, tables, jobs, number, after, others,
        )

    (dqkv_0, heads_gain_0, pull_0), (res_full_1,) = back(
        0, res_full_0, [("gather", low_1)], 11, grads_1
    )
    (dqkv_1, heads_gain_1, pull_1, out_grads), (in_total_0, ffn_parts_0) = back(
        1,
        res_full_1,
        [("scatter", pull_0), ("gather", ffn_sums[0])],
        12,
        dqkv_0,
        (mixed_0, mixed_1, res_full_0),
    )
    head_gain = heads_gain_0 + heads_gain_1
    dqkv = [v.reshape(slot_len, -1) for v in (dqkv_0, dqkv_1)]
    held = model // shards
    piece = hq * HEAD // shards
    blocks = held // piece
    head_sums = jnp.pad(
        (head_gain[:, :HEAD] + head_gain[:, HEAD:]).reshape(2, shards, HEAD // shards),
        ((0, 0), (0, 0), (0, held - HEAD // shards)),
    ).reshape(2, model)
    gain_columns = jnp.stack([grad_ffn_gain, head_sums[0], head_sums[1]], axis=1).astype(BF16)
    attn_grads = jnp.concatenate(
        [
            sum(dot(normal_full[b].reshape(flat), dqkv[b], TN) for b in range(slots)).astype(BF16),
            jnp.pad(gain_columns, ((0, 0), (0, 125))),
            out_grads,
        ],
        axis=1,
    )
    out_1, (in_total_1,) = leave_ffn(1, [("scatter", pull_1)], 13, attn_grads, True)
    attn_sums = lax.psum_scatter(
        follow(attn_grads, [ffn_sums[1], in_total_1]), "fsdp", scatter_dimension=0, tiled=True
    )
    (ffn_parts_1,) = transfer([("gather", ffn_sums[1])], 15, in_total_1)
    out_total_1 = lax.psum_scatter(
        follow(out_1, [attn_sums, ffn_parts_1]), "seq", scatter_dimension=0
    ).astype(F32)
    out_edge = attn_sums.shape[1] - model // blocks
    heads_all, _, out_parts = transfer(
        [("gather", attn_sums[:, :out_edge]), ("spread", attn_sums[:, out_edge:])],
        14,
        ffn_parts_1,
    )
    grad_out = jnp.swapaxes(
        out_parts.reshape(seqs, blocks, piece, model // blocks), 1, 2
    ).reshape(held, model)
    grad_tokens = []
    for b, (in_cot, cot) in enumerate(((in_total_0, res_cot_0), (in_total_1, res_cot_1))):
        pull, _ = normed_back(inputs[b], attn_gain, in_cot)
        grad_tokens.append((cot + pull).astype(BF16))
    output = [
        (live[b] * (hidden_res[b] + total)).astype(BF16)
        for b, total in enumerate((out_total_0, out_total_1))
    ]
    ffn_grad = ()
    for c, parts in enumerate((ffn_parts_0, ffn_parts_1)):
        ffn_grad = place_parts(order, parts.reshape(seqs, 3, part, model), c, ffn_grad)
    ffn_grad = [v.reshape(seqs * hidden_own, model) for v in ffn_grad]

    edge = hq * HEAD
    width = hkv_held * HEAD
    if hkv == hkv_held:
        grad_query, grad_key, grad_value, gain_sums, met = place_heads(
            order, heads_all, edge, width, (query_weight, key_weight, value_weight)
        )
        met = met[:, 0]
    else:
        heads_all = jnp.moveaxis(heads_all, 0, 1).astype(F32)
        last = edge + width
        grad_query = heads_all[..., :edge].reshape(held, query_width)
        grad_key = heads_all[..., edge : edge + hkv * HEAD].reshape(held, kv_width)
        grad_value = heads_all[..., last : last + hkv * HEAD].reshape(held, kv_width)
        gain_sums = jnp.sum(heads_all[..., last + width :], axis=1)
        met = sum(
            jnp.sum(grad * weight.astype(F32), axis=1)
            for grad, weight in (
                (grad_query, query_weight),
                (grad_key, key_weight),
                (grad_value, value_weight),
            )
        )
    grad_attn_gain = met / lax.dynamic_slice_in_dim(attn_gain, shard * held, held, 0)

    return (
        jnp.stack(output),
        jnp.stack(grad_tokens),
        grad_attn_gain,
        grad_query,
        grad_key,
        grad_value,
        gain_sums[: HEAD // shards, 1],
        gain_sums[: HEAD // shards, 2],
        grad_out.astype(F32),
        gain_sums[:, 0],
        ffn_grad[0],
        ffn_grad[1],
        ffn_grad[2],
    )


def solution(mesh):
    return jax.shard_map(
        on_device,
        mesh=mesh,
        in_specs=(
            P("fsdp", "seq", None),
            P("fsdp", "seq", None),
            P("fsdp"),
            P(),
            P("fsdp", None),
            P("fsdp", None),
            P("fsdp", None),
            P(),
            P(),
            P("fsdp", None),
            P(),
            P("fsdp", None),
            P("fsdp", None),
            P("fsdp", None),
        ),
        out_specs=(
            P("fsdp", "seq", None),
            P("fsdp", "seq", None),
            P("fsdp"),
            P("fsdp", None),
            P("fsdp", None),
            P("fsdp", None),
            P("fsdp"),
            P("fsdp"),
            P("fsdp", None),
            P("fsdp"),
            P("fsdp", None),
            P("fsdp", None),
            P("fsdp", None),
        ),
        check_vma=False,
    )
```

```python
import functools

import jax
import jax.numpy as jnp
import numpy as np
from jax import lax
from jax.experimental import pallas as pl
from jax.experimental.pallas import tpu as pltpu
from jax.sharding import PartitionSpec as P

EPSILON = 1e-05
ROPE_BASE = 1000000.0
NEGATIVE = -1e30
F32 = jnp.float32
BF16 = jnp.bfloat16
NN = (((1,), (0,)), ((), ()))
NT = (((1,), (1,)), ((), ()))
TN = (((0,), (0,)), ((), ()))
SMEM = pl.BlockSpec(memory_space=pltpu.SMEM)
VMEM = pl.BlockSpec(memory_space=pltpu.VMEM)
VMEM_LIMIT = 58 << 20
HEAD = 64
BLOCK = 256
CHUNKS = 2
ANY = pl.BlockSpec(memory_space=pl.ANY)


def dot(a, b, dims=NN):
    return lax.dot_general(a, b, dims, preferred_element_type=F32)


def over_one(place):
    return place + 1 - 2 * (place % 2)


def over_two(place):
    return (place + 2) % 4


def send(source, target, device, out_sem, in_sem):
    return pltpu.make_async_remote_copy(
        src_ref=source,
        dst_ref=target,
        send_sem=out_sem,
        recv_sem=in_sem,
        device_id={"seq": device},
        device_id_type=pl.DeviceIdType.MESH,
    )


def gather_job(sources, targets, scratch):
    (source,) = sources
    (target,) = targets
    outs, ins, here, held = scratch
    place = lax.axis_index("seq")
    one, two = over_one(place), over_two(place)
    half = source.shape[0] // 2
    load = pltpu.make_async_copy(source, held, here.at[0])
    store = pltpu.make_async_copy(held, target.at[0], here.at[1])
    first = send(source, target.at[1], one, outs.at[0], ins.at[0])
    second = send(source, target.at[2], two, outs.at[1], ins.at[1])
    top = pl.ds(0, half)
    low = pl.ds(half, half)
    third = send(target.at[2, top], target.at[3, top], one, outs.at[2], ins.at[2])
    fourth = send(target.at[1, low], target.at[3, low], two, outs.at[3], ins.at[3])

    def begin():
        first.start()
        second.start()
        load.start()

    def middle():
        load.wait()
        store.start()
        second.wait_recv()
        third.start()
        first.wait_recv()
        fourth.start()

    def finish():
        third.wait_recv()
        fourth.wait_recv()
        for copy in (first, second, third, fourth):
            copy.wait_send()
        store.wait()

    return no_greeting, begin, middle, finish


def scatter_job(sources, targets, scratch):
    (parts,) = sources
    (total,) = targets
    outs, ins, here, got_one, got_two, kept, own, last, summed = scratch
    place = lax.axis_index("seq")
    one, two = over_one(place), over_two(place)
    half = parts.shape[1] // 2
    top = pl.ds(0, half)
    low = pl.ds(half, half)
    sends = [
        send(parts.at[3, top], got_one.at[0], one, outs.at[0], ins.at[0]),
        send(parts.at[3, low], got_two.at[0], two, outs.at[1], ins.at[1]),
        send(parts.at[1, top], got_one.at[1], one, outs.at[2], ins.at[2]),
        send(parts.at[2, low], got_two.at[1], two, outs.at[3], ins.at[3]),
        send(kept.at[0], last.at[0], two, outs.at[4], ins.at[4]),
        send(kept.at[1], last.at[1], one, outs.at[5], ins.at[5]),
    ]
    loads = [
        pltpu.make_async_copy(parts.at[2, top], kept.at[0], here.at[0]),
        pltpu.make_async_copy(parts.at[1, low], kept.at[1], here.at[1]),
        pltpu.make_async_copy(parts.at[0], own, here.at[2]),
    ]
    store = pltpu.make_async_copy(summed, total, here.at[3])

    def begin():
        for copy in sends[:4]:
            copy.start()
        for copy in loads:
            copy.start()

    def middle():
        for k, got in enumerate((got_one, got_two)):
            loads[k].wait()
            sends[k].wait_recv()
            kept[k] = (kept[k].astype(F32) + got[0].astype(F32)).astype(BF16)
            sends[4 + k].start()

    def finish():
        loads[2].wait()
        for k, got in enumerate((got_one, got_two)):
            sends[2 + k].wait_recv()
            sends[4 + k].wait_recv()
            rows = slice(k * half, (k + 1) * half)
            summed[rows, :] = (
                own[rows, :].astype(F32) + got[1].astype(F32) + last[k].astype(F32)
            )
        store.start()
        for copy in sends:
            copy.wait_send()
        store.wait()

    return no_greeting, begin, middle, finish


def no_greeting(barrier):
    return 0


def nothing():
    pass


def greet(barrier, device):
    pl.semaphore_signal(
        barrier, inc=1, device_id=device, device_id_type=pl.DeviceIdType.MESH
    )


def deal_job(sources, targets, scratch):
    (source,) = sources
    (target,) = targets
    outs, ins, here = scratch
    rows = target.shape[0]
    count = source.shape[0] // rows
    place = lax.axis_index("seq")
    shard = lax.axis_index("fsdp")
    per = lax.axis_size("fsdp") // count
    part = shard % per
    is_source = shard // per == place
    to_self = jnp.logical_and(is_source, shard // count == part)
    origin = place * per + shard // count

    def copy(j):
        return pltpu.make_async_remote_copy(
            src_ref=source.at[pl.ds(j * rows, rows)],
            dst_ref=target,
            send_sem=outs.at[j],
            recv_sem=ins.at[0],
            device_id={"fsdp": part * count + j},
            device_id_type=pl.DeviceIdType.MESH,
        )

    def local(j):
        return pltpu.make_async_copy(source.at[pl.ds(j * rows, rows)], target, here.at[0])

    def greeting(barrier):
        pl.when(origin != shard)(lambda: greet(barrier, {"fsdp": origin}))
        return jnp.where(is_source, count, 0) - jnp.where(to_self, 1, 0)

    def each(act_remote, act_local):
        for j in range(count):
            mine = part * count + j == shard
            pl.when(jnp.logical_and(is_source, mine))(lambda j=j: act_local(local(j)))
            pl.when(jnp.logical_and(is_source, jnp.logical_not(mine)))(
                lambda j=j: act_remote(copy(j))
            )

    def begin():
        each(lambda c: c.start(), lambda c: c.start())

    def finish():
        each(lambda c: c.wait_send(), lambda c: c.wait())
        pl.when(origin != shard)(lambda: copy(0).wait_recv())

    return greeting, begin, nothing, finish


def line_job(sources, targets, scratch):
    (source,) = sources
    (target,) = targets
    far_out, far_in, near_out, near_in, here = scratch
    shards = target.shape[0]
    steps = shards // 2
    shard = lax.axis_index("fsdp")
    near = shard + 1 - 2 * (shard % 2)

    def away(start, k):
        return (start + 2 * k) % shards

    def send_line(origin, spot, device, out_sem, in_sem):
        return pltpu.make_async_remote_copy(
            src_ref=origin,
            dst_ref=target.at[spot],
            send_sem=out_sem,
            recv_sem=in_sem,
            device_id={"fsdp": device},
            device_id_type=pl.DeviceIdType.MESH,
        )

    own = pltpu.make_async_copy(source, target.at[shard], here.at[0])
    far = [
        send_line(source, shard, away(shard, k), far_out.at[k - 1], far_in.at[k - 1])
        for k in range(1, steps)
    ]
    far_came = [
        send_line(
            source, away(shard, steps - k), away(shard, k), far_out.at[k - 1], far_in.at[k - 1]
        )
        for k in range(1, steps)
    ]
    held = [shard] + [away(shard, steps - k) for k in range(1, steps)]
    close = [
        send_line(target.at[spot] if k else source, spot, near, near_out.at[k], near_in.at[k])
        for k, spot in enumerate(held)
    ]
    close_came = [
        send_line(source, away(near, steps - k) if k else near, near, near_out.at[k], near_in.at[k])
        for k in range(steps)
    ]

    def greeting(barrier):
        for k in range(1, steps):
            greet(barrier, {"fsdp": away(shard, k)})
        greet(barrier, {"fsdp": near})
        return steps

    def begin():
        own.start()
        for copy in far:
            copy.start()
        close[0].start()

    def finish():
        for k in range(1, steps):
            far_came[k - 1].wait_recv()
            close[k].start()
        for copy in close_came:
            copy.wait_recv()
        for copy in far + close:
            copy.wait_send()
        own.wait()

    return greeting, begin, nothing, finish


def spread_job(sources, targets, scratch):
    (source,) = sources
    gathered, target = targets
    *first, z_outs, z_ins, z_here = scratch
    _, begin_gather, middle_gather, finish_gather = gather_job(sources, [gathered], first)
    count = gathered.shape[0]
    place = lax.axis_index("seq")
    shard = lax.axis_index("fsdp")
    per = lax.axis_size("fsdp") // count
    piece = shard % count

    def owner(j):
        return true_chunk(place, j, count) * per + shard // count

    def chunk(j):
        return gathered.at[j] if j else source

    def copy(j):
        return pltpu.make_async_remote_copy(
            src_ref=chunk(j),
            dst_ref=target.at[piece],
            send_sem=z_outs.at[j],
            recv_sem=z_ins.at[piece],
            device_id={"fsdp": owner(j)},
            device_id_type=pl.DeviceIdType.MESH,
        )

    def arrival(p):
        return pltpu.make_async_remote_copy(
            src_ref=source,
            dst_ref=target.at[p],
            send_sem=z_outs.at[0],
            recv_sem=z_ins.at[p],
            device_id={"fsdp": owner(0)},
            device_id_type=pl.DeviceIdType.MESH,
        )

    def local(j):
        return pltpu.make_async_copy(chunk(j), target.at[piece], z_here.at[0])

    def origin(p):
        return (shard % per) * count + p

    def start(j):
        pl.when(owner(j) != shard)(lambda: copy(j).start())
        pl.when(owner(j) == shard)(lambda: local(j).start())

    def greeting(barrier):
        for p in range(count):
            pl.when(origin(p) != shard)(lambda p=p: greet(barrier, {"fsdp": origin(p)}))
        return jnp.where(shard % per == shard // count, count - 1, count)

    def begin():
        begin_gather()
        start(0)

    def middle():
        middle_gather()
        start(1)
        start(2)

    def finish():
        finish_gather()
        start(3)
        for j in range(count):
            pl.when(owner(j) != shard)(lambda j=j: copy(j).wait_send())
            pl.when(owner(j) == shard)(lambda j=j: local(j).wait())
        for p in range(count):
            pl.when(origin(p) != shard)(lambda p=p: arrival(p).wait_recv())

    return greeting, begin, middle, finish


def own_job(sources, targets, scratch):
    loaded, stored, held = scratch
    place = lax.axis_index("seq")
    count = lax.axis_size("seq")
    part = targets[0].shape[1]
    loads = []
    stores = []
    for c, target in enumerate(targets):
        for k, source in enumerate(sources):
            start = place * (source.shape[0] // count) + c * part
            spot = pl.ds(pl.multiple_of(start, part), part)
            n = c * len(sources) + k
            loads.append(pltpu.make_async_copy(source.at[spot], held.at[n], loaded.at[n]))
            stores.append(pltpu.make_async_copy(held.at[n], target.at[k], stored.at[n]))

    def begin():
        for load in loads:
            load.start()

    def middle():
        for load, store in zip(loads, stores):
            load.wait()
            store.start()

    def finish():
        for store in stores:
            store.wait()

    return no_greeting, begin, middle, finish


MAKERS = {
    "gather": gather_job,
    "scatter": scatter_job,
    "deal": deal_job,
    "spread": spread_job,
    "line": line_job,
    "own": own_job,
}


def job_scratch(job):
    kind, *arrays = job
    if kind == "scatter":
        _, rows, width = arrays[0].shape
        halves = pltpu.VMEM((2, rows // 2, width), BF16)
        return [
            pltpu.SemaphoreType.DMA((6,)),
            pltpu.SemaphoreType.DMA((6,)),
            pltpu.SemaphoreType.DMA((4,)),
            halves,
            halves,
            halves,
            pltpu.VMEM((rows, width), BF16),
            halves,
            pltpu.VMEM((rows, width), F32),
        ]
    if kind == "own":
        count = CHUNKS * len(arrays)
        rows, width = arrays[0].shape
        part = rows // lax.axis_size("seq") // CHUNKS
        return [
            pltpu.SemaphoreType.DMA((count,)),
            pltpu.SemaphoreType.DMA((count,)),
            pltpu.VMEM((count, part, width), BF16),
        ]
    moves = [
        pltpu.SemaphoreType.DMA((4,)),
        pltpu.SemaphoreType.DMA((4,)),
        pltpu.SemaphoreType.DMA((2,)),
    ]
    if kind == "deal":
        return moves
    if kind == "line":
        steps = lax.axis_size("fsdp") // 2
        return [pltpu.SemaphoreType.DMA((steps,))] * 4 + [pltpu.SemaphoreType.DMA((1,))]
    moves.append(pltpu.VMEM(arrays[0].shape, BF16))
    if kind == "spread":
        moves += [
            pltpu.SemaphoreType.DMA((4,)),
            pltpu.SemaphoreType.DMA((4,)),
            pltpu.SemaphoreType.DMA((1,)),
        ]
    return moves


def job_results(job):
    kind, *arrays = job
    shape = arrays[0].shape
    if kind == "gather":
        return [jax.ShapeDtypeStruct((4,) + shape, BF16)]
    if kind == "scatter":
        return [jax.ShapeDtypeStruct(shape[1:], F32)]
    if kind == "deal":
        return [jax.ShapeDtypeStruct((shape[0] // 4,) + shape[1:], BF16)]
    if kind == "spread":
        return [jax.ShapeDtypeStruct((4,) + shape, BF16)] * 2
    if kind == "line":
        return [jax.ShapeDtypeStruct((lax.axis_size("fsdp"),) + shape, BF16)]
    part = shape[0] // lax.axis_size("seq") // CHUNKS
    return [jax.ShapeDtypeStruct((len(arrays), part) + shape[1:], BF16)] * CHUNKS


def plain_job(job):
    kind, *arrays = job
    seqs = lax.axis_size("seq")
    shards = lax.axis_size("fsdp")
    per = shards // seqs
    ends = [(s, h, s * shards + s * per + h) for s in range(seqs) for h in range(per)]
    if kind == "gather":
        return [lax.all_gather(arrays[0], "seq", axis=0)]
    if kind == "scatter":
        return [lax.psum_scatter(arrays[0], "seq", scatter_dimension=0).astype(F32)]
    if kind == "deal":
        rows = arrays[0].shape[0] // seqs
        total = None
        for j in range(seqs):
            moves = [(end, s * shards + h * seqs + j) for s, h, end in ends]
            got = lax.ppermute(arrays[0][j * rows : (j + 1) * rows], ("seq", "fsdp"), moves)
            total = got if total is None else total + got
        return [total]
    if kind == "line":
        return [lax.all_gather(arrays[0], "fsdp", axis=0)]
    if kind == "spread":
        gathered = lax.all_gather(arrays[0], "seq", axis=0)
        pieces = []
        for p in range(seqs):
            total = None
            for q in range(seqs):
                moves = [
                    (s * shards + h * seqs + p, s * shards + q * per + h)
                    for s in range(seqs)
                    for h in range(per)
                ]
                got = lax.ppermute(gathered[q], ("seq", "fsdp"), moves)
                total = got if total is None else total + got
            pieces.append(total)
        return [gathered, jnp.stack(pieces)]
    own_rows = arrays[0].shape[0] // seqs
    part = own_rows // CHUNKS
    start = lax.axis_index("seq") * own_rows
    return [
        jnp.stack([lax.dynamic_slice_in_dim(w, start + c * part, part, 0) for w in arrays])
        for c in range(CHUNKS)
    ]


def meet(greetings):
    place = lax.axis_index("seq")
    barrier = pltpu.get_barrier_semaphore()
    for device in (over_one(place), over_two(place)):
        greet(barrier, {"seq": device})
    peers = 2
    for greeting in greetings:
        peers = peers + greeting(barrier)
    pl.semaphore_wait(barrier, peers)


def call(
    body, operands, in_specs, out_shape, out_specs, jobs, number, after=None,
    grid=(), scratch=(), cost=None, name=None, late=(),
):
    plain = lax.axis_size("seq") != 4
    results = [v for job in jobs for v in plain_job(job)] if plain else []
    inside = [] if plain else jobs
    extra = [] if after is None else [after]
    job_shapes = [job_scratch(job) for job in inside]
    job_outs = [job_results(job) for job in inside]
    n_in = len(operands)
    n_out = len(out_shape)

    def kernel(*refs):
        refs = list(refs)

        def take(count):
            taken, refs[:] = refs[:count], refs[count:]
            return taken

        ins = take(n_in)
        take(len(extra))
        sources = [take(len(job) - 1) for job in inside]
        outs = take(n_out)
        targets = [take(len(shapes)) for shapes in job_outs]
        held = take(len(scratch))
        loaded = take(len(late))
        marks = take(1) if late else []
        loads = [
            pltpu.make_async_copy(ins[n], ref, marks[0].at[k])
            for k, (n, ref) in enumerate(zip(late, loaded))
        ]
        for n, ref in zip(late, loaded):
            ins[n] = ref
        phases = [
            MAKERS[job[0]](source, target, take(len(shapes)))
            for job, source, target, shapes in zip(inside, sources, targets, job_shapes)
        ]

        def hook(k):
            if k == 0 and phases:
                meet([phase[0] for phase in phases])
            for phase in phases:
                phase[k + 1]()
            if k == 0:
                for load in loads:
                    load.start()
                for load in loads:
                    load.wait()

        body(hook, ins, outs, held)

    given = {}
    if inside:
        given = {"collective_id": number, "has_side_effects": True}
    arrays = [array for job in inside for array in job[1:]]
    in_specs = [ANY if n in late else spec for n, spec in enumerate(in_specs)]
    late_shapes = [pltpu.VMEM(operands[n].shape, operands[n].dtype) for n in late]
    if late:
        late_shapes.append(pltpu.SemaphoreType.DMA((len(late),)))
    shapes = [shape for shapes in job_outs for shape in shapes]
    made = pl.pallas_call(
        kernel,
        grid=grid,
        out_shape=tuple(out_shape) + tuple(shapes),
        in_specs=list(in_specs) + [ANY] * (len(extra) + len(arrays)),
        out_specs=tuple(out_specs) + (ANY,) * len(shapes),
        scratch_shapes=list(scratch)
        + late_shapes
        + [shape for shapes in job_shapes for shape in shapes],
        compiler_params=pltpu.CompilerParams(vmem_limit_bytes=VMEM_LIMIT, **given),
        cost_estimate=cost,
        name=name,
    )(*operands, *extra, *arrays)
    return list(made[:n_out]), list(made[n_out:]) + results


def transfer(jobs, number, after=None):
    if lax.axis_size("seq") != 4:
        return [v for job in jobs for v in plain_job(job)]

    def body(hook, ins, outs, held):
        for k in range(3):
            hook(k)

    return call(body, [], [], [], [], jobs, number, after, name="transfer")[1]


def partner(v):
    lane = lax.broadcasted_iota(jnp.int32, v.shape, 1)
    return jnp.where(lane % HEAD < HEAD // 2, pltpu.roll(v, 96, 1), pltpu.roll(v, 32, 1))


def head_mean(v, ones):
    high = v.astype(BF16)
    rest = (v - high.astype(F32)).astype(BF16)
    return dot(high, ones) + dot(rest, ones)


def true_chunk(place, c, count):
    if count != 4:
        return c
    low = 1 - place % 2 if c % 2 else place % 2
    high = 1 - place // 2 if c // 2 else place // 2
    return low + 2 * high


def prepare_heads(sizes, place, qkv_ref, qg_ref, kg_ref, cos_ref, sin_ref, ones, q_s, k_s, v_s):
    hq, hkv, _ = sizes
    seqs, rows_in, _ = qkv_ref.shape
    for c in range(seqs):
        j = true_chunk(place, c, seqs)
        rows = slice(c * rows_in, (c + 1) * rows_in)
        cos = cos_ref[rows, :]
        sin = sin_ref[rows, :]
        for p in range((hq + hkv) // 2):
            is_query = p < hq // 2
            x = qkv_ref[j, :, p * 128 : (p + 1) * 128].astype(F32)
            gain = qg_ref[...] * HEAD**-0.5 if is_query else kg_ref[...]
            y = x * lax.rsqrt(head_mean(x * x, ones) + EPSILON) * gain
            y = (y * cos + partner(y) * sin).astype(BF16)
            for t in range(2):
                part = y[:, t * HEAD : (t + 1) * HEAD]
                if is_query:
                    q_s[2 * p + t, rows, :] = part
                else:
                    k_s[2 * p - hq + t, rows, :] = part
        for t in range(hkv):
            start = (hq + hkv + t) * HEAD
            v_s[t, rows, :] = qkv_ref[j, :, start : start + HEAD]


def allowed_keys(block, first, keys, length):
    bound = jnp.minimum(first + lax.broadcasted_iota(jnp.int32, (block, 1), 0), length - 1)
    return lax.broadcasted_iota(jnp.int32, (block, keys), 1) <= bound


def attend_kernel(sizes, hook, ins, outs, held):
    len_ref, normal_ref, weight_ref, qg_ref, kg_ref, cos_ref, sin_ref, ones_ref, *out_w = ins
    out_ref, lse_ref, qkv_ref, *left = outs
    q_s, k_s, v_s, o_s = held
    hook(0)

    @pl.loop(0, qkv_ref.shape[0])
    def _(j):
        qkv_ref[j] = dot(normal_ref[j], weight_ref[...]).astype(BF16)

    hq, hkv, group = sizes
    seqs, rows_in, _ = qkv_ref.shape
    place = lax.axis_index("seq")
    prepare_heads(
        sizes, place, qkv_ref, qg_ref, kg_ref, cos_ref, sin_ref, ones_ref[...], q_s, k_s, v_s
    )
    for i in range(seqs * rows_in // BLOCK):
        keys = (i + 1) * BLOCK
        rows = slice(i * BLOCK, (i + 1) * BLOCK)
        keep = allowed_keys(BLOCK, i * BLOCK, keys, len_ref[0])

        def one_head(h, _):
            kv = h // group
            scores = dot(q_s[h, rows, :], k_s[kv, :keys, :], NT)
            scores = jnp.where(keep, scores, NEGATIVE)
            highest = jnp.max(scores, axis=1, keepdims=True)
            shifted = jnp.exp(scores - highest)
            total = jnp.sum(shifted, axis=1, keepdims=True)
            mixed = dot(shifted.astype(BF16), v_s[kv, :keys, :]) / total
            o_s[h, rows, :] = mixed.astype(BF16)
            lse_ref[h, rows, :] = highest + jnp.log(total)
            return 0

        lax.fori_loop(0, hq, one_head, 0, unroll=min(4, hq))
        if i == seqs * rows_in // BLOCK - 2:
            hook(1)
    for c in range(seqs):
        j = true_chunk(place, c, seqs)
        rows = slice(c * rows_in, (c + 1) * rows_in)
        for p in range(hq // 2):
            out_ref[j, :, p * 128 : (p + 1) * 128] = jnp.concatenate(
                [o_s[2 * p, rows, :], o_s[2 * p + 1, rows, :]], axis=1
            )
    for out_w_ref, left_ref in zip(out_w, left):
        for j in range(seqs):
            left_ref[j] = dot(out_ref[j], out_w_ref[...]).astype(BF16)
    hook(2)


def out_weight_grads(grads_ref, shards, slots):
    width = slots[0][0].shape[-1]
    model = slots[0][1].shape[-1]
    tile = min(256, width)
    piece = width // shards
    held = model // shards
    blocks = held // piece
    columns = model // blocks
    for t in range(width // tile):
        total = None
        for mixed_ref, res_ref in slots:
            rows = mixed_ref.shape[0] * mixed_ref.shape[1]
            mixed = mixed_ref[:, :, t * tile : (t + 1) * tile].reshape(rows, tile)
            term = dot(mixed, res_ref[...].reshape(rows, model), TN)
            total = term if total is None else total + term
        total = total.astype(BF16)
        for p in range(tile // piece):
            first = (t * (tile // piece) + p) * held
            for c in range(blocks):
                grads_ref[first + c * piece : first + (c + 1) * piece, :] = total[
                    p * piece : (p + 1) * piece, c * columns : (c + 1) * columns
                ]


def attend_back_kernel(sizes, shards, hook, ins, outs, held):
    (
        len_ref, qkv_ref, res_ref, out_w_ref, qkv_w_ref, lse_ref,
        qg_ref, kg_ref, cos_ref, sin_ref, ones_ref, *others,
    ) = ins
    dqkv_ref, dgain_ref, pull_ref, *out_grads = outs
    q_s, k_s, v_s, cot_s, dq_s, dk_s, dv_s = held
    hook(0)
    hq, hkv, group = sizes
    seqs, rows_in, _ = qkv_ref.shape
    place = lax.axis_index("seq")
    ones = ones_ref[...]
    prepare_heads(sizes, place, qkv_ref, qg_ref, kg_ref, cos_ref, sin_ref, ones, q_s, k_s, v_s)
    for c in range(seqs):
        j = true_chunk(place, c, seqs)
        cots = dot(res_ref[j], out_w_ref[...], NT).astype(BF16)
        for h in range(hq):
            cot_s[h, c * rows_in : (c + 1) * rows_in, :] = cots[:, h * HEAD : (h + 1) * HEAD]
    dk_s[...] = jnp.zeros_like(dk_s)
    dv_s[...] = jnp.zeros_like(dv_s)
    for i in range(seqs * rows_in // BLOCK):
        keys = (i + 1) * BLOCK
        rows = slice(i * BLOCK, (i + 1) * BLOCK)
        keep = allowed_keys(BLOCK, i * BLOCK, keys, len_ref[0])

        def one_head(h, _):
            kv = h // group
            q = q_s[h, rows, :]
            cot = cot_s[h, rows, :]
            k = k_s[kv, :keys, :]
            scores = jnp.where(keep, dot(q, k, NT), NEGATIVE)
            probs = jnp.exp(scores - lse_ref[h, rows, :])
            prob_cot = dot(cot, v_s[kv, :keys, :], NT)
            inner = jnp.sum(probs * prob_cot, axis=1, keepdims=True)
            score_cot = (probs * (prob_cot - inner)).astype(BF16)
            dq_s[h, rows, :] = dot(score_cot, k) * HEAD**-0.5
            dk_s[kv, :keys, :] += dot(score_cot, q, TN)
            dv_s[kv, :keys, :] += dot(probs.astype(BF16), cot, TN)
            return 0

        lax.fori_loop(0, hq, one_head, 0, unroll=min(4, hq))
        if i == seqs * rows_in // BLOCK - 2:
            for grads_ref in out_grads:
                before_ref, here_ref, res_before_ref = others
                out_weight_grads(
                    grads_ref, shards, ((before_ref, res_before_ref), (here_ref, res_ref))
                )
            hook(1)
    gain_sums = [jnp.zeros((1, 128), F32), jnp.zeros((1, 128), F32)]
    for c in range(seqs):
        j = true_chunk(place, c, seqs)
        rows = slice(c * rows_in, (c + 1) * rows_in)
        cos = cos_ref[rows, :]
        sin = sin_ref[rows, :]
        for p in range((hq + hkv) // 2):
            is_query = p < hq // 2
            x = qkv_ref[j, :, p * 128 : (p + 1) * 128].astype(F32)
            gain = qg_ref[...] if is_query else kg_ref[...]
            source, first = (dq_s, 2 * p) if is_query else (dk_s, 2 * p - hq)
            turned = jnp.concatenate([source[first, rows, :], source[first + 1, rows, :]], axis=1)
            scale = lax.rsqrt(head_mean(x * x, ones) + EPSILON)
            straight = turned * cos + partner(turned * sin)
            unit = x * scale
            which = 0 if is_query else 1
            gain_sums[which] += jnp.sum(straight * unit, axis=0, keepdims=True)
            pulled = gain * straight
            dx = scale * (pulled - unit * head_mean(unit * pulled, ones))
            dqkv_ref[j, :, p * 128 : (p + 1) * 128] = dx.astype(BF16)
        for p in range(hkv // 2):
            start = (hq + hkv) * HEAD + p * 128
            dqkv_ref[j, :, start : start + 128] = jnp.concatenate(
                [dv_s[2 * p, rows, :], dv_s[2 * p + 1, rows, :]], axis=1
            ).astype(BF16)
    dgain_ref[0:1, :] = gain_sums[0]
    dgain_ref[1:2, :] = gain_sums[1]

    @pl.loop(0, seqs)
    def _(j):
        pull_ref[j] = dot(dqkv_ref[j], qkv_w_ref[...], NT).astype(BF16)

    hook(2)


def position_tables(length):
    places = np.arange(length, dtype=np.float32)
    half = HEAD // 2
    freqs = np.float32(ROPE_BASE) ** (-(np.arange(half, dtype=np.float32) * 2.0) / HEAD)
    angles = places[:, None] * freqs.astype(np.float32)[None, :]
    cos = np.cos(angles).astype(np.float32)
    sin = np.sin(angles).astype(np.float32)
    ones = np.kron(np.eye(2), np.ones((HEAD, HEAD)) / HEAD)
    return (
        jnp.asarray(np.concatenate([cos] * 4, axis=1)),
        jnp.asarray(np.concatenate([-sin, sin, -sin, sin], axis=1)),
        jnp.asarray(ones, dtype=BF16),
    )


def attend(sizes, length, normal, weight, gains, tables, jobs, number, after, out_w=()):
    seqs, rows_in, _ = normal.shape
    hq, hkv, _ = sizes
    slot = seqs * rows_in
    return call(
        functools.partial(attend_kernel, sizes),
        [length, normal, weight, *gains, *tables, *out_w],
        [SMEM] + [VMEM] * (7 + len(out_w)),
        [
            jax.ShapeDtypeStruct((seqs, rows_in, hq * HEAD), BF16),
            jax.ShapeDtypeStruct((hq, slot, 1), F32),
            jax.ShapeDtypeStruct((seqs, rows_in, weight.shape[1]), BF16),
        ]
        + [jax.ShapeDtypeStruct(normal.shape, BF16)] * len(out_w),
        [VMEM] * (3 + len(out_w)),
        jobs,
        number,
        after,
        scratch=[
            pltpu.VMEM((hq, slot, HEAD), BF16),
            pltpu.VMEM((hkv, slot, HEAD), BF16),
            pltpu.VMEM((hkv, slot, HEAD), BF16),
            pltpu.VMEM((hq, slot, HEAD), BF16),
        ],
        cost=pl.CostEstimate(
            flops=56 * hq * slot * slot * HEAD, bytes_accessed=1 << 23, transcendentals=0
        ),
        name="attend",
        late=(1, 2) + tuple(range(8, 8 + len(out_w))),
    )


def attend_back(
    sizes, length, qkv, res, out_w, qkv_w, lse, gains, tables, jobs, number, after, others=()
):
    seqs, rows_in, width = qkv.shape
    hq, hkv, _ = sizes
    slot = seqs * rows_in
    shards = lax.axis_size("fsdp")
    model = res.shape[-1]
    columns = hq * HEAD // shards * model // (model // shards)
    return call(
        functools.partial(attend_back_kernel, sizes, shards),
        [length, qkv, res, out_w, qkv_w, lse, *gains, *tables, *others],
        [SMEM] + [VMEM] * (10 + len(others)),
        [
            jax.ShapeDtypeStruct((seqs, rows_in, width), BF16),
            jax.ShapeDtypeStruct((2, 128), F32),
            jax.ShapeDtypeStruct(res.shape, BF16),
        ]
        + [jax.ShapeDtypeStruct((model, columns), BF16)] * bool(others),
        [VMEM, VMEM, VMEM] + [VMEM] * bool(others),
        jobs,
        number,
        after,
        scratch=[
            pltpu.VMEM((hq, slot, HEAD), BF16),
            pltpu.VMEM((hkv, slot, HEAD), BF16),
            pltpu.VMEM((hkv, slot, HEAD), BF16),
            pltpu.VMEM((hq, slot, HEAD), BF16),
            pltpu.VMEM((hq, slot, HEAD), F32),
            pltpu.VMEM((hkv, slot, HEAD), F32),
            pltpu.VMEM((hkv, slot, HEAD), F32),
        ],
        cost=pl.CostEstimate(
            flops=88 * hq * slot * slot * HEAD, bytes_accessed=1 << 23, transcendentals=0
        ),
        name="attend_back",
        late=(1, 2, 3, 4, 5) + tuple(range(11, 11 + len(others))),
    )


def hooked(hook, step, steps, work):
    pl.when(step == 0)(lambda: hook(0))
    work(lambda: pl.when(step == (3 * steps) // 5)(lambda: hook(1)))
    pl.when(step == steps - 1)(lambda: hook(2))


def ffn_kernel(steps, hook, ins, outs, held):
    step = pl.program_id(0)
    weights_ref, loaded = held
    loads = [
        pltpu.make_async_copy(ins[2].at[:, k], weights_ref.at[k], loaded.at[k]) for k in range(3)
    ]

    def first(act):
        pl.when(step == 0)(act)

    def work(late):
        for load in loads:
            first(load.start)
        ffn_tile(late, first, loads, *ins[:2], weights_ref, ins[3:], *outs)

    hooked(hook, step, steps, work)


def ffn_tile(late, first, loads, mid_ref, cot_ref, weights_ref, sums, acts_ref, pull_ref):
    model = mid_ref.shape[-1]
    hidden = acts_ref.shape[-1]
    whole = (hidden, model)
    mid = mid_ref[...]
    first(loads[0].wait)
    gate = dot(mid, weights_ref[0].reshape(whole), NT)
    first(loads[1].wait)
    up = dot(mid, weights_ref[1].reshape(whole), NT)
    first(loads[2].wait)
    mids_cot = dot(cot_ref[...], weights_ref[2].reshape(whole), NT)
    late()
    sigmoid = jax.nn.sigmoid(gate)
    active = gate * sigmoid
    gate_cot = (mids_cot * up * sigmoid * (1.0 + gate * (1.0 - sigmoid))).astype(BF16)
    up_cot = (mids_cot * active).astype(BF16)
    acts_ref[0] = gate_cot
    acts_ref[1] = up_cot
    acts_ref[2] = (active * up).astype(BF16)
    pulled = dot(gate_cot, weights_ref[0].reshape(whole)) + dot(
        up_cot, weights_ref[1].reshape(whole)
    )
    for sum_ref in sums:
        pulled = pulled + sum_ref[...]
    pull_ref[...] = pulled.astype(pull_ref.dtype)


def ffn_both(mid, cot, weights, summed, last, jobs, number, after):
    tokens, model = mid.shape
    shards, _, part, _ = weights.shape
    hidden = shards * part
    tile = min(256, tokens)

    row_spec = pl.BlockSpec((tile, model), lambda i: (i, 0))
    extra = () if summed is None else (summed,)
    return call(
        functools.partial(ffn_kernel, tokens // tile),
        [mid, cot, weights, *extra],
        [row_spec, row_spec, ANY] + [row_spec] * len(extra),
        [
            jax.ShapeDtypeStruct((3, tokens, hidden), BF16),
            jax.ShapeDtypeStruct((tokens, model), BF16 if last else F32),
        ],
        [pl.BlockSpec((3, tile, hidden), lambda i: (0, i, 0)), row_spec],
        jobs,
        number,
        after,
        grid=(tokens // tile,),
        scratch=[
            pltpu.VMEM((3, shards, part, model), BF16),
            pltpu.SemaphoreType.DMA((3,)),
        ],
        cost=pl.CostEstimate(
            flops=16 * tokens * model * hidden,
            bytes_accessed=4 * tokens * model + 6 * hidden * model,
            transcendentals=0,
        ),
        name="ffn_both",
    )


def ffn_grad_kernel(slots, tiles, hook, ins, outs, held):
    acts = ins[:slots]
    others = ins[slots:]
    (out_ref,) = outs
    rows_ref, loaded = held
    kind = pl.program_id(0)
    step = kind * tiles + pl.program_id(1)
    loads = [
        pltpu.make_async_copy(other, rows_ref.at[k], loaded.at[k])
        for k, other in enumerate(others)
    ]

    def store(first):
        total = None
        for k, act in enumerate(acts):
            term = dot(act[0], rows_ref[first + k], TN)
            total = term if total is None else total + term
        out_ref[...] = total.astype(BF16).reshape(out_ref.shape)

    def work(late):
        for k, load in enumerate(loads):
            pl.when(step == 0)(load.start)
        for k, load in enumerate(loads):
            pl.when(step == (0 if k < slots else 2 * tiles))(load.wait)
        late()
        pl.when(kind < 2)(lambda: store(0))
        pl.when(kind == 2)(lambda: store(slots))

    hooked(hook, step, 3 * tiles, work)


def ffn_grads(acts, mids, cots, shards, jobs, number, after):
    slots = len(acts)
    _, tokens, hidden = acts[0].shape
    model = mids[0].shape[-1]
    part = hidden // shards
    tile = 256
    per = tile // part
    return call(
        functools.partial(ffn_grad_kernel, slots, hidden // tile),
        [*acts, *mids, *cots],
        [pl.BlockSpec((1, tokens, tile), lambda k, i: (k, 0, i))] * slots
        + [ANY] * (2 * slots),
        [jax.ShapeDtypeStruct((shards, 3, part, model), BF16)],
        [pl.BlockSpec((per, 1, part, model), lambda k, i: (i, k, 0, 0))],
        jobs,
        number,
        after,
        grid=(3, hidden // tile),
        scratch=[
            pltpu.VMEM((2 * slots, tokens, model), BF16),
            pltpu.SemaphoreType.DMA((2 * slots,)),
        ],
        cost=pl.CostEstimate(
            flops=9 * slots * tokens * model * hidden,
            bytes_accessed=4 * slots * tokens * model,
            transcendentals=0,
        ),
        name="ffn_grads",
    )


def ffn_down_kernel(chunks, steps, hook, ins, outs, held):
    acts = ins[:chunks]
    downs = ins[chunks:]
    (out_ref,) = outs

    def work(late):
        late()
        total = None
        for act, down in zip(acts, downs):
            hidden = act.shape[-1]
            term = dot(act[0], down[...].reshape(hidden, down.shape[-1]))
            total = term if total is None else total + term
        out_ref[...] = total.astype(BF16)

    hooked(hook, pl.program_id(0), steps, work)


def ffn_down(acts, weights, jobs, number, after, true_order=False):
    chunks = len(acts)
    _, tokens, hidden = acts[0].shape
    shards, _, part, model = weights[0].shape
    tile = min(256, tokens)
    def spot(i):
        if not true_order or lax.axis_size("seq") != 4:
            return i
        place = lax.axis_index("seq")
        low = (place % 2 + i % 2) % 2
        high = (place // 2 + i // 2) % 2
        return low + 2 * high

    act_spec = pl.BlockSpec((1, tile, hidden), lambda i: (2, i, 0))
    down_spec = pl.BlockSpec(
        (shards, 1, part, model),
        lambda i: (0, 2, 0, 0),
        pipeline_mode=pl.Buffered(buffer_count=1),
    )
    return call(
        functools.partial(ffn_down_kernel, chunks, tokens // tile),
        [*acts, *weights],
        [act_spec] * chunks + [down_spec] * chunks,
        [jax.ShapeDtypeStruct((tokens, model), BF16)],
        [pl.BlockSpec((tile, model), lambda i: (spot(i), 0))],
        jobs,
        number,
        after,
        grid=(tokens // tile,),
        cost=pl.CostEstimate(
            flops=4 * chunks * tokens * model * hidden,
            bytes_accessed=chunks * hidden * (tokens + model) * 2,
            transcendentals=0,
        ),
        name="ffn_down",
    )


def place_kernel(place_ref, parts_ref, *refs):
    for kind, out_ref in enumerate(refs[-3:]):
        out_ref[0, 0] = parts_ref[0, kind].astype(F32)


def place_parts(place, parts, chunk, held):
    seqs, _, part, model = parts.shape
    out = jax.ShapeDtypeStruct((seqs, CHUNKS, part, model), F32)
    out_spec = pl.BlockSpec(
        (1, 1, part, model), lambda j, at: (jnp.bitwise_xor(at[0], j), chunk, 0, 0)
    )
    return pl.pallas_call(
        place_kernel,
        out_shape=(out,) * 3,
        grid_spec=pltpu.PrefetchScalarGridSpec(
            num_scalar_prefetch=1,
            grid=(seqs,),
            in_specs=[pl.BlockSpec((1, 3, part, model), lambda j, at: (j, 0, 0, 0))]
            + [ANY] * len(held),
            out_specs=(out_spec,) * 3,
        ),
        input_output_aliases={2 + k: k for k in range(len(held))},
        compiler_params=pltpu.CompilerParams(vmem_limit_bytes=VMEM_LIMIT),
        cost_estimate=pl.CostEstimate(
            flops=0, bytes_accessed=18 * seqs * part * model, transcendentals=0
        ),
        name="place_parts",
    )(place, parts, *held)


def place_heads_kernel(
    place_ref, parts_ref, query_w_ref, key_w_ref, value_w_ref,
    query_ref, key_ref, value_ref, rest_ref, met_ref,
):
    edge = query_ref.shape[1]
    width = key_ref.shape[1]
    part = parts_ref[0].astype(F32)
    query_ref[...] = part[:, :edge]
    key_ref[...] = part[:, edge : edge + width]
    value_ref[...] = part[:, edge + width : edge + 2 * width]
    rest = part[:, edge + 2 * width :]
    met = jnp.zeros_like(met_ref)
    for grad_ref, weight_ref in (
        (query_ref, query_w_ref),
        (key_ref, key_w_ref),
        (value_ref, value_w_ref),
    ):
        product = grad_ref[...] * weight_ref[...].astype(F32)
        met = met + jnp.sum(product, axis=1, keepdims=True)

    @pl.when(pl.program_id(0) == 0)
    def _():
        rest_ref[...] = rest
        met_ref[...] = met

    @pl.when(pl.program_id(0) > 0)
    def _():
        rest_ref[...] += rest
        met_ref[...] += met


def place_heads(place, parts, edge, width, weights):
    seqs, rows, total = parts.shape
    rest = total - edge - 2 * width

    def column_spec(size):
        return pl.BlockSpec((rows, size), lambda j, at: (0, jnp.bitwise_xor(at[0], j)))

    return pl.pallas_call(
        place_heads_kernel,
        out_shape=[
            jax.ShapeDtypeStruct((rows, seqs * edge), F32),
            jax.ShapeDtypeStruct((rows, seqs * width), F32),
            jax.ShapeDtypeStruct((rows, seqs * width), F32),
            jax.ShapeDtypeStruct((rows, rest), F32),
            jax.ShapeDtypeStruct((rows, 128), F32),
        ],
        grid_spec=pltpu.PrefetchScalarGridSpec(
            num_scalar_prefetch=1,
            grid=(seqs,),
            in_specs=[
                pl.BlockSpec((1, rows, total), lambda j, at: (j, 0, 0)),
                column_spec(edge),
                column_spec(width),
                column_spec(width),
            ],
            out_specs=[
                column_spec(edge),
                column_spec(width),
                column_spec(width),
                pl.BlockSpec((rows, rest), lambda j, at: (0, 0)),
                pl.BlockSpec((rows, 128), lambda j, at: (0, 0)),
            ],
        ),
        compiler_params=pltpu.CompilerParams(vmem_limit_bytes=VMEM_LIMIT),
        name="place_heads",
    )(place, parts, *weights)


def scale_of(values):
    return lax.rsqrt(jnp.mean(values * values, axis=-1, keepdims=True) + EPSILON)


def normed(values, gain):
    return values * scale_of(values) * gain


def normed_back(values, gain, cot):
    scale = scale_of(values)
    pulled = cot * gain
    mean = jnp.mean(values * pulled, axis=-1, keepdims=True)
    return (
        scale * pulled - values * (scale * scale * scale) * mean,
        jnp.sum(cot * values * scale, axis=0),
    )


def follow(values, earlier):
    return lax.optimization_barrier((values, *earlier))[0]


def own_columns(weight, heads, place):
    width = heads * HEAD
    part = lax.dynamic_slice_in_dim(weight, place * width, width, 1)
    if heads % 2:
        part = jnp.pad(part, ((0, 0), (0, HEAD)))
    return part


def on_device(
    tokens,
    cotangent,
    lengths,
    attn_gain,
    query_weight,
    key_weight,
    value_weight,
    query_gain,
    key_gain,
    out_weight,
    ffn_gain,
    gate_weight,
    up_weight,
    down_weight,
):
    slots, rows, model = tokens.shape
    seqs = lax.axis_size("seq")
    shards = lax.axis_size("fsdp")
    place = lax.axis_index("seq")
    shard = lax.axis_index("fsdp")
    slot_len = rows * seqs
    query_width = query_weight.shape[1]
    kv_width = key_weight.shape[1]
    hq = query_width // seqs // HEAD
    hkv = kv_width // seqs // HEAD
    hkv_held = hkv + hkv % 2
    sizes = (hq, hkv_held, hq // hkv)
    order = (place if seqs == 4 else place * 0).reshape(1)
    tables = position_tables(slot_len)
    gains = (
        jnp.concatenate([query_gain, query_gain]).reshape(1, 2 * HEAD),
        jnp.concatenate([key_gain, key_gain]).reshape(1, 2 * HEAD),
    )

    flat = (slot_len, model)
    chunked = (seqs, rows, model)
    places = place * rows + jnp.arange(rows, dtype=jnp.int32)
    live = (places[None, :] < lengths[:, None]).astype(F32)[..., None]
    inputs = tokens.astype(F32)
    out_cot = cotangent.astype(F32) * live
    out_low = [out_cot[b].astype(BF16) for b in range(slots)]
    normal_in = [normed(inputs[b], attn_gain).astype(BF16) for b in range(slots)]

    qkv_own = jnp.concatenate(
        [
            own_columns(query_weight, hq, place),
            own_columns(key_weight, hkv, place),
            own_columns(value_weight, hkv, place),
        ],
        axis=1,
    )
    qkv_weight = lax.all_gather(qkv_own, "fsdp", axis=0, tiled=True)
    start = [
        ("gather", normal_in[0]),
        ("deal", out_weight),
        ("own", gate_weight, up_weight, down_weight),
    ]
    normal_0, out_own, *ffn_own = transfer(start, 1)
    hidden_own = gate_weight.shape[0] // seqs
    part = hidden_own // CHUNKS
    ffn_weights = [lax.all_gather(own, "fsdp", axis=0) for own in ffn_own]

    def leave(mixed):
        return dot(mixed.reshape(slot_len, -1), out_rows).astype(BF16).reshape(chunked)

    def enter_ffn(b, total):
        res = inputs[b] + total
        return res, normed(res, ffn_gain).astype(BF16)

    def heads(b, jobs, number, after, out_w=()):
        return attend(
            sizes, lengths[b : b + 1], normal_full[b].reshape(chunked), qkv_weight, gains, tables,
            jobs, number, after, out_w,
        )

    normal_full = [None] * slots
    cot_full = [None] * slots
    mid_full = [None] * slots
    normal_full[0] = normal_0
    (mixed_0, lse_0, qkv_0), (normal_full[1], out_rows) = heads(
        0, [("gather", normal_in[1]), ("line", out_own)], 2, normal_full[0]
    )
    out_rows = out_rows.reshape(-1, model)
    (mixed_1, lse_1, qkv_1, left_1), (total_0,) = heads(
        1, [("scatter", leave(mixed_0))], 3, mixed_0, (out_rows,)
    )
    qkv = [qkv_0, qkv_1]
    log_sums = [lse_0, lse_1]
    res_0, mid_0 = enter_ffn(0, total_0)
    mid_full[0], cot_full[0] = [
        v.reshape(flat)
        for v in transfer([("gather", mid_0), ("gather", out_low[0])], 4, mixed_1)
    ]

    acts = [[None] * slots for _ in range(CHUNKS)]
    pulled = [None] * slots

    def ffn_step(b, c, jobs, number, after):
        (acts[c][b], pulled[b]), results = ffn_both(
            mid_full[b], cot_full[b], ffn_weights[c], pulled[b], c == CHUNKS - 1,
            jobs, number, after,
        )
        return results

    def grad_step(c, jobs, number, after):
        (grads,), results = ffn_grads(
            acts[c], mid_full, cot_full, shards, jobs, number, after
        )
        return grads.reshape(shards, 3 * part, model), results

    def leave_ffn(b, jobs, number, after, true_order=False):
        (out,), results = ffn_down(
            [acts[c][b] for c in range(CHUNKS)], ffn_weights, jobs, number, after, true_order
        )
        return out.reshape(chunked), results

    total_1, full = ffn_step(
        0, 0, [("scatter", left_1), ("gather", out_low[1])], 5, mid_full[0]
    )
    cot_full[1] = full.reshape(flat)
    res_1, mid_1 = enter_ffn(1, total_1)
    hidden_res = [res_0, res_1]
    (full,) = ffn_step(0, 1, [("gather", mid_1)], 6, acts[0][0])
    mid_full[1] = full.reshape(flat)
    (mid_total_0,) = ffn_step(1, 0, [("scatter", pulled[0].reshape(chunked))], 7, acts[1][0])

    def pull_mid(b, total):
        pull, gain_part = normed_back(hidden_res[b], ffn_gain, total)
        cot = out_cot[b] + pull
        return cot, cot.astype(BF16), gain_part

    res_cot_0, low_0, ffn_gain_0 = pull_mid(0, mid_total_0)
    grads_0, (res_full_0,) = grad_step(0, [("gather", low_0)], 8, acts[0][1])
    ffn_sums = [lax.psum_scatter(grads_0, "fsdp", scatter_dimension=0)]
    out_0, _ = leave_ffn(0, [], 0, grads_0)
    (out_total_0,) = ffn_step(1, 1, [("scatter", out_0)], 9, out_0)
    grads_1, (mid_total_1,) = grad_step(
        1, [("scatter", pulled[1].reshape(chunked))], 10, acts[1][1]
    )
    ffn_sums.append(
        lax.psum_scatter(grads_1, "fsdp", scatter_dimension=0)
    )
    res_cot_1, low_1, ffn_gain_1 = pull_mid(1, mid_total_1)
    grad_ffn_gain = ffn_gain_0 + ffn_gain_1

    def back(b, full, jobs, number, after, others=()):
        return attend_back(
            sizes, lengths[b : b + 1], qkv[b], full, out_rows, qkv_weight, log_sums[b],
            gains, tables, jobs, number, after, others,
        )

    (dqkv_0, heads_gain_0, pull_0), (res_full_1,) = back(
        0, res_full_0, [("gather", low_1)], 11, grads_1
    )
    (dqkv_1, heads_gain_1, pull_1, out_grads), (in_total_0, ffn_parts_0) = back(
        1,
        res_full_1,
        [("scatter", pull_0), ("gather", ffn_sums[0])],
        12,
        dqkv_0,
        (mixed_0, mixed_1, res_full_0),
    )
    head_gain = heads_gain_0 + heads_gain_1
    dqkv = [v.reshape(slot_len, -1) for v in (dqkv_0, dqkv_1)]
    held = model // shards
    piece = hq * HEAD // shards
    blocks = held // piece
    head_sums = jnp.pad(
        (head_gain[:, :HEAD] + head_gain[:, HEAD:]).reshape(2, shards, HEAD // shards),
        ((0, 0), (0, 0), (0, held - HEAD // shards)),
    ).reshape(2, model)
    gain_columns = jnp.stack([grad_ffn_gain, head_sums[0], head_sums[1]], axis=1).astype(BF16)
    attn_grads = jnp.concatenate(
        [
            sum(dot(normal_full[b].reshape(flat), dqkv[b], TN) for b in range(slots)).astype(BF16),
            jnp.pad(gain_columns, ((0, 0), (0, 125))),
            out_grads,
        ],
        axis=1,
    )
    out_1, (in_total_1,) = leave_ffn(1, [("scatter", pull_1)], 13, attn_grads, True)
    attn_sums = lax.psum_scatter(
        follow(attn_grads, [ffn_sums[1], in_total_1]), "fsdp", scatter_dimension=0, tiled=True
    )
    (ffn_parts_1,) = transfer([("gather", ffn_sums[1])], 15, in_total_1)
    ffn_grad = ()
    for c, parts in enumerate((ffn_parts_0, ffn_parts_1)):
        ffn_grad = place_parts(order, parts.reshape(seqs, 3, part, model), c, ffn_grad)
    out_edge = attn_sums.shape[1] - model // blocks
    heads_all, _, out_parts = transfer(
        [("gather", attn_sums[:, :out_edge]), ("spread", attn_sums[:, out_edge:])],
        14,
        ffn_grad[0],
    )
    grad_out = jnp.swapaxes(
        out_parts.reshape(seqs, blocks, piece, model // blocks), 1, 2
    ).reshape(held, model)
    grad_tokens = []
    for b, (in_cot, cot) in enumerate(((in_total_0, res_cot_0), (in_total_1, res_cot_1))):
        pull, _ = normed_back(inputs[b], attn_gain, in_cot)
        grad_tokens.append((cot + pull).astype(BF16))
    out_total_1 = lax.psum_scatter(
        follow(out_1, [attn_sums, ffn_grad[0], *grad_tokens]), "seq", scatter_dimension=0
    ).astype(F32)
    output = [
        (live[b] * (hidden_res[b] + total)).astype(BF16)
        for b, total in enumerate((out_total_0, out_total_1))
    ]
    ffn_grad = [v.reshape(seqs * hidden_own, model) for v in ffn_grad]

    edge = hq * HEAD
    width = hkv_held * HEAD
    if hkv == hkv_held:
        grad_query, grad_key, grad_value, gain_sums, met = place_heads(
            order, heads_all, edge, width, (query_weight, key_weight, value_weight)
        )
        met = met[:, 0]
    else:
        heads_all = jnp.moveaxis(heads_all, 0, 1).astype(F32)
        last = edge + width
        grad_query = heads_all[..., :edge].reshape(held, query_width)
        grad_key = heads_all[..., edge : edge + hkv * HEAD].reshape(held, kv_width)
        grad_value = heads_all[..., last : last + hkv * HEAD].reshape(held, kv_width)
        gain_sums = jnp.sum(heads_all[..., last + width :], axis=1)
        met = sum(
            jnp.sum(grad * weight.astype(F32), axis=1)
            for grad, weight in (
                (grad_query, query_weight),
                (grad_key, key_weight),
                (grad_value, value_weight),
            )
        )
    grad_attn_gain = met / lax.dynamic_slice_in_dim(attn_gain, shard * held, held, 0)

    return (
        jnp.stack(output),
        jnp.stack(grad_tokens),
        grad_attn_gain,
        grad_query,
        grad_key,
        grad_value,
        gain_sums[: HEAD // shards, 1],
        gain_sums[: HEAD // shards, 2],
        grad_out.astype(F32),
        gain_sums[:, 0],
        ffn_grad[0],
        ffn_grad[1],
        ffn_grad[2],
    )


def solution(mesh):
    return jax.shard_map(
        on_device,
        mesh=mesh,
        in_specs=(
            P("fsdp", "seq", None),
            P("fsdp", "seq", None),
            P("fsdp"),
            P(),
            P("fsdp", None),
            P("fsdp", None),
            P("fsdp", None),
            P(),
            P(),
            P("fsdp", None),
            P(),
            P("fsdp", None),
            P("fsdp", None),
            P("fsdp", None),
        ),
        out_specs=(
            P("fsdp", "seq", None),
            P("fsdp", "seq", None),
            P("fsdp"),
            P("fsdp", None),
            P("fsdp", None),
            P("fsdp", None),
            P("fsdp"),
            P("fsdp"),
            P("fsdp", None),
            P("fsdp"),
            P("fsdp", None),
            P("fsdp", None),
            P("fsdp", None),
        ),
        check_vma=False,
    )
```

```python
import functools

import jax
import jax.numpy as jnp
import numpy as np
from jax import lax
from jax.experimental import pallas as pl
from jax.experimental.pallas import tpu as pltpu
from jax.sharding import PartitionSpec as P

EPSILON = 1e-05
ROPE_BASE = 1000000.0
NEGATIVE = -1e30
F32 = jnp.float32
BF16 = jnp.bfloat16
NN = (((1,), (0,)), ((), ()))
NT = (((1,), (1,)), ((), ()))
TN = (((0,), (0,)), ((), ()))
SMEM = pl.BlockSpec(memory_space=pltpu.SMEM)
VMEM = pl.BlockSpec(memory_space=pltpu.VMEM)
VMEM_LIMIT = 58 << 20
HEAD = 64
BLOCK = 256
CHUNKS = 2
ANY = pl.BlockSpec(memory_space=pl.ANY)


def dot(a, b, dims=NN):
    return lax.dot_general(a, b, dims, preferred_element_type=F32)


def over_one(place):
    return place + 1 - 2 * (place % 2)


def over_two(place):
    return (place + 2) % 4


def send(source, target, device, out_sem, in_sem):
    return pltpu.make_async_remote_copy(
        src_ref=source,
        dst_ref=target,
        send_sem=out_sem,
        recv_sem=in_sem,
        device_id={"seq": device},
        device_id_type=pl.DeviceIdType.MESH,
    )


def gather_job(sources, targets, scratch):
    (source,) = sources
    (target,) = targets
    outs, ins, here, held = scratch
    place = lax.axis_index("seq")
    one, two = over_one(place), over_two(place)
    half = source.shape[0] // 2
    load = pltpu.make_async_copy(source, held, here.at[0])
    store = pltpu.make_async_copy(held, target.at[0], here.at[1])
    first = send(source, target.at[1], one, outs.at[0], ins.at[0])
    second = send(source, target.at[2], two, outs.at[1], ins.at[1])
    top = pl.ds(0, half)
    low = pl.ds(half, half)
    third = send(target.at[2, top], target.at[3, top], one, outs.at[2], ins.at[2])
    fourth = send(target.at[1, low], target.at[3, low], two, outs.at[3], ins.at[3])

    def begin():
        first.start()
        second.start()
        load.start()

    def middle():
        load.wait()
        store.start()
        second.wait_recv()
        third.start()
        first.wait_recv()
        fourth.start()

    def finish():
        third.wait_recv()
        fourth.wait_recv()
        for copy in (first, second, third, fourth):
            copy.wait_send()
        store.wait()

    return no_greeting, begin, middle, finish


def scatter_job(sources, targets, scratch):
    (parts,) = sources
    (total,) = targets
    outs, ins, here, got_one, got_two, kept, own, last, summed = scratch
    place = lax.axis_index("seq")
    one, two = over_one(place), over_two(place)
    half = parts.shape[1] // 2
    top = pl.ds(0, half)
    low = pl.ds(half, half)
    sends = [
        send(parts.at[3, top], got_one.at[0], one, outs.at[0], ins.at[0]),
        send(parts.at[3, low], got_two.at[0], two, outs.at[1], ins.at[1]),
        send(parts.at[1, top], got_one.at[1], one, outs.at[2], ins.at[2]),
        send(parts.at[2, low], got_two.at[1], two, outs.at[3], ins.at[3]),
        send(kept.at[0], last.at[0], two, outs.at[4], ins.at[4]),
        send(kept.at[1], last.at[1], one, outs.at[5], ins.at[5]),
    ]
    loads = [
        pltpu.make_async_copy(parts.at[2, top], kept.at[0], here.at[0]),
        pltpu.make_async_copy(parts.at[1, low], kept.at[1], here.at[1]),
        pltpu.make_async_copy(parts.at[0], own, here.at[2]),
    ]
    store = pltpu.make_async_copy(summed, total, here.at[3])

    def begin():
        for copy in sends[:4]:
            copy.start()
        for copy in loads:
            copy.start()

    def middle():
        for k, got in enumerate((got_one, got_two)):
            loads[k].wait()
            sends[k].wait_recv()
            kept[k] = (kept[k].astype(F32) + got[0].astype(F32)).astype(BF16)
            sends[4 + k].start()

    def finish():
        loads[2].wait()
        for k, got in enumerate((got_one, got_two)):
            sends[2 + k].wait_recv()
            sends[4 + k].wait_recv()
            rows = slice(k * half, (k + 1) * half)
            summed[rows, :] = (
                own[rows, :].astype(F32) + got[1].astype(F32) + last[k].astype(F32)
            )
        store.start()
        for copy in sends:
            copy.wait_send()
        store.wait()

    return no_greeting, begin, middle, finish


def no_greeting(barrier):
    return 0


def nothing():
    pass


def greet(barrier, device):
    pl.semaphore_signal(
        barrier, inc=1, device_id=device, device_id_type=pl.DeviceIdType.MESH
    )


def deal_job(sources, targets, scratch):
    (source,) = sources
    (target,) = targets
    outs, ins, here = scratch
    rows = target.shape[0]
    count = source.shape[0] // rows
    place = lax.axis_index("seq")
    shard = lax.axis_index("fsdp")
    per = lax.axis_size("fsdp") // count
    part = shard % per
    is_source = shard // per == place
    to_self = jnp.logical_and(is_source, shard // count == part)
    origin = place * per + shard // count

    def copy(j):
        return pltpu.make_async_remote_copy(
            src_ref=source.at[pl.ds(j * rows, rows)],
            dst_ref=target,
            send_sem=outs.at[j],
            recv_sem=ins.at[0],
            device_id={"fsdp": part * count + j},
            device_id_type=pl.DeviceIdType.MESH,
        )

    def local(j):
        return pltpu.make_async_copy(source.at[pl.ds(j * rows, rows)], target, here.at[0])

    def greeting(barrier):
        pl.when(origin != shard)(lambda: greet(barrier, {"fsdp": origin}))
        return jnp.where(is_source, count, 0) - jnp.where(to_self, 1, 0)

    def each(act_remote, act_local):
        for j in range(count):
            mine = part * count + j == shard
            pl.when(jnp.logical_and(is_source, mine))(lambda j=j: act_local(local(j)))
            pl.when(jnp.logical_and(is_source, jnp.logical_not(mine)))(
                lambda j=j: act_remote(copy(j))
            )

    def begin():
        each(lambda c: c.start(), lambda c: c.start())

    def finish():
        each(lambda c: c.wait_send(), lambda c: c.wait())
        pl.when(origin != shard)(lambda: copy(0).wait_recv())

    return greeting, begin, nothing, finish


def line_job(sources, targets, scratch):
    (source,) = sources
    (target,) = targets
    far_out, far_in, near_out, near_in, here = scratch
    shards = target.shape[0]
    steps = shards // 2
    shard = lax.axis_index("fsdp")
    near = shard + 1 - 2 * (shard % 2)

    def away(start, k):
        return (start + 2 * k) % shards

    def send_line(origin, spot, device, out_sem, in_sem):
        return pltpu.make_async_remote_copy(
            src_ref=origin,
            dst_ref=target.at[spot],
            send_sem=out_sem,
            recv_sem=in_sem,
            device_id={"fsdp": device},
            device_id_type=pl.DeviceIdType.MESH,
        )

    own = pltpu.make_async_copy(source, target.at[shard], here.at[0])
    far = [
        send_line(source, shard, away(shard, k), far_out.at[k - 1], far_in.at[k - 1])
        for k in range(1, steps)
    ]
    far_came = [
        send_line(
            source, away(shard, steps - k), away(shard, k), far_out.at[k - 1], far_in.at[k - 1]
        )
        for k in range(1, steps)
    ]
    held = [shard] + [away(shard, steps - k) for k in range(1, steps)]
    close = [
        send_line(target.at[spot] if k else source, spot, near, near_out.at[k], near_in.at[k])
        for k, spot in enumerate(held)
    ]
    close_came = [
        send_line(source, away(near, steps - k) if k else near, near, near_out.at[k], near_in.at[k])
        for k in range(steps)
    ]

    def greeting(barrier):
        for k in range(1, steps):
            greet(barrier, {"fsdp": away(shard, k)})
        greet(barrier, {"fsdp": near})
        return steps

    def begin():
        own.start()
        for copy in far:
            copy.start()
        close[0].start()

    def finish():
        for k in range(1, steps):
            far_came[k - 1].wait_recv()
            close[k].start()
        for copy in close_came:
            copy.wait_recv()
        for copy in far + close:
            copy.wait_send()
        own.wait()

    return greeting, begin, nothing, finish


def spread_job(sources, targets, scratch):
    (source,) = sources
    gathered, target = targets
    *first, z_outs, z_ins, z_here = scratch
    _, begin_gather, middle_gather, finish_gather = gather_job(sources, [gathered], first)
    count = gathered.shape[0]
    place = lax.axis_index("seq")
    shard = lax.axis_index("fsdp")
    per = lax.axis_size("fsdp") // count
    piece = shard % count

    def owner(j):
        return true_chunk(place, j, count) * per + shard // count

    def chunk(j):
        return gathered.at[j] if j else source

    def copy(j):
        return pltpu.make_async_remote_copy(
            src_ref=chunk(j),
            dst_ref=target.at[piece],
            send_sem=z_outs.at[j],
            recv_sem=z_ins.at[piece],
            device_id={"fsdp": owner(j)},
            device_id_type=pl.DeviceIdType.MESH,
        )

    def arrival(p):
        return pltpu.make_async_remote_copy(
            src_ref=source,
            dst_ref=target.at[p],
            send_sem=z_outs.at[0],
            recv_sem=z_ins.at[p],
            device_id={"fsdp": owner(0)},
            device_id_type=pl.DeviceIdType.MESH,
        )

    def local(j):
        return pltpu.make_async_copy(chunk(j), target.at[piece], z_here.at[0])

    def origin(p):
        return (shard % per) * count + p

    def start(j):
        pl.when(owner(j) != shard)(lambda: copy(j).start())
        pl.when(owner(j) == shard)(lambda: local(j).start())

    def greeting(barrier):
        for p in range(count):
            pl.when(origin(p) != shard)(lambda p=p: greet(barrier, {"fsdp": origin(p)}))
        return jnp.where(shard % per == shard // count, count - 1, count)

    def begin():
        begin_gather()
        start(0)

    def middle():
        middle_gather()
        start(1)
        start(2)

    def finish():
        finish_gather()
        start(3)
        for j in range(count):
            pl.when(owner(j) != shard)(lambda j=j: copy(j).wait_send())
            pl.when(owner(j) == shard)(lambda j=j: local(j).wait())
        for p in range(count):
            pl.when(origin(p) != shard)(lambda p=p: arrival(p).wait_recv())

    return greeting, begin, middle, finish


def own_job(sources, targets, scratch):
    loaded, stored, held = scratch
    place = lax.axis_index("seq")
    count = lax.axis_size("seq")
    part = targets[0].shape[1]
    loads = []
    stores = []
    for c, target in enumerate(targets):
        for k, source in enumerate(sources):
            start = place * (source.shape[0] // count) + c * part
            spot = pl.ds(pl.multiple_of(start, part), part)
            n = c * len(sources) + k
            loads.append(pltpu.make_async_copy(source.at[spot], held.at[n], loaded.at[n]))
            stores.append(pltpu.make_async_copy(held.at[n], target.at[k], stored.at[n]))

    def begin():
        for load in loads:
            load.start()

    def middle():
        for load, store in zip(loads, stores):
            load.wait()
            store.start()

    def finish():
        for store in stores:
            store.wait()

    return no_greeting, begin, middle, finish


MAKERS = {
    "gather": gather_job,
    "scatter": scatter_job,
    "deal": deal_job,
    "spread": spread_job,
    "line": line_job,
    "own": own_job,
}


def job_scratch(job):
    kind, *arrays = job
    if kind == "scatter":
        _, rows, width = arrays[0].shape
        halves = pltpu.VMEM((2, rows // 2, width), BF16)
        return [
            pltpu.SemaphoreType.DMA((6,)),
            pltpu.SemaphoreType.DMA((6,)),
            pltpu.SemaphoreType.DMA((4,)),
            halves,
            halves,
            halves,
            pltpu.VMEM((rows, width), BF16),
            halves,
            pltpu.VMEM((rows, width), F32),
        ]
    if kind == "own":
        count = CHUNKS * len(arrays)
        rows, width = arrays[0].shape
        part = rows // lax.axis_size("seq") // CHUNKS
        return [
            pltpu.SemaphoreType.DMA((count,)),
            pltpu.SemaphoreType.DMA((count,)),
            pltpu.VMEM((count, part, width), BF16),
        ]
    moves = [
        pltpu.SemaphoreType.DMA((4,)),
        pltpu.SemaphoreType.DMA((4,)),
        pltpu.SemaphoreType.DMA((2,)),
    ]
    if kind == "deal":
        return moves
    if kind == "line":
        steps = lax.axis_size("fsdp") // 2
        return [pltpu.SemaphoreType.DMA((steps,))] * 4 + [pltpu.SemaphoreType.DMA((1,))]
    moves.append(pltpu.VMEM(arrays[0].shape, BF16))
    if kind == "spread":
        moves += [
            pltpu.SemaphoreType.DMA((4,)),
            pltpu.SemaphoreType.DMA((4,)),
            pltpu.SemaphoreType.DMA((1,)),
        ]
    return moves


def job_results(job):
    kind, *arrays = job
    shape = arrays[0].shape
    if kind == "gather":
        return [jax.ShapeDtypeStruct((4,) + shape, BF16)]
    if kind == "scatter":
        return [jax.ShapeDtypeStruct(shape[1:], F32)]
    if kind == "deal":
        return [jax.ShapeDtypeStruct((shape[0] // 4,) + shape[1:], BF16)]
    if kind == "spread":
        return [jax.ShapeDtypeStruct((4,) + shape, BF16)] * 2
    if kind == "line":
        return [jax.ShapeDtypeStruct((lax.axis_size("fsdp"),) + shape, BF16)]
    part = shape[0] // lax.axis_size("seq") // CHUNKS
    return [jax.ShapeDtypeStruct((len(arrays), part) + shape[1:], BF16)] * CHUNKS


def plain_job(job):
    kind, *arrays = job
    seqs = lax.axis_size("seq")
    shards = lax.axis_size("fsdp")
    per = shards // seqs
    ends = [(s, h, s * shards + s * per + h) for s in range(seqs) for h in range(per)]
    if kind == "gather":
        return [lax.all_gather(arrays[0], "seq", axis=0)]
    if kind == "scatter":
        return [lax.psum_scatter(arrays[0], "seq", scatter_dimension=0).astype(F32)]
    if kind == "deal":
        rows = arrays[0].shape[0] // seqs
        total = None
        for j in range(seqs):
            moves = [(end, s * shards + h * seqs + j) for s, h, end in ends]
            got = lax.ppermute(arrays[0][j * rows : (j + 1) * rows], ("seq", "fsdp"), moves)
            total = got if total is None else total + got
        return [total]
    if kind == "line":
        return [lax.all_gather(arrays[0], "fsdp", axis=0)]
    if kind == "spread":
        gathered = lax.all_gather(arrays[0], "seq", axis=0)
        pieces = []
        for p in range(seqs):
            total = None
            for q in range(seqs):
                moves = [
                    (s * shards + h * seqs + p, s * shards + q * per + h)
                    for s in range(seqs)
                    for h in range(per)
                ]
                got = lax.ppermute(gathered[q], ("seq", "fsdp"), moves)
                total = got if total is None else total + got
            pieces.append(total)
        return [gathered, jnp.stack(pieces)]
    own_rows = arrays[0].shape[0] // seqs
    part = own_rows // CHUNKS
    start = lax.axis_index("seq") * own_rows
    return [
        jnp.stack([lax.dynamic_slice_in_dim(w, start + c * part, part, 0) for w in arrays])
        for c in range(CHUNKS)
    ]


def meet(greetings):
    place = lax.axis_index("seq")
    barrier = pltpu.get_barrier_semaphore()
    for device in (over_one(place), over_two(place)):
        greet(barrier, {"seq": device})
    peers = 2
    for greeting in greetings:
        peers = peers + greeting(barrier)
    pl.semaphore_wait(barrier, peers)


def call(
    body, operands, in_specs, out_shape, out_specs, jobs, number, after=None,
    grid=(), scratch=(), cost=None, name=None, late=(),
):
    plain = lax.axis_size("seq") != 4
    results = [v for job in jobs for v in plain_job(job)] if plain else []
    inside = [] if plain else jobs
    extra = [] if after is None else [after]
    job_shapes = [job_scratch(job) for job in inside]
    job_outs = [job_results(job) for job in inside]
    n_in = len(operands)
    n_out = len(out_shape)

    def kernel(*refs):
        refs = list(refs)

        def take(count):
            taken, refs[:] = refs[:count], refs[count:]
            return taken

        ins = take(n_in)
        take(len(extra))
        sources = [take(len(job) - 1) for job in inside]
        outs = take(n_out)
        targets = [take(len(shapes)) for shapes in job_outs]
        held = take(len(scratch))
        loaded = take(len(late))
        marks = take(1) if late else []
        loads = [
            pltpu.make_async_copy(ins[n], ref, marks[0].at[k])
            for k, (n, ref) in enumerate(zip(late, loaded))
        ]
        for n, ref in zip(late, loaded):
            ins[n] = ref
        phases = [
            MAKERS[job[0]](source, target, take(len(shapes)))
            for job, source, target, shapes in zip(inside, sources, targets, job_shapes)
        ]

        def hook(k):
            if k == 0 and phases:
                meet([phase[0] for phase in phases])
            for phase in phases:
                phase[k + 1]()
            if k == 0:
                for load in loads:
                    load.start()
                for load in loads:
                    load.wait()

        body(hook, ins, outs, held)

    given = {}
    if inside:
        given = {"collective_id": number, "has_side_effects": True}
    arrays = [array for job in inside for array in job[1:]]
    in_specs = [ANY if n in late else spec for n, spec in enumerate(in_specs)]
    late_shapes = [pltpu.VMEM(operands[n].shape, operands[n].dtype) for n in late]
    if late:
        late_shapes.append(pltpu.SemaphoreType.DMA((len(late),)))
    shapes = [shape for shapes in job_outs for shape in shapes]
    made = pl.pallas_call(
        kernel,
        grid=grid,
        out_shape=tuple(out_shape) + tuple(shapes),
        in_specs=list(in_specs) + [ANY] * (len(extra) + len(arrays)),
        out_specs=tuple(out_specs) + (ANY,) * len(shapes),
        scratch_shapes=list(scratch)
        + late_shapes
        + [shape for shapes in job_shapes for shape in shapes],
        compiler_params=pltpu.CompilerParams(vmem_limit_bytes=VMEM_LIMIT, **given),
        cost_estimate=cost,
        name=name,
    )(*operands, *extra, *arrays)
    return list(made[:n_out]), list(made[n_out:]) + results


def transfer(jobs, number, after=None):
    if lax.axis_size("seq") != 4:
        return [v for job in jobs for v in plain_job(job)]

    def body(hook, ins, outs, held):
        for k in range(3):
            hook(k)

    return call(body, [], [], [], [], jobs, number, after, name="transfer")[1]


def partner(v):
    lane = lax.broadcasted_iota(jnp.int32, v.shape, 1)
    return jnp.where(lane % HEAD < HEAD // 2, pltpu.roll(v, 96, 1), pltpu.roll(v, 32, 1))


def head_mean(v, ones):
    high = v.astype(BF16)
    rest = (v - high.astype(F32)).astype(BF16)
    return dot(high, ones) + dot(rest, ones)


def true_chunk(place, c, count):
    if count != 4:
        return c
    low = 1 - place % 2 if c % 2 else place % 2
    high = 1 - place // 2 if c // 2 else place // 2
    return low + 2 * high


def prepare_heads(sizes, place, qkv_ref, qg_ref, kg_ref, cos_ref, sin_ref, ones, q_s, k_s, v_s):
    hq, hkv, _ = sizes
    seqs, rows_in, _ = qkv_ref.shape
    for c in range(seqs):
        j = true_chunk(place, c, seqs)
        rows = slice(c * rows_in, (c + 1) * rows_in)
        cos = cos_ref[rows, :]
        sin = sin_ref[rows, :]
        for p in range((hq + hkv) // 2):
            is_query = p < hq // 2
            x = qkv_ref[j, :, p * 128 : (p + 1) * 128].astype(F32)
            gain = qg_ref[...] * HEAD**-0.5 if is_query else kg_ref[...]
            y = x * lax.rsqrt(head_mean(x * x, ones) + EPSILON) * gain
            y = (y * cos + partner(y) * sin).astype(BF16)
            for t in range(2):
                part = y[:, t * HEAD : (t + 1) * HEAD]
                if is_query:
                    q_s[2 * p + t, rows, :] = part
                else:
                    k_s[2 * p - hq + t, rows, :] = part
        for t in range(hkv):
            start = (hq + hkv + t) * HEAD
            v_s[t, rows, :] = qkv_ref[j, :, start : start + HEAD]


def allowed_keys(block, first, keys, length):
    bound = jnp.minimum(first + lax.broadcasted_iota(jnp.int32, (block, 1), 0), length - 1)
    return lax.broadcasted_iota(jnp.int32, (block, keys), 1) <= bound


def attend_kernel(sizes, hook, ins, outs, held):
    len_ref, normal_ref, weight_ref, qg_ref, kg_ref, cos_ref, sin_ref, ones_ref, *out_w = ins
    out_ref, lse_ref, qkv_ref, *left = outs
    q_s, k_s, v_s, o_s = held
    hook(0)

    @pl.loop(0, qkv_ref.shape[0])
    def _(j):
        qkv_ref[j] = dot(normal_ref[j], weight_ref[...]).astype(BF16)

    hq, hkv, group = sizes
    seqs, rows_in, _ = qkv_ref.shape
    place = lax.axis_index("seq")
    prepare_heads(
        sizes, place, qkv_ref, qg_ref, kg_ref, cos_ref, sin_ref, ones_ref[...], q_s, k_s, v_s
    )
    for i in range(seqs * rows_in // BLOCK):
        keys = (i + 1) * BLOCK
        rows = slice(i * BLOCK, (i + 1) * BLOCK)
        keep = allowed_keys(BLOCK, i * BLOCK, keys, len_ref[0])

        def one_head(h, _):
            kv = h // group
            scores = dot(q_s[h, rows, :], k_s[kv, :keys, :], NT)
            scores = jnp.where(keep, scores, NEGATIVE)
            highest = jnp.max(scores, axis=1, keepdims=True)
            shifted = jnp.exp(scores - highest)
            total = jnp.sum(shifted, axis=1, keepdims=True)
            mixed = dot(shifted.astype(BF16), v_s[kv, :keys, :]) / total
            o_s[h, rows, :] = mixed.astype(BF16)
            lse_ref[h, rows, :] = highest + jnp.log(total)
            return 0

        lax.fori_loop(0, hq, one_head, 0, unroll=min(4, hq))
        if i == seqs * rows_in // BLOCK - 2:
            hook(1)
    for c in range(seqs):
        j = true_chunk(place, c, seqs)
        rows = slice(c * rows_in, (c + 1) * rows_in)
        for p in range(hq // 2):
            out_ref[j, :, p * 128 : (p + 1) * 128] = jnp.concatenate(
                [o_s[2 * p, rows, :], o_s[2 * p + 1, rows, :]], axis=1
            )
    for out_w_ref, left_ref in zip(out_w, left):
        for j in range(seqs):
            left_ref[j] = dot(out_ref[j], out_w_ref[...]).astype(BF16)
    hook(2)


def out_weight_grads(grads_ref, shards, slots):
    width = slots[0][0].shape[-1]
    model = slots[0][1].shape[-1]
    tile = min(256, width)
    piece = width // shards
    held = model // shards
    blocks = held // piece
    columns = model // blocks
    for t in range(width // tile):
        total = None
        for mixed_ref, res_ref in slots:
            rows = mixed_ref.shape[0] * mixed_ref.shape[1]
            mixed = mixed_ref[:, :, t * tile : (t + 1) * tile].reshape(rows, tile)
            term = dot(mixed, res_ref[...].reshape(rows, model), TN)
            total = term if total is None else total + term
        total = total.astype(BF16)
        for p in range(tile // piece):
            first = (t * (tile // piece) + p) * held
            for c in range(blocks):
                grads_ref[first + c * piece : first + (c + 1) * piece, :] = total[
                    p * piece : (p + 1) * piece, c * columns : (c + 1) * columns
                ]


def attend_back_kernel(sizes, shards, hook, ins, outs, held):
    (
        len_ref, qkv_ref, res_ref, out_w_ref, qkv_w_ref, lse_ref,
        qg_ref, kg_ref, cos_ref, sin_ref, ones_ref, *others,
    ) = ins
    dqkv_ref, dgain_ref, pull_ref, *out_grads = outs
    q_s, k_s, v_s, cot_s, dq_s, dk_s, dv_s = held
    hook(0)
    hq, hkv, group = sizes
    seqs, rows_in, _ = qkv_ref.shape
    place = lax.axis_index("seq")
    ones = ones_ref[...]
    prepare_heads(sizes, place, qkv_ref, qg_ref, kg_ref, cos_ref, sin_ref, ones, q_s, k_s, v_s)
    for c in range(seqs):
        j = true_chunk(place, c, seqs)
        cots = dot(res_ref[j], out_w_ref[...], NT).astype(BF16)
        for h in range(hq):
            cot_s[h, c * rows_in : (c + 1) * rows_in, :] = cots[:, h * HEAD : (h + 1) * HEAD]
    dk_s[...] = jnp.zeros_like(dk_s)
    dv_s[...] = jnp.zeros_like(dv_s)
    for i in range(seqs * rows_in // BLOCK):
        keys = (i + 1) * BLOCK
        rows = slice(i * BLOCK, (i + 1) * BLOCK)
        keep = allowed_keys(BLOCK, i * BLOCK, keys, len_ref[0])

        def one_head(h, _):
            kv = h // group
            q = q_s[h, rows, :]
            cot = cot_s[h, rows, :]
            k = k_s[kv, :keys, :]
            scores = jnp.where(keep, dot(q, k, NT), NEGATIVE)
            probs = jnp.exp(scores - lse_ref[h, rows, :])
            prob_cot = dot(cot, v_s[kv, :keys, :], NT)
            inner = jnp.sum(probs * prob_cot, axis=1, keepdims=True)
            score_cot = (probs * (prob_cot - inner)).astype(BF16)
            dq_s[h, rows, :] = dot(score_cot, k) * HEAD**-0.5
            dk_s[kv, :keys, :] += dot(score_cot, q, TN)
            dv_s[kv, :keys, :] += dot(probs.astype(BF16), cot, TN)
            return 0

        lax.fori_loop(0, hq, one_head, 0, unroll=min(4, hq))
        if i == seqs * rows_in // BLOCK - 2:
            for grads_ref in out_grads:
                before_ref, here_ref, res_before_ref = others
                out_weight_grads(
                    grads_ref, shards, ((before_ref, res_before_ref), (here_ref, res_ref))
                )
            hook(1)
    gain_sums = [jnp.zeros((1, 128), F32), jnp.zeros((1, 128), F32)]
    for c in range(seqs):
        j = true_chunk(place, c, seqs)
        rows = slice(c * rows_in, (c + 1) * rows_in)
        cos = cos_ref[rows, :]
        sin = sin_ref[rows, :]
        for p in range((hq + hkv) // 2):
            is_query = p < hq // 2
            x = qkv_ref[j, :, p * 128 : (p + 1) * 128].astype(F32)
            gain = qg_ref[...] if is_query else kg_ref[...]
            source, first = (dq_s, 2 * p) if is_query else (dk_s, 2 * p - hq)
            turned = jnp.concatenate([source[first, rows, :], source[first + 1, rows, :]], axis=1)
            scale = lax.rsqrt(head_mean(x * x, ones) + EPSILON)
            straight = turned * cos + partner(turned * sin)
            unit = x * scale
            which = 0 if is_query else 1
            gain_sums[which] += jnp.sum(straight * unit, axis=0, keepdims=True)
            pulled = gain * straight
            dx = scale * (pulled - unit * head_mean(unit * pulled, ones))
            dqkv_ref[j, :, p * 128 : (p + 1) * 128] = dx.astype(BF16)
        for p in range(hkv // 2):
            start = (hq + hkv) * HEAD + p * 128
            dqkv_ref[j, :, start : start + 128] = jnp.concatenate(
                [dv_s[2 * p, rows, :], dv_s[2 * p + 1, rows, :]], axis=1
            ).astype(BF16)
    dgain_ref[0:1, :] = gain_sums[0]
    dgain_ref[1:2, :] = gain_sums[1]

    @pl.loop(0, seqs)
    def _(j):
        pull_ref[j] = dot(dqkv_ref[j], qkv_w_ref[...], NT).astype(BF16)

    hook(2)


def position_tables(length):
    places = np.arange(length, dtype=np.float32)
    half = HEAD // 2
    freqs = np.float32(ROPE_BASE) ** (-(np.arange(half, dtype=np.float32) * 2.0) / HEAD)
    angles = places[:, None] * freqs.astype(np.float32)[None, :]
    cos = np.cos(angles).astype(np.float32)
    sin = np.sin(angles).astype(np.float32)
    ones = np.kron(np.eye(2), np.ones((HEAD, HEAD)) / HEAD)
    return (
        jnp.asarray(np.concatenate([cos] * 4, axis=1)),
        jnp.asarray(np.concatenate([-sin, sin, -sin, sin], axis=1)),
        jnp.asarray(ones, dtype=BF16),
    )


def attend(sizes, length, normal, weight, gains, tables, jobs, number, after, out_w=()):
    seqs, rows_in, _ = normal.shape
    hq, hkv, _ = sizes
    slot = seqs * rows_in
    return call(
        functools.partial(attend_kernel, sizes),
        [length, normal, weight, *gains, *tables, *out_w],
        [SMEM] + [VMEM] * (7 + len(out_w)),
        [
            jax.ShapeDtypeStruct((seqs, rows_in, hq * HEAD), BF16),
            jax.ShapeDtypeStruct((hq, slot, 1), F32),
            jax.ShapeDtypeStruct((seqs, rows_in, weight.shape[1]), BF16),
        ]
        + [jax.ShapeDtypeStruct(normal.shape, BF16)] * len(out_w),
        [VMEM] * (3 + len(out_w)),
        jobs,
        number,
        after,
        scratch=[
            pltpu.VMEM((hq, slot, HEAD), BF16),
            pltpu.VMEM((hkv, slot, HEAD), BF16),
            pltpu.VMEM((hkv, slot, HEAD), BF16),
            pltpu.VMEM((hq, slot, HEAD), BF16),
        ],
        cost=pl.CostEstimate(
            flops=56 * hq * slot * slot * HEAD, bytes_accessed=1 << 23, transcendentals=0
        ),
        name="attend",
        late=(1, 2) + tuple(range(8, 8 + len(out_w))),
    )


def attend_back(
    sizes, length, qkv, res, out_w, qkv_w, lse, gains, tables, jobs, number, after, others=()
):
    seqs, rows_in, width = qkv.shape
    hq, hkv, _ = sizes
    slot = seqs * rows_in
    shards = lax.axis_size("fsdp")
    model = res.shape[-1]
    columns = hq * HEAD // shards * model // (model // shards)
    return call(
        functools.partial(attend_back_kernel, sizes, shards),
        [length, qkv, res, out_w, qkv_w, lse, *gains, *tables, *others],
        [SMEM] + [VMEM] * (10 + len(others)),
        [
            jax.ShapeDtypeStruct((seqs, rows_in, width), BF16),
            jax.ShapeDtypeStruct((2, 128), F32),
            jax.ShapeDtypeStruct(res.shape, BF16),
        ]
        + [jax.ShapeDtypeStruct((model, columns), BF16)] * bool(others),
        [VMEM, VMEM, VMEM] + [VMEM] * bool(others),
        jobs,
        number,
        after,
        scratch=[
            pltpu.VMEM((hq, slot, HEAD), BF16),
            pltpu.VMEM((hkv, slot, HEAD), BF16),
            pltpu.VMEM((hkv, slot, HEAD), BF16),
            pltpu.VMEM((hq, slot, HEAD), BF16),
            pltpu.VMEM((hq, slot, HEAD), F32),
            pltpu.VMEM((hkv, slot, HEAD), F32),
            pltpu.VMEM((hkv, slot, HEAD), F32),
        ],
        cost=pl.CostEstimate(
            flops=88 * hq * slot * slot * HEAD, bytes_accessed=1 << 23, transcendentals=0
        ),
        name="attend_back",
        late=(1, 2, 3, 4, 5) + tuple(range(11, 11 + len(others))),
    )


def hooked(hook, step, steps, work):
    pl.when(step == 0)(lambda: hook(0))
    work(lambda: pl.when(step == (3 * steps) // 5)(lambda: hook(1)))
    pl.when(step == steps - 1)(lambda: hook(2))


def ffn_kernel(steps, hook, ins, outs, held):
    step = pl.program_id(0)
    weights_ref, loaded = held
    loads = [
        pltpu.make_async_copy(ins[2].at[:, k], weights_ref.at[k], loaded.at[k]) for k in range(3)
    ]

    def first(act):
        pl.when(step == 0)(act)

    def work(late):
        for load in loads:
            first(load.start)
        ffn_tile(late, first, loads, *ins[:2], weights_ref, ins[3:], *outs)

    hooked(hook, step, steps, work)


def ffn_tile(late, first, loads, mid_ref, cot_ref, weights_ref, sums, acts_ref, pull_ref):
    model = mid_ref.shape[-1]
    hidden = acts_ref.shape[-1]
    whole = (hidden, model)
    mid = mid_ref[...]
    first(loads[0].wait)
    gate = dot(mid, weights_ref[0].reshape(whole), NT)
    first(loads[1].wait)
    up = dot(mid, weights_ref[1].reshape(whole), NT)
    first(loads[2].wait)
    mids_cot = dot(cot_ref[...], weights_ref[2].reshape(whole), NT)
    late()
    sigmoid = jax.nn.sigmoid(gate)
    active = gate * sigmoid
    gate_cot = (mids_cot * up * sigmoid * (1.0 + gate * (1.0 - sigmoid))).astype(BF16)
    up_cot = (mids_cot * active).astype(BF16)
    acts_ref[0] = gate_cot
    acts_ref[1] = up_cot
    acts_ref[2] = (active * up).astype(BF16)
    pulled = dot(gate_cot, weights_ref[0].reshape(whole)) + dot(
        up_cot, weights_ref[1].reshape(whole)
    )
    for sum_ref in sums:
        pulled = pulled + sum_ref[...]
    pull_ref[...] = pulled.astype(pull_ref.dtype)


def ffn_both(mid, cot, weights, summed, last, jobs, number, after):
    tokens, model = mid.shape
    shards, _, part, _ = weights.shape
    hidden = shards * part
    tile = min(256, tokens)

    row_spec = pl.BlockSpec((tile, model), lambda i: (i, 0))
    extra = () if summed is None else (summed,)
    return call(
        functools.partial(ffn_kernel, tokens // tile),
        [mid, cot, weights, *extra],
        [row_spec, row_spec, ANY] + [row_spec] * len(extra),
        [
            jax.ShapeDtypeStruct((3, tokens, hidden), BF16),
            jax.ShapeDtypeStruct((tokens, model), BF16 if last else F32),
        ],
        [pl.BlockSpec((3, tile, hidden), lambda i: (0, i, 0)), row_spec],
        jobs,
        number,
        after,
        grid=(tokens // tile,),
        scratch=[
            pltpu.VMEM((3, shards, part, model), BF16),
            pltpu.SemaphoreType.DMA((3,)),
        ],
        cost=pl.CostEstimate(
            flops=16 * tokens * model * hidden,
            bytes_accessed=4 * tokens * model + 6 * hidden * model,
            transcendentals=0,
        ),
        name="ffn_both",
    )


def ffn_grad_kernel(slots, tiles, hook, ins, outs, held):
    acts = ins[:slots]
    others = ins[slots:]
    (out_ref,) = outs
    rows_ref, loaded = held
    kind = pl.program_id(0)
    step = kind * tiles + pl.program_id(1)
    loads = [
        pltpu.make_async_copy(other, rows_ref.at[k], loaded.at[k])
        for k, other in enumerate(others)
    ]

    def store(first):
        total = None
        for k, act in enumerate(acts):
            term = dot(act[0], rows_ref[first + k], TN)
            total = term if total is None else total + term
        out_ref[...] = total.astype(BF16).reshape(out_ref.shape)

    def work(late):
        for k, load in enumerate(loads):
            pl.when(step == 0)(load.start)
        for k, load in enumerate(loads):
            pl.when(step == (0 if k < slots else 2 * tiles))(load.wait)
        late()
        pl.when(kind < 2)(lambda: store(0))
        pl.when(kind == 2)(lambda: store(slots))

    hooked(hook, step, 3 * tiles, work)


def ffn_grads(acts, mids, cots, shards, jobs, number, after):
    slots = len(acts)
    _, tokens, hidden = acts[0].shape
    model = mids[0].shape[-1]
    part = hidden // shards
    tile = 256
    per = tile // part
    return call(
        functools.partial(ffn_grad_kernel, slots, hidden // tile),
        [*acts, *mids, *cots],
        [pl.BlockSpec((1, tokens, tile), lambda k, i: (k, 0, i))] * slots
        + [ANY] * (2 * slots),
        [jax.ShapeDtypeStruct((shards, 3, part, model), BF16)],
        [pl.BlockSpec((per, 1, part, model), lambda k, i: (i, k, 0, 0))],
        jobs,
        number,
        after,
        grid=(3, hidden // tile),
        scratch=[
            pltpu.VMEM((2 * slots, tokens, model), BF16),
            pltpu.SemaphoreType.DMA((2 * slots,)),
        ],
        cost=pl.CostEstimate(
            flops=9 * slots * tokens * model * hidden,
            bytes_accessed=4 * slots * tokens * model,
            transcendentals=0,
        ),
        name="ffn_grads",
    )


def ffn_down_kernel(chunks, steps, hook, ins, outs, held):
    acts = ins[:chunks]
    downs = ins[chunks:]
    (out_ref,) = outs

    def work(late):
        late()
        total = None
        for act, down in zip(acts, downs):
            hidden = act.shape[-1]
            term = dot(act[0], down[...].reshape(hidden, down.shape[-1]))
            total = term if total is None else total + term
        out_ref[...] = total.astype(BF16)

    hooked(hook, pl.program_id(0), steps, work)


def ffn_down(acts, weights, jobs, number, after, true_order=False):
    chunks = len(acts)
    _, tokens, hidden = acts[0].shape
    shards, _, part, model = weights[0].shape
    tile = min(256, tokens)
    def spot(i):
        if not true_order or lax.axis_size("seq") != 4:
            return i
        place = lax.axis_index("seq")
        low = (place % 2 + i % 2) % 2
        high = (place // 2 + i // 2) % 2
        return low + 2 * high

    act_spec = pl.BlockSpec((1, tile, hidden), lambda i: (2, i, 0))
    down_spec = pl.BlockSpec(
        (shards, 1, part, model),
        lambda i: (0, 2, 0, 0),
        pipeline_mode=pl.Buffered(buffer_count=1),
    )
    return call(
        functools.partial(ffn_down_kernel, chunks, tokens // tile),
        [*acts, *weights],
        [act_spec] * chunks + [down_spec] * chunks,
        [jax.ShapeDtypeStruct((tokens, model), BF16)],
        [pl.BlockSpec((tile, model), lambda i: (spot(i), 0))],
        jobs,
        number,
        after,
        grid=(tokens // tile,),
        cost=pl.CostEstimate(
            flops=4 * chunks * tokens * model * hidden,
            bytes_accessed=chunks * hidden * (tokens + model) * 2,
            transcendentals=0,
        ),
        name="ffn_down",
    )


def place_kernel(place_ref, parts_ref, *refs):
    for kind, out_ref in enumerate(refs[-3:]):
        out_ref[0, 0] = parts_ref[0, kind].astype(F32)


def place_parts(place, parts, chunk, held):
    seqs, _, part, model = parts.shape
    out = jax.ShapeDtypeStruct((seqs, CHUNKS, part, model), F32)
    out_spec = pl.BlockSpec(
        (1, 1, part, model), lambda j, at: (jnp.bitwise_xor(at[0], j), chunk, 0, 0)
    )
    return pl.pallas_call(
        place_kernel,
        out_shape=(out,) * 3,
        grid_spec=pltpu.PrefetchScalarGridSpec(
            num_scalar_prefetch=1,
            grid=(seqs,),
            in_specs=[pl.BlockSpec((1, 3, part, model), lambda j, at: (j, 0, 0, 0))]
            + [ANY] * len(held),
            out_specs=(out_spec,) * 3,
        ),
        input_output_aliases={2 + k: k for k in range(len(held))},
        compiler_params=pltpu.CompilerParams(vmem_limit_bytes=VMEM_LIMIT),
        cost_estimate=pl.CostEstimate(
            flops=0, bytes_accessed=18 * seqs * part * model, transcendentals=0
        ),
        name="place_parts",
    )(place, parts, *held)


def place_heads_kernel(
    place_ref, parts_ref, query_w_ref, key_w_ref, value_w_ref,
    query_ref, key_ref, value_ref, rest_ref, met_ref,
):
    edge = query_ref.shape[1]
    width = key_ref.shape[1]
    part = parts_ref[0].astype(F32)
    query_ref[...] = part[:, :edge]
    key_ref[...] = part[:, edge : edge + width]
    value_ref[...] = part[:, edge + width : edge + 2 * width]
    rest = part[:, edge + 2 * width :]
    met = jnp.zeros_like(met_ref)
    for grad_ref, weight_ref in (
        (query_ref, query_w_ref),
        (key_ref, key_w_ref),
        (value_ref, value_w_ref),
    ):
        product = grad_ref[...] * weight_ref[...].astype(F32)
        met = met + jnp.sum(product, axis=1, keepdims=True)

    @pl.when(pl.program_id(0) == 0)
    def _():
        rest_ref[...] = rest
        met_ref[...] = met

    @pl.when(pl.program_id(0) > 0)
    def _():
        rest_ref[...] += rest
        met_ref[...] += met


def place_heads(place, parts, edge, width, weights):
    seqs, rows, total = parts.shape
    rest = total - edge - 2 * width

    def column_spec(size):
        return pl.BlockSpec((rows, size), lambda j, at: (0, jnp.bitwise_xor(at[0], j)))

    return pl.pallas_call(
        place_heads_kernel,
        out_shape=[
            jax.ShapeDtypeStruct((rows, seqs * edge), F32),
            jax.ShapeDtypeStruct((rows, seqs * width), F32),
            jax.ShapeDtypeStruct((rows, seqs * width), F32),
            jax.ShapeDtypeStruct((rows, rest), F32),
            jax.ShapeDtypeStruct((rows, 128), F32),
        ],
        grid_spec=pltpu.PrefetchScalarGridSpec(
            num_scalar_prefetch=1,
            grid=(seqs,),
            in_specs=[
                pl.BlockSpec((1, rows, total), lambda j, at: (j, 0, 0)),
                column_spec(edge),
                column_spec(width),
                column_spec(width),
            ],
            out_specs=[
                column_spec(edge),
                column_spec(width),
                column_spec(width),
                pl.BlockSpec((rows, rest), lambda j, at: (0, 0)),
                pl.BlockSpec((rows, 128), lambda j, at: (0, 0)),
            ],
        ),
        compiler_params=pltpu.CompilerParams(vmem_limit_bytes=VMEM_LIMIT),
        name="place_heads",
    )(place, parts, *weights)


def scale_of(values):
    return lax.rsqrt(jnp.mean(values * values, axis=-1, keepdims=True) + EPSILON)


def normed(values, gain):
    return values * scale_of(values) * gain


def normed_back(values, gain, cot):
    scale = scale_of(values)
    pulled = cot * gain
    mean = jnp.mean(values * pulled, axis=-1, keepdims=True)
    return (
        scale * pulled - values * (scale * scale * scale) * mean,
        jnp.sum(cot * values * scale, axis=0),
    )


def follow(values, earlier):
    return lax.optimization_barrier((values, *earlier))[0]


def own_columns(weight, heads, place):
    width = heads * HEAD
    part = lax.dynamic_slice_in_dim(weight, place * width, width, 1)
    if heads % 2:
        part = jnp.pad(part, ((0, 0), (0, HEAD)))
    return part


def on_device(
    tokens,
    cotangent,
    lengths,
    attn_gain,
    query_weight,
    key_weight,
    value_weight,
    query_gain,
    key_gain,
    out_weight,
    ffn_gain,
    gate_weight,
    up_weight,
    down_weight,
):
    slots, rows, model = tokens.shape
    seqs = lax.axis_size("seq")
    shards = lax.axis_size("fsdp")
    place = lax.axis_index("seq")
    shard = lax.axis_index("fsdp")
    slot_len = rows * seqs
    query_width = query_weight.shape[1]
    kv_width = key_weight.shape[1]
    hq = query_width // seqs // HEAD
    hkv = kv_width // seqs // HEAD
    hkv_held = hkv + hkv % 2
    sizes = (hq, hkv_held, hq // hkv)
    order = (place if seqs == 4 else place * 0).reshape(1)
    tables = position_tables(slot_len)
    gains = (
        jnp.concatenate([query_gain, query_gain]).reshape(1, 2 * HEAD),
        jnp.concatenate([key_gain, key_gain]).reshape(1, 2 * HEAD),
    )

    flat = (slot_len, model)
    chunked = (seqs, rows, model)
    places = place * rows + jnp.arange(rows, dtype=jnp.int32)
    live = (places[None, :] < lengths[:, None]).astype(F32)[..., None]
    inputs = tokens.astype(F32)
    out_cot = cotangent.astype(F32) * live
    out_low = [out_cot[b].astype(BF16) for b in range(slots)]
    normal_in = [normed(inputs[b], attn_gain).astype(BF16) for b in range(slots)]

    qkv_own = jnp.concatenate(
        [
            own_columns(query_weight, hq, place),
            own_columns(key_weight, hkv, place),
            own_columns(value_weight, hkv, place),
        ],
        axis=1,
    )
    qkv_weight = lax.all_gather(qkv_own, "fsdp", axis=0, tiled=True)
    start = [
        ("gather", normal_in[0]),
        ("deal", out_weight),
        ("own", gate_weight, up_weight, down_weight),
    ]
    normal_0, out_own, *ffn_own = transfer(start, 1)
    hidden_own = gate_weight.shape[0] // seqs
    part = hidden_own // CHUNKS
    ffn_weights = [lax.all_gather(own, "fsdp", axis=0) for own in ffn_own]

    def leave(mixed):
        return dot(mixed.reshape(slot_len, -1), out_rows).astype(BF16).reshape(chunked)

    def enter_ffn(b, total):
        res = inputs[b] + total
        return res, normed(res, ffn_gain).astype(BF16)

    def heads(b, jobs, number, after, out_w=()):
        return attend(
            sizes, lengths[b : b + 1], normal_full[b].reshape(chunked), qkv_weight, gains, tables,
            jobs, number, after, out_w,
        )

    normal_full = [None] * slots
    cot_full = [None] * slots
    mid_full = [None] * slots
    normal_full[0] = normal_0
    (mixed_0, lse_0, qkv_0), (normal_full[1], out_rows) = heads(
        0, [("gather", normal_in[1]), ("line", out_own)], 2, normal_full[0]
    )
    out_rows = out_rows.reshape(-1, model)
    (mixed_1, lse_1, qkv_1, left_1), (total_0,) = heads(
        1, [("scatter", leave(mixed_0))], 3, mixed_0, (out_rows,)
    )
    qkv = [qkv_0, qkv_1]
    log_sums = [lse_0, lse_1]
    res_0, mid_0 = enter_ffn(0, total_0)
    mid_full[0], cot_full[0] = [
        v.reshape(flat)
        for v in transfer([("gather", mid_0), ("gather", out_low[0])], 4, mixed_1)
    ]

    acts = [[None] * slots for _ in range(CHUNKS)]
    pulled = [None] * slots

    def ffn_step(b, c, jobs, number, after):
        (acts[c][b], pulled[b]), results = ffn_both(
            mid_full[b], cot_full[b], ffn_weights[c], pulled[b], c == CHUNKS - 1,
            jobs, number, after,
        )
        return results

    def grad_step(c, jobs, number, after):
        (grads,), results = ffn_grads(
            acts[c], mid_full, cot_full, shards, jobs, number, after
        )
        return grads.reshape(shards, 3 * part, model), results

    def leave_ffn(b, jobs, number, after, true_order=False):
        (out,), results = ffn_down(
            [acts[c][b] for c in range(CHUNKS)], ffn_weights, jobs, number, after, true_order
        )
        return out.reshape(chunked), results

    total_1, full = ffn_step(
        0, 0, [("scatter", left_1), ("gather", out_low[1])], 5, mid_full[0]
    )
    cot_full[1] = full.reshape(flat)
    res_1, mid_1 = enter_ffn(1, total_1)
    hidden_res = [res_0, res_1]
    (full,) = ffn_step(0, 1, [("gather", mid_1)], 6, acts[0][0])
    mid_full[1] = full.reshape(flat)
    (mid_total_0,) = ffn_step(1, 0, [("scatter", pulled[0].reshape(chunked))], 7, acts[1][0])

    def pull_mid(b, total):
        pull, gain_part = normed_back(hidden_res[b], ffn_gain, total)
        cot = out_cot[b] + pull
        return cot, cot.astype(BF16), gain_part

    res_cot_0, low_0, ffn_gain_0 = pull_mid(0, mid_total_0)
    grads_0, (res_full_0,) = grad_step(0, [("gather", low_0)], 8, acts[0][1])
    ffn_sums = [lax.psum_scatter(grads_0, "fsdp", scatter_dimension=0)]
    out_0, _ = leave_ffn(0, [], 0, grads_0)
    (out_total_0,) = ffn_step(1, 1, [("scatter", out_0)], 9, out_0)
    grads_1, (mid_total_1,) = grad_step(
        1, [("scatter", pulled[1].reshape(chunked))], 10, acts[1][1]
    )
    ffn_sums.append(
        lax.psum_scatter(grads_1, "fsdp", scatter_dimension=0)
    )
    res_cot_1, low_1, ffn_gain_1 = pull_mid(1, mid_total_1)
    grad_ffn_gain = ffn_gain_0 + ffn_gain_1

    def back(b, full, jobs, number, after, others=()):
        return attend_back(
            sizes, lengths[b : b + 1], qkv[b], full, out_rows, qkv_weight, log_sums[b],
            gains, tables, jobs, number, after, others,
        )

    (dqkv_0, heads_gain_0, pull_0), (res_full_1,) = back(
        0, res_full_0, [("gather", low_1)], 11, grads_1
    )
    (dqkv_1, heads_gain_1, pull_1, out_grads), (in_total_0, ffn_parts_0) = back(
        1,
        res_full_1,
        [("scatter", pull_0), ("gather", ffn_sums[0])],
        12,
        dqkv_0,
        (mixed_0, mixed_1, res_full_0),
    )
    head_gain = heads_gain_0 + heads_gain_1
    dqkv = [v.reshape(slot_len, -1) for v in (dqkv_0, dqkv_1)]
    held = model // shards
    piece = hq * HEAD // shards
    blocks = held // piece
    head_sums = jnp.pad(
        (head_gain[:, :HEAD] + head_gain[:, HEAD:]).reshape(2, shards, HEAD // shards),
        ((0, 0), (0, 0), (0, held - HEAD // shards)),
    ).reshape(2, model)
    gain_columns = jnp.stack([grad_ffn_gain, head_sums[0], head_sums[1]], axis=1).astype(BF16)
    attn_grads = jnp.concatenate(
        [
            sum(dot(normal_full[b].reshape(flat), dqkv[b], TN) for b in range(slots)).astype(BF16),
            jnp.pad(gain_columns, ((0, 0), (0, 125))),
            out_grads,
        ],
        axis=1,
    )
    ffn_grad = place_parts(order, ffn_parts_0.reshape(seqs, 3, part, model), 0, ())
    out_1, (in_total_1,) = leave_ffn(1, [("scatter", pull_1)], 13, ffn_sums[1], True)
    attn_sums = lax.psum_scatter(
        follow(attn_grads, [ffn_sums[1], ffn_grad[0]]), "fsdp", scatter_dimension=0, tiled=True
    )
    (ffn_parts_1,) = transfer([("gather", ffn_sums[1])], 15, in_total_1)
    ffn_grad = place_parts(order, ffn_parts_1.reshape(seqs, 3, part, model), 1, ffn_grad)
    out_edge = attn_sums.shape[1] - model // blocks
    heads_all, _, out_parts = transfer(
        [("gather", attn_sums[:, :out_edge]), ("spread", attn_sums[:, out_edge:])],
        14,
        ffn_grad[0],
    )
    grad_out = jnp.swapaxes(
        out_parts.reshape(seqs, blocks, piece, model // blocks), 1, 2
    ).reshape(held, model)
    grad_tokens = []
    for b, (in_cot, cot) in enumerate(((in_total_0, res_cot_0), (in_total_1, res_cot_1))):
        pull, _ = normed_back(inputs[b], attn_gain, in_cot)
        grad_tokens.append((cot + pull).astype(BF16))
    out_total_1 = lax.psum_scatter(
        follow(out_1, [attn_sums, ffn_parts_1]), "seq", scatter_dimension=0
    ).astype(F32)
    output = [
        (live[b] * (hidden_res[b] + total)).astype(BF16)
        for b, total in enumerate((out_total_0, out_total_1))
    ]
    ffn_grad = [v.reshape(seqs * hidden_own, model) for v in ffn_grad]

    edge = hq * HEAD
    width = hkv_held * HEAD
    if hkv == hkv_held:
        grad_query, grad_key, grad_value, gain_sums, met = place_heads(
            order, heads_all, edge, width, (query_weight, key_weight, value_weight)
        )
        met = met[:, 0]
    else:
        heads_all = jnp.moveaxis(heads_all, 0, 1).astype(F32)
        last = edge + width
        grad_query = heads_all[..., :edge].reshape(held, query_width)
        grad_key = heads_all[..., edge : edge + hkv * HEAD].reshape(held, kv_width)
        grad_value = heads_all[..., last : last + hkv * HEAD].reshape(held, kv_width)
        gain_sums = jnp.sum(heads_all[..., last + width :], axis=1)
        met = sum(
            jnp.sum(grad * weight.astype(F32), axis=1)
            for grad, weight in (
                (grad_query, query_weight),
                (grad_key, key_weight),
                (grad_value, value_weight),
            )
        )
    grad_attn_gain = met / lax.dynamic_slice_in_dim(attn_gain, shard * held, held, 0)

    return (
        jnp.stack(output),
        jnp.stack(grad_tokens),
        grad_attn_gain,
        grad_query,
        grad_key,
        grad_value,
        gain_sums[: HEAD // shards, 1],
        gain_sums[: HEAD // shards, 2],
        grad_out.astype(F32),
        gain_sums[:, 0],
        ffn_grad[0],
        ffn_grad[1],
        ffn_grad[2],
    )


def solution(mesh):
    return jax.shard_map(
        on_device,
        mesh=mesh,
        in_specs=(
            P("fsdp", "seq", None),
            P("fsdp", "seq", None),
            P("fsdp"),
            P(),
            P("fsdp", None),
            P("fsdp", None),
            P("fsdp", None),
            P(),
            P(),
            P("fsdp", None),
            P(),
            P("fsdp", None),
            P("fsdp", None),
            P("fsdp", None),
        ),
        out_specs=(
            P("fsdp", "seq", None),
            P("fsdp", "seq", None),
            P("fsdp"),
            P("fsdp", None),
            P("fsdp", None),
            P("fsdp", None),
            P("fsdp"),
            P("fsdp"),
            P("fsdp", None),
            P("fsdp"),
            P("fsdp", None),
            P("fsdp", None),
            P("fsdp", None),
        ),
        check_vma=False,
    )
```

```python
import functools

import jax
import jax.numpy as jnp
import numpy as np
from jax import lax
from jax.experimental import pallas as pl
from jax.experimental.pallas import tpu as pltpu
from jax.sharding import PartitionSpec as P

EPSILON = 1e-05
ROPE_BASE = 1000000.0
NEGATIVE = -1e30
F32 = jnp.float32
BF16 = jnp.bfloat16
NN = (((1,), (0,)), ((), ()))
NT = (((1,), (1,)), ((), ()))
TN = (((0,), (0,)), ((), ()))
SMEM = pl.BlockSpec(memory_space=pltpu.SMEM)
VMEM = pl.BlockSpec(memory_space=pltpu.VMEM)
VMEM_LIMIT = 58 << 20
HEAD = 64
BLOCK = 256
CHUNKS = 2
ANY = pl.BlockSpec(memory_space=pl.ANY)


def dot(a, b, dims=NN):
    return lax.dot_general(a, b, dims, preferred_element_type=F32)


def over_one(place):
    return place + 1 - 2 * (place % 2)


def over_two(place):
    return (place + 2) % 4


def send(source, target, device, out_sem, in_sem):
    return pltpu.make_async_remote_copy(
        src_ref=source,
        dst_ref=target,
        send_sem=out_sem,
        recv_sem=in_sem,
        device_id={"seq": device},
        device_id_type=pl.DeviceIdType.MESH,
    )


def gather_job(sources, targets, scratch):
    (source,) = sources
    (target,) = targets
    outs, ins, here, held = scratch
    place = lax.axis_index("seq")
    one, two = over_one(place), over_two(place)
    half = source.shape[0] // 2
    load = pltpu.make_async_copy(source, held, here.at[0])
    store = pltpu.make_async_copy(held, target.at[0], here.at[1])
    first = send(source, target.at[1], one, outs.at[0], ins.at[0])
    second = send(source, target.at[2], two, outs.at[1], ins.at[1])
    top = pl.ds(0, half)
    low = pl.ds(half, half)
    third = send(target.at[2, top], target.at[3, top], one, outs.at[2], ins.at[2])
    fourth = send(target.at[1, low], target.at[3, low], two, outs.at[3], ins.at[3])

    def begin():
        first.start()
        second.start()
        load.start()

    def middle():
        load.wait()
        store.start()
        second.wait_recv()
        third.start()
        first.wait_recv()
        fourth.start()

    def finish():
        third.wait_recv()
        fourth.wait_recv()
        for copy in (first, second, third, fourth):
            copy.wait_send()
        store.wait()

    return no_greeting, begin, middle, finish


def scatter_job(sources, targets, scratch):
    (parts,) = sources
    (total,) = targets
    outs, ins, here, got_one, got_two, kept, own, last, summed = scratch
    place = lax.axis_index("seq")
    one, two = over_one(place), over_two(place)
    half = parts.shape[1] // 2
    top = pl.ds(0, half)
    low = pl.ds(half, half)
    sends = [
        send(parts.at[3, top], got_one.at[0], one, outs.at[0], ins.at[0]),
        send(parts.at[3, low], got_two.at[0], two, outs.at[1], ins.at[1]),
        send(parts.at[1, top], got_one.at[1], one, outs.at[2], ins.at[2]),
        send(parts.at[2, low], got_two.at[1], two, outs.at[3], ins.at[3]),
        send(kept.at[0], last.at[0], two, outs.at[4], ins.at[4]),
        send(kept.at[1], last.at[1], one, outs.at[5], ins.at[5]),
    ]
    loads = [
        pltpu.make_async_copy(parts.at[2, top], kept.at[0], here.at[0]),
        pltpu.make_async_copy(parts.at[1, low], kept.at[1], here.at[1]),
        pltpu.make_async_copy(parts.at[0], own, here.at[2]),
    ]
    store = pltpu.make_async_copy(summed, total, here.at[3])

    def begin():
        for copy in sends[:4]:
            copy.start()
        for copy in loads:
            copy.start()

    def middle():
        for k, got in enumerate((got_one, got_two)):
            loads[k].wait()
            sends[k].wait_recv()
            kept[k] = (kept[k].astype(F32) + got[0].astype(F32)).astype(BF16)
            sends[4 + k].start()

    def finish():
        loads[2].wait()
        for k, got in enumerate((got_one, got_two)):
            sends[2 + k].wait_recv()
            sends[4 + k].wait_recv()
            rows = slice(k * half, (k + 1) * half)
            summed[rows, :] = (
                own[rows, :].astype(F32) + got[1].astype(F32) + last[k].astype(F32)
            )
        store.start()
        for copy in sends:
            copy.wait_send()
        store.wait()

    return no_greeting, begin, middle, finish


def no_greeting(barrier):
    return 0


def nothing():
    pass


def greet(barrier, device):
    pl.semaphore_signal(
        barrier, inc=1, device_id=device, device_id_type=pl.DeviceIdType.MESH
    )


def deal_job(sources, targets, scratch):
    (source,) = sources
    (target,) = targets
    outs, ins, here = scratch
    rows = target.shape[0]
    count = source.shape[0] // rows
    place = lax.axis_index("seq")
    shard = lax.axis_index("fsdp")
    per = lax.axis_size("fsdp") // count
    part = shard % per
    is_source = shard // per == place
    to_self = jnp.logical_and(is_source, shard // count == part)
    origin = place * per + shard // count

    def copy(j):
        return pltpu.make_async_remote_copy(
            src_ref=source.at[pl.ds(j * rows, rows)],
            dst_ref=target,
            send_sem=outs.at[j],
            recv_sem=ins.at[0],
            device_id={"fsdp": part * count + j},
            device_id_type=pl.DeviceIdType.MESH,
        )

    def local(j):
        return pltpu.make_async_copy(source.at[pl.ds(j * rows, rows)], target, here.at[0])

    def greeting(barrier):
        pl.when(origin != shard)(lambda: greet(barrier, {"fsdp": origin}))
        return jnp.where(is_source, count, 0) - jnp.where(to_self, 1, 0)

    def each(act_remote, act_local):
        for j in range(count):
            mine = part * count + j == shard
            pl.when(jnp.logical_and(is_source, mine))(lambda j=j: act_local(local(j)))
            pl.when(jnp.logical_and(is_source, jnp.logical_not(mine)))(
                lambda j=j: act_remote(copy(j))
            )

    def begin():
        each(lambda c: c.start(), lambda c: c.start())

    def finish():
        each(lambda c: c.wait_send(), lambda c: c.wait())
        pl.when(origin != shard)(lambda: copy(0).wait_recv())

    return greeting, begin, nothing, finish


def line_job(sources, targets, scratch):
    (source,) = sources
    (target,) = targets
    far_out, far_in, near_out, near_in, here = scratch
    shards = target.shape[0]
    steps = shards // 2
    shard = lax.axis_index("fsdp")
    near = shard + 1 - 2 * (shard % 2)

    def away(start, k):
        return (start + 2 * k) % shards

    def send_line(origin, spot, device, out_sem, in_sem):
        return pltpu.make_async_remote_copy(
            src_ref=origin,
            dst_ref=target.at[spot],
            send_sem=out_sem,
            recv_sem=in_sem,
            device_id={"fsdp": device},
            device_id_type=pl.DeviceIdType.MESH,
        )

    own = pltpu.make_async_copy(source, target.at[shard], here.at[0])
    far = [
        send_line(source, shard, away(shard, k), far_out.at[k - 1], far_in.at[k - 1])
        for k in range(1, steps)
    ]
    far_came = [
        send_line(
            source, away(shard, steps - k), away(shard, k), far_out.at[k - 1], far_in.at[k - 1]
        )
        for k in range(1, steps)
    ]
    held = [shard] + [away(shard, steps - k) for k in range(1, steps)]
    close = [
        send_line(target.at[spot] if k else source, spot, near, near_out.at[k], near_in.at[k])
        for k, spot in enumerate(held)
    ]
    close_came = [
        send_line(source, away(near, steps - k) if k else near, near, near_out.at[k], near_in.at[k])
        for k in range(steps)
    ]

    def greeting(barrier):
        for k in range(1, steps):
            greet(barrier, {"fsdp": away(shard, k)})
        greet(barrier, {"fsdp": near})
        return steps

    def begin():
        own.start()
        for copy in far:
            copy.start()
        close[0].start()

    def finish():
        for k in range(1, steps):
            far_came[k - 1].wait_recv()
            close[k].start()
        for copy in close_came:
            copy.wait_recv()
        for copy in far + close:
            copy.wait_send()
        own.wait()

    return greeting, begin, nothing, finish


def spread_job(sources, targets, scratch):
    (source,) = sources
    gathered, target = targets
    *first, z_outs, z_ins, z_here = scratch
    _, begin_gather, middle_gather, finish_gather = gather_job(sources, [gathered], first)
    count = gathered.shape[0]
    place = lax.axis_index("seq")
    shard = lax.axis_index("fsdp")
    per = lax.axis_size("fsdp") // count
    piece = shard % count

    def owner(j):
        return true_chunk(place, j, count) * per + shard // count

    def chunk(j):
        return gathered.at[j] if j else source

    def copy(j):
        return pltpu.make_async_remote_copy(
            src_ref=chunk(j),
            dst_ref=target.at[piece],
            send_sem=z_outs.at[j],
            recv_sem=z_ins.at[piece],
            device_id={"fsdp": owner(j)},
            device_id_type=pl.DeviceIdType.MESH,
        )

    def arrival(p):
        return pltpu.make_async_remote_copy(
            src_ref=source,
            dst_ref=target.at[p],
            send_sem=z_outs.at[0],
            recv_sem=z_ins.at[p],
            device_id={"fsdp": owner(0)},
            device_id_type=pl.DeviceIdType.MESH,
        )

    def local(j):
        return pltpu.make_async_copy(chunk(j), target.at[piece], z_here.at[0])

    def origin(p):
        return (shard % per) * count + p

    def start(j):
        pl.when(owner(j) != shard)(lambda: copy(j).start())
        pl.when(owner(j) == shard)(lambda: local(j).start())

    def greeting(barrier):
        for p in range(count):
            pl.when(origin(p) != shard)(lambda p=p: greet(barrier, {"fsdp": origin(p)}))
        return jnp.where(shard % per == shard // count, count - 1, count)

    def begin():
        begin_gather()
        start(0)

    def middle():
        middle_gather()
        start(1)
        start(2)

    def finish():
        finish_gather()
        start(3)
        for j in range(count):
            pl.when(owner(j) != shard)(lambda j=j: copy(j).wait_send())
            pl.when(owner(j) == shard)(lambda j=j: local(j).wait())
        for p in range(count):
            pl.when(origin(p) != shard)(lambda p=p: arrival(p).wait_recv())

    return greeting, begin, middle, finish


def own_job(sources, targets, scratch):
    loaded, stored, held = scratch
    place = lax.axis_index("seq")
    count = lax.axis_size("seq")
    part = targets[0].shape[1]
    loads = []
    stores = []
    for c, target in enumerate(targets):
        for k, source in enumerate(sources):
            start = place * (source.shape[0] // count) + c * part
            spot = pl.ds(pl.multiple_of(start, part), part)
            n = c * len(sources) + k
            loads.append(pltpu.make_async_copy(source.at[spot], held.at[n], loaded.at[n]))
            stores.append(pltpu.make_async_copy(held.at[n], target.at[k], stored.at[n]))

    def begin():
        for load in loads:
            load.start()

    def middle():
        for load, store in zip(loads, stores):
            load.wait()
            store.start()

    def finish():
        for store in stores:
            store.wait()

    return no_greeting, begin, middle, finish


MAKERS = {
    "gather": gather_job,
    "scatter": scatter_job,
    "deal": deal_job,
    "spread": spread_job,
    "line": line_job,
    "own": own_job,
}


def job_scratch(job):
    kind, *arrays = job
    if kind == "scatter":
        _, rows, width = arrays[0].shape
        halves = pltpu.VMEM((2, rows // 2, width), BF16)
        return [
            pltpu.SemaphoreType.DMA((6,)),
            pltpu.SemaphoreType.DMA((6,)),
            pltpu.SemaphoreType.DMA((4,)),
            halves,
            halves,
            halves,
            pltpu.VMEM((rows, width), BF16),
            halves,
            pltpu.VMEM((rows, width), F32),
        ]
    if kind == "own":
        count = CHUNKS * len(arrays)
        rows, width = arrays[0].shape
        part = rows // lax.axis_size("seq") // CHUNKS
        return [
            pltpu.SemaphoreType.DMA((count,)),
            pltpu.SemaphoreType.DMA((count,)),
            pltpu.VMEM((count, part, width), BF16),
        ]
    moves = [
        pltpu.SemaphoreType.DMA((4,)),
        pltpu.SemaphoreType.DMA((4,)),
        pltpu.SemaphoreType.DMA((2,)),
    ]
    if kind == "deal":
        return moves
    if kind == "line":
        steps = lax.axis_size("fsdp") // 2
        return [pltpu.SemaphoreType.DMA((steps,))] * 4 + [pltpu.SemaphoreType.DMA((1,))]
    moves.append(pltpu.VMEM(arrays[0].shape, BF16))
    if kind == "spread":
        moves += [
            pltpu.SemaphoreType.DMA((4,)),
            pltpu.SemaphoreType.DMA((4,)),
            pltpu.SemaphoreType.DMA((1,)),
        ]
    return moves


def job_results(job):
    kind, *arrays = job
    shape = arrays[0].shape
    if kind == "gather":
        return [jax.ShapeDtypeStruct((4,) + shape, BF16)]
    if kind == "scatter":
        return [jax.ShapeDtypeStruct(shape[1:], F32)]
    if kind == "deal":
        return [jax.ShapeDtypeStruct((shape[0] // 4,) + shape[1:], BF16)]
    if kind == "spread":
        return [jax.ShapeDtypeStruct((4,) + shape, BF16)] * 2
    if kind == "line":
        return [jax.ShapeDtypeStruct((lax.axis_size("fsdp"),) + shape, BF16)]
    part = shape[0] // lax.axis_size("seq") // CHUNKS
    return [jax.ShapeDtypeStruct((len(arrays), part) + shape[1:], BF16)] * CHUNKS


def plain_job(job):
    kind, *arrays = job
    seqs = lax.axis_size("seq")
    shards = lax.axis_size("fsdp")
    per = shards // seqs
    ends = [(s, h, s * shards + s * per + h) for s in range(seqs) for h in range(per)]
    if kind == "gather":
        return [lax.all_gather(arrays[0], "seq", axis=0)]
    if kind == "scatter":
        return [lax.psum_scatter(arrays[0], "seq", scatter_dimension=0).astype(F32)]
    if kind == "deal":
        rows = arrays[0].shape[0] // seqs
        total = None
        for j in range(seqs):
            moves = [(end, s * shards + h * seqs + j) for s, h, end in ends]
            got = lax.ppermute(arrays[0][j * rows : (j + 1) * rows], ("seq", "fsdp"), moves)
            total = got if total is None else total + got
        return [total]
    if kind == "line":
        return [lax.all_gather(arrays[0], "fsdp", axis=0)]
    if kind == "spread":
        gathered = lax.all_gather(arrays[0], "seq", axis=0)
        pieces = []
        for p in range(seqs):
            total = None
            for q in range(seqs):
                moves = [
                    (s * shards + h * seqs + p, s * shards + q * per + h)
                    for s in range(seqs)
                    for h in range(per)
                ]
                got = lax.ppermute(gathered[q], ("seq", "fsdp"), moves)
                total = got if total is None else total + got
            pieces.append(total)
        return [gathered, jnp.stack(pieces)]
    own_rows = arrays[0].shape[0] // seqs
    part = own_rows // CHUNKS
    start = lax.axis_index("seq") * own_rows
    return [
        jnp.stack([lax.dynamic_slice_in_dim(w, start + c * part, part, 0) for w in arrays])
        for c in range(CHUNKS)
    ]


def meet(greetings):
    place = lax.axis_index("seq")
    barrier = pltpu.get_barrier_semaphore()
    for device in (over_one(place), over_two(place)):
        greet(barrier, {"seq": device})
    peers = 2
    for greeting in greetings:
        peers = peers + greeting(barrier)
    pl.semaphore_wait(barrier, peers)


def call(
    body, operands, in_specs, out_shape, out_specs, jobs, number, after=None,
    grid=(), scratch=(), cost=None, name=None, late=(),
):
    plain = lax.axis_size("seq") != 4
    results = [v for job in jobs for v in plain_job(job)] if plain else []
    inside = [] if plain else jobs
    extra = [] if after is None else [after]
    job_shapes = [job_scratch(job) for job in inside]
    job_outs = [job_results(job) for job in inside]
    n_in = len(operands)
    n_out = len(out_shape)

    def kernel(*refs):
        refs = list(refs)

        def take(count):
            taken, refs[:] = refs[:count], refs[count:]
            return taken

        ins = take(n_in)
        take(len(extra))
        sources = [take(len(job) - 1) for job in inside]
        outs = take(n_out)
        targets = [take(len(shapes)) for shapes in job_outs]
        held = take(len(scratch))
        loaded = take(len(late))
        marks = take(1) if late else []
        loads = [
            pltpu.make_async_copy(ins[n], ref, marks[0].at[k])
            for k, (n, ref) in enumerate(zip(late, loaded))
        ]
        for n, ref in zip(late, loaded):
            ins[n] = ref
        phases = [
            MAKERS[job[0]](source, target, take(len(shapes)))
            for job, source, target, shapes in zip(inside, sources, targets, job_shapes)
        ]

        def hook(k):
            if k == 0 and phases:
                meet([phase[0] for phase in phases])
            for phase in phases:
                phase[k + 1]()
            if k == 0:
                for load in loads:
                    load.start()
                for load in loads:
                    load.wait()

        body(hook, ins, outs, held)

    given = {}
    if inside:
        given = {"collective_id": number, "has_side_effects": True}
    arrays = [array for job in inside for array in job[1:]]
    in_specs = [ANY if n in late else spec for n, spec in enumerate(in_specs)]
    late_shapes = [pltpu.VMEM(operands[n].shape, operands[n].dtype) for n in late]
    if late:
        late_shapes.append(pltpu.SemaphoreType.DMA((len(late),)))
    shapes = [shape for shapes in job_outs for shape in shapes]
    made = pl.pallas_call(
        kernel,
        grid=grid,
        out_shape=tuple(out_shape) + tuple(shapes),
        in_specs=list(in_specs) + [ANY] * (len(extra) + len(arrays)),
        out_specs=tuple(out_specs) + (ANY,) * len(shapes),
        scratch_shapes=list(scratch)
        + late_shapes
        + [shape for shapes in job_shapes for shape in shapes],
        compiler_params=pltpu.CompilerParams(vmem_limit_bytes=VMEM_LIMIT, **given),
        cost_estimate=cost,
        name=name,
    )(*operands, *extra, *arrays)
    return list(made[:n_out]), list(made[n_out:]) + results


def transfer(jobs, number, after=None):
    if lax.axis_size("seq") != 4:
        return [v for job in jobs for v in plain_job(job)]

    def body(hook, ins, outs, held):
        for k in range(3):
            hook(k)

    return call(body, [], [], [], [], jobs, number, after, name="transfer")[1]


def partner(v):
    lane = lax.broadcasted_iota(jnp.int32, v.shape, 1)
    return jnp.where(lane % HEAD < HEAD // 2, pltpu.roll(v, 96, 1), pltpu.roll(v, 32, 1))


def head_mean(v, ones):
    high = v.astype(BF16)
    rest = (v - high.astype(F32)).astype(BF16)
    return dot(high, ones) + dot(rest, ones)


def true_chunk(place, c, count):
    if count != 4:
        return c
    low = 1 - place % 2 if c % 2 else place % 2
    high = 1 - place // 2 if c // 2 else place // 2
    return low + 2 * high


def prepare_heads(sizes, place, qkv_ref, qg_ref, kg_ref, cos_ref, sin_ref, ones, q_s, k_s, v_s):
    hq, hkv, _ = sizes
    seqs, rows_in, _ = qkv_ref.shape
    for c in range(seqs):
        j = true_chunk(place, c, seqs)
        rows = slice(c * rows_in, (c + 1) * rows_in)
        cos = cos_ref[rows, :]
        sin = sin_ref[rows, :]
        for p in range((hq + hkv) // 2):
            is_query = p < hq // 2
            x = qkv_ref[j, :, p * 128 : (p + 1) * 128].astype(F32)
            gain = qg_ref[...] * HEAD**-0.5 if is_query else kg_ref[...]
            y = x * lax.rsqrt(head_mean(x * x, ones) + EPSILON) * gain
            y = (y * cos + partner(y) * sin).astype(BF16)
            for t in range(2):
                part = y[:, t * HEAD : (t + 1) * HEAD]
                if is_query:
                    q_s[2 * p + t, rows, :] = part
                else:
                    k_s[2 * p - hq + t, rows, :] = part
        for t in range(hkv):
            start = (hq + hkv + t) * HEAD
            v_s[t, rows, :] = qkv_ref[j, :, start : start + HEAD]


def allowed_keys(block, first, keys, length):
    bound = jnp.minimum(first + lax.broadcasted_iota(jnp.int32, (block, 1), 0), length - 1)
    return lax.broadcasted_iota(jnp.int32, (block, keys), 1) <= bound


def attend_kernel(sizes, hook, ins, outs, held):
    len_ref, normal_ref, weight_ref, qg_ref, kg_ref, cos_ref, sin_ref, ones_ref, *out_w = ins
    out_ref, lse_ref, qkv_ref, *left = outs
    q_s, k_s, v_s, o_s = held
    hook(0)

    @pl.loop(0, qkv_ref.shape[0])
    def _(j):
        qkv_ref[j] = dot(normal_ref[j], weight_ref[...]).astype(BF16)

    hq, hkv, group = sizes
    seqs, rows_in, _ = qkv_ref.shape
    place = lax.axis_index("seq")
    prepare_heads(
        sizes, place, qkv_ref, qg_ref, kg_ref, cos_ref, sin_ref, ones_ref[...], q_s, k_s, v_s
    )
    for i in range(seqs * rows_in // BLOCK):
        keys = (i + 1) * BLOCK
        rows = slice(i * BLOCK, (i + 1) * BLOCK)
        keep = allowed_keys(BLOCK, i * BLOCK, keys, len_ref[0])

        def one_head(h, _):
            kv = h // group
            scores = dot(q_s[h, rows, :], k_s[kv, :keys, :], NT)
            scores = jnp.where(keep, scores, NEGATIVE)
            highest = jnp.max(scores, axis=1, keepdims=True)
            shifted = jnp.exp(scores - highest)
            total = jnp.sum(shifted, axis=1, keepdims=True)
            mixed = dot(shifted.astype(BF16), v_s[kv, :keys, :]) / total
            o_s[h, rows, :] = mixed.astype(BF16)
            lse_ref[h, rows, :] = highest + jnp.log(total)
            return 0

        lax.fori_loop(0, hq, one_head, 0, unroll=min(4, hq))
        if i == seqs * rows_in // BLOCK - 2:
            hook(1)
    for c in range(seqs):
        j = true_chunk(place, c, seqs)
        rows = slice(c * rows_in, (c + 1) * rows_in)
        for p in range(hq // 2):
            out_ref[j, :, p * 128 : (p + 1) * 128] = jnp.concatenate(
                [o_s[2 * p, rows, :], o_s[2 * p + 1, rows, :]], axis=1
            )
    for out_w_ref, left_ref in zip(out_w, left):
        for j in range(seqs):
            left_ref[j] = dot(out_ref[j], out_w_ref[...]).astype(BF16)
    hook(2)


def out_weight_grads(grads_ref, shards, slots):
    width = slots[0][0].shape[-1]
    model = slots[0][1].shape[-1]
    tile = min(256, width)
    piece = width // shards
    held = model // shards
    blocks = held // piece
    columns = model // blocks
    for t in range(width // tile):
        total = None
        for mixed_ref, res_ref in slots:
            rows = mixed_ref.shape[0] * mixed_ref.shape[1]
            mixed = mixed_ref[:, :, t * tile : (t + 1) * tile].reshape(rows, tile)
            term = dot(mixed, res_ref[...].reshape(rows, model), TN)
            total = term if total is None else total + term
        total = total.astype(BF16)
        for p in range(tile // piece):
            first = (t * (tile // piece) + p) * held
            for c in range(blocks):
                grads_ref[first + c * piece : first + (c + 1) * piece, :] = total[
                    p * piece : (p + 1) * piece, c * columns : (c + 1) * columns
                ]


def attend_back_kernel(sizes, shards, hook, ins, outs, held):
    (
        len_ref, qkv_ref, res_ref, out_w_ref, qkv_w_ref, lse_ref,
        qg_ref, kg_ref, cos_ref, sin_ref, ones_ref, *others,
    ) = ins
    dqkv_ref, dgain_ref, pull_ref, *out_grads = outs
    q_s, k_s, v_s, cot_s, dq_s, dk_s, dv_s = held
    hook(0)
    hq, hkv, group = sizes
    seqs, rows_in, _ = qkv_ref.shape
    place = lax.axis_index("seq")
    ones = ones_ref[...]
    prepare_heads(sizes, place, qkv_ref, qg_ref, kg_ref, cos_ref, sin_ref, ones, q_s, k_s, v_s)
    for c in range(seqs):
        j = true_chunk(place, c, seqs)
        cots = dot(res_ref[j], out_w_ref[...], NT).astype(BF16)
        for h in range(hq):
            cot_s[h, c * rows_in : (c + 1) * rows_in, :] = cots[:, h * HEAD : (h + 1) * HEAD]
    dk_s[...] = jnp.zeros_like(dk_s)
    dv_s[...] = jnp.zeros_like(dv_s)
    for i in range(seqs * rows_in // BLOCK):
        keys = (i + 1) * BLOCK
        rows = slice(i * BLOCK, (i + 1) * BLOCK)
        keep = allowed_keys(BLOCK, i * BLOCK, keys, len_ref[0])

        def one_head(h, _):
            kv = h // group
            q = q_s[h, rows, :]
            cot = cot_s[h, rows, :]
            k = k_s[kv, :keys, :]
            scores = jnp.where(keep, dot(q, k, NT), NEGATIVE)
            probs = jnp.exp(scores - lse_ref[h, rows, :])
            prob_cot = dot(cot, v_s[kv, :keys, :], NT)
            inner = jnp.sum(probs * prob_cot, axis=1, keepdims=True)
            score_cot = (probs * (prob_cot - inner)).astype(BF16)
            dq_s[h, rows, :] = dot(score_cot, k) * HEAD**-0.5
            dk_s[kv, :keys, :] += dot(score_cot, q, TN)
            dv_s[kv, :keys, :] += dot(probs.astype(BF16), cot, TN)
            return 0

        lax.fori_loop(0, hq, one_head, 0, unroll=min(4, hq))
        if i == seqs * rows_in // BLOCK - 2:
            for grads_ref in out_grads:
                before_ref, here_ref, res_before_ref = others
                out_weight_grads(
                    grads_ref, shards, ((before_ref, res_before_ref), (here_ref, res_ref))
                )
            hook(1)
    gain_sums = [jnp.zeros((1, 128), F32), jnp.zeros((1, 128), F32)]
    for c in range(seqs):
        j = true_chunk(place, c, seqs)
        rows = slice(c * rows_in, (c + 1) * rows_in)
        cos = cos_ref[rows, :]
        sin = sin_ref[rows, :]
        for p in range((hq + hkv) // 2):
            is_query = p < hq // 2
            x = qkv_ref[j, :, p * 128 : (p + 1) * 128].astype(F32)
            gain = qg_ref[...] if is_query else kg_ref[...]
            source, first = (dq_s, 2 * p) if is_query else (dk_s, 2 * p - hq)
            turned = jnp.concatenate([source[first, rows, :], source[first + 1, rows, :]], axis=1)
            scale = lax.rsqrt(head_mean(x * x, ones) + EPSILON)
            straight = turned * cos + partner(turned * sin)
            unit = x * scale
            which = 0 if is_query else 1
            gain_sums[which] += jnp.sum(straight * unit, axis=0, keepdims=True)
            pulled = gain * straight
            dx = scale * (pulled - unit * head_mean(unit * pulled, ones))
            dqkv_ref[j, :, p * 128 : (p + 1) * 128] = dx.astype(BF16)
        for p in range(hkv // 2):
            start = (hq + hkv) * HEAD + p * 128
            dqkv_ref[j, :, start : start + 128] = jnp.concatenate(
                [dv_s[2 * p, rows, :], dv_s[2 * p + 1, rows, :]], axis=1
            ).astype(BF16)
    dgain_ref[0:1, :] = gain_sums[0]
    dgain_ref[1:2, :] = gain_sums[1]

    @pl.loop(0, seqs)
    def _(j):
        pull_ref[j] = dot(dqkv_ref[j], qkv_w_ref[...], NT).astype(BF16)

    hook(2)


def position_tables(length):
    places = np.arange(length, dtype=np.float32)
    half = HEAD // 2
    freqs = np.float32(ROPE_BASE) ** (-(np.arange(half, dtype=np.float32) * 2.0) / HEAD)
    angles = places[:, None] * freqs.astype(np.float32)[None, :]
    cos = np.cos(angles).astype(np.float32)
    sin = np.sin(angles).astype(np.float32)
    ones = np.kron(np.eye(2), np.ones((HEAD, HEAD)) / HEAD)
    return (
        jnp.asarray(np.concatenate([cos] * 4, axis=1)),
        jnp.asarray(np.concatenate([-sin, sin, -sin, sin], axis=1)),
        jnp.asarray(ones, dtype=BF16),
    )


def attend(sizes, length, normal, weight, gains, tables, jobs, number, after, out_w=()):
    seqs, rows_in, _ = normal.shape
    hq, hkv, _ = sizes
    slot = seqs * rows_in
    return call(
        functools.partial(attend_kernel, sizes),
        [length, normal, weight, *gains, *tables, *out_w],
        [SMEM] + [VMEM] * (7 + len(out_w)),
        [
            jax.ShapeDtypeStruct((seqs, rows_in, hq * HEAD), BF16),
            jax.ShapeDtypeStruct((hq, slot, 1), F32),
            jax.ShapeDtypeStruct((seqs, rows_in, weight.shape[1]), BF16),
        ]
        + [jax.ShapeDtypeStruct(normal.shape, BF16)] * len(out_w),
        [VMEM] * (3 + len(out_w)),
        jobs,
        number,
        after,
        scratch=[
            pltpu.VMEM((hq, slot, HEAD), BF16),
            pltpu.VMEM((hkv, slot, HEAD), BF16),
            pltpu.VMEM((hkv, slot, HEAD), BF16),
            pltpu.VMEM((hq, slot, HEAD), BF16),
        ],
        cost=pl.CostEstimate(
            flops=56 * hq * slot * slot * HEAD, bytes_accessed=1 << 23, transcendentals=0
        ),
        name="attend",
        late=(1, 2) + tuple(range(8, 8 + len(out_w))),
    )


def attend_back(
    sizes, length, qkv, res, out_w, qkv_w, lse, gains, tables, jobs, number, after, others=()
):
    seqs, rows_in, width = qkv.shape
    hq, hkv, _ = sizes
    slot = seqs * rows_in
    shards = lax.axis_size("fsdp")
    model = res.shape[-1]
    columns = hq * HEAD // shards * model // (model // shards)
    return call(
        functools.partial(attend_back_kernel, sizes, shards),
        [length, qkv, res, out_w, qkv_w, lse, *gains, *tables, *others],
        [SMEM] + [VMEM] * (10 + len(others)),
        [
            jax.ShapeDtypeStruct((seqs, rows_in, width), BF16),
            jax.ShapeDtypeStruct((2, 128), F32),
            jax.ShapeDtypeStruct(res.shape, BF16),
        ]
        + [jax.ShapeDtypeStruct((model, columns), BF16)] * bool(others),
        [VMEM, VMEM, VMEM] + [VMEM] * bool(others),
        jobs,
        number,
        after,
        scratch=[
            pltpu.VMEM((hq, slot, HEAD), BF16),
            pltpu.VMEM((hkv, slot, HEAD), BF16),
            pltpu.VMEM((hkv, slot, HEAD), BF16),
            pltpu.VMEM((hq, slot, HEAD), BF16),
            pltpu.VMEM((hq, slot, HEAD), F32),
            pltpu.VMEM((hkv, slot, HEAD), F32),
            pltpu.VMEM((hkv, slot, HEAD), F32),
        ],
        cost=pl.CostEstimate(
            flops=88 * hq * slot * slot * HEAD, bytes_accessed=1 << 23, transcendentals=0
        ),
        name="attend_back",
        late=(1, 2, 3, 4, 5) + tuple(range(11, 11 + len(others))),
    )


def hooked(hook, step, steps, work):
    pl.when(step == 0)(lambda: hook(0))
    work(lambda: pl.when(step == (3 * steps) // 5)(lambda: hook(1)))
    pl.when(step == steps - 1)(lambda: hook(2))


def ffn_kernel(steps, hook, ins, outs, held):
    step = pl.program_id(0)
    weights_ref, loaded = held
    loads = [
        pltpu.make_async_copy(ins[2].at[:, k], weights_ref.at[k], loaded.at[k]) for k in range(3)
    ]

    def first(act):
        pl.when(step == 0)(act)

    def work(late):
        for load in loads:
            first(load.start)
        ffn_tile(late, first, loads, *ins[:2], weights_ref, ins[3:], *outs)

    hooked(hook, step, steps, work)


def ffn_tile(late, first, loads, mid_ref, cot_ref, weights_ref, sums, acts_ref, pull_ref):
    model = mid_ref.shape[-1]
    hidden = acts_ref.shape[-1]
    whole = (hidden, model)
    mid = mid_ref[...]
    first(loads[0].wait)
    gate = dot(mid, weights_ref[0].reshape(whole), NT)
    first(loads[1].wait)
    up = dot(mid, weights_ref[1].reshape(whole), NT)
    first(loads[2].wait)
    mids_cot = dot(cot_ref[...], weights_ref[2].reshape(whole), NT)
    late()
    sigmoid = jax.nn.sigmoid(gate)
    active = gate * sigmoid
    gate_cot = (mids_cot * up * sigmoid * (1.0 + gate * (1.0 - sigmoid))).astype(BF16)
    up_cot = (mids_cot * active).astype(BF16)
    acts_ref[0] = gate_cot
    acts_ref[1] = up_cot
    acts_ref[2] = (active * up).astype(BF16)
    pulled = dot(gate_cot, weights_ref[0].reshape(whole)) + dot(
        up_cot, weights_ref[1].reshape(whole)
    )
    for sum_ref in sums:
        pulled = pulled + sum_ref[...]
    pull_ref[...] = pulled.astype(pull_ref.dtype)


def ffn_both(mid, cot, weights, summed, last, jobs, number, after):
    tokens, model = mid.shape
    shards, _, part, _ = weights.shape
    hidden = shards * part
    tile = min(256, tokens)

    row_spec = pl.BlockSpec((tile, model), lambda i: (i, 0))
    extra = () if summed is None else (summed,)
    return call(
        functools.partial(ffn_kernel, tokens // tile),
        [mid, cot, weights, *extra],
        [row_spec, row_spec, ANY] + [row_spec] * len(extra),
        [
            jax.ShapeDtypeStruct((3, tokens, hidden), BF16),
            jax.ShapeDtypeStruct((tokens, model), BF16 if last else F32),
        ],
        [pl.BlockSpec((3, tile, hidden), lambda i: (0, i, 0)), row_spec],
        jobs,
        number,
        after,
        grid=(tokens // tile,),
        scratch=[
            pltpu.VMEM((3, shards, part, model), BF16),
            pltpu.SemaphoreType.DMA((3,)),
        ],
        cost=pl.CostEstimate(
            flops=16 * tokens * model * hidden,
            bytes_accessed=4 * tokens * model + 6 * hidden * model,
            transcendentals=0,
        ),
        name="ffn_both",
    )


def ffn_grad_kernel(slots, tiles, hook, ins, outs, held):
    acts = ins[:slots]
    others = ins[slots:]
    (out_ref,) = outs
    rows_ref, loaded = held
    kind = pl.program_id(0)
    step = kind * tiles + pl.program_id(1)
    loads = [
        pltpu.make_async_copy(other, rows_ref.at[k], loaded.at[k])
        for k, other in enumerate(others)
    ]

    def store(first):
        total = None
        for k, act in enumerate(acts):
            term = dot(act[0], rows_ref[first + k], TN)
            total = term if total is None else total + term
        out_ref[...] = total.astype(BF16).reshape(out_ref.shape)

    def work(late):
        for k, load in enumerate(loads):
            pl.when(step == 0)(load.start)
        for k, load in enumerate(loads):
            pl.when(step == (0 if k < slots else 2 * tiles))(load.wait)
        late()
        pl.when(kind < 2)(lambda: store(0))
        pl.when(kind == 2)(lambda: store(slots))

    hooked(hook, step, 3 * tiles, work)


def ffn_grads(acts, mids, cots, shards, jobs, number, after):
    slots = len(acts)
    _, tokens, hidden = acts[0].shape
    model = mids[0].shape[-1]
    part = hidden // shards
    tile = 256
    per = tile // part
    return call(
        functools.partial(ffn_grad_kernel, slots, hidden // tile),
        [*acts, *mids, *cots],
        [pl.BlockSpec((1, tokens, tile), lambda k, i: (k, 0, i))] * slots
        + [ANY] * (2 * slots),
        [jax.ShapeDtypeStruct((shards, 3, part, model), BF16)],
        [pl.BlockSpec((per, 1, part, model), lambda k, i: (i, k, 0, 0))],
        jobs,
        number,
        after,
        grid=(3, hidden // tile),
        scratch=[
            pltpu.VMEM((2 * slots, tokens, model), BF16),
            pltpu.SemaphoreType.DMA((2 * slots,)),
        ],
        cost=pl.CostEstimate(
            flops=9 * slots * tokens * model * hidden,
            bytes_accessed=4 * slots * tokens * model,
            transcendentals=0,
        ),
        name="ffn_grads",
    )


def ffn_down_kernel(chunks, steps, hook, ins, outs, held):
    acts = ins[:chunks]
    downs = ins[chunks:]
    (out_ref,) = outs

    def work(late):
        late()
        total = None
        for act, down in zip(acts, downs):
            hidden = act.shape[-1]
            term = dot(act[0], down[...].reshape(hidden, down.shape[-1]))
            total = term if total is None else total + term
        out_ref[...] = total.astype(BF16)

    hooked(hook, pl.program_id(0), steps, work)


def ffn_down(acts, weights, jobs, number, after, true_order=False):
    chunks = len(acts)
    _, tokens, hidden = acts[0].shape
    shards, _, part, model = weights[0].shape
    tile = min(256, tokens)
    def spot(i):
        if not true_order or lax.axis_size("seq") != 4:
            return i
        place = lax.axis_index("seq")
        low = (place % 2 + i % 2) % 2
        high = (place // 2 + i // 2) % 2
        return low + 2 * high

    act_spec = pl.BlockSpec((1, tile, hidden), lambda i: (2, i, 0))
    down_spec = pl.BlockSpec(
        (shards, 1, part, model),
        lambda i: (0, 2, 0, 0),
        pipeline_mode=pl.Buffered(buffer_count=1),
    )
    return call(
        functools.partial(ffn_down_kernel, chunks, tokens // tile),
        [*acts, *weights],
        [act_spec] * chunks + [down_spec] * chunks,
        [jax.ShapeDtypeStruct((tokens, model), BF16)],
        [pl.BlockSpec((tile, model), lambda i: (spot(i), 0))],
        jobs,
        number,
        after,
        grid=(tokens // tile,),
        cost=pl.CostEstimate(
            flops=4 * chunks * tokens * model * hidden,
            bytes_accessed=chunks * hidden * (tokens + model) * 2,
            transcendentals=0,
        ),
        name="ffn_down",
    )


def place_kernel(place_ref, parts_ref, *refs):
    for kind, out_ref in enumerate(refs[-3:]):
        out_ref[0, 0] = parts_ref[0, kind].astype(F32)


def place_parts(place, parts, chunk, held):
    seqs, _, part, model = parts.shape
    out = jax.ShapeDtypeStruct((seqs, CHUNKS, part, model), F32)
    out_spec = pl.BlockSpec(
        (1, 1, part, model), lambda j, at: (jnp.bitwise_xor(at[0], j), chunk, 0, 0)
    )
    return pl.pallas_call(
        place_kernel,
        out_shape=(out,) * 3,
        grid_spec=pltpu.PrefetchScalarGridSpec(
            num_scalar_prefetch=1,
            grid=(seqs,),
            in_specs=[pl.BlockSpec((1, 3, part, model), lambda j, at: (j, 0, 0, 0))]
            + [ANY] * len(held),
            out_specs=(out_spec,) * 3,
        ),
        input_output_aliases={2 + k: k for k in range(len(held))},
        compiler_params=pltpu.CompilerParams(vmem_limit_bytes=VMEM_LIMIT),
        cost_estimate=pl.CostEstimate(
            flops=0, bytes_accessed=18 * seqs * part * model, transcendentals=0
        ),
        name="place_parts",
    )(place, parts, *held)


def place_heads_kernel(
    place_ref, parts_ref, query_w_ref, key_w_ref, value_w_ref,
    query_ref, key_ref, value_ref, rest_ref, met_ref,
):
    edge = query_ref.shape[1]
    width = key_ref.shape[1]
    part = parts_ref[0].astype(F32)
    query_ref[...] = part[:, :edge]
    key_ref[...] = part[:, edge : edge + width]
    value_ref[...] = part[:, edge + width : edge + 2 * width]
    rest = part[:, edge + 2 * width :]
    met = jnp.zeros_like(met_ref)
    for grad_ref, weight_ref in (
        (query_ref, query_w_ref),
        (key_ref, key_w_ref),
        (value_ref, value_w_ref),
    ):
        product = grad_ref[...] * weight_ref[...].astype(F32)
        met = met + jnp.sum(product, axis=1, keepdims=True)

    @pl.when(pl.program_id(0) == 0)
    def _():
        rest_ref[...] = rest
        met_ref[...] = met

    @pl.when(pl.program_id(0) > 0)
    def _():
        rest_ref[...] += rest
        met_ref[...] += met


def place_heads(place, parts, edge, width, weights):
    seqs, rows, total = parts.shape
    rest = total - edge - 2 * width

    def column_spec(size):
        return pl.BlockSpec((rows, size), lambda j, at: (0, jnp.bitwise_xor(at[0], j)))

    return pl.pallas_call(
        place_heads_kernel,
        out_shape=[
            jax.ShapeDtypeStruct((rows, seqs * edge), F32),
            jax.ShapeDtypeStruct((rows, seqs * width), F32),
            jax.ShapeDtypeStruct((rows, seqs * width), F32),
            jax.ShapeDtypeStruct((rows, rest), F32),
            jax.ShapeDtypeStruct((rows, 128), F32),
        ],
        grid_spec=pltpu.PrefetchScalarGridSpec(
            num_scalar_prefetch=1,
            grid=(seqs,),
            in_specs=[
                pl.BlockSpec((1, rows, total), lambda j, at: (j, 0, 0)),
                column_spec(edge),
                column_spec(width),
                column_spec(width),
            ],
            out_specs=[
                column_spec(edge),
                column_spec(width),
                column_spec(width),
                pl.BlockSpec((rows, rest), lambda j, at: (0, 0)),
                pl.BlockSpec((rows, 128), lambda j, at: (0, 0)),
            ],
        ),
        compiler_params=pltpu.CompilerParams(vmem_limit_bytes=VMEM_LIMIT),
        name="place_heads",
    )(place, parts, *weights)


def scale_of(values):
    return lax.rsqrt(jnp.mean(values * values, axis=-1, keepdims=True) + EPSILON)


def normed(values, gain):
    return values * scale_of(values) * gain


def normed_back(values, gain, cot):
    scale = scale_of(values)
    pulled = cot * gain
    mean = jnp.mean(values * pulled, axis=-1, keepdims=True)
    return (
        scale * pulled - values * (scale * scale * scale) * mean,
        jnp.sum(cot * values * scale, axis=0),
    )


def follow(values, earlier):
    return lax.optimization_barrier((values, *earlier))[0]


def own_columns(weight, heads, place):
    width = heads * HEAD
    part = lax.dynamic_slice_in_dim(weight, place * width, width, 1)
    if heads % 2:
        part = jnp.pad(part, ((0, 0), (0, HEAD)))
    return part


def on_device(
    tokens,
    cotangent,
    lengths,
    attn_gain,
    query_weight,
    key_weight,
    value_weight,
    query_gain,
    key_gain,
    out_weight,
    ffn_gain,
    gate_weight,
    up_weight,
    down_weight,
):
    slots, rows, model = tokens.shape
    seqs = lax.axis_size("seq")
    shards = lax.axis_size("fsdp")
    place = lax.axis_index("seq")
    shard = lax.axis_index("fsdp")
    slot_len = rows * seqs
    query_width = query_weight.shape[1]
    kv_width = key_weight.shape[1]
    hq = query_width // seqs // HEAD
    hkv = kv_width // seqs // HEAD
    hkv_held = hkv + hkv % 2
    sizes = (hq, hkv_held, hq // hkv)
    order = (place if seqs == 4 else place * 0).reshape(1)
    tables = position_tables(slot_len)
    gains = (
        jnp.concatenate([query_gain, query_gain]).reshape(1, 2 * HEAD),
        jnp.concatenate([key_gain, key_gain]).reshape(1, 2 * HEAD),
    )

    flat = (slot_len, model)
    chunked = (seqs, rows, model)
    places = place * rows + jnp.arange(rows, dtype=jnp.int32)
    live = (places[None, :] < lengths[:, None]).astype(F32)[..., None]
    inputs = tokens.astype(F32)
    out_cot = cotangent.astype(F32) * live
    out_low = [out_cot[b].astype(BF16) for b in range(slots)]
    normal_in = [normed(inputs[b], attn_gain).astype(BF16) for b in range(slots)]

    qkv_own = jnp.concatenate(
        [
            own_columns(query_weight, hq, place),
            own_columns(key_weight, hkv, place),
            own_columns(value_weight, hkv, place),
        ],
        axis=1,
    )
    qkv_weight = lax.all_gather(qkv_own, "fsdp", axis=0, tiled=True)
    start = [
        ("gather", normal_in[0]),
        ("deal", out_weight),
        ("own", gate_weight, up_weight, down_weight),
    ]
    normal_0, out_own, *ffn_own = transfer(start, 1)
    hidden_own = gate_weight.shape[0] // seqs
    part = hidden_own // CHUNKS
    ffn_weights = [lax.all_gather(own, "fsdp", axis=0) for own in ffn_own]

    def leave(mixed):
        return dot(mixed.reshape(slot_len, -1), out_rows).astype(BF16).reshape(chunked)

    def enter_ffn(b, total):
        res = inputs[b] + total
        return res, normed(res, ffn_gain).astype(BF16)

    def heads(b, jobs, number, after, out_w=()):
        return attend(
            sizes, lengths[b : b + 1], normal_full[b].reshape(chunked), qkv_weight, gains, tables,
            jobs, number, after, out_w,
        )

    normal_full = [None] * slots
    cot_full = [None] * slots
    mid_full = [None] * slots
    normal_full[0] = normal_0
    (mixed_0, lse_0, qkv_0), (normal_full[1], out_rows) = heads(
        0, [("gather", normal_in[1]), ("line", out_own)], 2, normal_full[0]
    )
    out_rows = out_rows.reshape(-1, model)
    (mixed_1, lse_1, qkv_1, left_1), (total_0,) = heads(
        1, [("scatter", leave(mixed_0))], 3, mixed_0, (out_rows,)
    )
    qkv = [qkv_0, qkv_1]
    log_sums = [lse_0, lse_1]
    res_0, mid_0 = enter_ffn(0, total_0)
    mid_full[0], cot_full[0] = [
        v.reshape(flat)
        for v in transfer([("gather", mid_0), ("gather", out_low[0])], 4, mixed_1)
    ]

    acts = [[None] * slots for _ in range(CHUNKS)]
    pulled = [None] * slots

    def ffn_step(b, c, jobs, number, after):
        (acts[c][b], pulled[b]), results = ffn_both(
            mid_full[b], cot_full[b], ffn_weights[c], pulled[b], c == CHUNKS - 1,
            jobs, number, after,
        )
        return results

    def grad_step(c, jobs, number, after):
        (grads,), results = ffn_grads(
            acts[c], mid_full, cot_full, shards, jobs, number, after
        )
        return grads.reshape(shards, 3 * part, model), results

    def leave_ffn(b, jobs, number, after, true_order=False):
        (out,), results = ffn_down(
            [acts[c][b] for c in range(CHUNKS)], ffn_weights, jobs, number, after, true_order
        )
        return out.reshape(chunked), results

    total_1, full = ffn_step(
        0, 0, [("scatter", left_1), ("gather", out_low[1])], 5, mid_full[0]
    )
    cot_full[1] = full.reshape(flat)
    res_1, mid_1 = enter_ffn(1, total_1)
    hidden_res = [res_0, res_1]
    (full,) = ffn_step(0, 1, [("gather", mid_1)], 6, acts[0][0])
    mid_full[1] = full.reshape(flat)
    (mid_total_0,) = ffn_step(1, 0, [("scatter", pulled[0].reshape(chunked))], 7, acts[1][0])

    def pull_mid(b, total):
        pull, gain_part = normed_back(hidden_res[b], ffn_gain, total)
        cot = out_cot[b] + pull
        return cot, cot.astype(BF16), gain_part

    res_cot_0, low_0, ffn_gain_0 = pull_mid(0, mid_total_0)
    grads_0, (res_full_0,) = grad_step(0, [("gather", low_0)], 8, acts[0][1])
    ffn_sums = [lax.psum_scatter(grads_0, "fsdp", scatter_dimension=0)]
    out_0, _ = leave_ffn(0, [], 0, grads_0)
    (out_total_0,) = ffn_step(1, 1, [("scatter", out_0)], 9, out_0)
    grads_1, (mid_total_1,) = grad_step(
        1, [("scatter", pulled[1].reshape(chunked))], 10, acts[1][1]
    )
    ffn_sums.append(
        lax.psum_scatter(grads_1, "fsdp", scatter_dimension=0)
    )
    res_cot_1, low_1, ffn_gain_1 = pull_mid(1, mid_total_1)
    grad_ffn_gain = ffn_gain_0 + ffn_gain_1

    def back(b, full, jobs, number, after, others=()):
        return attend_back(
            sizes, lengths[b : b + 1], qkv[b], full, out_rows, qkv_weight, log_sums[b],
            gains, tables, jobs, number, after, others,
        )

    (dqkv_0, heads_gain_0, pull_0), (res_full_1,) = back(
        0, res_full_0, [("gather", low_1)], 11, grads_1
    )
    (dqkv_1, heads_gain_1, pull_1, out_grads), (in_total_0, ffn_parts_0) = back(
        1,
        res_full_1,
        [("scatter", pull_0), ("gather", ffn_sums[0])],
        12,
        dqkv_0,
        (mixed_0, mixed_1, res_full_0),
    )
    head_gain = heads_gain_0 + heads_gain_1
    dqkv = [v.reshape(slot_len, -1) for v in (dqkv_0, dqkv_1)]
    held = model // shards
    piece = hq * HEAD // shards
    blocks = held // piece
    head_sums = jnp.pad(
        (head_gain[:, :HEAD] + head_gain[:, HEAD:]).reshape(2, shards, HEAD // shards),
        ((0, 0), (0, 0), (0, held - HEAD // shards)),
    ).reshape(2, model)
    gain_columns = jnp.stack([grad_ffn_gain, head_sums[0], head_sums[1]], axis=1).astype(BF16)
    attn_grads = jnp.concatenate(
        [
            sum(dot(normal_full[b].reshape(flat), dqkv[b], TN) for b in range(slots)).astype(BF16),
            jnp.pad(gain_columns, ((0, 0), (0, 125))),
            out_grads,
        ],
        axis=1,
    )
    pull, _ = normed_back(inputs[0], attn_gain, in_total_0)
    tokens_0 = (res_cot_0 + pull).astype(BF16)
    ffn_grad = place_parts(order, ffn_parts_0.reshape(seqs, 3, part, model), 0, ())
    out_1, (in_total_1,) = leave_ffn(1, [("scatter", pull_1)], 13, ffn_sums[1], True)
    attn_sums = lax.psum_scatter(
        follow(attn_grads, [ffn_sums[1], ffn_grad[0], tokens_0]), "fsdp", scatter_dimension=0, tiled=True
    )
    (ffn_parts_1,) = transfer([("gather", ffn_sums[1])], 15, in_total_1)
    ffn_grad = place_parts(order, ffn_parts_1.reshape(seqs, 3, part, model), 1, ffn_grad)
    out_edge = attn_sums.shape[1] - model // blocks
    heads_all, _, out_parts = transfer(
        [("gather", attn_sums[:, :out_edge]), ("spread", attn_sums[:, out_edge:])],
        14,
        ffn_grad[0],
    )
    grad_out = jnp.swapaxes(
        out_parts.reshape(seqs, blocks, piece, model // blocks), 1, 2
    ).reshape(held, model)
    pull, _ = normed_back(inputs[1], attn_gain, in_total_1)
    grad_tokens = [tokens_0, (res_cot_1 + pull).astype(BF16)]
    out_total_1 = lax.psum_scatter(
        follow(out_1, [attn_sums, ffn_parts_1]), "seq", scatter_dimension=0
    ).astype(F32)
    output = [
        (live[b] * (hidden_res[b] + total)).astype(BF16)
        for b, total in enumerate((out_total_0, out_total_1))
    ]
    ffn_grad = [v.reshape(seqs * hidden_own, model) for v in ffn_grad]

    edge = hq * HEAD
    width = hkv_held * HEAD
    if hkv == hkv_held:
        grad_query, grad_key, grad_value, gain_sums, met = place_heads(
            order, heads_all, edge, width, (query_weight, key_weight, value_weight)
        )
        met = met[:, 0]
    else:
        heads_all = jnp.moveaxis(heads_all, 0, 1).astype(F32)
        last = edge + width
        grad_query = heads_all[..., :edge].reshape(held, query_width)
        grad_key = heads_all[..., edge : edge + hkv * HEAD].reshape(held, kv_width)
        grad_value = heads_all[..., last : last + hkv * HEAD].reshape(held, kv_width)
        gain_sums = jnp.sum(heads_all[..., last + width :], axis=1)
        met = sum(
            jnp.sum(grad * weight.astype(F32), axis=1)
            for grad, weight in (
                (grad_query, query_weight),
                (grad_key, key_weight),
                (grad_value, value_weight),
            )
        )
    grad_attn_gain = met / lax.dynamic_slice_in_dim(attn_gain, shard * held, held, 0)

    return (
        jnp.stack(output),
        jnp.stack(grad_tokens),
        grad_attn_gain,
        grad_query,
        grad_key,
        grad_value,
        gain_sums[: HEAD // shards, 1],
        gain_sums[: HEAD // shards, 2],
        grad_out.astype(F32),
        gain_sums[:, 0],
        ffn_grad[0],
        ffn_grad[1],
        ffn_grad[2],
    )


def solution(mesh):
    return jax.shard_map(
        on_device,
        mesh=mesh,
        in_specs=(
            P("fsdp", "seq", None),
            P("fsdp", "seq", None),
            P("fsdp"),
            P(),
            P("fsdp", None),
            P("fsdp", None),
            P("fsdp", None),
            P(),
            P(),
            P("fsdp", None),
            P(),
            P("fsdp", None),
            P("fsdp", None),
            P("fsdp", None),
        ),
        out_specs=(
            P("fsdp", "seq", None),
            P("fsdp", "seq", None),
            P("fsdp"),
            P("fsdp", None),
            P("fsdp", None),
            P("fsdp", None),
            P("fsdp"),
            P("fsdp"),
            P("fsdp", None),
            P("fsdp"),
            P("fsdp", None),
            P("fsdp", None),
            P("fsdp", None),
        ),
        check_vma=False,
    )
```
